32 devices in a mesh: seq: 8 (over z, y), head: 4 (over x, core).
Axes of the slice: x: 2, y: 2, z: 4, core: 2. Of those that a mesh axis runs over, the one named last changes fastest.
Arguments:
- block_input: bfloat16 [4096, 1024], P('seq'), may hold values from -6 to 6
- norm1_gain: bfloat16 [1024], replicated, may hold values from 0.5 to 1.5
- w_query: bfloat16 [1024, 1024], P(None, 'head'), may hold values from -0.1875 to 0.1875
- w_key: bfloat16 [1024, 1024], P(None, 'head'), may hold values from -0.1875 to 0.1875
- w_value: bfloat16 [1024, 2048], P(None, 'head'), may hold values from -0.1875 to 0.1875
- w_gate: bfloat16 [1024, 2048], P(None, 'head'), may hold values from -0.1875 to 0.1875
- w_decay: bfloat16 [1024, 8], P(None, 'head'), may hold values from -0.1875 to 0.1875
- w_beta: bfloat16 [1024, 8], P(None, 'head'), may hold values from -0.1875 to 0.1875
- conv_query: bfloat16 [4, 1024], P(None, 'head'), may hold values from -3 to 3
- conv_key: bfloat16 [4, 1024], P(None, 'head'), may hold values from -3 to 3
- conv_value: bfloat16 [4, 2048], P(None, 'head'), may hold values from -3 to 3
- decay_rate: float32 [8], P('head'), may hold values from 4.8828126e-05 to 0.08
- out_gain: bfloat16 [256], replicated, may hold values from 0.5 to 1.5
- w_out: bfloat16 [2048, 1024], P('head'), may hold values from -0.25 to 0.25
- norm2_gain: bfloat16 [1024], replicated, may hold values from 0.5 to 1.5
- w_ffn_gate: bfloat16 [1024, 2816], P(None, 'head'), may hold values from -0.1875 to 0.1875
- w_ffn_up: bfloat16 [1024, 2816], P(None, 'head'), may hold values from -0.1875 to 0.1875
- w_ffn_down: bfloat16 [2816, 1024], P('head'), may hold values from -0.21875 to 0.21875
- cotangent: bfloat16 [4096, 1024], P('seq'), may hold values from -6 to 6
Outputs:
- out: bfloat16 [4096, 1024], P('seq')
- d_block_input: float32 [4096, 1024], P('seq')
- d_norm1_gain: float32 [1024], P('seq')
- d_w_query: float32 [1024, 1024], P('seq', 'head')
- d_w_key: float32 [1024, 1024], P('seq', 'head')
- d_w_value: float32 [1024, 2048], P('seq', 'head')
- gate_weight_gradient: float32 [1024, 2048], P('seq', 'head')
- d_w_decay: float32 [1024, 8], P('seq', 'head')
- d_w_beta: float32 [1024, 8], P('seq', 'head')
- d_conv_query: float32 [4, 1024], P(None, 'head')
- d_conv_key: float32 [4, 1024], P(None, 'head')
- d_conv_value: float32 [4, 2048], P(None, 'head')
- d_decay_rate: float32 [8], P('head')
- d_out_gain: float32 [256], P('seq')
- d_w_out: float32 [2048, 1024], P('head', 'seq')
- d_norm2_gain: float32 [1024], P('seq')
- d_w_ffn_gate: float32 [1024, 2816], P('seq', 'head')
- d_w_ffn_up: float32 [1024, 2816], P('seq', 'head')
- d_w_ffn_down: float32 [2816, 1024], P('head', 'seq')
The draws below stay inside these ranges and needn't reach their ends.
All inputs are finite; a program needn't handle non-finite values.
Results may differ from the reference program's by a relative error of at most 0.033.
Values may be sent and summed in bfloat16 or wider, within the bound.
No kernel may reach another device: no remote copies, remote signals or barrier semaphores. Data moves between devices by JAX's collectives and lax.ppermute only.
A program may use at most 192 MiB of HBM per device.

```python
import math
import jax
import jax.numpy as jnp
from jax import lax

D = 1024
HEADS = 8
KEY = 128
VALUE = 256
FF = 2816
TAPS = 4
GROUP = 64
TOKENS = 4096
HK = 1024
HV = 2048


def level_of(own_key, dims, pieces, least, high):
    loudness = 1.0
    for axis_at, blocks in pieces:
        steps = jax.random.uniform(jax.random.fold_in(jax.random.fold_in(own_key, 6), axis_at), (blocks,), jnp.float32, least / len(pieces), high / len(pieces))
        loudness = loudness * jnp.repeat(jnp.exp(steps), dims[axis_at] // blocks).reshape((-1,) + (1,) * (len(dims) - 1 - axis_at))
    return loudness


def noise(rng, extent, deviation, reach, split=(), dtype=jnp.bfloat16):
    level = level_of(rng, extent, split, -0.22, 0.18) if split else 1.0
    values = jax.random.normal(rng, extent, jnp.float32) * deviation * level
    return jnp.minimum(jnp.maximum(values, -reach), reach).astype(dtype)


def setup_inputs(seed: int = 0) -> dict:
    streams_of = jax.random.split(jax.random.key(seed), 20)
    return {
        "block_input": noise(streams_of[0], (TOKENS, D), 1.0, 6.0, ((0, 8),)),
        "norm1_gain": jnp.clip(1.0 + 0.1 * jax.random.normal(streams_of[1], (D,), jnp.float32), 0.5, 1.5).astype(jnp.bfloat16),
        "w_query": noise(streams_of[2], (D, HK), D ** -0.5, 0.1875, ((1, 4),)),
        "w_key": noise(streams_of[3], (D, HK), D ** -0.5, 0.1875, ((1, 4),)),
        "w_value": noise(streams_of[4], (D, HV), D ** -0.5, 0.1875, ((1, 4),)),
        "w_gate": noise(streams_of[5], (D, HV), D ** -0.5, 0.1875, ((1, 4),)),
        "w_decay": noise(streams_of[6], (D, HEADS), D ** -0.5, 0.1875, ((1, 4),)),
        "w_beta": noise(streams_of[7], (D, HEADS), D ** -0.5, 0.1875, ((1, 4),)),
        "conv_query": noise(streams_of[8], (TAPS, HK), TAPS ** -0.5, 3.0, ((1, 4),)),
        "conv_key": noise(streams_of[9], (TAPS, HK), TAPS ** -0.5, 3.0, ((1, 4),)),
        "conv_value": noise(streams_of[10], (TAPS, HV), TAPS ** -0.5, 3.0, ((1, 4),)),
        "decay_rate": jnp.clip(jnp.exp(math.log(0.08) - 7.4014754 * jax.random.uniform(streams_of[11], (HEADS,), jnp.float32) ** level_of(streams_of[11], (HEADS,), ((0, 4),), -0.2, 0.2)), 4.882812572759576e-05, 0.08),
        "out_gain": jnp.clip(1.0 + 0.1 * jax.random.normal(streams_of[12], (VALUE,), jnp.float32), 0.5, 1.5).astype(jnp.bfloat16),
        "w_out": noise(streams_of[13], (HV, D), (HV // 4) ** -0.5, 0.25, ((0, 4),)),
        "norm2_gain": jnp.clip(1.0 + 0.1 * jax.random.normal(streams_of[14], (D,), jnp.float32), 0.5, 1.5).astype(jnp.bfloat16),
        "w_ffn_gate": noise(streams_of[15], (D, FF), D ** -0.5, 0.1875, ((1, 4),)),
        "w_ffn_up": noise(streams_of[16], (D, FF), D ** -0.5, 0.1875, ((1, 4),)),
        "w_ffn_down": noise(streams_of[17], (FF, D), (FF // 4) ** -0.5, 0.21875, ((0, 4),)),
        "cotangent": noise(streams_of[18], (TOKENS, D), 1.0, 6.0, ((0, 8),)),
    }


highest_precision = lax.Precision.HIGHEST
epsilon = 1e-06

@jax.custom_vjp
def low(v):
    return lax.optimization_barrier(v.astype(jnp.bfloat16)).astype(jnp.float32)

@jax.custom_vjp
def low_back(v):
    return v

def low_keep(v):
    return (low(v), None)

def low_pass(kept, grad):
    return (grad,)

def back_keep(v):
    return (v, None)

def back_low(kept, grad):
    return (low(grad),)
low.defvjp(low_keep, low_pass)
low_back.defvjp(back_keep, back_low)

def row_norm(values, gain_vec):
    return values * lax.rsqrt(lax.optimization_barrier(jnp.mean(values * values, axis=-1, keepdims=True)) + epsilon) * gain_vec

def unit_rows(values, scale_factor):
    return values * lax.rsqrt(lax.optimization_barrier(jnp.sum(values * values, axis=-1, keepdims=True)) + epsilon) * scale_factor

def matmul_high(first_operand, second_operand):
    return jnp.dot(first_operand, second_operand, precision=highest_precision)

def causal_conv(series, conv_taps):
    tap_reach = TAPS - 1
    length = series.shape[0]
    padded = jnp.pad(series, ((tap_reach, 0), (0, 0)))
    summed = conv_taps[0] * padded[tap_reach:]
    for offset in range(1, TAPS):
        summed = summed + conv_taps[offset] * padded[tap_reach - offset:tap_reach - offset + length]
    return summed

def delta_rule(queries, keys_act, values_act, log_decay, beta_gate):
    blocks = TOKENS // GROUP

    def token_step(incoming_state, table_entries):
        current_query, current_key, value_now, decay_now, beta_now = table_entries
        projected_rows = jnp.einsum('bq,bqz->bz', current_key, incoming_state, precision=highest_precision)
        erased = incoming_state - beta_now[:, None, None] * current_key[:, :, None] * projected_rows[:, None, :]
        written = beta_now[:, None, None] * current_key[:, :, None] * value_now[:, None, :]
        incoming_state = jnp.exp(decay_now)[:, None, None] * erased + written
        current_output = jnp.einsum('bq,bqz->bz', current_query, incoming_state, precision=highest_precision)
        return (incoming_state, current_output)

    def group_step(incoming_state, block_items):
        return lax.scan(token_step, incoming_state, block_items)
    group_step = jax.checkpoint(group_step)
    shaped = tuple((array_in.reshape((blocks, GROUP) + array_in.shape[1:]) for array_in in (queries, keys_act, values_act, log_decay, beta_gate)))
    initial = jnp.zeros((HEADS, KEY, VALUE), jnp.float32)
    final_state, outputs = lax.scan(group_step, initial, shaped)
    return outputs.reshape(TOKENS, HEADS, VALUE)

def block_forward(block_input, norm1_gain, w_query, w_key, w_value, w_gate, w_decay, w_beta, conv_query, conv_key, conv_value, decay_rate, out_gain, w_out, norm2_gain, w_ffn_gate, w_ffn_up, w_ffn_down):
    normed = low(row_norm(block_input, norm1_gain))
    query_pre = low_back(low(matmul_high(normed, w_query)))
    key_pre = low_back(low(matmul_high(normed, w_key)))
    value_pre = low_back(low(matmul_high(normed, w_value)))
    gate_pre = low_back(matmul_high(normed, w_gate))
    decay_pre = low_back(matmul_high(normed, w_decay))
    beta_pre = low_back(matmul_high(normed, w_beta))
    queries = jax.nn.silu(causal_conv(query_pre, conv_query)).reshape(TOKENS, HEADS, KEY)
    keys_act = jax.nn.silu(causal_conv(key_pre, conv_key)).reshape(TOKENS, HEADS, KEY)
    values_act = jax.nn.silu(causal_conv(value_pre, conv_value)).reshape(TOKENS, HEADS, VALUE)
    queries = low(unit_rows(queries, KEY ** (-0.5)))
    keys_act = low(unit_rows(keys_act, 1.0))
    values_act = low(values_act)
    log_decay = -decay_rate * jax.nn.softplus(decay_pre)
    beta_gate = jax.nn.sigmoid(beta_pre)
    mixed = delta_rule(queries, keys_act, values_act, log_decay, beta_gate)
    gated = row_norm(mixed, out_gain) * jax.nn.silu(gate_pre.reshape(TOKENS, HEADS, VALUE))
    gated = low(gated.reshape(TOKENS, HV))
    branch = low_back(matmul_high(gated, w_out))
    middle = block_input + branch
    normed2 = low(row_norm(middle, norm2_gain))
    ffn_gate = low_back(matmul_high(normed2, w_ffn_gate))
    ffn_up = low_back(matmul_high(normed2, w_ffn_up))
    hidden = low(jax.nn.silu(ffn_gate) * ffn_up)
    return middle + low_back(matmul_high(hidden, w_ffn_down))

def reference(block_input, norm1_gain, w_query, w_key, w_value, w_gate, w_decay, w_beta, conv_query, conv_key, conv_value, decay_rate, out_gain, w_out, norm2_gain, w_ffn_gate, w_ffn_up, w_ffn_down, cotangent):
    primals = [array_in.astype(jnp.float32) for array_in in (block_input, norm1_gain, w_query, w_key, w_value, w_gate, w_decay, w_beta, conv_query, conv_key, conv_value, decay_rate, out_gain, w_out, norm2_gain, w_ffn_gate, w_ffn_up, w_ffn_down)]
    layer_out, pullback = jax.vjp(block_forward, *primals)
    gradients = pullback(cotangent.astype(jnp.float32))
    return (layer_out.astype(jnp.bfloat16), gradients[0], gradients[1], gradients[2], gradients[3], gradients[4], gradients[5], gradients[6], gradients[7], gradients[8], gradients[9], gradients[10], gradients[11], gradients[12], gradients[13], gradients[14], gradients[15], gradients[16], gradients[17])
```

```python
import jax
import jax.numpy as jnp
from jax import lax
from jax.sharding import PartitionSpec as P

KEY = 128
VALUE = 256
GROUP = 64


highest_precision = lax.Precision.HIGHEST
epsilon = 1e-06


def from_behind(block, axis, distance):
    devices = range(lax.axis_size(axis))
    route = [(i - distance, i) for i in devices if i - distance in devices]
    return lax.ppermute(block, axis, route)


def swap_with(block, axis, distance):
    route = [(i, i ^ distance) for i in range(lax.axis_size(axis))]
    return lax.ppermute(block, axis, route)


def butterfly_sum(block, axis):
    distance = 1
    while distance < lax.axis_size(axis):
        block = block + swap_with(block, axis, distance)
        distance *= 2
    return block


def sum_over_heads(partial):
    rows = partial.shape[0] // 2
    odd = lax.axis_index("head") % 2 == 1
    low, high = partial[:rows], partial[rows:]
    own = jnp.where(odd, high, low).astype(jnp.float32)
    own = own + swap_with(jnp.where(odd, low, high).astype(jnp.bfloat16), "head", 1).astype(jnp.float32)
    distance = 2
    while distance < lax.axis_size("head"):
        sent = own.astype(jnp.bfloat16)
        own = sent.astype(jnp.float32) + swap_with(sent, "head", distance).astype(jnp.float32)
        distance *= 2
    kept = own.astype(jnp.bfloat16)
    other = swap_with(kept, "head", 1)
    return jnp.concatenate(
        [jnp.where(odd, other, kept), jnp.where(odd, kept, other)], axis=0
    ).astype(jnp.float32)


def exclusive_scan(transfer, offset, sign):
    own_t, own_b = transfer, offset
    send_t, send_b = transfer, offset
    before_t = before_b = None
    distance = 1
    size = lax.axis_size("seq")

    def product(a, b):
        return jnp.einsum("hij,hjk->hik", a, b, precision=lax.Precision.HIGH)

    while distance < size:
        last = distance * 2 >= size
        joined = send_b if last else jnp.concatenate([send_t, send_b], axis=2)
        got = from_behind(joined.astype(jnp.bfloat16), "seq", sign * distance).astype(jnp.float32)
        if last:
            got_t, got_b = None, got
        else:
            got_t, got_b = got[..., :KEY], got[..., KEY:]
        if before_t is None:
            before_t, before_b = got_t, got_b
        else:
            before_b = before_b + product(before_t, got_b)
            before_t = None if last else product(before_t, got_t)
        if not last:
            send_t = product(own_t, before_t)
            send_b = product(own_t, before_b) + own_b
        distance *= 2
    return before_b


def matmul_bf(first_operand, second_operand):
    return jnp.dot(first_operand, second_operand, preferred_element_type=jnp.float32)


def inner_rows(first_operand, second_operand):
    return lax.dot_general(
        first_operand, second_operand, (((0,), (0,)), ((), ())), preferred_element_type=jnp.float32
    )


def against_rows(first_operand, second_operand):
    return lax.dot_general(
        first_operand, second_operand, (((1,), (1,)), ((), ())), preferred_element_type=jnp.float32
    )


def round_trip(values):
    return lax.optimization_barrier(values.astype(jnp.bfloat16)).astype(jnp.float32)


def row_norm(values, gain_vec):
    return (
        values * lax.rsqrt(jnp.mean(values * values, axis=-1, keepdims=True) + epsilon) * gain_vec
    )


def unit_rows(values, scale_factor):
    return (
        values
        * lax.rsqrt(jnp.sum(values * values, axis=-1, keepdims=True) + epsilon)
        * scale_factor
    )


def mixer_inputs(extended, conv_taps, decay_pre, beta_pre, decay_rate):
    length, head_count = decay_pre.shape
    tap_reach = conv_taps.shape[0] - 1
    summed = conv_taps[0] * extended[tap_reach:]
    for offset in range(1, conv_taps.shape[0]):
        summed = (
            summed + conv_taps[offset] * extended[tap_reach - offset : tap_reach - offset + length]
        )
    active = jax.nn.silu(summed)
    key_cols = head_count * KEY
    queries = unit_rows(active[:, :key_cols].reshape(length, head_count, KEY), KEY ** (-0.5))
    keys_act = unit_rows(active[:, key_cols : 2 * key_cols].reshape(length, head_count, KEY), 1.0)
    values_act = active[:, 2 * key_cols :].reshape(length, head_count, VALUE)
    log_decay = -decay_rate * jax.nn.softplus(decay_pre)
    beta_gate = jax.nn.sigmoid(beta_pre)
    return (queries, keys_act, values_act, log_decay, beta_gate)


def group_parts(keys_act, values_act, log_decay, beta_gate):
    length, head_count = log_decay.shape
    blocks = length // GROUP
    keys_c = keys_act.reshape(blocks, GROUP, head_count, KEY)
    values_c = values_act.reshape(blocks, GROUP, head_count, VALUE)
    decay_c = log_decay.reshape(blocks, GROUP, head_count)
    beta_c = jnp.transpose(beta_gate.reshape(blocks, GROUP, head_count), (0, 2, 1))
    places = jnp.arange(GROUP)
    inclusive = (places[:, None] >= places[None, :]).astype(jnp.float32)
    strict = (places[:, None] > places[None, :]).astype(jnp.float32)
    cumulative = jnp.einsum("ij,njh->nhi", inclusive, decay_c, precision=highest_precision)
    spread = cumulative[..., :, None] - cumulative[..., None, :]
    decay_mat = jnp.exp(jnp.where(inclusive > 0, spread, 0.0)) * inclusive
    key_key = jnp.einsum("nihk,njhk->nhij", keys_c, keys_c, precision=highest_precision)
    system = jnp.eye(GROUP, dtype=jnp.float32) + beta_c[..., :, None] * decay_mat * key_key * strict
    growth = jnp.exp(cumulative)
    scaled_values = jnp.einsum("nhc,nchv->nhcv", beta_c, values_c, precision=highest_precision)
    scaled_keys = jnp.einsum("nhc,nchk->nhck", beta_c * growth, keys_c, precision=highest_precision)
    solved_values = lax.linalg.triangular_solve(
        system, scaled_values, left_side=True, lower=True, unit_diagonal=True
    )
    solved_keys = lax.linalg.triangular_solve(
        system, scaled_keys, left_side=True, lower=True, unit_diagonal=True
    )
    tail_decay = jnp.exp(cumulative[..., -1:] - cumulative)
    keys_tail = jnp.einsum("nhc,nchk->nhck", tail_decay, keys_c, precision=highest_precision)
    final_growth = growth[..., -1]
    transfer = final_growth[..., None, None] * jnp.eye(KEY, dtype=jnp.float32) - jnp.einsum(
        "nhck,nhcl->nhkl", keys_tail, solved_keys, precision=highest_precision
    )
    offset_state = jnp.einsum(
        "nhck,nhcv->nhkv", keys_tail, solved_values, precision=highest_precision
    )
    return (keys_c, decay_mat, growth, solved_values, solved_keys, transfer, offset_state)


def compose_maps(earlier, latter_map):
    joined = jnp.einsum("hij,hjk->hik", latter_map[0], earlier[0], precision=highest_precision)
    shifted = (
        jnp.einsum("hij,hjk->hik", latter_map[0], earlier[1], precision=highest_precision)
        + latter_map[1]
    )
    return (joined, shifted)


def identity_map(head_count):
    eye_stack = jnp.broadcast_to(jnp.eye(KEY, dtype=jnp.float32), (head_count, KEY, KEY))
    return (eye_stack, jnp.zeros((head_count, KEY, VALUE), jnp.float32))


def fold_maps(transfers, offsets, head_count):

    def fold_step(composite, table_entries):
        return (compose_maps(composite, table_entries), None)

    composite, unused = lax.scan(fold_step, identity_map(head_count), (transfers, offsets))
    return composite


def run_mixer(queries, parts, state_in):
    keys_c, decay_mat, growth, solved_values, solved_keys, transfer, offset_state = parts
    blocks, head_count = (growth.shape[0], growth.shape[1])
    length = blocks * GROUP
    queries_c = queries.reshape(blocks, GROUP, head_count, KEY)

    def carry_step(incoming_state, table_entries):
        following = (
            jnp.einsum(
                "hij,hjv->hiv", table_entries[0], incoming_state, precision=highest_precision
            )
            + table_entries[1]
        )
        return (following, incoming_state)

    state_out, starts = lax.scan(carry_step, state_in, (transfer, offset_state))
    corrected = solved_values - jnp.einsum(
        "nhck,nhkv->nhcv", solved_keys, starts, precision=highest_precision
    )
    query_key = (
        jnp.einsum("nihk,njhk->nhij", queries_c, keys_c, precision=highest_precision) * decay_mat
    )
    carried = jnp.einsum("nchk,nhkv->nchv", queries_c, starts, precision=highest_precision)
    carried = carried * jnp.transpose(growth, (0, 2, 1))[..., None]
    local_part = jnp.einsum("nhij,nhjv->nihv", query_key, corrected, precision=highest_precision)
    return ((carried + local_part).reshape(length, head_count, VALUE), state_out)


def start_gradient(queries, parts, grad_mixed):
    keys_c, decay_mat, growth, solved_values, solved_keys, transfer, offset_state = parts
    blocks, head_count = (growth.shape[0], growth.shape[1])
    queries_c = queries.reshape(blocks, GROUP, head_count, KEY)
    grad_c = grad_mixed.reshape(blocks, GROUP, head_count, VALUE)
    grown = grad_c * jnp.transpose(growth, (0, 2, 1))[..., None]
    from_carried = jnp.einsum("nchk,nchv->nhkv", queries_c, grown, precision=highest_precision)
    query_key = (
        jnp.einsum("nihk,njhk->nhij", queries_c, keys_c, precision=highest_precision) * decay_mat
    )
    grad_corrected = jnp.einsum("nhij,nihv->nhjv", query_key, grad_c, precision=highest_precision)
    grad_starts = from_carried - jnp.einsum(
        "nhck,nhcv->nhkv", solved_keys, grad_corrected, precision=highest_precision
    )

    def back_step(pending, table_entries):
        earlier = table_entries[1] + jnp.einsum(
            "hji,hjv->hiv", table_entries[0], pending, precision=highest_precision
        )
        return (earlier, None)

    initial = jnp.zeros((head_count, KEY, VALUE), jnp.float32)
    direct, unused = lax.scan(back_step, initial, (transfer, grad_starts), reverse=True)
    return direct


def gate_norm(mixed, gate_pre, gain_vec):
    length, head_count = (mixed.shape[0], mixed.shape[1])
    gate_view = gate_pre.reshape(length, head_count, VALUE)
    return (row_norm(mixed, gain_vec) * jax.nn.silu(gate_view)).reshape(length, head_count * VALUE)


def swiglu(gate_in, up_in):
    return jax.nn.silu(gate_in) * up_in


def per_device(
    block_input,
    norm1_gain,
    w_query,
    w_key,
    w_value,
    w_gate,
    w_decay,
    w_beta,
    conv_query,
    conv_key,
    conv_value,
    decay_rate,
    out_gain,
    w_out,
    norm2_gain,
    w_ffn_gate,
    w_ffn_up,
    w_ffn_down,
    cotangent,
):
    length = block_input.shape[0]
    head_count = w_decay.shape[1]
    key_cols = w_query.shape[1]
    tap_reach = conv_query.shape[0] - 1
    inputs32 = block_input.astype(jnp.float32)
    normed32, norm1_back = jax.vjp(row_norm, inputs32, norm1_gain.astype(jnp.float32))
    normed = normed32.astype(jnp.bfloat16)
    query_pre = matmul_bf(normed, w_query).astype(jnp.bfloat16)
    key_pre = matmul_bf(normed, w_key).astype(jnp.bfloat16)
    value_pre = matmul_bf(normed, w_value).astype(jnp.bfloat16)
    gate_pre = matmul_bf(normed, w_gate)
    decay_pre = matmul_bf(normed, w_decay)
    beta_pre = matmul_bf(normed, w_beta)
    stacked = jnp.concatenate([query_pre, key_pre, value_pre], axis=1)
    edge_rows = from_behind(stacked[length - tap_reach :], "seq", 1)
    extended = jnp.concatenate([edge_rows, stacked], axis=0).astype(jnp.float32)
    conv_taps = jnp.concatenate([conv_query, conv_key, conv_value], axis=1).astype(jnp.float32)
    prepared, prepare_back = jax.vjp(
        mixer_inputs, extended, conv_taps, decay_pre, beta_pre, decay_rate
    )
    queries = round_trip(prepared[0])
    keys_act = round_trip(prepared[1])
    values_act = round_trip(prepared[2])
    log_decay, beta_gate = (prepared[3], prepared[4])
    parts, parts_back = jax.vjp(group_parts, keys_act, values_act, log_decay, beta_gate)
    transfer, offset_state = fold_maps(parts[5], parts[6], head_count)

    state_in = exclusive_scan(transfer, offset_state, 1)
    mixer_result, mixer_back = jax.vjp(run_mixer, queries, parts, state_in)
    gated32, gate_back = jax.vjp(gate_norm, mixer_result[0], gate_pre, out_gain.astype(jnp.float32))
    gated = gated32.astype(jnp.bfloat16)
    branch = sum_over_heads(matmul_bf(gated, w_out))
    middle = inputs32 + branch
    normed2_32, norm2_back = jax.vjp(row_norm, middle, norm2_gain.astype(jnp.float32))
    normed2 = normed2_32.astype(jnp.bfloat16)
    ffn_gate = matmul_bf(normed2, w_ffn_gate)
    ffn_up = matmul_bf(normed2, w_ffn_up)
    hidden32, swiglu_back = jax.vjp(swiglu, ffn_gate, ffn_up)
    hidden = hidden32.astype(jnp.bfloat16)
    ffn_out = lax.psum(matmul_bf(hidden, w_ffn_down).astype(jnp.bfloat16), "head").astype(
        jnp.float32
    )
    layer_out = (middle + ffn_out).astype(jnp.bfloat16)
    grad_down = inner_rows(cotangent, hidden)
    grad_hidden = against_rows(cotangent, w_ffn_down)
    grad_fgate, grad_fup = swiglu_back(grad_hidden)
    grad_fgate = grad_fgate.astype(jnp.bfloat16)
    grad_fup = grad_fup.astype(jnp.bfloat16)
    grad_wfg = inner_rows(normed2, grad_fgate)
    grad_wfu = inner_rows(normed2, grad_fup)
    grad_normed2 = sum_over_heads(
        against_rows(grad_fgate, w_ffn_gate) + against_rows(grad_fup, w_ffn_up)
    )
    grad_middle_n, grad_gain2 = norm2_back(grad_normed2)
    grad_middle = cotangent.astype(jnp.float32) + grad_middle_n
    grad_branch = grad_middle.astype(jnp.bfloat16)
    grad_wout = inner_rows(grad_branch, gated)
    early = lax.psum_scatter(
        jnp.concatenate([grad_wfg, grad_wfu, grad_down, grad_wout], axis=1).astype(jnp.bfloat16),
        "seq",
        scatter_dimension=0,
        tiled=True,
    ).astype(jnp.float32)
    grad_gated = against_rows(grad_branch, w_out)
    grad_mixed, grad_gate_pre, grad_outgain = gate_back(grad_gated)
    direct = start_gradient(queries, parts, grad_mixed)
    flipped = jnp.swapaxes(transfer, 1, 2)

    grad_state = exclusive_scan(flipped, direct, -1)
    grad_q, grad_parts, unused = mixer_back((grad_mixed, grad_state))
    grad_k, grad_v, grad_log, grad_beta = parts_back(grad_parts)
    grad_ext, grad_taps, grad_decay_pre, grad_beta_pre, grad_rate = prepare_back(
        (grad_q, grad_k, grad_v, grad_log, grad_beta)
    )
    remote = from_behind(grad_ext[:tap_reach], "seq", -1)
    padding = jnp.zeros((length - tap_reach, grad_ext.shape[1]), jnp.float32)
    grad_stacked = (grad_ext[tap_reach:] + jnp.concatenate([padding, remote], axis=0)).astype(
        jnp.bfloat16
    )
    grad_qp = grad_stacked[:, :key_cols]
    grad_kp = grad_stacked[:, key_cols : 2 * key_cols]
    grad_vp = grad_stacked[:, 2 * key_cols :]
    grad_gp = grad_gate_pre.astype(jnp.bfloat16)
    grad_dp = grad_decay_pre.astype(jnp.bfloat16)
    grad_bp = grad_beta_pre.astype(jnp.bfloat16)
    grad_wq = inner_rows(normed, grad_qp)
    grad_wk = inner_rows(normed, grad_kp)
    grad_wv = inner_rows(normed, grad_vp)
    grad_wg = inner_rows(normed, grad_gp)
    grad_wd = inner_rows(normed, grad_dp)
    grad_wb = inner_rows(normed, grad_bp)
    grad_normed_part = (
        against_rows(grad_qp, w_query)
        + against_rows(grad_kp, w_key)
        + against_rows(grad_vp, w_value)
        + against_rows(grad_gp, w_gate)
        + against_rows(grad_dp, w_decay)
        + against_rows(grad_bp, w_beta)
    )
    late = lax.psum_scatter(
        jnp.concatenate([grad_wq, grad_wk, grad_wv, grad_wg, grad_wd, grad_wb], axis=1).astype(
            jnp.bfloat16
        ),
        "seq",
        scatter_dimension=0,
        tiled=True,
    ).astype(jnp.float32)
    grad_normed = sum_over_heads(grad_normed_part)
    grad_input_n, grad_gain1 = norm1_back(grad_normed)
    grad_input = grad_middle + grad_input_n
    width = grad_gain1.shape[0]
    small = jnp.concatenate(
        [
            grad_taps,
            grad_gain2[None],
            jnp.pad(jnp.concatenate([grad_outgain, grad_rate]), (0, width - VALUE - head_count))[None],
        ],
        axis=0,
    )
    small = butterfly_sum(small, "seq")
    taps_sum = small[: conv_taps.shape[0]]
    gain2_sum = small[conv_taps.shape[0]]
    rate_sum = small[conv_taps.shape[0] + 1, VALUE : VALUE + head_count]
    outgain_sum = butterfly_sum(small[conv_taps.shape[0] + 1, :VALUE], "head")
    gain1_sum = butterfly_sum(grad_gain1, "seq")

    def own_part(vec):
        piece = vec.shape[0] // lax.axis_size("seq")
        return lax.dynamic_slice(vec, (lax.axis_index("seq") * piece,), (piece,))

    ff_cols = w_ffn_gate.shape[1]
    value_cols = w_value.shape[1]
    a = 2 * key_cols + value_cols
    b = a + value_cols
    return (
        layer_out,
        grad_input,
        own_part(gain1_sum),
        late[:, :key_cols],
        late[:, key_cols : 2 * key_cols],
        late[:, 2 * key_cols : a],
        late[:, a:b],
        late[:, b : b + head_count],
        late[:, b + head_count :],
        taps_sum[:, :key_cols],
        taps_sum[:, key_cols : 2 * key_cols],
        taps_sum[:, 2 * key_cols :],
        rate_sum,
        own_part(outgain_sum),
        early[:, 3 * ff_cols :].T,
        own_part(gain2_sum),
        early[:, :ff_cols],
        early[:, ff_cols : 2 * ff_cols],
        early[:, 2 * ff_cols : 3 * ff_cols].T,
    )


def solution(mesh):
    return jax.shard_map(
        per_device,
        mesh=mesh,
        in_specs=(
            P("seq", None),
            P(),
            P(None, "head"),
            P(None, "head"),
            P(None, "head"),
            P(None, "head"),
            P(None, "head"),
            P(None, "head"),
            P(None, "head"),
            P(None, "head"),
            P(None, "head"),
            P("head"),
            P(),
            P("head", None),
            P(),
            P(None, "head"),
            P(None, "head"),
            P("head", None),
            P("seq", None),
        ),
        out_specs=(
            P("seq", None),
            P("seq", None),
            P("seq"),
            P("seq", "head"),
            P("seq", "head"),
            P("seq", "head"),
            P("seq", "head"),
            P("seq", "head"),
            P("seq", "head"),
            P(None, "head"),
            P(None, "head"),
            P(None, "head"),
            P("head"),
            P("seq"),
            P("head", "seq"),
            P("seq"),
            P("seq", "head"),
            P("seq", "head"),
            P("head", "seq"),
        ),
        check_vma=False,
    )
```

```python
import functools

import jax
import jax.numpy as jnp
from jax import lax
from jax.experimental import pallas as pl
from jax.experimental.pallas import tpu as pltpu
from jax.sharding import PartitionSpec as P

KEY = 128
VALUE = 256
CHUNK = 128
EDGE = 16
SUB = 16
VMEM_BYTES = 48 * 1024 * 1024

epsilon = 1e-06
f32 = jnp.float32
bf16 = jnp.bfloat16
highest_precision = lax.Precision.HIGHEST


def dot(first, second, over_first=1, over_second=0):
    return lax.dot_general(
        first.astype(bf16),
        second.astype(bf16),
        (((over_first,), (over_second,)), ((), ())),
        preferred_element_type=f32,
    )


def dot_exact(first, second):
    return jnp.dot(first, second, precision=highest_precision, preferred_element_type=f32)


def grid_places(extent):
    rows = lax.broadcasted_iota(jnp.int32, (extent, extent), 0)
    cols = lax.broadcasted_iota(jnp.int32, (extent, extent), 1)
    return rows, cols


def as_row(column, diagonal):
    return jnp.sum(jnp.where(diagonal, column, 0.0), axis=0, keepdims=True)


def as_column(row, diagonal):
    return jnp.sum(jnp.where(diagonal, row, 0.0), axis=1, keepdims=True)


def unit_lower_inverse(strict_part, rows, cols):
    extent = strict_part.shape[0]
    count = extent // SUB
    blocks = jnp.concatenate(
        [strict_part[b * SUB : (b + 1) * SUB, b * SUB : (b + 1) * SUB] for b in range(count)], axis=0
    ).reshape(count, SUB, SUB)
    inner = lax.broadcasted_iota(jnp.int32, (count, SUB, SUB), 1)
    inner_cols = lax.broadcasted_iota(jnp.int32, (count, SUB, SUB), 2)
    solved = (inner == inner_cols).astype(f32)
    for j in range(SUB - 1):
        solved = solved - blocks[:, :, j : j + 1] * solved[:, j : j + 1, :]
    flat = solved.reshape(extent, SUB)
    inverse = jnp.where(rows // SUB == cols // SUB, jnp.concatenate([flat] * count, axis=1), 0.0)
    size = SUB
    while size < extent:
        below = (rows // (2 * size) == cols // (2 * size)) & (rows // size > cols // size)
        corner = jnp.where(below, strict_part, 0.0)
        inverse = inverse - dot_exact(dot_exact(inverse, corner), inverse)
        size *= 2
    return inverse


def decay_terms(ld_row, rows, cols):
    cum_col = jnp.sum(jnp.where(rows >= cols, ld_row, 0.0), axis=1, keepdims=True)
    cum_row = as_row(cum_col, rows == cols)
    last = cum_col[CHUNK - 1 :, :]
    between = jnp.where(rows >= cols, jnp.exp(jnp.where(rows >= cols, cum_col - cum_row, 0.0)), 0.0)
    return between, jnp.exp(cum_col), jnp.exp(last - cum_col), jnp.exp(last)


def conv_sum(padded_ref, taps_ref, length):
    taps = taps_ref[...].astype(f32)
    summed = taps[0:1] * padded_ref[EDGE : EDGE + length, :]
    for offset in range(1, taps_ref.shape[0]):
        summed = summed + taps[offset : offset + 1] * padded_ref[EDGE - offset : EDGE - offset + length, :]
    return summed


def prep_kernel(
    q_ref, k_ref, v_ref, tq_ref, tk_ref, tv_ref, ld_ref, beta_ref,
    qn_ref, kn_ref, vn_ref, zq_ref, zk_ref, zv_ref,
    inv_ref, att_ref, u_ref, w_ref, start_ref, final_ref,
    wide_scr, narrow_scr,
):
    length = qn_ref.shape[0]
    narrow_scr[...] = q_ref[...].astype(f32)
    z = conv_sum(narrow_scr, tq_ref, length)
    zq_ref[...] = z
    a = z * jax.nn.sigmoid(z)
    qn_ref[...] = (
        a * (lax.rsqrt(jnp.sum(a * a, axis=-1, keepdims=True) + epsilon) * KEY ** (-0.5))
    ).astype(bf16)
    narrow_scr[...] = k_ref[...].astype(f32)
    z = conv_sum(narrow_scr, tk_ref, length)
    zk_ref[...] = z
    a = z * jax.nn.sigmoid(z)
    kn_ref[...] = (a * lax.rsqrt(jnp.sum(a * a, axis=-1, keepdims=True) + epsilon)).astype(bf16)
    wide_scr[...] = v_ref[...].astype(f32)
    z = conv_sum(wide_scr, tv_ref, length)
    zv_ref[...] = z
    vn_ref[...] = (z * jax.nn.sigmoid(z)).astype(bf16)

    rows, cols = grid_places(CHUNK)
    diagonal = rows == cols
    kept = []
    for c in range(length // CHUNK):
        at = slice(c * CHUNK, (c + 1) * CHUNK)
        between, grow, tail, whole = decay_terms(ld_ref[0, :, at], rows, cols)
        beta = as_column(beta_ref[0, :, at], diagonal)
        keys = kn_ref[at, :]
        products = dot(jnp.concatenate([keys, qn_ref[at, :]], axis=0), keys, 1, 1)
        system = jnp.where(rows > cols, beta * between * products[:CHUNK], 0.0)
        inverse = unit_lower_inverse(system, rows, cols)
        inv_ref[0, at, :] = inverse.astype(bf16)
        att_ref[0, at, :] = (products[CHUNK:] * between).astype(bf16)
        keys32 = keys.astype(f32)
        right = jnp.concatenate([(beta * grow) * keys32, beta * vn_ref[at, :].astype(f32)], axis=1)
        solved = dot(inverse, right)
        w_ref[0, at, :] = solved[:, :KEY].astype(bf16)
        u_ref[0, at, :] = solved[:, KEY:]
        kept.append((solved, (tail * keys32).astype(bf16), whole))
    state = jnp.concatenate([diagonal.astype(f32), jnp.zeros((KEY, VALUE), f32)], axis=1)
    for c, (solved, tail_keys, whole) in enumerate(kept):
        start_ref[0, c * KEY : (c + 1) * KEY, :] = state
        source = jnp.concatenate([jnp.zeros((CHUNK, KEY), f32), solved[:, KEY:]], axis=1)
        corrected = source - dot(solved[:, :KEY], state)
        state = whole * state + dot(tail_keys, corrected, 0, 0)
    final_ref[0, :, :] = state


def forward_kernel(
    qn_ref, ld_ref, att_ref, u_ref, w_ref, start_ref, state_ref, gate_ref, gain_ref,
    gated_ref, mixed_ref, corr_ref, begin_ref,
):
    length = qn_ref.shape[0]
    rows, cols = grid_places(CHUNK)
    entering = state_ref[0]
    gain = gain_ref[...]
    for c in range(length // CHUNK):
        at = slice(c * CHUNK, (c + 1) * CHUNK)
        places = slice(c * KEY, (c + 1) * KEY)
        between, grow, tail, whole = decay_terms(ld_ref[0, :, at], rows, cols)
        begin = start_ref[0, places, KEY:] + dot(start_ref[0, places, :KEY], entering)
        begin_ref[0, places, :] = begin.astype(bf16)
        corrected = u_ref[0, at, :] - dot(w_ref[0, at, :], begin)
        corr_ref[0, at, :] = corrected.astype(bf16)
        mixed = dot(grow * qn_ref[at, :].astype(f32), begin) + dot(att_ref[0, at, :], corrected)
        mixed_ref[at, :] = mixed
        root = lax.rsqrt(jnp.mean(mixed * mixed, axis=-1, keepdims=True) + epsilon)
        gate = gate_ref[at, :]
        gated_ref[at, :] = (mixed * root * gain * (gate * jax.nn.sigmoid(gate))).astype(bf16)


def gate_back_kernel(
    dgated_ref, mixed_ref, gate_ref, gain_ref, qn_ref, kn_ref, ld_ref, att_ref, w_ref,
    dgate_ref, dmixed_ref, dcorr_ref, dgain_ref, after_ref, final_ref,
):
    length = qn_ref.shape[0]
    rows, cols = grid_places(CHUNK)
    gain = gain_ref[...]
    kept = []
    dgain = jnp.zeros((1, VALUE), f32)
    for c in range(length // CHUNK):
        at = slice(c * CHUNK, (c + 1) * CHUNK)
        mixed, gate, dgated = mixed_ref[at, :], gate_ref[at, :], dgated_ref[at, :]
        root = lax.rsqrt(jnp.mean(mixed * mixed, axis=-1, keepdims=True) + epsilon)
        normal = mixed * root
        sig = jax.nn.sigmoid(gate)
        act = gate * sig
        dgain = dgain + jnp.sum(dgated * normal * act, axis=0, keepdims=True)
        dgate_ref[at, :] = (dgated * normal * gain * (sig * (1.0 + gate * (1.0 - sig)))).astype(bf16)
        dnormal = dgated * act * gain
        dmixed = root * (dnormal - normal * jnp.mean(dnormal * normal, axis=-1, keepdims=True))
        dmixed_ref[0, at, :] = dmixed.astype(bf16)
        between, grow, tail, whole = decay_terms(ld_ref[0, :, at], rows, cols)
        dcorr = dot(att_ref[0, at, :], dmixed, 0, 0)
        dcorr_ref[0, at, :] = dcorr
        gradient = dot(grow * qn_ref[at, :].astype(f32), dmixed, 0, 0) - dot(w_ref[0, at, :], dcorr, 0, 0)
        kept.append((gradient, (tail * kn_ref[at, :].astype(f32)).astype(bf16), whole))
    dgain_ref[0, :, :] = dgain
    pending = jnp.concatenate([(rows == cols).astype(f32), jnp.zeros((KEY, VALUE), f32)], axis=1)
    for c in reversed(range(length // CHUNK)):
        gradient, tail_keys, whole = kept[c]
        at = slice(c * CHUNK, (c + 1) * CHUNK)
        after_ref[0, c * KEY : (c + 1) * KEY, :] = pending
        source = jnp.concatenate([jnp.zeros((KEY, KEY), f32), gradient], axis=1)
        pending = whole * pending + source - dot(w_ref[0, at, :], dot(tail_keys, pending), 0, 0)
    final_ref[0, :, :] = pending


def silu_slope(z):
    sig = jax.nn.sigmoid(z)
    return z * sig, sig * (1.0 + z * (1.0 - sig))


def conv_back(dz, pre_ref, taps_ref, dz_scr, pre_scr, dpre_ref, tail_ref, edge_ref, dtaps_ref):
    length = dz.shape[0]
    reach = taps_ref.shape[0] - 1
    taps = taps_ref[...].astype(f32)
    dz_scr[EDGE : EDGE + length, :] = dz
    pre_scr[...] = pre_ref[...].astype(f32)
    total = taps[0:1] * dz
    sums = [jnp.sum(dz * pre_scr[EDGE : EDGE + length, :], axis=0, keepdims=True)]
    for offset in range(1, reach + 1):
        total = total + taps[offset : offset + 1] * dz_scr[EDGE + offset : EDGE + offset + length, :]
        sums.append(
            jnp.sum(dz * pre_scr[EDGE - offset : EDGE - offset + length, :], axis=0, keepdims=True)
        )
    dpre_ref[...] = total.astype(bf16)
    tail_ref[...] = total[length - 8 :, :]
    edge = taps[1:2] * dz_scr[EDGE - 7 : EDGE + 1, :]
    for offset in range(2, reach + 1):
        edge = edge + taps[offset : offset + 1] * dz_scr[EDGE - 8 + offset : EDGE + offset, :]
    edge_ref[...] = edge
    dtaps_ref[...] = jnp.concatenate(sums, axis=0)


def backward_kernel(
    gstate_ref, after_ref, dmixed_ref, dcorr_ref, begin_ref, corr_ref, inv_ref, att_ref, u_ref, w_ref,
    qn_ref, kn_ref, vn_ref, zq_ref, zk_ref, zv_ref, q_ref, k_ref, v_ref, tq_ref, tk_ref, tv_ref,
    ld_ref, beta_ref,
    dq_ref, dk_ref, dv_ref, tailq_ref, tailk_ref, tailv_ref, edgeq_ref, edgek_ref, edgev_ref,
    dtq_ref, dtk_ref, dtv_ref, dld_ref, dbeta_ref,
    dqn_scr, dkn_scr, dvn_scr, dn_scr, pn_scr, dw_scr, pw_scr,
):
    length = qn_ref.shape[0]
    rows, cols = grid_places(CHUNK)
    diagonal = rows == cols
    leaving = gstate_ref[0]
    for c in range(length // CHUNK):
        at = slice(c * CHUNK, (c + 1) * CHUNK)
        places = slice(c * KEY, (c + 1) * KEY)
        between, grow, tail, whole = decay_terms(ld_ref[0, :, at], rows, cols)
        beta = as_column(beta_ref[0, :, at], diagonal)
        keys, queries = kn_ref[at, :], qn_ref[at, :]
        keys32, queries32, values32 = keys.astype(f32), queries.astype(f32), vn_ref[at, :].astype(f32)
        dstate = after_ref[0, places, KEY:] + dot(after_ref[0, places, :KEY], leaving)
        dmixed, corrected, begin = dmixed_ref[0, at, :], corr_ref[0, at, :], begin_ref[0, places, :]
        dcorr = dcorr_ref[0, at, :] + dot(tail * keys32, dstate)
        datt = dot(dmixed, corrected, 1, 1)
        from_begin = dot(jnp.concatenate([dmixed, dcorr.astype(bf16)], axis=0), begin, 1, 1)
        dgrown, dw = from_begin[:CHUNK], -from_begin[CHUNK:]
        dtail_keys = dot(corrected, dstate, 1, 1)
        dwhole = jnp.sum(dstate * begin.astype(f32))
        back = dot(inv_ref[0, at, :], jnp.concatenate([dw, dcorr], axis=1), 0, 0)
        dright_keys, dright_values = back[:, :KEY], back[:, KEY:]
        dsystem = -dot(
            back, jnp.concatenate([w_ref[0, at, :], u_ref[0, at, :].astype(bf16)], axis=1), 1, 1
        )
        products = dot(jnp.concatenate([keys, queries], axis=0), keys, 1, 1)
        decayed = jnp.where(rows > cols, between * products[:CHUNK], 0.0)
        dsys_decayed = dsystem * decayed
        dbeta = jnp.sum(dsys_decayed, axis=1, keepdims=True)
        pairs = beta * dsys_decayed + datt * (between * products[CHUNK:])
        dkk = jnp.where(rows > cols, dsystem * (beta * between), 0.0)
        dqk = datt * between
        dqk16, dkk16 = dqk.astype(bf16), dkk.astype(bf16)
        dqn_scr[at, :] = dot(dqk16, keys) + grow * dgrown
        dkn_scr[at, :] = (
            dot(jnp.concatenate([dqk16, dkk16], axis=0), jnp.concatenate([queries, keys], axis=0), 0, 0)
            + dot(dkk16, keys)
            + tail * dtail_keys
            + (beta * grow) * dright_keys
        )
        dvn_scr[at, :] = beta * dright_values
        keys_part = grow * jnp.sum(dright_keys * keys32, axis=1, keepdims=True)
        dbeta = dbeta + jnp.sum(dright_values * values32, axis=1, keepdims=True) + keys_part
        from_tail = tail * jnp.sum(dtail_keys * keys32, axis=1, keepdims=True)
        dcum = (
            jnp.sum(pairs, axis=1, keepdims=True)
            - as_column(jnp.sum(pairs, axis=0, keepdims=True), diagonal)
            + grow * jnp.sum(dgrown * queries32, axis=1, keepdims=True)
            + beta * keys_part
            - from_tail
        )
        dlast = whole * dwhole + jnp.sum(from_tail, axis=0, keepdims=True)
        dld_ref[0, :, at] = jnp.sum(jnp.where(rows >= cols, dcum, 0.0), axis=0, keepdims=True) + dlast
        dbeta_ref[0, :, at] = as_row(dbeta, diagonal)

    for scr in (dn_scr, dw_scr):
        scr[0:EDGE, :] = jnp.zeros((EDGE, scr.shape[1]), f32)
        scr[EDGE + length :, :] = jnp.zeros((EDGE, scr.shape[1]), f32)
    act, slope = silu_slope(zq_ref[...])
    root = lax.rsqrt(jnp.sum(act * act, axis=-1, keepdims=True) + epsilon)
    normal = act * root
    dy = dqn_scr[...] * KEY ** (-0.5)
    dz = root * (dy - normal * jnp.sum(normal * dy, axis=-1, keepdims=True)) * slope
    conv_back(dz, q_ref, tq_ref, dn_scr, pn_scr, dq_ref, tailq_ref, edgeq_ref, dtq_ref)
    act, slope = silu_slope(zk_ref[...])
    root = lax.rsqrt(jnp.sum(act * act, axis=-1, keepdims=True) + epsilon)
    normal = act * root
    dy = dkn_scr[...]
    dz = root * (dy - normal * jnp.sum(normal * dy, axis=-1, keepdims=True)) * slope
    conv_back(dz, k_ref, tk_ref, dn_scr, pn_scr, dk_ref, tailk_ref, edgek_ref, dtk_ref)
    act, slope = silu_slope(zv_ref[...])
    conv_back(dvn_scr[...] * slope, v_ref, tv_ref, dw_scr, pw_scr, dv_ref, tailv_ref, edgev_ref, dtv_ref)


def tall(rows, cols):
    return pl.BlockSpec((rows, cols), lambda h: (0, h))


def deep(rows, cols):
    return pl.BlockSpec((1, rows, cols), lambda h: (h, 0, 0))


def shared(rows, cols):
    return pl.BlockSpec((rows, cols), lambda h: (0, 0))


def shape_of(dims, dtype):
    return jax.ShapeDtypeStruct(dims, dtype)


def call_heads(kernel, head_count, in_specs, outputs, scratch, flops, args):
    out_specs = [spec for spec, shape in outputs]
    out_shape = [shape for spec, shape in outputs]
    moved = sum(a.size * a.dtype.itemsize for a in list(args) + out_shape)
    return pl.pallas_call(
        kernel,
        grid=(head_count,),
        in_specs=in_specs,
        out_specs=out_specs,
        out_shape=out_shape,
        scratch_shapes=scratch,
        compiler_params=pltpu.CompilerParams(vmem_limit_bytes=VMEM_BYTES),
        cost_estimate=pl.CostEstimate(flops=flops, bytes_accessed=moved, transcendentals=0),
    )(*args)


def prepare(query_ext, key_ext, value_ext, conv_query, conv_key, conv_value, ld, beta):
    length = query_ext.shape[0] - EDGE
    heads = ld.shape[0]
    states = (length // CHUNK) * KEY
    taps = conv_query.shape[0]
    narrow, wide = tall(length, KEY), tall(length, VALUE)
    nshape = (length, heads * KEY)
    wshape = (length, heads * VALUE)
    outputs = [
        (narrow, shape_of(nshape, bf16)),
        (narrow, shape_of(nshape, bf16)),
        (wide, shape_of(wshape, bf16)),
        (narrow, shape_of(nshape, f32)),
        (narrow, shape_of(nshape, f32)),
        (wide, shape_of(wshape, f32)),
        (deep(length, CHUNK), shape_of((heads, length, CHUNK), bf16)),
        (deep(length, CHUNK), shape_of((heads, length, CHUNK), bf16)),
        (deep(length, VALUE), shape_of((heads, length, VALUE), f32)),
        (deep(length, KEY), shape_of((heads, length, KEY), bf16)),
        (deep(states, KEY + VALUE), shape_of((heads, states, KEY + VALUE), f32)),
        (deep(KEY, KEY + VALUE), shape_of((heads, KEY, KEY + VALUE), f32)),
    ]
    in_specs = [
        tall(length + EDGE, KEY), tall(length + EDGE, KEY), tall(length + EDGE, VALUE),
        tall(taps, KEY), tall(taps, KEY), tall(taps, VALUE),
        deep(1, length), deep(1, length),
    ]
    scratch = [pltpu.VMEM((length + EDGE, VALUE), f32), pltpu.VMEM((length + EDGE, KEY), f32)]
    args = (query_ext, key_ext, value_ext, conv_query, conv_key, conv_value, ld, beta)
    return call_heads(prep_kernel, heads, in_specs, outputs, scratch, 2000000000, args)


def run_forward(qn, ld, att, u, w, starts, state_in, gate_pre, gain):
    length = qn.shape[0]
    heads = ld.shape[0]
    states = starts.shape[1]
    wide = tall(length, VALUE)
    wshape = (length, heads * VALUE)
    outputs = [
        (wide, shape_of(wshape, bf16)),
        (wide, shape_of(wshape, f32)),
        (deep(length, VALUE), shape_of((heads, length, VALUE), bf16)),
        (deep(states, VALUE), shape_of((heads, states, VALUE), bf16)),
    ]
    in_specs = [
        tall(length, KEY), deep(1, length), deep(length, CHUNK), deep(length, VALUE), deep(length, KEY),
        deep(states, KEY + VALUE), deep(KEY, VALUE), wide, shared(1, VALUE),
    ]
    args = (qn, ld, att, u, w, starts, state_in, gate_pre, gain)
    return call_heads(forward_kernel, heads, in_specs, outputs, [], 500000000, args)


def gate_back(dgated, mixed, gate_pre, gain, qn, kn, ld, att, w):
    length = qn.shape[0]
    heads = ld.shape[0]
    states = (length // CHUNK) * KEY
    wide = tall(length, VALUE)
    outputs = [
        (wide, shape_of((length, heads * VALUE), bf16)),
        (deep(length, VALUE), shape_of((heads, length, VALUE), bf16)),
        (deep(length, VALUE), shape_of((heads, length, VALUE), f32)),
        (deep(1, VALUE), shape_of((heads, 1, VALUE), f32)),
        (deep(states, KEY + VALUE), shape_of((heads, states, KEY + VALUE), f32)),
        (deep(KEY, KEY + VALUE), shape_of((heads, KEY, KEY + VALUE), f32)),
    ]
    in_specs = [
        wide, wide, wide, shared(1, VALUE), tall(length, KEY), tall(length, KEY), deep(1, length),
        deep(length, CHUNK), deep(length, KEY),
    ]
    args = (dgated, mixed, gate_pre, gain, qn, kn, ld, att, w)
    return call_heads(gate_back_kernel, heads, in_specs, outputs, [], 700000000, args)


def run_backward(
    gstate, after, dmixed, dcorr, begin, corr, inverse, att, u, w, qn, kn, vn, zq, zk, zv,
    query_ext, key_ext, value_ext, conv_query, conv_key, conv_value, ld, beta,
):
    length = qn.shape[0]
    heads = ld.shape[0]
    states = after.shape[1]
    taps = conv_query.shape[0]
    narrow, wide = tall(length, KEY), tall(length, VALUE)
    ncols, wcols = heads * KEY, heads * VALUE
    outputs = [
        (narrow, shape_of((length, ncols), bf16)),
        (narrow, shape_of((length, ncols), bf16)),
        (wide, shape_of((length, wcols), bf16)),
        (tall(8, KEY), shape_of((8, ncols), f32)),
        (tall(8, KEY), shape_of((8, ncols), f32)),
        (tall(8, VALUE), shape_of((8, wcols), f32)),
        (tall(8, KEY), shape_of((8, ncols), f32)),
        (tall(8, KEY), shape_of((8, ncols), f32)),
        (tall(8, VALUE), shape_of((8, wcols), f32)),
        (tall(taps, KEY), shape_of((taps, ncols), f32)),
        (tall(taps, KEY), shape_of((taps, ncols), f32)),
        (tall(taps, VALUE), shape_of((taps, wcols), f32)),
        (deep(1, length), shape_of((heads, 1, length), f32)),
        (deep(1, length), shape_of((heads, 1, length), f32)),
    ]
    in_specs = [
        deep(KEY, VALUE), deep(states, KEY + VALUE), deep(length, VALUE), deep(length, VALUE),
        deep(states, VALUE), deep(length, VALUE), deep(length, CHUNK), deep(length, CHUNK),
        deep(length, VALUE), deep(length, KEY),
        narrow, narrow, wide, narrow, narrow, wide,
        tall(length + EDGE, KEY), tall(length + EDGE, KEY), tall(length + EDGE, VALUE),
        tall(taps, KEY), tall(taps, KEY), tall(taps, VALUE),
        deep(1, length), deep(1, length),
    ]
    scratch = [
        pltpu.VMEM((length, KEY), f32), pltpu.VMEM((length, KEY), f32), pltpu.VMEM((length, VALUE), f32),
        pltpu.VMEM((length + 2 * EDGE, KEY), f32), pltpu.VMEM((length + EDGE, KEY), f32),
        pltpu.VMEM((length + 2 * EDGE, VALUE), f32), pltpu.VMEM((length + EDGE, VALUE), f32),
    ]
    args = (
        gstate, after, dmixed, dcorr, begin, corr, inverse, att, u, w, qn, kn, vn, zq, zk, zv,
        query_ext, key_ext, value_ext, conv_query, conv_key, conv_value, ld, beta,
    )
    return call_heads(backward_kernel, heads, in_specs, outputs, scratch, 1500000000, args)


def weight_kernel(count, *refs):
    lefts, rights, out_ref = refs[:count], refs[count:-1], refs[-1]
    at = 0
    for left, right in zip(lefts, rights):
        width = right.shape[1]
        out_ref[:, at : at + width] = dot(left[...], right[...], 0, 0).astype(bf16)
        at += width


def weight_gradients(pairs):
    lefts = [left for left, right in pairs]
    rights = [right for left, right in pairs]
    length, width = lefts[0].shape
    block = 256
    total = sum(r.shape[1] for r in rights)
    args = lefts + rights
    out = shape_of((width, total), bf16)
    moved = sum(a.size * a.dtype.itemsize for a in args + [out])
    return pl.pallas_call(
        functools.partial(weight_kernel, len(pairs)),
        grid=(width // block,),
        in_specs=[pl.BlockSpec((length, block), lambda i: (0, i)) for left in lefts]
        + [pl.BlockSpec(r.shape, lambda i: (0, 0)) for r in rights],
        out_specs=pl.BlockSpec((block, total), lambda i: (i, 0)),
        out_shape=out,
        compiler_params=pltpu.CompilerParams(vmem_limit_bytes=VMEM_BYTES),
        cost_estimate=pl.CostEstimate(
            flops=2 * length * width * total, bytes_accessed=moved, transcendentals=0
        ),
    )(*args)


def from_behind(block, axis, distance):
    devices = range(lax.axis_size(axis))
    route = [(i - distance, i) for i in devices if i - distance in devices]
    return lax.ppermute(block, axis, route)


def swap_with(block, axis, distance):
    route = [(i, i ^ distance) for i in range(lax.axis_size(axis))]
    return lax.ppermute(block, axis, route)


def butterfly_sum(block, axis):
    distance = 1
    while distance < lax.axis_size(axis):
        block = block + swap_with(block, axis, distance)
        distance *= 2
    return block


def sum_over_heads(partial):
    rows = partial.shape[0] // 2
    odd = lax.axis_index("head") % 2 == 1
    low, high = partial[:rows], partial[rows:]
    own = jnp.where(odd, high, low).astype(f32)
    own = own + swap_with(jnp.where(odd, low, high).astype(bf16), "head", 1).astype(f32)
    distance = 2
    while distance < lax.axis_size("head"):
        sent = own.astype(bf16)
        own = sent.astype(f32) + swap_with(sent, "head", distance).astype(f32)
        distance *= 2
    kept = own.astype(bf16)
    other = swap_with(kept, "head", 1)
    return jnp.concatenate(
        [jnp.where(odd, other, kept), jnp.where(odd, kept, other)], axis=0
    ).astype(f32)


def exclusive_scan(joined, sign):
    own_t, own_b = joined[..., :KEY], joined[..., KEY:]
    send = joined
    before_t = before_b = None
    distance = 1
    size = lax.axis_size("seq")

    def product(a, b):
        return jnp.einsum("hij,hjk->hik", a, b, precision=lax.Precision.HIGH)

    while distance < size:
        last = distance * 2 >= size
        got = from_behind(
            (send[..., KEY:] if last else send).astype(bf16), "seq", sign * distance
        ).astype(f32)
        if before_t is None:
            before_t, before_b = got[..., :KEY], got[..., KEY:]
        else:
            moved = product(before_t, got)
            if last:
                before_b = before_b + moved
            else:
                before_t, before_b = moved[..., :KEY], before_b + moved[..., KEY:]
        if not last:
            send = product(own_t, jnp.concatenate([before_t, before_b], axis=-1))
            send = jnp.concatenate([send[..., :KEY], send[..., KEY:] + own_b], axis=-1)
        distance *= 2
    return before_b


def matmul_bf(first_operand, second_operand):
    return jnp.dot(first_operand, second_operand, preferred_element_type=f32)


def against_rows(first_operand, second_operand):
    return lax.dot_general(
        first_operand, second_operand, (((1,), (1,)), ((), ())), preferred_element_type=f32
    )


def row_norm(values, gain_vec):
    return (
        values * lax.rsqrt(jnp.mean(values * values, axis=-1, keepdims=True) + epsilon) * gain_vec
    )


def swiglu(gate_in, up_in):
    return jax.nn.silu(gate_in) * up_in


def per_device(
    block_input,
    norm1_gain,
    w_query,
    w_key,
    w_value,
    w_gate,
    w_decay,
    w_beta,
    conv_query,
    conv_key,
    conv_value,
    decay_rate,
    out_gain,
    w_out,
    norm2_gain,
    w_ffn_gate,
    w_ffn_up,
    w_ffn_down,
    cotangent,
):
    length = block_input.shape[0]
    head_count = w_decay.shape[1]
    key_cols = w_query.shape[1]
    value_cols = w_value.shape[1]
    ff_cols = w_ffn_gate.shape[1]
    edge_input = from_behind(block_input[length - EDGE :], "seq", 1)
    gain1 = norm1_gain.astype(f32)
    inputs32 = block_input.astype(f32)
    normed32, norm1_back = jax.vjp(row_norm, inputs32, gain1)
    normed = normed32.astype(bf16)
    edge_normed = row_norm(edge_input.astype(f32), gain1).astype(bf16)
    normed_ext = jnp.concatenate([edge_normed, normed], axis=0)
    gate_pre = matmul_bf(normed, w_gate)
    w_scalars = jnp.concatenate([w_decay, w_beta], axis=1)
    scalars = lax.dot_general(
        w_scalars, normed, (((0,), (1,)), ((), ())), preferred_element_type=f32
    )
    decay_pre, beta_pre = scalars[:head_count], scalars[head_count:]
    soft = jax.nn.softplus(decay_pre)
    rate = decay_rate[:, None]
    log_decay = (-rate * soft).reshape(head_count, 1, length)
    beta_gate = jax.nn.sigmoid(beta_pre)
    beta3 = beta_gate.reshape(head_count, 1, length)
    query_ext = matmul_bf(normed_ext, w_query).astype(bf16)
    key_ext = matmul_bf(normed_ext, w_key).astype(bf16)
    value_ext = matmul_bf(normed_ext, w_value).astype(bf16)
    qn, kn, vn, zq, zk, zv, inverse, att, u, w, starts, composite = prepare(
        query_ext, key_ext, value_ext, conv_query, conv_key, conv_value, log_decay, beta3
    )
    state_in = exclusive_scan(composite, 1)
    gain_row = out_gain.astype(f32)[None]
    gated, mixed, corr, begin = run_forward(
        qn, log_decay, att, u, w, starts, state_in, gate_pre, gain_row
    )
    branch = sum_over_heads(matmul_bf(gated, w_out))
    middle = inputs32 + branch
    normed2_32, norm2_back = jax.vjp(row_norm, middle, norm2_gain.astype(f32))
    normed2 = normed2_32.astype(bf16)
    ffn_gate = matmul_bf(normed2, w_ffn_gate)
    ffn_up = matmul_bf(normed2, w_ffn_up)
    hidden32, swiglu_back = jax.vjp(swiglu, ffn_gate, ffn_up)
    hidden = hidden32.astype(bf16)
    grad_hidden = against_rows(cotangent, w_ffn_down)
    grad_fgate, grad_fup = swiglu_back(grad_hidden)
    grad_fgate = grad_fgate.astype(bf16)
    grad_fup = grad_fup.astype(bf16)
    grad_normed2 = sum_over_heads(
        against_rows(grad_fgate, w_ffn_gate) + against_rows(grad_fup, w_ffn_up)
    )
    ffn_out = lax.psum(matmul_bf(hidden, w_ffn_down).astype(bf16), "head").astype(f32)
    layer_out = (middle + ffn_out).astype(bf16)
    grad_middle_n, grad_gain2 = norm2_back(grad_normed2)
    grad_middle = cotangent.astype(f32) + grad_middle_n
    grad_branch = grad_middle.astype(bf16)
    grad_gated = against_rows(grad_branch, w_out)
    grad_gp, grad_mixed, grad_corr, grad_outgain, after, composite_back = gate_back(
        grad_gated, mixed, gate_pre, gain_row, qn, kn, log_decay, att, w
    )
    early = lax.psum_scatter(
        weight_gradients(
            [
                (normed2, grad_fgate),
                (normed2, grad_fup),
                (cotangent, hidden),
                (grad_branch, gated),
            ]
        ),
        "seq",
        scatter_dimension=0,
        tiled=True,
    ).astype(f32)
    grad_state = exclusive_scan(composite_back, -1)
    (
        grad_qp, grad_kp, grad_vp, tail_q, tail_k, tail_v, edge_q, edge_k, edge_v,
        taps_q, taps_k, taps_v, grad_log, grad_beta,
    ) = run_backward(
        grad_state, after, grad_mixed, grad_corr, begin, corr, inverse, att, u, w,
        qn, kn, vn, zq, zk, zv, query_ext, key_ext, value_ext,
        conv_query, conv_key, conv_value, log_decay, beta3,
    )
    edges = from_behind(jnp.concatenate([edge_q, edge_k, edge_v], axis=1), "seq", -1)
    tails = (jnp.concatenate([tail_q, tail_k, tail_v], axis=1) + edges).astype(bf16)

    def with_tail(main, low, high):
        return jnp.concatenate([main[: length - 8], tails[:, low:high]], axis=0)

    grad_qp = with_tail(grad_qp, 0, key_cols)
    grad_kp = with_tail(grad_kp, key_cols, 2 * key_cols)
    grad_vp = with_tail(grad_vp, 2 * key_cols, 2 * key_cols + value_cols)
    grad_log = grad_log.reshape(head_count, length)
    grad_beta = grad_beta.reshape(head_count, length)
    grad_dp = (-rate * jax.nn.sigmoid(decay_pre) * grad_log).astype(bf16)
    grad_bp = (beta_gate * (1.0 - beta_gate) * grad_beta).astype(bf16)
    grad_rate = -jnp.sum(grad_log * soft, axis=1)
    pad = ((0, 0), (0, 128 - 2 * head_count))
    grad_scalars = jnp.pad(jnp.concatenate([grad_dp, grad_bp], axis=0).T, pad)
    late = lax.psum_scatter(
        weight_gradients(
            [
                (normed, grad_qp),
                (normed, grad_kp),
                (normed, grad_vp),
                (normed, grad_gp),
                (normed, grad_scalars),
            ]
        ),
        "seq",
        scatter_dimension=0,
        tiled=True,
    ).astype(f32)
    grad_normed_part = (
        against_rows(grad_qp, w_query)
        + against_rows(grad_kp, w_key)
        + against_rows(grad_vp, w_value)
        + against_rows(grad_gp, w_gate)
        + against_rows(grad_scalars, jnp.pad(w_scalars, pad))
    )
    grad_normed = sum_over_heads(grad_normed_part)
    grad_input_n, grad_gain1 = norm1_back(grad_normed)
    grad_input = grad_middle + grad_input_n
    width = grad_gain1.shape[0]
    taps_count = conv_query.shape[0]
    grad_outgain = jnp.sum(grad_outgain, axis=(0, 1))
    small = jnp.concatenate(
        [
            jnp.concatenate([taps_q, taps_k, taps_v], axis=1),
            grad_gain2[None],
            jnp.pad(jnp.concatenate([grad_outgain, grad_rate]), (0, width - VALUE - head_count))[None],
        ],
        axis=0,
    )
    small = butterfly_sum(small, "seq")
    taps_sum = small[:taps_count]
    gain2_sum = small[taps_count]
    rate_sum = small[taps_count + 1, VALUE : VALUE + head_count]
    outgain_sum = butterfly_sum(small[taps_count + 1, :VALUE], "head")
    gain1_sum = butterfly_sum(grad_gain1, "seq")

    def own_part(vec):
        piece = vec.shape[0] // lax.axis_size("seq")
        return lax.dynamic_slice(vec, (lax.axis_index("seq") * piece,), (piece,))

    a = 2 * key_cols + value_cols
    b = a + value_cols
    return (
        layer_out,
        grad_input,
        own_part(gain1_sum),
        late[:, :key_cols],
        late[:, key_cols : 2 * key_cols],
        late[:, 2 * key_cols : a],
        late[:, a:b],
        late[:, b : b + head_count],
        late[:, b + head_count : b + 2 * head_count],
        taps_sum[:, :key_cols],
        taps_sum[:, key_cols : 2 * key_cols],
        taps_sum[:, 2 * key_cols :],
        rate_sum,
        own_part(outgain_sum),
        early[:, 3 * ff_cols :].T,
        own_part(gain2_sum),
        early[:, :ff_cols],
        early[:, ff_cols : 2 * ff_cols],
        early[:, 2 * ff_cols : 3 * ff_cols].T,
    )


def solution(mesh):
    return jax.shard_map(
        per_device,
        mesh=mesh,
        in_specs=(
            P("seq", None),
            P(),
            P(None, "head"),
            P(None, "head"),
            P(None, "head"),
            P(None, "head"),
            P(None, "head"),
            P(None, "head"),
            P(None, "head"),
            P(None, "head"),
            P(None, "head"),
            P("head"),
            P(),
            P("head", None),
            P(),
            P(None, "head"),
            P(None, "head"),
            P("head", None),
            P("seq", None),
        ),
        out_specs=(
            P("seq", None),
            P("seq", None),
            P("seq"),
            P("seq", "head"),
            P("seq", "head"),
            P("seq", "head"),
            P("seq", "head"),
            P("seq", "head"),
            P("seq", "head"),
            P(None, "head"),
            P(None, "head"),
            P(None, "head"),
            P("head"),
            P("seq"),
            P("head", "seq"),
            P("seq"),
            P("seq", "head"),
            P("seq", "head"),
            P("head", "seq"),
        ),
        check_vma=False,
    )
```

```python
import functools

import jax
import jax.numpy as jnp
from jax import lax
from jax.experimental import pallas as pl
from jax.experimental.pallas import tpu as pltpu
from jax.sharding import PartitionSpec as P

KEY = 128
VALUE = 256
CHUNK = 128
EDGE = 16
SUB = 16
VMEM_BYTES = 60 * 1024 * 1024

epsilon = 1e-06
f32 = jnp.float32
bf16 = jnp.bfloat16
highest_precision = lax.Precision.HIGHEST


def dot(first, second, over_first=1, over_second=0):
    return lax.dot_general(
        first.astype(bf16),
        second.astype(bf16),
        (((over_first,), (over_second,)), ((), ())),
        preferred_element_type=f32,
    )


def halves(values):
    high = values.astype(bf16)
    return high, (values - high.astype(f32)).astype(bf16)


def dot_fine(first, second):
    first_high, first_low = halves(first)
    second_high, second_low = halves(second)
    width = second.shape[1]
    wide = dot(first_high, jnp.concatenate([second_high, second_low], axis=1))
    return wide[:, :width] + wide[:, width:] + dot(first_low, second_high)


def grid_places(extent):
    rows = lax.broadcasted_iota(jnp.int32, (extent, extent), 0)
    cols = lax.broadcasted_iota(jnp.int32, (extent, extent), 1)
    return rows, cols


def as_row(column, diagonal):
    return jnp.sum(jnp.where(diagonal, column, 0.0), axis=0, keepdims=True)


def as_column(row, diagonal):
    return jnp.sum(jnp.where(diagonal, row, 0.0), axis=1, keepdims=True)


def unit_lower_inverses(systems, rows, cols):
    extent = systems[0].shape[0]
    count = extent // SUB
    units = len(systems)
    same = rows // SUB == cols // SUB
    packed = jnp.concatenate(
        [jnp.sum(jnp.where(same, s, 0.0).reshape(count, SUB, extent), axis=0) for s in systems], axis=0
    )
    stacked = jnp.concatenate(halves(packed), axis=0)
    shape = (units, SUB, extent)
    places = lax.broadcasted_iota(jnp.int32, shape, 1)
    solved = (places == lax.broadcasted_iota(jnp.int32, shape, 2) % SUB).astype(f32)
    for j in range(SUB - 1):
        spread = dot(stacked, (same & (rows % SUB == j)).astype(f32))
        column = spread[: units * SUB] + spread[units * SUB :]
        solved = solved - column.reshape(shape) * solved[:, j : j + 1, :]
    inverses = [
        jnp.where(same, jnp.concatenate([solved[n]] * count, axis=0), 0.0) for n in range(units)
    ]
    size = SUB
    while size < extent:
        below = (rows // (2 * size) == cols // (2 * size)) & (rows // size > cols // size)
        joined = [
            dot_fine(inverse, jnp.where(below, s, 0.0)) for inverse, s in zip(inverses, systems)
        ]
        joined = [dot_fine(product, inverse) for product, inverse in zip(joined, inverses)]
        inverses = [inverse - product for inverse, product in zip(inverses, joined)]
        size *= 2
    return inverses


def decay_terms(ld_row, rows, cols):
    cum_col = jnp.sum(jnp.where(rows >= cols, ld_row, 0.0), axis=1, keepdims=True)
    cum_row = as_row(cum_col, rows == cols)
    last = cum_col[CHUNK - 1 :, :]
    between = jnp.where(rows >= cols, jnp.exp(jnp.where(rows >= cols, cum_col - cum_row, 0.0)), 0.0)
    return between, jnp.exp(cum_col), jnp.exp(last - cum_col), jnp.exp(last)


def conv_sum(padded_ref, taps_ref, length):
    taps = taps_ref[...].astype(f32)
    summed = taps[0:1] * padded_ref[EDGE : EDGE + length, :]
    for offset in range(1, taps_ref.shape[0]):
        summed = summed + taps[offset : offset + 1] * padded_ref[EDGE - offset : EDGE - offset + length, :]
    return summed


def unit_rows(values, scale, heads):
    parts = []
    for h in range(heads):
        part = values[:, h * KEY : (h + 1) * KEY]
        parts.append(
            part * (lax.rsqrt(jnp.sum(part * part, axis=-1, keepdims=True) + epsilon) * scale)
        )
    return jnp.concatenate(parts, axis=1)


def prep_kernel(
    q_ref, k_ref, v_ref, tq_ref, tk_ref, tv_ref, ld_ref, beta_ref,
    qn_ref, kn_ref, vn_ref, inv_ref, att_ref, u_ref, w_ref, start_ref, final_ref,
    wide_scr, narrow_scr,
):
    length = qn_ref.shape[0]
    heads = ld_ref.shape[0]
    chunks = length // CHUNK
    narrow_scr[...] = k_ref[...].astype(f32)
    z = conv_sum(narrow_scr, tk_ref, length)
    kn_ref[...] = unit_rows(z * jax.nn.sigmoid(z), 1.0, heads).astype(bf16)
    narrow_scr[...] = q_ref[...].astype(f32)
    z = conv_sum(narrow_scr, tq_ref, length)
    qn_ref[...] = unit_rows(z * jax.nn.sigmoid(z), KEY ** (-0.5), heads).astype(bf16)
    wide_scr[...] = v_ref[...].astype(f32)
    z = conv_sum(wide_scr, tv_ref, length)
    vn_ref[...] = (z * jax.nn.sigmoid(z)).astype(bf16)

    rows, cols = grid_places(CHUNK)
    diagonal = rows == cols
    units = [(h, c) for c in range(chunks) for h in range(heads)]
    systems, vectors = [], []
    for h, c in units:
        at = slice(c * CHUNK, (c + 1) * CHUNK)
        keyed = slice(h * KEY, (h + 1) * KEY)
        between, grow, tail, whole = decay_terms(ld_ref[h, :, at], rows, cols)
        beta = as_column(beta_ref[h, :, at], diagonal)
        keys = kn_ref[at, keyed]
        products = dot(jnp.concatenate([keys, qn_ref[at, keyed]], axis=0), keys, 1, 1)
        systems.append(jnp.where(rows > cols, beta * between * products[:CHUNK], 0.0))
        att_ref[h, at, :] = (products[CHUNK:] * between).astype(bf16)
        vectors.append((beta, grow, tail, whole))
    inverses = unit_lower_inverses(systems, rows, cols)
    kept = []
    for (h, c), inverse, (beta, grow, tail, whole) in zip(units, inverses, vectors):
        at = slice(c * CHUNK, (c + 1) * CHUNK)
        keys32 = kn_ref[at, h * KEY : (h + 1) * KEY].astype(f32)
        values32 = vn_ref[at, h * VALUE : (h + 1) * VALUE].astype(f32)
        inv_ref[h, at, :] = inverse.astype(bf16)
        solved = dot(inverse, jnp.concatenate([(beta * grow) * keys32, beta * values32], axis=1))
        w_ref[h, at, :] = solved[:, :KEY].astype(bf16)
        u_ref[h, at, :] = solved[:, KEY:].astype(bf16)
        kept.append((tail * keys32).astype(bf16))
    begin = jnp.concatenate([diagonal.astype(f32), jnp.zeros((KEY, VALUE), f32)], axis=1)
    states = [begin] * heads
    for (h, c), tail_keys, (beta, grow, tail, whole) in zip(units, kept, vectors):
        at = slice(c * CHUNK, (c + 1) * CHUNK)
        state = states[h]
        start_ref[h, c * KEY : (c + 1) * KEY, :] = state.astype(bf16)
        source = jnp.concatenate([jnp.zeros((CHUNK, KEY), f32), u_ref[h, at, :].astype(f32)], axis=1)
        corrected = source - dot(w_ref[h, at, :], state)
        states[h] = whole * state + dot(tail_keys, corrected, 0, 0)
    for h in range(heads):
        final_ref[h, :, :] = states[h]


def forward_kernel(
    qn_ref, ld_ref, att_ref, u_ref, w_ref, start_ref, state_ref, gate_ref, gain_ref,
    gated_ref, mixed_ref, corr_ref, begin_ref,
):
    length = qn_ref.shape[0]
    rows, cols = grid_places(CHUNK)
    entering = state_ref[0]
    gain = gain_ref[...]
    for c in range(length // CHUNK):
        at = slice(c * CHUNK, (c + 1) * CHUNK)
        places = slice(c * KEY, (c + 1) * KEY)
        between, grow, tail, whole = decay_terms(ld_ref[0, :, at], rows, cols)
        begin = start_ref[0, places, KEY:].astype(f32) + dot(start_ref[0, places, :KEY], entering)
        begin_ref[0, places, :] = begin.astype(bf16)
        corrected = u_ref[0, at, :].astype(f32) - dot(w_ref[0, at, :], begin)
        corr_ref[0, at, :] = corrected.astype(bf16)
        mixed = dot(grow * qn_ref[at, :].astype(f32), begin) + dot(att_ref[0, at, :], corrected)
        mixed_ref[at, :] = mixed
        root = lax.rsqrt(jnp.mean(mixed * mixed, axis=-1, keepdims=True) + epsilon)
        gate = gate_ref[at, :]
        gated_ref[at, :] = (mixed * root * gain * (gate * jax.nn.sigmoid(gate))).astype(bf16)


def gate_back_kernel(
    dgated_ref, mixed_ref, gate_ref, gain_ref, qn_ref, kn_ref, ld_ref, att_ref, w_ref,
    dgate_ref, dmixed_ref, dcorr_ref, dgain_ref, after_ref, final_ref,
):
    length = qn_ref.shape[0]
    rows, cols = grid_places(CHUNK)
    gain = gain_ref[...]
    kept = []
    dgain = jnp.zeros((1, VALUE), f32)
    for c in range(length // CHUNK):
        at = slice(c * CHUNK, (c + 1) * CHUNK)
        mixed, gate, dgated = mixed_ref[at, :], gate_ref[at, :], dgated_ref[at, :]
        root = lax.rsqrt(jnp.mean(mixed * mixed, axis=-1, keepdims=True) + epsilon)
        normal = mixed * root
        sig = jax.nn.sigmoid(gate)
        act = gate * sig
        dgain = dgain + jnp.sum(dgated * normal * act, axis=0, keepdims=True)
        dgate_ref[at, :] = (dgated * normal * gain * (sig * (1.0 + gate * (1.0 - sig)))).astype(bf16)
        dnormal = dgated * act * gain
        dmixed = root * (dnormal - normal * jnp.mean(dnormal * normal, axis=-1, keepdims=True))
        dmixed_ref[0, at, :] = dmixed.astype(bf16)
        between, grow, tail, whole = decay_terms(ld_ref[0, :, at], rows, cols)
        dcorr = dot(att_ref[0, at, :], dmixed, 0, 0)
        dcorr_ref[0, at, :] = dcorr.astype(bf16)
        gradient = dot(grow * qn_ref[at, :].astype(f32), dmixed, 0, 0) - dot(w_ref[0, at, :], dcorr, 0, 0)
        kept.append((gradient, (tail * kn_ref[at, :].astype(f32)).astype(bf16), whole))
    dgain_ref[0, :, :] = dgain
    pending = jnp.concatenate([(rows == cols).astype(f32), jnp.zeros((KEY, VALUE), f32)], axis=1)
    for c in reversed(range(length // CHUNK)):
        gradient, tail_keys, whole = kept[c]
        at = slice(c * CHUNK, (c + 1) * CHUNK)
        after_ref[0, c * KEY : (c + 1) * KEY, :] = pending.astype(bf16)
        source = jnp.concatenate([jnp.zeros((KEY, KEY), f32), gradient], axis=1)
        pending = whole * pending + source - dot(w_ref[0, at, :], dot(tail_keys, pending), 0, 0)
    final_ref[0, :, :] = pending


def silu_slope(z):
    sig = jax.nn.sigmoid(z)
    return z * sig, sig * (1.0 + z * (1.0 - sig))


def conv_back(dz, taps_ref, dz_scr, pre_scr, dpre_ref, tail_ref, edge_ref, dtaps_ref):
    length = dz.shape[0]
    reach = taps_ref.shape[0] - 1
    taps = taps_ref[...].astype(f32)
    dz_scr[EDGE : EDGE + length, :] = dz
    total = taps[0:1] * dz
    sums = [jnp.sum(dz * pre_scr[EDGE : EDGE + length, :], axis=0, keepdims=True)]
    for offset in range(1, reach + 1):
        total = total + taps[offset : offset + 1] * dz_scr[EDGE + offset : EDGE + offset + length, :]
        sums.append(
            jnp.sum(dz * pre_scr[EDGE - offset : EDGE - offset + length, :], axis=0, keepdims=True)
        )
    dpre_ref[...] = total.astype(bf16)
    tail_ref[...] = total[length - 8 :, :]
    edge = taps[1:2] * dz_scr[EDGE - 7 : EDGE + 1, :]
    for offset in range(2, reach + 1):
        edge = edge + taps[offset : offset + 1] * dz_scr[EDGE - 8 + offset : EDGE + offset, :]
    edge_ref[...] = edge
    dtaps_ref[...] = jnp.concatenate(sums, axis=0)


def backward_kernel(
    gstate_ref, after_ref, dmixed_ref, dcorr_ref, begin_ref, corr_ref, inv_ref, att_ref, u_ref, w_ref,
    qn_ref, kn_ref, vn_ref, q_ref, k_ref, v_ref, tq_ref, tk_ref, tv_ref,
    ld_ref, beta_ref,
    dq_ref, dk_ref, dv_ref, tailq_ref, tailk_ref, tailv_ref, edgeq_ref, edgek_ref, edgev_ref,
    dtq_ref, dtk_ref, dtv_ref, dld_ref, dbeta_ref,
    dqn_scr, dkn_scr, dvn_scr, dn_scr, pn_scr, dw_scr, pw_scr,
):
    length = qn_ref.shape[0]
    rows, cols = grid_places(CHUNK)
    diagonal = rows == cols
    leaving = gstate_ref[0]
    for c in range(length // CHUNK):
        at = slice(c * CHUNK, (c + 1) * CHUNK)
        places = slice(c * KEY, (c + 1) * KEY)
        between, grow, tail, whole = decay_terms(ld_ref[0, :, at], rows, cols)
        beta = as_column(beta_ref[0, :, at], diagonal)
        keys, queries = kn_ref[at, :], qn_ref[at, :]
        keys32, queries32, values32 = keys.astype(f32), queries.astype(f32), vn_ref[at, :].astype(f32)
        dstate = after_ref[0, places, KEY:].astype(f32) + dot(after_ref[0, places, :KEY], leaving)
        dmixed, corrected, begin = dmixed_ref[0, at, :], corr_ref[0, at, :], begin_ref[0, places, :]
        dcorr = dcorr_ref[0, at, :].astype(f32) + dot(tail * keys32, dstate)
        datt = dot(dmixed, corrected, 1, 1)
        from_begin = dot(jnp.concatenate([dmixed, dcorr.astype(bf16)], axis=0), begin, 1, 1)
        dgrown, dw = from_begin[:CHUNK], -from_begin[CHUNK:]
        dtail_keys = dot(corrected, dstate, 1, 1)
        dwhole = jnp.sum(dstate * begin.astype(f32))
        back = dot(inv_ref[0, at, :], jnp.concatenate([dw, dcorr], axis=1), 0, 0)
        dright_keys, dright_values = back[:, :KEY], back[:, KEY:]
        dsystem = -dot(
            back, jnp.concatenate([w_ref[0, at, :], u_ref[0, at, :]], axis=1), 1, 1
        )
        products = dot(jnp.concatenate([keys, queries], axis=0), keys, 1, 1)
        decayed = jnp.where(rows > cols, between * products[:CHUNK], 0.0)
        dsys_decayed = dsystem * decayed
        dbeta = jnp.sum(dsys_decayed, axis=1, keepdims=True)
        pairs = beta * dsys_decayed + datt * (between * products[CHUNK:])
        dkk = jnp.where(rows > cols, dsystem * (beta * between), 0.0)
        dqk = datt * between
        dqk16, dkk16 = dqk.astype(bf16), dkk.astype(bf16)
        dqn_scr[at, :] = dot(dqk16, keys) + grow * dgrown
        dkn_scr[at, :] = (
            dot(jnp.concatenate([dqk16, dkk16], axis=0), jnp.concatenate([queries, keys], axis=0), 0, 0)
            + dot(dkk16, keys)
            + tail * dtail_keys
            + (beta * grow) * dright_keys
        )
        dvn_scr[at, :] = beta * dright_values
        keys_part = grow * jnp.sum(dright_keys * keys32, axis=1, keepdims=True)
        dbeta = dbeta + jnp.sum(dright_values * values32, axis=1, keepdims=True) + keys_part
        from_tail = tail * jnp.sum(dtail_keys * keys32, axis=1, keepdims=True)
        dcum = (
            jnp.sum(pairs, axis=1, keepdims=True)
            - as_column(jnp.sum(pairs, axis=0, keepdims=True), diagonal)
            + grow * jnp.sum(dgrown * queries32, axis=1, keepdims=True)
            + beta * keys_part
            - from_tail
        )
        dlast = whole * dwhole + jnp.sum(from_tail, axis=0, keepdims=True)
        dld_ref[0, :, at] = jnp.sum(jnp.where(rows >= cols, dcum, 0.0), axis=0, keepdims=True) + dlast
        dbeta_ref[0, :, at] = as_row(dbeta, diagonal)

    for scr in (dn_scr, dw_scr):
        scr[0:EDGE, :] = jnp.zeros((EDGE, scr.shape[1]), f32)
        scr[EDGE + length :, :] = jnp.zeros((EDGE, scr.shape[1]), f32)
    pn_scr[...] = q_ref[...].astype(f32)
    act, slope = silu_slope(conv_sum(pn_scr, tq_ref, length))
    root = lax.rsqrt(jnp.sum(act * act, axis=-1, keepdims=True) + epsilon)
    normal = act * root
    dy = dqn_scr[...] * KEY ** (-0.5)
    dz = root * (dy - normal * jnp.sum(normal * dy, axis=-1, keepdims=True)) * slope
    conv_back(dz, tq_ref, dn_scr, pn_scr, dq_ref, tailq_ref, edgeq_ref, dtq_ref)
    pn_scr[...] = k_ref[...].astype(f32)
    act, slope = silu_slope(conv_sum(pn_scr, tk_ref, length))
    root = lax.rsqrt(jnp.sum(act * act, axis=-1, keepdims=True) + epsilon)
    normal = act * root
    dy = dkn_scr[...]
    dz = root * (dy - normal * jnp.sum(normal * dy, axis=-1, keepdims=True)) * slope
    conv_back(dz, tk_ref, dn_scr, pn_scr, dk_ref, tailk_ref, edgek_ref, dtk_ref)
    pw_scr[...] = v_ref[...].astype(f32)
    act, slope = silu_slope(conv_sum(pw_scr, tv_ref, length))
    conv_back(dvn_scr[...] * slope, tv_ref, dw_scr, pw_scr, dv_ref, tailv_ref, edgev_ref, dtv_ref)


def tall(rows, cols):
    return pl.BlockSpec((rows, cols), lambda h: (0, h))


def deep(rows, cols):
    return pl.BlockSpec((1, rows, cols), lambda h: (h, 0, 0))


def shared(rows, cols):
    return pl.BlockSpec((rows, cols), lambda h: (0, 0))


def shape_of(dims, dtype):
    return jax.ShapeDtypeStruct(dims, dtype)


def call_heads(kernel, head_count, in_specs, outputs, scratch, flops, args):
    out_specs = [spec for spec, shape in outputs]
    out_shape = [shape for spec, shape in outputs]
    moved = sum(a.size * a.dtype.itemsize for a in list(args) + out_shape)
    return pl.pallas_call(
        kernel,
        grid=(head_count,),
        in_specs=in_specs,
        out_specs=out_specs,
        out_shape=out_shape,
        scratch_shapes=scratch,
        compiler_params=pltpu.CompilerParams(vmem_limit_bytes=VMEM_BYTES),
        cost_estimate=pl.CostEstimate(flops=flops, bytes_accessed=moved, transcendentals=0),
    )(*args)


def prepare(query_ext, key_ext, value_ext, conv_query, conv_key, conv_value, ld, beta):
    length = query_ext.shape[0] - EDGE
    heads = ld.shape[0]
    states = (length // CHUNK) * KEY
    out_shape = [
        shape_of((length, heads * KEY), bf16),
        shape_of((length, heads * KEY), bf16),
        shape_of((length, heads * VALUE), bf16),
        shape_of((heads, length, CHUNK), bf16),
        shape_of((heads, length, CHUNK), bf16),
        shape_of((heads, length, VALUE), bf16),
        shape_of((heads, length, KEY), bf16),
        shape_of((heads, states, KEY + VALUE), bf16),
        shape_of((heads, KEY, KEY + VALUE), f32),
    ]
    args = (query_ext, key_ext, value_ext, conv_query, conv_key, conv_value, ld, beta)
    moved = sum(a.size * a.dtype.itemsize for a in list(args) + out_shape)
    return pl.pallas_call(
        prep_kernel,
        out_shape=out_shape,
        in_specs=[pl.BlockSpec(memory_space=pltpu.VMEM)] * len(args),
        out_specs=[pl.BlockSpec(memory_space=pltpu.VMEM)] * len(out_shape),
        scratch_shapes=[
            pltpu.VMEM((length + EDGE, heads * VALUE), f32),
            pltpu.VMEM((length + EDGE, heads * KEY), f32),
        ],
        compiler_params=pltpu.CompilerParams(vmem_limit_bytes=VMEM_BYTES),
        cost_estimate=pl.CostEstimate(flops=2000000000, bytes_accessed=moved, transcendentals=0),
    )(*args)


def run_forward(qn, ld, att, u, w, starts, state_in, gate_pre, gain):
    length = qn.shape[0]
    heads = ld.shape[0]
    states = starts.shape[1]
    wide = tall(length, VALUE)
    wshape = (length, heads * VALUE)
    outputs = [
        (wide, shape_of(wshape, bf16)),
        (wide, shape_of(wshape, f32)),
        (deep(length, VALUE), shape_of((heads, length, VALUE), bf16)),
        (deep(states, VALUE), shape_of((heads, states, VALUE), bf16)),
    ]
    in_specs = [
        tall(length, KEY), deep(1, length), deep(length, CHUNK), deep(length, VALUE), deep(length, KEY),
        deep(states, KEY + VALUE), deep(KEY, VALUE), wide, shared(1, VALUE),
    ]
    args = (qn, ld, att, u, w, starts, state_in, gate_pre, gain)
    return call_heads(forward_kernel, heads, in_specs, outputs, [], 500000000, args)


def gate_back(dgated, mixed, gate_pre, gain, qn, kn, ld, att, w):
    length = qn.shape[0]
    heads = ld.shape[0]
    states = (length // CHUNK) * KEY
    wide = tall(length, VALUE)
    outputs = [
        (wide, shape_of((length, heads * VALUE), bf16)),
        (deep(length, VALUE), shape_of((heads, length, VALUE), bf16)),
        (deep(length, VALUE), shape_of((heads, length, VALUE), bf16)),
        (deep(1, VALUE), shape_of((heads, 1, VALUE), f32)),
        (deep(states, KEY + VALUE), shape_of((heads, states, KEY + VALUE), bf16)),
        (deep(KEY, KEY + VALUE), shape_of((heads, KEY, KEY + VALUE), f32)),
    ]
    in_specs = [
        wide, wide, wide, shared(1, VALUE), tall(length, KEY), tall(length, KEY), deep(1, length),
        deep(length, CHUNK), deep(length, KEY),
    ]
    args = (dgated, mixed, gate_pre, gain, qn, kn, ld, att, w)
    return call_heads(gate_back_kernel, heads, in_specs, outputs, [], 700000000, args)


def run_backward(
    gstate, after, dmixed, dcorr, begin, corr, inverse, att, u, w, qn, kn, vn,
    query_ext, key_ext, value_ext, conv_query, conv_key, conv_value, ld, beta,
):
    length = qn.shape[0]
    heads = ld.shape[0]
    states = after.shape[1]
    taps = conv_query.shape[0]
    narrow, wide = tall(length, KEY), tall(length, VALUE)
    ncols, wcols = heads * KEY, heads * VALUE
    outputs = [
        (narrow, shape_of((length, ncols), bf16)),
        (narrow, shape_of((length, ncols), bf16)),
        (wide, shape_of((length, wcols), bf16)),
        (tall(8, KEY), shape_of((8, ncols), f32)),
        (tall(8, KEY), shape_of((8, ncols), f32)),
        (tall(8, VALUE), shape_of((8, wcols), f32)),
        (tall(8, KEY), shape_of((8, ncols), f32)),
        (tall(8, KEY), shape_of((8, ncols), f32)),
        (tall(8, VALUE), shape_of((8, wcols), f32)),
        (tall(taps, KEY), shape_of((taps, ncols), f32)),
        (tall(taps, KEY), shape_of((taps, ncols), f32)),
        (tall(taps, VALUE), shape_of((taps, wcols), f32)),
        (deep(1, length), shape_of((heads, 1, length), f32)),
        (deep(1, length), shape_of((heads, 1, length), f32)),
    ]
    in_specs = [
        deep(KEY, VALUE), deep(states, KEY + VALUE), deep(length, VALUE), deep(length, VALUE),
        deep(states, VALUE), deep(length, VALUE), deep(length, CHUNK), deep(length, CHUNK),
        deep(length, VALUE), deep(length, KEY),
        narrow, narrow, wide,
        tall(length + EDGE, KEY), tall(length + EDGE, KEY), tall(length + EDGE, VALUE),
        tall(taps, KEY), tall(taps, KEY), tall(taps, VALUE),
        deep(1, length), deep(1, length),
    ]
    scratch = [
        pltpu.VMEM((length, KEY), f32), pltpu.VMEM((length, KEY), f32), pltpu.VMEM((length, VALUE), f32),
        pltpu.VMEM((length + 2 * EDGE, KEY), f32), pltpu.VMEM((length + EDGE, KEY), f32),
        pltpu.VMEM((length + 2 * EDGE, VALUE), f32), pltpu.VMEM((length + EDGE, VALUE), f32),
    ]
    args = (
        gstate, after, dmixed, dcorr, begin, corr, inverse, att, u, w, qn, kn, vn,
        query_ext, key_ext, value_ext, conv_query, conv_key, conv_value, ld, beta,
    )
    return call_heads(backward_kernel, heads, in_specs, outputs, scratch, 1500000000, args)


def weight_kernel(count, *refs):
    lefts, rights, out_ref = refs[:count], refs[count:-1], refs[-1]
    at = 0
    for left, right in zip(lefts, rights):
        width = right.shape[1]
        out_ref[:, at : at + width] = dot(left[...], right[...]).astype(bf16)
        at += width


def weight_gradients(pairs):
    lefts = [left for left, right in pairs]
    rights = [right for left, right in pairs]
    width, length = lefts[0].shape
    block = 256
    total = sum(r.shape[1] for r in rights)
    args = lefts + rights
    out = shape_of((width, total), bf16)
    moved = sum(a.size * a.dtype.itemsize for a in args + [out])
    return pl.pallas_call(
        functools.partial(weight_kernel, len(pairs)),
        grid=(width // block,),
        in_specs=[pl.BlockSpec((block, length), lambda i: (i, 0)) for left in lefts]
        + [pl.BlockSpec(r.shape, lambda i: (0, 0)) for r in rights],
        out_specs=pl.BlockSpec((block, total), lambda i: (i, 0)),
        out_shape=out,
        compiler_params=pltpu.CompilerParams(vmem_limit_bytes=VMEM_BYTES),
        cost_estimate=pl.CostEstimate(
            flops=2 * length * width * total, bytes_accessed=moved, transcendentals=0
        ),
    )(*args)


def from_behind(block, axis, distance):
    devices = range(lax.axis_size(axis))
    route = [(i - distance, i) for i in devices if i - distance in devices]
    return lax.ppermute(block, axis, route)


def swap_with(block, axis, distance):
    route = [(i, i ^ distance) for i in range(lax.axis_size(axis))]
    return lax.ppermute(block, axis, route)


def butterfly_sum(block, axis):
    distance = 1
    while distance < lax.axis_size(axis):
        block = block + swap_with(block, axis, distance)
        distance *= 2
    return block


def sum_over_heads(partial):
    rows = partial.shape[0] // 2
    odd = lax.axis_index("head") % 2 == 1
    low, high = partial[:rows], partial[rows:]
    own = jnp.where(odd, high, low).astype(f32)
    own = own + swap_with(jnp.where(odd, low, high).astype(bf16), "head", 1).astype(f32)
    distance = 2
    while distance < lax.axis_size("head"):
        sent = own.astype(bf16)
        own = sent.astype(f32) + swap_with(sent, "head", distance).astype(f32)
        distance *= 2
    kept = own.astype(bf16)
    other = swap_with(kept, "head", 1)
    return jnp.concatenate(
        [jnp.where(odd, other, kept), jnp.where(odd, kept, other)], axis=0
    ).astype(f32)


def exclusive_scan(joined, sign):
    own_t, own_b = joined[..., :KEY], joined[..., KEY:]
    send = joined
    before_t = before_b = None
    distance = 1
    size = lax.axis_size("seq")

    def product(a, b):
        return jnp.einsum("hij,hjk->hik", a, b, precision=lax.Precision.HIGH)

    while distance < size:
        last = distance * 2 >= size
        got = from_behind(
            (send[..., KEY:] if last else send).astype(bf16), "seq", sign * distance
        ).astype(f32)
        if before_t is None:
            before_t, before_b = got[..., :KEY], got[..., KEY:]
        else:
            moved = product(before_t, got)
            if last:
                before_b = before_b + moved
            else:
                before_t, before_b = moved[..., :KEY], before_b + moved[..., KEY:]
        if not last:
            send = product(own_t, jnp.concatenate([before_t, before_b], axis=-1))
            send = jnp.concatenate([send[..., :KEY], send[..., KEY:] + own_b], axis=-1)
        distance *= 2
    return before_b


def halving_scatter(left, right, order):
    size = lax.axis_size("seq")
    bits = size.bit_length() - 1
    here = lax.axis_index("seq")
    axes = list(range(bits))[::-1]
    rows, length = left.shape
    view = left.reshape((2,) * bits + (rows // size, length))
    held = None
    for bit in order[:bits] + list(range(len(order), bits)):
        axis = axes.index(bit)
        axes.remove(bit)
        mine = (here // 2**bit) % 2

        def part(array, which):
            return lax.dynamic_index_in_dim(array, which, axis, keepdims=False)

        if held is None:
            shape = (2,) * (bits - 1) + (rows // size, right.shape[1])
            sent = matmul_bf(part(view, 1 - mine).reshape(-1, length), right)
            got = swap_with(sent.astype(bf16), "seq", 2**bit).astype(f32)
            held = (matmul_bf(part(view, mine).reshape(-1, length), right) + got).reshape(shape)
        else:
            got = swap_with(part(held, 1 - mine).astype(bf16), "seq", 2**bit).astype(f32)
            held = part(held, mine) + got
    return held


def matmul_bf(first_operand, second_operand):
    return jnp.dot(first_operand, second_operand, preferred_element_type=f32)


def against_rows(first_operand, second_operand):
    return lax.dot_general(
        first_operand, second_operand, (((1,), (1,)), ((), ())), preferred_element_type=f32
    )


def row_norm(values, gain_vec):
    return (
        values * lax.rsqrt(jnp.mean(values * values, axis=-1, keepdims=True) + epsilon) * gain_vec
    )


def swiglu(gate_in, up_in):
    return jax.nn.silu(gate_in) * up_in


def per_device(
    block_input,
    norm1_gain,
    w_query,
    w_key,
    w_value,
    w_gate,
    w_decay,
    w_beta,
    conv_query,
    conv_key,
    conv_value,
    decay_rate,
    out_gain,
    w_out,
    norm2_gain,
    w_ffn_gate,
    w_ffn_up,
    w_ffn_down,
    cotangent,
):
    length = block_input.shape[0]
    head_count = w_decay.shape[1]
    key_cols = w_query.shape[1]
    value_cols = w_value.shape[1]
    ff_cols = w_ffn_gate.shape[1]
    edge_input = from_behind(block_input[length - EDGE :], "seq", 1)
    gain1 = norm1_gain.astype(f32)
    inputs32 = block_input.astype(f32)
    normed32, norm1_back = jax.vjp(row_norm, inputs32, gain1)
    normed = normed32.astype(bf16)
    normal1 = row_norm(inputs32, 1.0)
    edge_normed = row_norm(edge_input.astype(f32), gain1).astype(bf16)
    normed_ext = jnp.concatenate([edge_normed, normed], axis=0)
    gate_pre = matmul_bf(normed, w_gate)
    w_scalars = jnp.concatenate([w_decay, w_beta], axis=1)
    scalars = lax.dot_general(
        w_scalars, normed, (((0,), (1,)), ((), ())), preferred_element_type=f32
    )
    decay_pre, beta_pre = scalars[:head_count], scalars[head_count:]
    soft = jax.nn.softplus(decay_pre)
    rate = decay_rate[:, None]
    log_decay = (-rate * soft).reshape(head_count, 1, length)
    beta_gate = jax.nn.sigmoid(beta_pre)
    beta3 = beta_gate.reshape(head_count, 1, length)
    query_ext = matmul_bf(normed_ext, w_query).astype(bf16)
    key_ext = matmul_bf(normed_ext, w_key).astype(bf16)
    value_ext = matmul_bf(normed_ext, w_value).astype(bf16)
    qn, kn, vn, inverse, att, u, w, starts, composite = prepare(
        query_ext, key_ext, value_ext, conv_query, conv_key, conv_value, log_decay, beta3
    )
    state_in = exclusive_scan(composite, 1)
    gain_row = out_gain.astype(f32)[None]
    gated, mixed, corr, begin = run_forward(
        qn, log_decay, att, u, w, starts, state_in, gate_pre, gain_row
    )
    branch = sum_over_heads(matmul_bf(gated, w_out))
    middle = inputs32 + branch
    normed2_32, norm2_back = jax.vjp(row_norm, middle, norm2_gain.astype(f32))
    normed2 = normed2_32.astype(bf16)
    ffn_gate = matmul_bf(normed2, w_ffn_gate)
    ffn_up = matmul_bf(normed2, w_ffn_up)
    hidden32, swiglu_back = jax.vjp(swiglu, ffn_gate, ffn_up)
    hidden = hidden32.astype(bf16)
    grad_hidden = against_rows(cotangent, w_ffn_down)
    grad_fgate, grad_fup = swiglu_back(grad_hidden)
    grad_fgate = grad_fgate.astype(bf16)
    grad_fup = grad_fup.astype(bf16)
    grad_normed2 = sum_over_heads(
        against_rows(grad_fgate, w_ffn_gate) + against_rows(grad_fup, w_ffn_up)
    )
    ffn_out = lax.psum(matmul_bf(hidden, w_ffn_down).astype(bf16), "head").astype(f32)
    layer_out = (middle + ffn_out).astype(bf16)
    grad_middle_n, grad_gain2 = norm2_back(grad_normed2)
    grad_middle = cotangent.astype(f32) + grad_middle_n
    grad_branch = grad_middle.astype(bf16)
    grad_gated = against_rows(grad_branch, w_out)
    grad_gp, grad_mixed, grad_corr, grad_outgain, after, composite_back = gate_back(
        grad_gated, mixed, gate_pre, gain_row, qn, kn, log_decay, att, w
    )
    early = weight_gradients(
        [
            (normed2.T, grad_fgate),
            (normed2.T, grad_fup),
            (cotangent.T, hidden),
            (grad_branch.T, gated),
            (normed.T, grad_gp),
        ]
    )
    grad_state, early = lax.optimization_barrier((exclusive_scan(composite_back, -1), early))
    early = lax.psum_scatter(early, "seq", scatter_dimension=0, tiled=True).astype(f32)
    (
        grad_qp, grad_kp, grad_vp, tail_q, tail_k, tail_v, edge_q, edge_k, edge_v,
        taps_q, taps_k, taps_v, grad_log, grad_beta,
    ) = run_backward(
        grad_state, after, grad_mixed, grad_corr, begin, corr, inverse, att, u, w,
        qn, kn, vn, query_ext, key_ext, value_ext,
        conv_query, conv_key, conv_value, log_decay, beta3,
    )
    edges = from_behind(jnp.concatenate([edge_q, edge_k, edge_v], axis=1), "seq", -1)
    tails = (jnp.concatenate([tail_q, tail_k, tail_v], axis=1) + edges).astype(bf16)

    grad_qp = jnp.concatenate([grad_qp[: length - 8], tails[:, :key_cols]], axis=0)
    grad_kp = jnp.concatenate([grad_kp[: length - 8], tails[:, key_cols : 2 * key_cols]], axis=0)
    grad_vp = jnp.concatenate([grad_vp[: length - 8], tails[:, 2 * key_cols :]], axis=0)
    grad_log = grad_log.reshape(head_count, length)
    grad_beta = grad_beta.reshape(head_count, length)
    grad_dp = (-rate * jax.nn.sigmoid(decay_pre) * grad_log).astype(bf16)
    grad_bp = (beta_gate * (1.0 - beta_gate) * grad_beta).astype(bf16)
    grad_rate = -jnp.sum(grad_log * soft, axis=1)
    grad_scalars = jnp.concatenate([grad_dp, grad_bp], axis=0)
    normed_t = normed.T
    late_qk = halving_scatter(normed_t, jnp.concatenate([grad_qp, grad_kp], axis=1), [0, 1])
    late_v = halving_scatter(normed_t, grad_vp, [1, 0])
    grad_normed_part = (
        against_rows(grad_qp, w_query)
        + against_rows(grad_kp, w_key)
        + against_rows(grad_vp, w_value)
        + against_rows(grad_gp, w_gate)
        + lax.dot_general(
            grad_scalars, w_scalars, (((0,), (1,)), ((), ())), preferred_element_type=f32
        )
    )
    grad_gain1 = jnp.sum(grad_normed_part * normal1, axis=0)
    grad_normed = sum_over_heads(grad_normed_part)
    grad_input = grad_middle + norm1_back(grad_normed)[0]
    width = grad_gain1.shape[0]
    taps_count = conv_query.shape[0]
    grad_outgain = jnp.sum(grad_outgain, axis=(0, 1))
    small = jnp.concatenate(
        [
            jnp.concatenate([taps_q, taps_k, taps_v], axis=1),
            grad_gain2[None],
            jnp.pad(jnp.concatenate([grad_rate, grad_outgain]), (0, width - VALUE - head_count))[None],
            matmul_bf(grad_scalars, normed),
            grad_gain1[None],
        ],
        axis=0,
    )
    small = butterfly_sum(small, "seq")
    taps_sum = small[:taps_count]
    gain2_sum = small[taps_count]
    rate_sum = small[taps_count + 1, :head_count]
    scalars_sum = small[taps_count + 2 : taps_count + 2 + 2 * head_count]
    shared_sum = butterfly_sum(
        jnp.concatenate([small[-1], small[taps_count + 1, head_count : head_count + VALUE]]), "head"
    )
    gain1_sum, outgain_sum = shared_sum[:width], shared_sum[width:]

    def own_part(vec):
        piece = vec.shape[-1] // lax.axis_size("seq")
        return lax.dynamic_slice_in_dim(vec, lax.axis_index("seq") * piece, piece, axis=-1)

    scalars_sum = own_part(scalars_sum).T
    out_at = 3 * ff_cols
    gate_at = out_at + gated.shape[1]
    return (
        layer_out,
        grad_input,
        own_part(gain1_sum),
        late_qk[:, :key_cols],
        late_qk[:, key_cols:],
        late_v,
        early[:, gate_at:],
        scalars_sum[:, :head_count],
        scalars_sum[:, head_count:],
        taps_sum[:, :key_cols],
        taps_sum[:, key_cols : 2 * key_cols],
        taps_sum[:, 2 * key_cols :],
        rate_sum,
        own_part(outgain_sum),
        early[:, out_at:gate_at].T,
        own_part(gain2_sum),
        early[:, :ff_cols],
        early[:, ff_cols : 2 * ff_cols],
        early[:, 2 * ff_cols : 3 * ff_cols].T,
    )


def solution(mesh):
    return jax.shard_map(
        per_device,
        mesh=mesh,
        in_specs=(
            P("seq", None),
            P(),
            P(None, "head"),
            P(None, "head"),
            P(None, "head"),
            P(None, "head"),
            P(None, "head"),
            P(None, "head"),
            P(None, "head"),
            P(None, "head"),
            P(None, "head"),
            P("head"),
            P(),
            P("head", None),
            P(),
            P(None, "head"),
            P(None, "head"),
            P("head", None),
            P("seq", None),
        ),
        out_specs=(
            P("seq", None),
            P("seq", None),
            P("seq"),
            P("seq", "head"),
            P("seq", "head"),
            P("seq", "head"),
            P("seq", "head"),
            P("seq", "head"),
            P("seq", "head"),
            P(None, "head"),
            P(None, "head"),
            P(None, "head"),
            P("head"),
            P("seq"),
            P("head", "seq"),
            P("seq"),
            P("seq", "head"),
            P("seq", "head"),
            P("head", "seq"),
        ),
        check_vma=False,
    )
```

```python
import functools

import jax
import jax.numpy as jnp
from jax import lax
from jax.experimental import pallas as pl
from jax.experimental.pallas import tpu as pltpu
from jax.sharding import PartitionSpec as P

KEY = 128
VALUE = 256
CHUNK = 128
EDGE = 16
SUB = 16
VMEM_BYTES = 60 * 1024 * 1024

epsilon = 1e-06
f32 = jnp.float32
bf16 = jnp.bfloat16
highest_precision = lax.Precision.HIGHEST


def dot(first, second, over_first=1, over_second=0):
    return lax.dot_general(
        first.astype(bf16),
        second.astype(bf16),
        (((over_first,), (over_second,)), ((), ())),
        preferred_element_type=f32,
    )


def halves(values):
    high = values.astype(bf16)
    return high, (values - high.astype(f32)).astype(bf16)


def dot_fine(first, second):
    first_high, first_low = halves(first)
    second_high, second_low = halves(second)
    width = second.shape[1]
    wide = dot(first_high, jnp.concatenate([second_high, second_low], axis=1))
    return wide[:, :width] + wide[:, width:] + dot(first_low, second_high)


def grid_places(extent):
    rows = lax.broadcasted_iota(jnp.int32, (extent, extent), 0)
    cols = lax.broadcasted_iota(jnp.int32, (extent, extent), 1)
    return rows, cols


def as_row(column, diagonal):
    return jnp.sum(jnp.where(diagonal, column, 0.0), axis=0, keepdims=True)


def as_column(row, diagonal):
    return jnp.sum(jnp.where(diagonal, row, 0.0), axis=1, keepdims=True)


def unit_lower_inverses(systems, rows, cols):
    extent = systems[0].shape[0]
    count = extent // SUB
    units = len(systems)
    same = rows // SUB == cols // SUB
    packed = jnp.concatenate(
        [jnp.sum(jnp.where(same, s, 0.0).reshape(count, SUB, extent), axis=0) for s in systems], axis=0
    )
    stacked = jnp.concatenate(halves(packed), axis=0)
    shape = (units, SUB, extent)
    places = lax.broadcasted_iota(jnp.int32, shape, 1)
    solved = (places == lax.broadcasted_iota(jnp.int32, shape, 2) % SUB).astype(f32)
    for j in range(SUB - 1):
        spread = dot(stacked, (same & (rows % SUB == j)).astype(f32))
        column = spread[: units * SUB] + spread[units * SUB :]
        solved = solved - column.reshape(shape) * solved[:, j : j + 1, :]
    inverses = [
        jnp.where(same, jnp.concatenate([solved[n]] * count, axis=0), 0.0) for n in range(units)
    ]
    size = SUB
    while size < extent:
        below = (rows // (2 * size) == cols // (2 * size)) & (rows // size > cols // size)
        joined = [
            dot_fine(inverse, jnp.where(below, s, 0.0)) for inverse, s in zip(inverses, systems)
        ]
        joined = [dot_fine(product, inverse) for product, inverse in zip(joined, inverses)]
        inverses = [inverse - product for inverse, product in zip(inverses, joined)]
        size *= 2
    return inverses


def decay_terms(ld_row, rows, cols):
    cum_col = jnp.sum(jnp.where(rows >= cols, ld_row, 0.0), axis=1, keepdims=True)
    cum_row = as_row(cum_col, rows == cols)
    last = cum_col[CHUNK - 1 :, :]
    between = jnp.where(rows >= cols, jnp.exp(jnp.where(rows >= cols, cum_col - cum_row, 0.0)), 0.0)
    return between, jnp.exp(cum_col), jnp.exp(last - cum_col), jnp.exp(last)


def conv_sum(padded_ref, taps_ref, length):
    taps = taps_ref[...].astype(f32)
    summed = taps[0:1] * padded_ref[EDGE : EDGE + length, :]
    for offset in range(1, taps_ref.shape[0]):
        summed = summed + taps[offset : offset + 1] * padded_ref[EDGE - offset : EDGE - offset + length, :]
    return summed


def unit_rows(values, scale, heads):
    parts = []
    for h in range(heads):
        part = values[:, h * KEY : (h + 1) * KEY]
        parts.append(
            part * (lax.rsqrt(jnp.sum(part * part, axis=-1, keepdims=True) + epsilon) * scale)
        )
    return jnp.concatenate(parts, axis=1)


def row_norm(values, gain_vec):
    return (
        values * lax.rsqrt(jnp.mean(values * values, axis=-1, keepdims=True) + epsilon) * gain_vec
    )


def prep_kernel(
    x_ref, edge_ref, gain_ref, wq_ref, wk_ref, wv_ref, wd_ref, wb_ref, rate_ref, tq_ref, tk_ref, tv_ref,
    normed_ref, decay_ref, q_ref, k_ref, v_ref, ld_ref, beta_ref,
    qn_ref, kn_ref, vn_ref, inv_ref, att_ref, u_ref, w_ref, start_ref, final_ref,
    normed_scr, wide_scr, narrow_scr,
):
    length = qn_ref.shape[0]
    heads = ld_ref.shape[0]
    chunks = length // CHUNK
    gain = gain_ref[...]
    normed_scr[:EDGE, :] = row_norm(edge_ref[...].astype(f32), gain).astype(bf16)
    normed = row_norm(x_ref[...].astype(f32), gain).astype(bf16)
    normed_scr[EDGE:, :] = normed
    normed_ref[...] = normed
    decay_pre = dot(normed, wd_ref[...])
    decay_ref[...] = decay_pre
    softplus = jnp.maximum(decay_pre, 0.0) + jnp.log1p(jnp.exp(-jnp.abs(decay_pre)))
    log_decay = -rate_ref[...] * softplus
    beta_gate = jax.nn.sigmoid(dot(normed, wb_ref[...]))
    pre = dot(normed_scr[...], wk_ref[...]).astype(bf16)
    k_ref[...] = pre
    narrow_scr[...] = pre.astype(f32)
    z = conv_sum(narrow_scr, tk_ref, length)
    kn_ref[...] = unit_rows(z * jax.nn.sigmoid(z), 1.0, heads).astype(bf16)
    pre = dot(normed_scr[...], wq_ref[...]).astype(bf16)
    q_ref[...] = pre
    narrow_scr[...] = pre.astype(f32)
    z = conv_sum(narrow_scr, tq_ref, length)
    qn_ref[...] = unit_rows(z * jax.nn.sigmoid(z), KEY ** (-0.5), heads).astype(bf16)
    pre = dot(normed_scr[...], wv_ref[...]).astype(bf16)
    v_ref[...] = pre
    wide_scr[...] = pre.astype(f32)
    z = conv_sum(wide_scr, tv_ref, length)
    vn_ref[...] = (z * jax.nn.sigmoid(z)).astype(bf16)

    rows, cols = grid_places(CHUNK)
    diagonal = rows == cols
    units = [(h, c) for c in range(chunks) for h in range(heads)]
    systems, vectors = [], []
    for h, c in units:
        at = slice(c * CHUNK, (c + 1) * CHUNK)
        keyed = slice(h * KEY, (h + 1) * KEY)
        ld_row = as_row(log_decay[at, h : h + 1], diagonal)
        ld_ref[h, :, at] = ld_row
        between, grow, tail, whole = decay_terms(ld_row, rows, cols)
        beta = beta_gate[at, h : h + 1]
        beta_ref[h, :, at] = as_row(beta, diagonal)
        keys = kn_ref[at, keyed]
        products = dot(jnp.concatenate([keys, qn_ref[at, keyed]], axis=0), keys, 1, 1)
        systems.append(jnp.where(rows > cols, beta * between * products[:CHUNK], 0.0))
        att_ref[h, at, :] = (products[CHUNK:] * between).astype(bf16)
        vectors.append((beta, grow, tail, whole))
    inverses = unit_lower_inverses(systems, rows, cols)
    kept = []
    for (h, c), inverse, (beta, grow, tail, whole) in zip(units, inverses, vectors):
        at = slice(c * CHUNK, (c + 1) * CHUNK)
        keys32 = kn_ref[at, h * KEY : (h + 1) * KEY].astype(f32)
        values32 = vn_ref[at, h * VALUE : (h + 1) * VALUE].astype(f32)
        inv_ref[h, at, :] = inverse.astype(bf16)
        solved = dot(inverse, jnp.concatenate([(beta * grow) * keys32, beta * values32], axis=1))
        w_ref[h, at, :] = solved[:, :KEY].astype(bf16)
        u_ref[h, at, :] = solved[:, KEY:].astype(bf16)
        kept.append((tail * keys32).astype(bf16))
    begin = jnp.concatenate([diagonal.astype(f32), jnp.zeros((KEY, VALUE), f32)], axis=1)
    states = [begin] * heads
    for (h, c), tail_keys, (beta, grow, tail, whole) in zip(units, kept, vectors):
        at = slice(c * CHUNK, (c + 1) * CHUNK)
        state = states[h]
        start_ref[h, c * KEY : (c + 1) * KEY, :] = state.astype(bf16)
        source = jnp.concatenate([jnp.zeros((CHUNK, KEY), f32), u_ref[h, at, :].astype(f32)], axis=1)
        corrected = source - dot(w_ref[h, at, :], state)
        states[h] = whole * state + dot(tail_keys, corrected, 0, 0)
    for h in range(heads):
        final_ref[h, :, :] = states[h]


def forward_kernel(
    qn_ref, ld_ref, att_ref, u_ref, w_ref, start_ref, state_ref, gate_ref, gain_ref, wout_ref,
    gated_ref, mixed_ref, corr_ref, begin_ref, branch_ref, sum_scr,
):
    length = qn_ref.shape[0]
    rows, cols = grid_places(CHUNK)
    entering = state_ref[0]
    gain = gain_ref[...]
    for c in range(length // CHUNK):
        at = slice(c * CHUNK, (c + 1) * CHUNK)
        places = slice(c * KEY, (c + 1) * KEY)
        between, grow, tail, whole = decay_terms(ld_ref[0, :, at], rows, cols)
        begin = start_ref[0, places, KEY:].astype(f32) + dot(start_ref[0, places, :KEY], entering)
        begin_ref[0, places, :] = begin.astype(bf16)
        corrected = u_ref[0, at, :].astype(f32) - dot(w_ref[0, at, :], begin)
        corr_ref[0, at, :] = corrected.astype(bf16)
        mixed = dot(grow * qn_ref[at, :].astype(f32), begin) + dot(att_ref[0, at, :], corrected)
        mixed_ref[at, :] = mixed
        root = lax.rsqrt(jnp.mean(mixed * mixed, axis=-1, keepdims=True) + epsilon)
        gate = gate_ref[at, :]
        gated_ref[at, :] = (mixed * root * gain * (gate * jax.nn.sigmoid(gate))).astype(bf16)
    part = dot(gated_ref[...], wout_ref[...])

    @pl.when(pl.program_id(0) == 0)
    def start_sum():
        sum_scr[...] = part

    @pl.when(pl.program_id(0) > 0)
    def add_sum():
        sum_scr[...] += part

    @pl.when(pl.program_id(0) == pl.num_programs(0) - 1)
    def give_sum():
        branch_ref[...] = sum_scr[...].astype(bf16)


def gate_back_kernel(
    dgated_ref, mixed_ref, gate_ref, gain_ref, qn_ref, kn_ref, ld_ref, att_ref, w_ref,
    dgate_ref, dmixed_ref, dcorr_ref, dgain_ref, after_ref, final_ref,
):
    length = qn_ref.shape[0]
    rows, cols = grid_places(CHUNK)
    gain = gain_ref[...]
    kept = []
    dgain = jnp.zeros((1, VALUE), f32)
    for c in range(length // CHUNK):
        at = slice(c * CHUNK, (c + 1) * CHUNK)
        mixed, gate, dgated = mixed_ref[at, :], gate_ref[at, :], dgated_ref[at, :]
        root = lax.rsqrt(jnp.mean(mixed * mixed, axis=-1, keepdims=True) + epsilon)
        normal = mixed * root
        sig = jax.nn.sigmoid(gate)
        act = gate * sig
        dgain = dgain + jnp.sum(dgated * normal * act, axis=0, keepdims=True)
        dgate_ref[at, :] = (dgated * normal * gain * (sig * (1.0 + gate * (1.0 - sig)))).astype(bf16)
        dnormal = dgated * act * gain
        dmixed = root * (dnormal - normal * jnp.mean(dnormal * normal, axis=-1, keepdims=True))
        dmixed_ref[0, at, :] = dmixed.astype(bf16)
        between, grow, tail, whole = decay_terms(ld_ref[0, :, at], rows, cols)
        dcorr = dot(att_ref[0, at, :], dmixed, 0, 0)
        dcorr_ref[0, at, :] = dcorr.astype(bf16)
        gradient = dot(grow * qn_ref[at, :].astype(f32), dmixed, 0, 0) - dot(w_ref[0, at, :], dcorr, 0, 0)
        kept.append((gradient, (tail * kn_ref[at, :].astype(f32)).astype(bf16), whole))
    dgain_ref[0, :, :] = dgain
    pending = jnp.concatenate([(rows == cols).astype(f32), jnp.zeros((KEY, VALUE), f32)], axis=1)
    for c in reversed(range(length // CHUNK)):
        gradient, tail_keys, whole = kept[c]
        at = slice(c * CHUNK, (c + 1) * CHUNK)
        after_ref[0, c * KEY : (c + 1) * KEY, :] = pending.astype(bf16)
        source = jnp.concatenate([jnp.zeros((KEY, KEY), f32), gradient], axis=1)
        pending = whole * pending + source - dot(w_ref[0, at, :], dot(tail_keys, pending), 0, 0)
    final_ref[0, :, :] = pending


def silu_slope(z):
    sig = jax.nn.sigmoid(z)
    return z * sig, sig * (1.0 + z * (1.0 - sig))


def conv_back(dz, taps_ref, dz_scr, pre_scr, dpre_ref, tail_ref, edge_ref, dtaps_ref):
    length = dz.shape[0]
    reach = taps_ref.shape[0] - 1
    taps = taps_ref[...].astype(f32)
    dz_scr[EDGE : EDGE + length, :] = dz
    total = taps[0:1] * dz
    sums = [jnp.sum(dz * pre_scr[EDGE : EDGE + length, :], axis=0, keepdims=True)]
    for offset in range(1, reach + 1):
        total = total + taps[offset : offset + 1] * dz_scr[EDGE + offset : EDGE + offset + length, :]
        sums.append(
            jnp.sum(dz * pre_scr[EDGE - offset : EDGE - offset + length, :], axis=0, keepdims=True)
        )
    dpre_ref[...] = total.astype(bf16)
    tail_ref[...] = total[length - 8 :, :]
    edge = taps[1:2] * dz_scr[EDGE - 7 : EDGE + 1, :]
    for offset in range(2, reach + 1):
        edge = edge + taps[offset : offset + 1] * dz_scr[EDGE - 8 + offset : EDGE + offset, :]
    edge_ref[...] = edge
    dtaps_ref[...] = jnp.concatenate(sums, axis=0)


def backward_kernel(
    gstate_ref, after_ref, dmixed_ref, dcorr_ref, begin_ref, corr_ref, inv_ref, att_ref, u_ref, w_ref,
    qn_ref, kn_ref, vn_ref, q_ref, k_ref, v_ref, tq_ref, tk_ref, tv_ref,
    ld_ref, beta_ref,
    dq_ref, dk_ref, dv_ref, tailq_ref, tailk_ref, tailv_ref, edgeq_ref, edgek_ref, edgev_ref,
    dtq_ref, dtk_ref, dtv_ref, dld_ref, dbeta_ref,
    dqn_scr, dkn_scr, dvn_scr, dn_scr, pn_scr, dw_scr, pw_scr,
):
    length = qn_ref.shape[0]
    rows, cols = grid_places(CHUNK)
    diagonal = rows == cols
    leaving = gstate_ref[0]
    for c in range(length // CHUNK):
        at = slice(c * CHUNK, (c + 1) * CHUNK)
        places = slice(c * KEY, (c + 1) * KEY)
        between, grow, tail, whole = decay_terms(ld_ref[0, :, at], rows, cols)
        beta = as_column(beta_ref[0, :, at], diagonal)
        keys, queries = kn_ref[at, :], qn_ref[at, :]
        keys32, queries32, values32 = keys.astype(f32), queries.astype(f32), vn_ref[at, :].astype(f32)
        dstate = after_ref[0, places, KEY:].astype(f32) + dot(after_ref[0, places, :KEY], leaving)
        dmixed, corrected, begin = dmixed_ref[0, at, :], corr_ref[0, at, :], begin_ref[0, places, :]
        dcorr = dcorr_ref[0, at, :].astype(f32) + dot(tail * keys32, dstate)
        datt = dot(dmixed, corrected, 1, 1)
        from_begin = dot(jnp.concatenate([dmixed, dcorr.astype(bf16)], axis=0), begin, 1, 1)
        dgrown, dw = from_begin[:CHUNK], -from_begin[CHUNK:]
        dtail_keys = dot(corrected, dstate, 1, 1)
        dwhole = jnp.sum(dstate * begin.astype(f32))
        back = dot(inv_ref[0, at, :], jnp.concatenate([dw, dcorr], axis=1), 0, 0)
        dright_keys, dright_values = back[:, :KEY], back[:, KEY:]
        dsystem = -dot(
            back, jnp.concatenate([w_ref[0, at, :], u_ref[0, at, :]], axis=1), 1, 1
        )
        products = dot(jnp.concatenate([keys, queries], axis=0), keys, 1, 1)
        decayed = jnp.where(rows > cols, between * products[:CHUNK], 0.0)
        dsys_decayed = dsystem * decayed
        dbeta = jnp.sum(dsys_decayed, axis=1, keepdims=True)
        pairs = beta * dsys_decayed + datt * (between * products[CHUNK:])
        dkk = jnp.where(rows > cols, dsystem * (beta * between), 0.0)
        dqk = datt * between
        dqk16, dkk16 = dqk.astype(bf16), dkk.astype(bf16)
        dqn_scr[at, :] = dot(dqk16, keys) + grow * dgrown
        dkn_scr[at, :] = (
            dot(jnp.concatenate([dqk16, dkk16], axis=0), jnp.concatenate([queries, keys], axis=0), 0, 0)
            + dot(dkk16, keys)
            + tail * dtail_keys
            + (beta * grow) * dright_keys
        )
        dvn_scr[at, :] = beta * dright_values
        keys_part = grow * jnp.sum(dright_keys * keys32, axis=1, keepdims=True)
        dbeta = dbeta + jnp.sum(dright_values * values32, axis=1, keepdims=True) + keys_part
        from_tail = tail * jnp.sum(dtail_keys * keys32, axis=1, keepdims=True)
        dcum = (
            jnp.sum(pairs, axis=1, keepdims=True)
            - as_column(jnp.sum(pairs, axis=0, keepdims=True), diagonal)
            + grow * jnp.sum(dgrown * queries32, axis=1, keepdims=True)
            + beta * keys_part
            - from_tail
        )
        dlast = whole * dwhole + jnp.sum(from_tail, axis=0, keepdims=True)
        dld_ref[0, :, at] = jnp.sum(jnp.where(rows >= cols, dcum, 0.0), axis=0, keepdims=True) + dlast
        dbeta_ref[0, :, at] = as_row(dbeta, diagonal)

    for scr in (dn_scr, dw_scr):
        scr[0:EDGE, :] = jnp.zeros((EDGE, scr.shape[1]), f32)
        scr[EDGE + length :, :] = jnp.zeros((EDGE, scr.shape[1]), f32)
    pn_scr[...] = q_ref[...].astype(f32)
    act, slope = silu_slope(conv_sum(pn_scr, tq_ref, length))
    root = lax.rsqrt(jnp.sum(act * act, axis=-1, keepdims=True) + epsilon)
    normal = act * root
    dy = dqn_scr[...] * KEY ** (-0.5)
    dz = root * (dy - normal * jnp.sum(normal * dy, axis=-1, keepdims=True)) * slope
    conv_back(dz, tq_ref, dn_scr, pn_scr, dq_ref, tailq_ref, edgeq_ref, dtq_ref)
    pn_scr[...] = k_ref[...].astype(f32)
    act, slope = silu_slope(conv_sum(pn_scr, tk_ref, length))
    root = lax.rsqrt(jnp.sum(act * act, axis=-1, keepdims=True) + epsilon)
    normal = act * root
    dy = dkn_scr[...]
    dz = root * (dy - normal * jnp.sum(normal * dy, axis=-1, keepdims=True)) * slope
    conv_back(dz, tk_ref, dn_scr, pn_scr, dk_ref, tailk_ref, edgek_ref, dtk_ref)
    pw_scr[...] = v_ref[...].astype(f32)
    act, slope = silu_slope(conv_sum(pw_scr, tv_ref, length))
    conv_back(dvn_scr[...] * slope, tv_ref, dw_scr, pw_scr, dv_ref, tailv_ref, edgev_ref, dtv_ref)


def tall(rows, cols):
    return pl.BlockSpec((rows, cols), lambda h: (0, h))


def deep(rows, cols):
    return pl.BlockSpec((1, rows, cols), lambda h: (h, 0, 0))


def shared(rows, cols):
    return pl.BlockSpec((rows, cols), lambda h: (0, 0))


def shape_of(dims, dtype):
    return jax.ShapeDtypeStruct(dims, dtype)


def call_heads(kernel, head_count, in_specs, outputs, scratch, flops, args):
    out_specs = [spec for spec, shape in outputs]
    out_shape = [shape for spec, shape in outputs]
    moved = sum(a.size * a.dtype.itemsize for a in list(args) + out_shape)
    return pl.pallas_call(
        kernel,
        grid=(head_count,),
        in_specs=in_specs,
        out_specs=out_specs,
        out_shape=out_shape,
        scratch_shapes=scratch,
        compiler_params=pltpu.CompilerParams(vmem_limit_bytes=VMEM_BYTES),
        cost_estimate=pl.CostEstimate(flops=flops, bytes_accessed=moved, transcendentals=0),
    )(*args)


def prepare(x, edge, gain, w_query, w_key, w_value, w_decay, w_beta, rate, conv_query, conv_key, conv_value):
    length, width = x.shape
    heads = w_decay.shape[1]
    states = (length // CHUNK) * KEY
    ncols, wcols = heads * KEY, heads * VALUE
    out_shape = [
        shape_of((length, width), bf16),
        shape_of((length, heads), f32),
        shape_of((length + EDGE, ncols), bf16),
        shape_of((length + EDGE, ncols), bf16),
        shape_of((length + EDGE, wcols), bf16),
        shape_of((heads, 1, length), f32),
        shape_of((heads, 1, length), f32),
        shape_of((length, ncols), bf16),
        shape_of((length, ncols), bf16),
        shape_of((length, wcols), bf16),
        shape_of((heads, length, CHUNK), bf16),
        shape_of((heads, length, CHUNK), bf16),
        shape_of((heads, length, VALUE), bf16),
        shape_of((heads, length, KEY), bf16),
        shape_of((heads, states, KEY + VALUE), bf16),
        shape_of((heads, KEY, KEY + VALUE), f32),
    ]
    args = (
        x, edge, gain, w_query, w_key, w_value, w_decay, w_beta, rate, conv_query, conv_key, conv_value
    )
    moved = sum(a.size * a.dtype.itemsize for a in list(args) + out_shape)
    return pl.pallas_call(
        prep_kernel,
        out_shape=out_shape,
        in_specs=[pl.BlockSpec(memory_space=pltpu.VMEM)] * len(args),
        out_specs=[pl.BlockSpec(memory_space=pltpu.VMEM)] * len(out_shape),
        scratch_shapes=[
            pltpu.VMEM((length + EDGE, width), bf16),
            pltpu.VMEM((length + EDGE, wcols), f32),
            pltpu.VMEM((length + EDGE, ncols), f32),
        ],
        compiler_params=pltpu.CompilerParams(vmem_limit_bytes=VMEM_BYTES),
        cost_estimate=pl.CostEstimate(flops=2000000000, bytes_accessed=moved, transcendentals=0),
    )(*args)


def run_forward(qn, ld, att, u, w, starts, state_in, gate_pre, gain, w_out):
    length = qn.shape[0]
    heads = ld.shape[0]
    states = starts.shape[1]
    wide = tall(length, VALUE)
    wshape = (length, heads * VALUE)
    outputs = [
        (wide, shape_of(wshape, bf16)),
        (wide, shape_of(wshape, f32)),
        (deep(length, VALUE), shape_of((heads, length, VALUE), bf16)),
        (deep(states, VALUE), shape_of((heads, states, VALUE), bf16)),
        (shared(length, w_out.shape[1]), shape_of((length, w_out.shape[1]), bf16)),
    ]
    in_specs = [
        tall(length, KEY), deep(1, length), deep(length, CHUNK), deep(length, VALUE), deep(length, KEY),
        deep(states, KEY + VALUE), deep(KEY, VALUE), wide, shared(1, VALUE),
        pl.BlockSpec((VALUE, w_out.shape[1]), lambda h: (h, 0)),
    ]
    args = (qn, ld, att, u, w, starts, state_in, gate_pre, gain, w_out)
    scratch = [pltpu.VMEM((length, w_out.shape[1]), f32)]
    return call_heads(forward_kernel, heads, in_specs, outputs, scratch, 1000000000, args)


def gate_back(dgated, mixed, gate_pre, gain, qn, kn, ld, att, w):
    length = qn.shape[0]
    heads = ld.shape[0]
    states = (length // CHUNK) * KEY
    wide = tall(length, VALUE)
    outputs = [
        (wide, shape_of((length, heads * VALUE), bf16)),
        (deep(length, VALUE), shape_of((heads, length, VALUE), bf16)),
        (deep(length, VALUE), shape_of((heads, length, VALUE), bf16)),
        (deep(1, VALUE), shape_of((heads, 1, VALUE), f32)),
        (deep(states, KEY + VALUE), shape_of((heads, states, KEY + VALUE), bf16)),
        (deep(KEY, KEY + VALUE), shape_of((heads, KEY, KEY + VALUE), f32)),
    ]
    in_specs = [
        wide, wide, wide, shared(1, VALUE), tall(length, KEY), tall(length, KEY), deep(1, length),
        deep(length, CHUNK), deep(length, KEY),
    ]
    args = (dgated, mixed, gate_pre, gain, qn, kn, ld, att, w)
    return call_heads(gate_back_kernel, heads, in_specs, outputs, [], 700000000, args)


def run_backward(
    gstate, after, dmixed, dcorr, begin, corr, inverse, att, u, w, qn, kn, vn,
    query_ext, key_ext, value_ext, conv_query, conv_key, conv_value, ld, beta,
):
    length = qn.shape[0]
    heads = ld.shape[0]
    states = after.shape[1]
    taps = conv_query.shape[0]
    narrow, wide = tall(length, KEY), tall(length, VALUE)
    ncols, wcols = heads * KEY, heads * VALUE
    outputs = [
        (narrow, shape_of((length, ncols), bf16)),
        (narrow, shape_of((length, ncols), bf16)),
        (wide, shape_of((length, wcols), bf16)),
        (tall(8, KEY), shape_of((8, ncols), f32)),
        (tall(8, KEY), shape_of((8, ncols), f32)),
        (tall(8, VALUE), shape_of((8, wcols), f32)),
        (tall(8, KEY), shape_of((8, ncols), f32)),
        (tall(8, KEY), shape_of((8, ncols), f32)),
        (tall(8, VALUE), shape_of((8, wcols), f32)),
        (tall(taps, KEY), shape_of((taps, ncols), f32)),
        (tall(taps, KEY), shape_of((taps, ncols), f32)),
        (tall(taps, VALUE), shape_of((taps, wcols), f32)),
        (deep(1, length), shape_of((heads, 1, length), f32)),
        (deep(1, length), shape_of((heads, 1, length), f32)),
    ]
    in_specs = [
        deep(KEY, VALUE), deep(states, KEY + VALUE), deep(length, VALUE), deep(length, VALUE),
        deep(states, VALUE), deep(length, VALUE), deep(length, CHUNK), deep(length, CHUNK),
        deep(length, VALUE), deep(length, KEY),
        narrow, narrow, wide,
        tall(length + EDGE, KEY), tall(length + EDGE, KEY), tall(length + EDGE, VALUE),
        tall(taps, KEY), tall(taps, KEY), tall(taps, VALUE),
        deep(1, length), deep(1, length),
    ]
    scratch = [
        pltpu.VMEM((length, KEY), f32), pltpu.VMEM((length, KEY), f32), pltpu.VMEM((length, VALUE), f32),
        pltpu.VMEM((length + 2 * EDGE, KEY), f32), pltpu.VMEM((length + EDGE, KEY), f32),
        pltpu.VMEM((length + 2 * EDGE, VALUE), f32), pltpu.VMEM((length + EDGE, VALUE), f32),
    ]
    args = (
        gstate, after, dmixed, dcorr, begin, corr, inverse, att, u, w, qn, kn, vn,
        query_ext, key_ext, value_ext, conv_query, conv_key, conv_value, ld, beta,
    )
    return call_heads(backward_kernel, heads, in_specs, outputs, scratch, 1500000000, args)


def weight_kernel(count, first, *refs):
    lefts, rights, out_ref = refs[:count], refs[count : 2 * count], refs[-1]
    at = first
    for left, right in zip(lefts, rights):
        width = right.shape[1]
        out_ref[:, at : at + width] = dot(left[...], right[...], 0, 0).astype(bf16)
        at += width


def weight_gradients(pairs, room=0, into=None):
    lefts = [left for left, right in pairs]
    rights = [right for left, right in pairs]
    length, width = lefts[0].shape
    block = 256
    total = sum(r.shape[1] for r in rights)
    args = lefts + rights
    out = shape_of((width, room + total), bf16) if into is None else shape_of(into.shape, bf16)
    in_specs = [pl.BlockSpec((length, block), lambda i: (0, i)) for left in lefts]
    in_specs += [pl.BlockSpec(r.shape, lambda i: (0, 0)) for r in rights]
    moved = sum(a.size * a.dtype.itemsize for a in args) + 2 * width * total
    aliases = {}
    if into is not None:
        aliases = {len(args): 0}
        args = args + [into]
        in_specs.append(pl.BlockSpec(memory_space=pl.ANY))
    return pl.pallas_call(
        functools.partial(weight_kernel, len(pairs), room),
        grid=(width // block,),
        in_specs=in_specs,
        out_specs=pl.BlockSpec((block, room + total), lambda i: (i, 0)),
        out_shape=out,
        input_output_aliases=aliases,
        compiler_params=pltpu.CompilerParams(vmem_limit_bytes=VMEM_BYTES),
        cost_estimate=pl.CostEstimate(
            flops=2 * length * width * total, bytes_accessed=moved, transcendentals=0
        ),
    )(*args)


def from_behind(block, axis, distance):
    devices = range(lax.axis_size(axis))
    route = [(i - distance, i) for i in devices if i - distance in devices]
    return lax.ppermute(block, axis, route)


def swap_with(block, axis, distance):
    route = [(i, i ^ distance) for i in range(lax.axis_size(axis))]
    return lax.ppermute(block, axis, route)


def butterfly_steps(block, axis):
    distance = 1
    while distance < lax.axis_size(axis):
        block = block + swap_with(block, axis, distance)
        yield block
        distance *= 2


def last_of(steps, held=None):
    for held in steps:
        pass
    return held


def sum_over_heads(partial, beside=iter(())):
    def exchange(sent, distance):
        got = swap_with(sent, "head", distance)
        other = next(beside, None)
        return got if other is None else lax.optimization_barrier((got, other))[0]

    rows = partial.shape[0] // 2
    odd = lax.axis_index("head") % 2 == 1
    low, high = partial[:rows], partial[rows:]
    own = jnp.where(odd, high, low).astype(f32)
    own = own + exchange(jnp.where(odd, low, high).astype(bf16), 1).astype(f32)
    distance = 2
    while distance < lax.axis_size("head"):
        sent = own.astype(bf16)
        own = sent.astype(f32) + exchange(sent, distance).astype(f32)
        distance *= 2
    kept = own.astype(bf16)
    other = exchange(kept, 1)
    return jnp.concatenate(
        [jnp.where(odd, other, kept), jnp.where(odd, kept, other)], axis=0
    ).astype(f32)


def exclusive_scan(joined, sign, beside):
    own_t, own_b = joined[..., :KEY], joined[..., KEY:]
    send = joined
    before_t = before_b = None
    distance = 1
    size = lax.axis_size("seq")

    def product(a, b):
        return jnp.einsum("hij,hjk->hik", a, b, precision=lax.Precision.HIGH)

    while distance < size:
        last = distance * 2 >= size
        got = from_behind(
            (send[..., KEY:] if last else send).astype(bf16), "seq", sign * distance
        )
        if before_t is None:
            got, beside = lax.optimization_barrier((got, beside))
        got = got.astype(f32)
        if before_t is None:
            before_t, before_b = got[..., :KEY], got[..., KEY:]
        else:
            moved = product(before_t, got)
            if last:
                before_b = before_b + moved
            else:
                before_t, before_b = moved[..., :KEY], before_b + moved[..., KEY:]
        if not last:
            send = product(own_t, jnp.concatenate([before_t, before_b], axis=-1))
            send = jnp.concatenate([send[..., :KEY], send[..., KEY:] + own_b], axis=-1)
        distance *= 2
    return before_b, beside


def split_shards(left, bit):
    size = lax.axis_size("seq")
    bits = size.bit_length() - 1
    mine = (lax.axis_index("seq") // 2**bit) % 2
    view = left.reshape((left.shape[0],) + (2,) * bits + (left.shape[1] // size,))

    def part(which):
        return lax.dynamic_index_in_dim(view, which, bits - bit, keepdims=False).reshape(
            left.shape[0], -1
        )

    return part(1 - mine), part(mine)


def halving_scatter(parts, right, order):
    size = lax.axis_size("seq")
    bits = size.bit_length() - 1
    here = lax.axis_index("seq")
    order = [bit for bit in order if bit < bits] + list(range(len(order), bits))
    away, home = parts
    sent = inner_rows(away, right).astype(bf16)
    got = swap_with(sent, "seq", 2 ** order[0]).astype(f32)
    held = inner_rows(home, right) + got
    axes = [bit for bit in range(bits)[::-1] if bit != order[0]]
    yield held
    held = held.reshape((2,) * (bits - 1) + (held.shape[0] // 2 ** (bits - 1), right.shape[1]))
    for bit in order[1:]:
        axis = axes.index(bit)
        axes.remove(bit)
        mine = (here // 2**bit) % 2
        sent = lax.dynamic_index_in_dim(held, 1 - mine, axis, keepdims=False).astype(bf16)
        got = swap_with(sent, "seq", 2**bit).astype(f32)
        held = lax.dynamic_index_in_dim(held, mine, axis, keepdims=False) + got
        yield held


def inner_rows(first_operand, second_operand):
    return lax.dot_general(
        first_operand, second_operand, (((0,), (0,)), ((), ())), preferred_element_type=f32
    )


def matmul_bf(first_operand, second_operand):
    return jnp.dot(first_operand, second_operand, preferred_element_type=f32)


def against_rows(first_operand, second_operand):
    return lax.dot_general(
        first_operand, second_operand, (((1,), (1,)), ((), ())), preferred_element_type=f32
    )


def swiglu(gate_in, up_in):
    return jax.nn.silu(gate_in) * up_in


def per_device(
    block_input,
    norm1_gain,
    w_query,
    w_key,
    w_value,
    w_gate,
    w_decay,
    w_beta,
    conv_query,
    conv_key,
    conv_value,
    decay_rate,
    out_gain,
    w_out,
    norm2_gain,
    w_ffn_gate,
    w_ffn_up,
    w_ffn_down,
    cotangent,
):
    length = block_input.shape[0]
    head_count = w_decay.shape[1]
    key_cols = w_query.shape[1]
    value_cols = w_value.shape[1]
    ff_cols = w_ffn_gate.shape[1]
    size = lax.axis_size("seq")
    edge_input = from_behind(block_input[length - EDGE :], "seq", 1)
    gain1 = norm1_gain.astype(f32)
    (
        normed, decay_cols, query_ext, key_ext, value_ext, log_decay, beta3,
        qn, kn, vn, inverse, att, u, w, starts, composite,
    ) = prepare(
        block_input, edge_input, gain1[None], w_query, w_key, w_value, w_decay, w_beta,
        decay_rate[None], conv_query, conv_key, conv_value,
    )
    inputs32 = block_input.astype(f32)
    gate_pre = matmul_bf(normed, w_gate)
    normed_near, normed_far = split_shards(normed, 0), split_shards(normed, 1 % (size.bit_length() - 1))
    state_in, (gate_pre, normed_near, normed_far) = exclusive_scan(
        composite, 1, (gate_pre, normed_near, normed_far)
    )
    gain_row = out_gain.astype(f32)[None]
    gated, mixed, corr, begin, branch_part = run_forward(
        qn, log_decay, att, u, w, starts, state_in, gate_pre, gain_row, w_out
    )
    branch = sum_over_heads(branch_part)
    middle = inputs32 + branch
    normed2_32, norm2_back = jax.vjp(row_norm, middle, norm2_gain.astype(f32))
    normed2 = normed2_32.astype(bf16)
    ffn_gate = matmul_bf(normed2, w_ffn_gate)
    ffn_up = matmul_bf(normed2, w_ffn_up)
    hidden32, swiglu_back = jax.vjp(swiglu, ffn_gate, ffn_up)
    hidden = hidden32.astype(bf16)
    grad_hidden = against_rows(cotangent, w_ffn_down)
    grad_fgate, grad_fup = swiglu_back(grad_hidden)
    grad_fgate = grad_fgate.astype(bf16)
    grad_fup = grad_fup.astype(bf16)
    early = weight_gradients(
        [(normed2, grad_fgate), (normed2, grad_fup), (cotangent, hidden)],
        room=gated.shape[1] + gate_pre.shape[1],
    )
    grad_normed2 = sum_over_heads(
        (against_rows(grad_fgate, w_ffn_gate) + against_rows(grad_fup, w_ffn_up)).astype(bf16)
    )
    grad_normed2, early = lax.optimization_barrier((grad_normed2, early))
    ffn_part = matmul_bf(hidden, w_ffn_down).astype(bf16)
    grad_middle_n, grad_gain2 = norm2_back(grad_normed2)
    grad_middle = cotangent.astype(f32) + grad_middle_n
    grad_branch = grad_middle.astype(bf16)
    grad_gated = against_rows(grad_branch, w_out)
    grad_gp, grad_mixed, grad_corr, grad_outgain, after, composite_back = gate_back(
        grad_gated, mixed, gate_pre, gain_row, qn, kn, log_decay, att, w
    )
    composite_back, ffn_part = lax.optimization_barrier((composite_back, ffn_part))
    ffn_out = sum_over_heads(ffn_part)
    layer_out = (middle + ffn_out).astype(bf16)
    early = weight_gradients([(grad_branch, gated), (normed, grad_gp)], into=early)
    grad_state, early = exclusive_scan(composite_back, -1, early)
    early = lax.psum_scatter(early, "seq", scatter_dimension=0, tiled=True).astype(f32)
    (
        grad_qp, grad_kp, grad_vp, tail_q, tail_k, tail_v, edge_q, edge_k, edge_v,
        taps_q, taps_k, taps_v, grad_log, grad_beta,
    ) = run_backward(
        grad_state, after, grad_mixed, grad_corr, begin, corr, inverse, att, u, w,
        qn, kn, vn, query_ext, key_ext, value_ext,
        conv_query, conv_key, conv_value, log_decay, beta3,
    )
    edges = from_behind(jnp.concatenate([edge_q, edge_k, edge_v], axis=1), "seq", -1)
    tails = (jnp.concatenate([tail_q, tail_k, tail_v], axis=1) + edges).astype(bf16)

    grad_qp = jnp.concatenate([grad_qp[: length - 8], tails[:, :key_cols]], axis=0)
    grad_kp = jnp.concatenate([grad_kp[: length - 8], tails[:, key_cols : 2 * key_cols]], axis=0)
    grad_vp = jnp.concatenate([grad_vp[: length - 8], tails[:, 2 * key_cols :]], axis=0)
    decay_pre = decay_cols.T
    soft = jax.nn.softplus(decay_pre)
    rate = decay_rate[:, None]
    beta_gate = beta3.reshape(head_count, length)
    w_scalars = jnp.concatenate([w_decay, w_beta], axis=1)
    normal1 = row_norm(inputs32, 1.0)
    grad_log = grad_log.reshape(head_count, length)
    grad_beta = grad_beta.reshape(head_count, length)
    grad_dp = (-rate * jax.nn.sigmoid(decay_pre) * grad_log).astype(bf16)
    grad_bp = (beta_gate * (1.0 - beta_gate) * grad_beta).astype(bf16)
    grad_rate = -jnp.sum(grad_log * soft, axis=1)
    grad_scalars = jnp.concatenate([grad_dp, grad_bp], axis=0)
    late_qk = last_of(halving_scatter(normed_near, jnp.concatenate([grad_qp, grad_kp], axis=1), [0, 1]))
    late_v = last_of(halving_scatter(normed_far, grad_vp, [1, 0]))
    grad_normed_part = (
        against_rows(grad_qp, w_query)
        + against_rows(grad_kp, w_key)
        + against_rows(grad_vp, w_value)
        + against_rows(grad_gp, w_gate)
        + lax.dot_general(
            grad_scalars, w_scalars, (((0,), (1,)), ((), ())), preferred_element_type=f32
        )
    )
    grad_gain1 = jnp.sum(grad_normed_part * normal1, axis=0)
    width = grad_gain1.shape[0]
    taps_count = conv_query.shape[0]
    grad_outgain = jnp.sum(grad_outgain, axis=(0, 1))
    small = jnp.concatenate(
        [
            jnp.concatenate([taps_q, taps_k, taps_v], axis=1),
            grad_gain2[None],
            jnp.pad(jnp.concatenate([grad_rate, grad_outgain]), (0, width - VALUE - head_count))[None],
            matmul_bf(grad_scalars, normed),
            grad_gain1[None],
        ],
        axis=0,
    )
    small_steps = butterfly_steps(small, "seq")
    small_taken = []

    def small_beside():
        for block in small_steps:
            small_taken.append(block)
            yield block

    grad_normed = sum_over_heads(grad_normed_part.astype(bf16), small_beside())
    small = last_of(small_steps, small_taken[-1])
    shared_sum = last_of(
        butterfly_steps(
            jnp.concatenate([small[-1], small[taps_count + 1, head_count : head_count + VALUE]]), "head"
        )
    )
    norm1_back = jax.vjp(row_norm, inputs32, gain1)[1]
    grad_input = grad_middle + norm1_back(grad_normed)[0]
    taps_sum = small[:taps_count]
    gain2_sum = small[taps_count]
    rate_sum = small[taps_count + 1, :head_count]
    scalars_sum = small[taps_count + 2 : taps_count + 2 + 2 * head_count]
    gain1_sum, outgain_sum = shared_sum[:width], shared_sum[width:]

    def own_part(vec):
        piece = vec.shape[-1] // lax.axis_size("seq")
        return lax.dynamic_slice_in_dim(vec, lax.axis_index("seq") * piece, piece, axis=-1)

    scalars_sum = own_part(scalars_sum).T
    out_cols = gated.shape[1]
    mid_cols = out_cols + gate_pre.shape[1]
    return (
        layer_out,
        grad_input,
        own_part(gain1_sum),
        late_qk[:, :key_cols],
        late_qk[:, key_cols:],
        late_v,
        early[:, out_cols:mid_cols],
        scalars_sum[:, :head_count],
        scalars_sum[:, head_count:],
        taps_sum[:, :key_cols],
        taps_sum[:, key_cols : 2 * key_cols],
        taps_sum[:, 2 * key_cols :],
        rate_sum,
        own_part(outgain_sum),
        early[:, :out_cols].T,
        own_part(gain2_sum),
        early[:, mid_cols : mid_cols + ff_cols],
        early[:, mid_cols + ff_cols : mid_cols + 2 * ff_cols],
        early[:, mid_cols + 2 * ff_cols :].T,
    )


def solution(mesh):
    return jax.shard_map(
        per_device,
        mesh=mesh,
        in_specs=(
            P("seq", None),
            P(),
            P(None, "head"),
            P(None, "head"),
            P(None, "head"),
            P(None, "head"),
            P(None, "head"),
            P(None, "head"),
            P(None, "head"),
            P(None, "head"),
            P(None, "head"),
            P("head"),
            P(),
            P("head", None),
            P(),
            P(None, "head"),
            P(None, "head"),
            P("head", None),
            P("seq", None),
        ),
        out_specs=(
            P("seq", None),
            P("seq", None),
            P("seq"),
            P("seq", "head"),
            P("seq", "head"),
            P("seq", "head"),
            P("seq", "head"),
            P("seq", "head"),
            P("seq", "head"),
            P(None, "head"),
            P(None, "head"),
            P(None, "head"),
            P("head"),
            P("seq"),
            P("head", "seq"),
            P("seq"),
            P("seq", "head"),
            P("seq", "head"),
            P("head", "seq"),
        ),
        check_vma=False,
    )
```

```python
import functools

import jax
import jax.numpy as jnp
from jax import lax
from jax.experimental import pallas as pl
from jax.experimental.pallas import tpu as pltpu
from jax.sharding import PartitionSpec as P

KEY = 128
VALUE = 256
CHUNK = 128
EDGE = 16
SUB = 16
VMEM_BYTES = 60 * 1024 * 1024
COST = pl.CostEstimate(flops=0, bytes_accessed=0, transcendentals=0)

epsilon = 1e-06
f32 = jnp.float32
bf16 = jnp.bfloat16
highest_precision = lax.Precision.HIGHEST


def dot(first, second, over_first=1, over_second=0):
    return lax.dot_general(
        first.astype(bf16),
        second.astype(bf16),
        (((over_first,), (over_second,)), ((), ())),
        preferred_element_type=f32,
    )


def halves(values):
    high = values.astype(bf16)
    return high, (values - high.astype(f32)).astype(bf16)


def dot_fine(first, second):
    first_high, first_low = halves(first)
    second_high, second_low = halves(second)
    width = second.shape[1]
    wide = dot(first_high, jnp.concatenate([second_high, second_low], axis=1))
    return wide[:, :width] + wide[:, width:] + dot(first_low, second_high)


def grid_places(extent):
    rows = lax.broadcasted_iota(jnp.int32, (extent, extent), 0)
    cols = lax.broadcasted_iota(jnp.int32, (extent, extent), 1)
    return rows, cols


def as_row(column, diagonal):
    return jnp.sum(jnp.where(diagonal, column, 0.0), axis=0, keepdims=True)


def as_column(row, diagonal):
    return jnp.sum(jnp.where(diagonal, row, 0.0), axis=1, keepdims=True)


def unit_lower_inverses(systems, rows, cols):
    extent = systems[0].shape[0]
    count = extent // SUB
    units = len(systems)
    same = rows // SUB == cols // SUB
    packed = jnp.concatenate(
        [jnp.sum(jnp.where(same, s, 0.0).reshape(count, SUB, extent), axis=0) for s in systems], axis=0
    )
    stacked = jnp.concatenate(halves(packed), axis=0)
    shape = (units, SUB, extent)
    places = lax.broadcasted_iota(jnp.int32, shape, 1)
    solved = (places == lax.broadcasted_iota(jnp.int32, shape, 2) % SUB).astype(f32)
    for j in range(SUB - 1):
        spread = dot(stacked, (same & (rows % SUB == j)).astype(f32))
        column = spread[: units * SUB] + spread[units * SUB :]
        solved = solved - column.reshape(shape) * solved[:, j : j + 1, :]
    inverses = [
        jnp.where(same, jnp.concatenate([solved[n]] * count, axis=0), 0.0) for n in range(units)
    ]
    size = SUB
    while size < extent:
        below = (rows // (2 * size) == cols // (2 * size)) & (rows // size > cols // size)
        joined = [
            dot_fine(inverse, jnp.where(below, s, 0.0)) for inverse, s in zip(inverses, systems)
        ]
        joined = [dot_fine(product, inverse) for product, inverse in zip(joined, inverses)]
        inverses = [inverse - product for inverse, product in zip(inverses, joined)]
        size *= 2
    return inverses


def decay_terms(ld_row, rows, cols):
    cum_col = jnp.sum(jnp.where(rows >= cols, ld_row, 0.0), axis=1, keepdims=True)
    cum_row = as_row(cum_col, rows == cols)
    last = cum_col[CHUNK - 1 :, :]
    between = jnp.where(rows >= cols, jnp.exp(jnp.where(rows >= cols, cum_col - cum_row, 0.0)), 0.0)
    return between, jnp.exp(cum_col), jnp.exp(last - cum_col), jnp.exp(last)


def conv_sum(padded_ref, taps_ref, length):
    taps = taps_ref[...].astype(f32)
    summed = taps[0:1] * padded_ref[EDGE : EDGE + length, :]
    for offset in range(1, taps_ref.shape[0]):
        summed = summed + taps[offset : offset + 1] * padded_ref[EDGE - offset : EDGE - offset + length, :]
    return summed


def unit_rows(values, scale, heads):
    parts = []
    for h in range(heads):
        part = values[:, h * KEY : (h + 1) * KEY]
        parts.append(
            part * (lax.rsqrt(jnp.sum(part * part, axis=-1, keepdims=True) + epsilon) * scale)
        )
    return jnp.concatenate(parts, axis=1)


def row_norm(values, gain_vec):
    return (
        values * lax.rsqrt(jnp.mean(values * values, axis=-1, keepdims=True) + epsilon) * gain_vec
    )


def prep_kernel(
    x_ref, edge_ref, gain_ref, wq_ref, wk_ref, wv_ref, wd_ref, wb_ref, rate_ref, tq_ref, tk_ref, tv_ref,
    normed_ref, decay_ref, q_ref, k_ref, v_ref, ld_ref, beta_ref,
    qn_ref, kn_ref, vn_ref, inv_ref, att_ref, u_ref, w_ref, start_ref, final_ref,
    normed_scr, wide_scr, narrow_scr,
):
    length = qn_ref.shape[0]
    heads = ld_ref.shape[0]
    chunks = length // CHUNK
    gain = gain_ref[...]
    normed_scr[:EDGE, :] = row_norm(edge_ref[...].astype(f32), gain).astype(bf16)
    normed = row_norm(x_ref[...].astype(f32), gain).astype(bf16)
    normed_scr[EDGE:, :] = normed
    normed_ref[...] = normed
    decay_pre = dot(normed, wd_ref[...], 1, 1)
    decay_ref[...] = decay_pre
    softplus = jnp.maximum(decay_pre, 0.0) + jnp.log1p(jnp.exp(-jnp.abs(decay_pre)))
    log_decay = -rate_ref[...] * softplus
    beta_gate = jax.nn.sigmoid(dot(normed, wb_ref[...], 1, 1))
    pre = dot(normed_scr[...], wk_ref[...]).astype(bf16)
    k_ref[...] = pre
    narrow_scr[...] = pre.astype(f32)
    z = conv_sum(narrow_scr, tk_ref, length)
    kn_ref[...] = unit_rows(z * jax.nn.sigmoid(z), 1.0, heads).astype(bf16)
    pre = dot(normed_scr[...], wq_ref[...]).astype(bf16)
    q_ref[...] = pre
    narrow_scr[...] = pre.astype(f32)
    z = conv_sum(narrow_scr, tq_ref, length)
    qn_ref[...] = unit_rows(z * jax.nn.sigmoid(z), KEY ** (-0.5), heads).astype(bf16)
    pre = dot(normed_scr[...], wv_ref[...]).astype(bf16)
    v_ref[...] = pre
    wide_scr[...] = pre.astype(f32)
    z = conv_sum(wide_scr, tv_ref, length)
    vn_ref[...] = (z * jax.nn.sigmoid(z)).astype(bf16)

    rows, cols = grid_places(CHUNK)
    diagonal = rows == cols
    units = [(h, c) for c in range(chunks) for h in range(heads)]
    systems, vectors = [], []
    for h, c in units:
        at = slice(c * CHUNK, (c + 1) * CHUNK)
        keyed = slice(h * KEY, (h + 1) * KEY)
        ld_row = as_row(log_decay[at, h : h + 1], diagonal)
        ld_ref[h, :, at] = ld_row
        between, grow, tail, whole = decay_terms(ld_row, rows, cols)
        beta = beta_gate[at, h : h + 1]
        beta_ref[h, :, at] = as_row(beta, diagonal)
        keys = kn_ref[at, keyed]
        products = dot(jnp.concatenate([keys, qn_ref[at, keyed]], axis=0), keys, 1, 1)
        systems.append(jnp.where(rows > cols, beta * between * products[:CHUNK], 0.0))
        att_ref[h, at, :] = (products[CHUNK:] * between).astype(bf16)
        vectors.append((beta, grow, tail, whole))
    inverses = unit_lower_inverses(systems, rows, cols)
    kept = []
    for (h, c), inverse, (beta, grow, tail, whole) in zip(units, inverses, vectors):
        at = slice(c * CHUNK, (c + 1) * CHUNK)
        keys32 = kn_ref[at, h * KEY : (h + 1) * KEY].astype(f32)
        values32 = vn_ref[at, h * VALUE : (h + 1) * VALUE].astype(f32)
        inv_ref[h, at, :] = inverse.astype(bf16)
        solved = dot(inverse, jnp.concatenate([(beta * grow) * keys32, beta * values32], axis=1))
        w_ref[h, at, :] = solved[:, :KEY].astype(bf16)
        u_ref[h, at, :] = solved[:, KEY:].astype(bf16)
        kept.append((tail * keys32).astype(bf16))
    begin = jnp.concatenate([diagonal.astype(f32), jnp.zeros((KEY, VALUE), f32)], axis=1)
    states = [begin] * heads
    for (h, c), tail_keys, (beta, grow, tail, whole) in zip(units, kept, vectors):
        at = slice(c * CHUNK, (c + 1) * CHUNK)
        state = states[h]
        start_ref[h, c * KEY : (c + 1) * KEY, :] = state.astype(bf16)
        source = jnp.concatenate([jnp.zeros((CHUNK, KEY), f32), u_ref[h, at, :].astype(f32)], axis=1)
        corrected = source - dot(w_ref[h, at, :], state)
        states[h] = whole * state + dot(tail_keys, corrected, 0, 0)
    for h in range(heads):
        final_ref[h, :, :] = states[h]


def forward_kernel(
    qn_ref, ld_ref, att_ref, u_ref, w_ref, start_ref, state_ref, gate_ref, gain_ref, wout_ref,
    gated_ref, mixed_ref, corr_ref, begin_ref, branch_ref, sum_scr,
):
    length = qn_ref.shape[0]
    rows, cols = grid_places(CHUNK)
    entering = state_ref[0]
    gain = gain_ref[...]
    for c in range(length // CHUNK):
        at = slice(c * CHUNK, (c + 1) * CHUNK)
        places = slice(c * KEY, (c + 1) * KEY)
        between, grow, tail, whole = decay_terms(ld_ref[0, :, at], rows, cols)
        begin = start_ref[0, places, KEY:].astype(f32) + dot(start_ref[0, places, :KEY], entering)
        begin_ref[0, places, :] = begin.astype(bf16)
        corrected = u_ref[0, at, :].astype(f32) - dot(w_ref[0, at, :], begin)
        corr_ref[0, at, :] = corrected.astype(bf16)
        mixed = dot(grow * qn_ref[at, :].astype(f32), begin) + dot(att_ref[0, at, :], corrected)
        mixed_ref[at, :] = mixed
        root = lax.rsqrt(jnp.mean(mixed * mixed, axis=-1, keepdims=True) + epsilon)
        gate = gate_ref[at, :]
        gated_ref[at, :] = (mixed * root * gain * (gate * jax.nn.sigmoid(gate))).astype(bf16)
    part = dot(gated_ref[...], wout_ref[...])

    @pl.when(pl.program_id(0) == 0)
    def start_sum():
        sum_scr[...] = part

    @pl.when(pl.program_id(0) > 0)
    def add_sum():
        sum_scr[...] += part

    @pl.when(pl.program_id(0) == pl.num_programs(0) - 1)
    def give_sum():
        branch_ref[...] = sum_scr[...].astype(bf16)


def gate_back_kernel(
    dgated_ref, mixed_ref, gate_ref, gain_ref, qn_ref, kn_ref, ld_ref, att_ref, w_ref,
    dgate_ref, dmixed_ref, dcorr_ref, dgain_ref, after_ref, final_ref,
):
    length = qn_ref.shape[0]
    rows, cols = grid_places(CHUNK)
    gain = gain_ref[...]
    kept = []
    dgain = jnp.zeros((1, VALUE), f32)
    for c in range(length // CHUNK):
        at = slice(c * CHUNK, (c + 1) * CHUNK)
        mixed, gate, dgated = mixed_ref[at, :], gate_ref[at, :], dgated_ref[at, :]
        root = lax.rsqrt(jnp.mean(mixed * mixed, axis=-1, keepdims=True) + epsilon)
        normal = mixed * root
        sig = jax.nn.sigmoid(gate)
        act = gate * sig
        dgain = dgain + jnp.sum(dgated * normal * act, axis=0, keepdims=True)
        dgate_ref[at, :] = (dgated * normal * gain * (sig * (1.0 + gate * (1.0 - sig)))).astype(bf16)
        dnormal = dgated * act * gain
        dmixed = root * (dnormal - normal * jnp.mean(dnormal * normal, axis=-1, keepdims=True))
        dmixed_ref[0, at, :] = dmixed.astype(bf16)
        between, grow, tail, whole = decay_terms(ld_ref[0, :, at], rows, cols)
        dcorr = dot(att_ref[0, at, :], dmixed, 0, 0)
        dcorr_ref[0, at, :] = dcorr.astype(bf16)
        gradient = dot(grow * qn_ref[at, :].astype(f32), dmixed, 0, 0) - dot(w_ref[0, at, :], dcorr, 0, 0)
        kept.append((gradient, (tail * kn_ref[at, :].astype(f32)).astype(bf16), whole))
    dgain_ref[0, :, :] = dgain
    pending = jnp.concatenate([(rows == cols).astype(f32), jnp.zeros((KEY, VALUE), f32)], axis=1)
    for c in reversed(range(length // CHUNK)):
        gradient, tail_keys, whole = kept[c]
        at = slice(c * CHUNK, (c + 1) * CHUNK)
        after_ref[0, c * KEY : (c + 1) * KEY, :] = pending.astype(bf16)
        source = jnp.concatenate([jnp.zeros((KEY, KEY), f32), gradient], axis=1)
        pending = whole * pending + source - dot(w_ref[0, at, :], dot(tail_keys, pending), 0, 0)
    final_ref[0, :, :] = pending


def silu_slope(z):
    sig = jax.nn.sigmoid(z)
    return z * sig, sig * (1.0 + z * (1.0 - sig))


def conv_back(dz, taps_ref, dz_scr, pre_scr, dpre_ref, tail_ref, edge_ref, dtaps_ref):
    length = dz.shape[0]
    reach = taps_ref.shape[0] - 1
    taps = taps_ref[...].astype(f32)
    dz_scr[EDGE : EDGE + length, :] = dz
    total = taps[0:1] * dz
    sums = [jnp.sum(dz * pre_scr[EDGE : EDGE + length, :], axis=0, keepdims=True)]
    for offset in range(1, reach + 1):
        total = total + taps[offset : offset + 1] * dz_scr[EDGE + offset : EDGE + offset + length, :]
        sums.append(
            jnp.sum(dz * pre_scr[EDGE - offset : EDGE - offset + length, :], axis=0, keepdims=True)
        )
    dpre_ref[...] = total.astype(bf16)
    tail_ref[...] = total[length - 8 :, :]
    edge = taps[1:2] * dz_scr[EDGE - 7 : EDGE + 1, :]
    for offset in range(2, reach + 1):
        edge = edge + taps[offset : offset + 1] * dz_scr[EDGE - 8 + offset : EDGE + offset, :]
    edge_ref[...] = edge
    dtaps_ref[...] = jnp.concatenate(sums, axis=0)


def backward_kernel(
    gstate_ref, after_ref, dmixed_ref, dcorr_ref, begin_ref, corr_ref, inv_ref, att_ref, u_ref, w_ref,
    qn_ref, kn_ref, vn_ref, q_ref, k_ref, v_ref, tq_ref, tk_ref, tv_ref,
    ld_ref, beta_ref,
    dq_ref, dk_ref, dv_ref, tailq_ref, tailk_ref, tailv_ref, edgeq_ref, edgek_ref, edgev_ref,
    dtq_ref, dtk_ref, dtv_ref, dld_ref, dbeta_ref,
    dqn_scr, dkn_scr, dvn_scr, dn_scr, pn_scr, dw_scr, pw_scr,
):
    length = qn_ref.shape[0]
    rows, cols = grid_places(CHUNK)
    diagonal = rows == cols
    leaving = gstate_ref[0]
    for c in range(length // CHUNK):
        at = slice(c * CHUNK, (c + 1) * CHUNK)
        places = slice(c * KEY, (c + 1) * KEY)
        between, grow, tail, whole = decay_terms(ld_ref[0, :, at], rows, cols)
        beta = as_column(beta_ref[0, :, at], diagonal)
        keys, queries = kn_ref[at, :], qn_ref[at, :]
        keys32, queries32, values32 = keys.astype(f32), queries.astype(f32), vn_ref[at, :].astype(f32)
        dstate = after_ref[0, places, KEY:].astype(f32) + dot(after_ref[0, places, :KEY], leaving)
        dmixed, corrected, begin = dmixed_ref[0, at, :], corr_ref[0, at, :], begin_ref[0, places, :]
        dcorr = dcorr_ref[0, at, :].astype(f32) + dot(tail * keys32, dstate)
        datt = dot(dmixed, corrected, 1, 1)
        from_begin = dot(jnp.concatenate([dmixed, dcorr.astype(bf16)], axis=0), begin, 1, 1)
        dgrown, dw = from_begin[:CHUNK], -from_begin[CHUNK:]
        dtail_keys = dot(corrected, dstate, 1, 1)
        dwhole = jnp.sum(dstate * begin.astype(f32))
        back = dot(inv_ref[0, at, :], jnp.concatenate([dw, dcorr], axis=1), 0, 0)
        dright_keys, dright_values = back[:, :KEY], back[:, KEY:]
        dsystem = -dot(
            back, jnp.concatenate([w_ref[0, at, :], u_ref[0, at, :]], axis=1), 1, 1
        )
        products = dot(jnp.concatenate([keys, queries], axis=0), keys, 1, 1)
        decayed = jnp.where(rows > cols, between * products[:CHUNK], 0.0)
        dsys_decayed = dsystem * decayed
        dbeta = jnp.sum(dsys_decayed, axis=1, keepdims=True)
        pairs = beta * dsys_decayed + datt * (between * products[CHUNK:])
        dkk = jnp.where(rows > cols, dsystem * (beta * between), 0.0)
        dqk = datt * between
        dqk16, dkk16 = dqk.astype(bf16), dkk.astype(bf16)
        dqn_scr[at, :] = dot(dqk16, keys) + grow * dgrown
        dkn_scr[at, :] = (
            dot(jnp.concatenate([dqk16, dkk16], axis=0), jnp.concatenate([queries, keys], axis=0), 0, 0)
            + dot(dkk16, keys)
            + tail * dtail_keys
            + (beta * grow) * dright_keys
        )
        dvn_scr[at, :] = beta * dright_values
        keys_part = grow * jnp.sum(dright_keys * keys32, axis=1, keepdims=True)
        dbeta = dbeta + jnp.sum(dright_values * values32, axis=1, keepdims=True) + keys_part
        from_tail = tail * jnp.sum(dtail_keys * keys32, axis=1, keepdims=True)
        dcum = (
            jnp.sum(pairs, axis=1, keepdims=True)
            - as_column(jnp.sum(pairs, axis=0, keepdims=True), diagonal)
            + grow * jnp.sum(dgrown * queries32, axis=1, keepdims=True)
            + beta * keys_part
            - from_tail
        )
        dlast = whole * dwhole + jnp.sum(from_tail, axis=0, keepdims=True)
        dld_ref[0, :, at] = jnp.sum(jnp.where(rows >= cols, dcum, 0.0), axis=0, keepdims=True) + dlast
        dbeta_ref[0, :, at] = as_row(dbeta, diagonal)

    for scr in (dn_scr, dw_scr):
        scr[0:EDGE, :] = jnp.zeros((EDGE, scr.shape[1]), f32)
        scr[EDGE + length :, :] = jnp.zeros((EDGE, scr.shape[1]), f32)
    pn_scr[...] = q_ref[...].astype(f32)
    act, slope = silu_slope(conv_sum(pn_scr, tq_ref, length))
    root = lax.rsqrt(jnp.sum(act * act, axis=-1, keepdims=True) + epsilon)
    normal = act * root
    dy = dqn_scr[...] * KEY ** (-0.5)
    dz = root * (dy - normal * jnp.sum(normal * dy, axis=-1, keepdims=True)) * slope
    conv_back(dz, tq_ref, dn_scr, pn_scr, dq_ref, tailq_ref, edgeq_ref, dtq_ref)
    pn_scr[...] = k_ref[...].astype(f32)
    act, slope = silu_slope(conv_sum(pn_scr, tk_ref, length))
    root = lax.rsqrt(jnp.sum(act * act, axis=-1, keepdims=True) + epsilon)
    normal = act * root
    dy = dkn_scr[...]
    dz = root * (dy - normal * jnp.sum(normal * dy, axis=-1, keepdims=True)) * slope
    conv_back(dz, tk_ref, dn_scr, pn_scr, dk_ref, tailk_ref, edgek_ref, dtk_ref)
    pw_scr[...] = v_ref[...].astype(f32)
    act, slope = silu_slope(conv_sum(pw_scr, tv_ref, length))
    conv_back(dvn_scr[...] * slope, tv_ref, dw_scr, pw_scr, dv_ref, tailv_ref, edgev_ref, dtv_ref)


def tall(rows, cols):
    return pl.BlockSpec((rows, cols), lambda h: (0, h))


def deep(rows, cols):
    return pl.BlockSpec((1, rows, cols), lambda h: (h, 0, 0))


def shared(rows, cols):
    return pl.BlockSpec((rows, cols), lambda h: (0, 0))


def shape_of(dims, dtype):
    return jax.ShapeDtypeStruct(dims, dtype)


def call_heads(kernel, head_count, in_specs, outputs, scratch, args):
    out_specs = [spec for spec, shape in outputs]
    out_shape = [shape for spec, shape in outputs]
    return pl.pallas_call(
        kernel,
        grid=(head_count,),
        in_specs=in_specs,
        out_specs=out_specs,
        out_shape=out_shape,
        scratch_shapes=scratch,
        compiler_params=pltpu.CompilerParams(vmem_limit_bytes=VMEM_BYTES),
        cost_estimate=COST,
    )(*args)


def prepare(x, edge, gain, w_query, w_key, w_value, w_decay, w_beta, rate, conv_query, conv_key, conv_value):
    length, width = x.shape
    heads = w_decay.shape[0]
    states = (length // CHUNK) * KEY
    ncols, wcols = heads * KEY, heads * VALUE
    out_shape = [
        shape_of((length, width), bf16),
        shape_of((length, heads), f32),
        shape_of((length + EDGE, ncols), bf16),
        shape_of((length + EDGE, ncols), bf16),
        shape_of((length + EDGE, wcols), bf16),
        shape_of((heads, 1, length), f32),
        shape_of((heads, 1, length), f32),
        shape_of((length, ncols), bf16),
        shape_of((length, ncols), bf16),
        shape_of((length, wcols), bf16),
        shape_of((heads, length, CHUNK), bf16),
        shape_of((heads, length, CHUNK), bf16),
        shape_of((heads, length, VALUE), bf16),
        shape_of((heads, length, KEY), bf16),
        shape_of((heads, states, KEY + VALUE), bf16),
        shape_of((heads, KEY, KEY + VALUE), f32),
    ]
    args = (
        x, edge, gain, w_query, w_key, w_value, w_decay, w_beta, rate, conv_query, conv_key, conv_value
    )
    return pl.pallas_call(
        prep_kernel,
        out_shape=out_shape,
        in_specs=[pl.BlockSpec(memory_space=pltpu.VMEM)] * len(args),
        out_specs=[pl.BlockSpec(memory_space=pltpu.VMEM)] * len(out_shape),
        scratch_shapes=[
            pltpu.VMEM((length + EDGE, width), bf16),
            pltpu.VMEM((length + EDGE, wcols), f32),
            pltpu.VMEM((length + EDGE, ncols), f32),
        ],
        compiler_params=pltpu.CompilerParams(vmem_limit_bytes=VMEM_BYTES),
        cost_estimate=COST,
    )(*args)


def run_forward(qn, ld, att, u, w, starts, state_in, gate_pre, gain, w_out):
    length = qn.shape[0]
    heads = ld.shape[0]
    states = starts.shape[1]
    wide = tall(length, VALUE)
    wshape = (length, heads * VALUE)
    outputs = [
        (wide, shape_of(wshape, bf16)),
        (wide, shape_of(wshape, f32)),
        (deep(length, VALUE), shape_of((heads, length, VALUE), bf16)),
        (deep(states, VALUE), shape_of((heads, states, VALUE), bf16)),
        (shared(length, w_out.shape[1]), shape_of((length, w_out.shape[1]), bf16)),
    ]
    in_specs = [
        tall(length, KEY), deep(1, length), deep(length, CHUNK), deep(length, VALUE), deep(length, KEY),
        deep(states, KEY + VALUE), deep(KEY, VALUE), wide, shared(1, VALUE),
        pl.BlockSpec((VALUE, w_out.shape[1]), lambda h: (h, 0)),
    ]
    args = (qn, ld, att, u, w, starts, state_in, gate_pre, gain, w_out)
    scratch = [pltpu.VMEM((length, w_out.shape[1]), f32)]
    return call_heads(forward_kernel, heads, in_specs, outputs, scratch, args)


def gate_back(dgated, mixed, gate_pre, gain, qn, kn, ld, att, w):
    length = qn.shape[0]
    heads = ld.shape[0]
    states = (length // CHUNK) * KEY
    wide = tall(length, VALUE)
    outputs = [
        (wide, shape_of((length, heads * VALUE), bf16)),
        (deep(length, VALUE), shape_of((heads, length, VALUE), bf16)),
        (deep(length, VALUE), shape_of((heads, length, VALUE), bf16)),
        (deep(1, VALUE), shape_of((heads, 1, VALUE), f32)),
        (deep(states, KEY + VALUE), shape_of((heads, states, KEY + VALUE), bf16)),
        (deep(KEY, KEY + VALUE), shape_of((heads, KEY, KEY + VALUE), f32)),
    ]
    in_specs = [
        wide, wide, wide, shared(1, VALUE), tall(length, KEY), tall(length, KEY), deep(1, length),
        deep(length, CHUNK), deep(length, KEY),
    ]
    args = (dgated, mixed, gate_pre, gain, qn, kn, ld, att, w)
    return call_heads(gate_back_kernel, heads, in_specs, outputs, [], args)


def run_backward(
    gstate, after, dmixed, dcorr, begin, corr, inverse, att, u, w, qn, kn, vn,
    query_ext, key_ext, value_ext, conv_query, conv_key, conv_value, ld, beta,
):
    length = qn.shape[0]
    heads = ld.shape[0]
    states = after.shape[1]
    taps = conv_query.shape[0]
    narrow, wide = tall(length, KEY), tall(length, VALUE)
    ncols, wcols = heads * KEY, heads * VALUE
    outputs = [
        (narrow, shape_of((length, ncols), bf16)),
        (narrow, shape_of((length, ncols), bf16)),
        (wide, shape_of((length, wcols), bf16)),
        (tall(8, KEY), shape_of((8, ncols), f32)),
        (tall(8, KEY), shape_of((8, ncols), f32)),
        (tall(8, VALUE), shape_of((8, wcols), f32)),
        (tall(8, KEY), shape_of((8, ncols), f32)),
        (tall(8, KEY), shape_of((8, ncols), f32)),
        (tall(8, VALUE), shape_of((8, wcols), f32)),
        (tall(taps, KEY), shape_of((taps, ncols), f32)),
        (tall(taps, KEY), shape_of((taps, ncols), f32)),
        (tall(taps, VALUE), shape_of((taps, wcols), f32)),
        (deep(1, length), shape_of((heads, 1, length), f32)),
        (deep(1, length), shape_of((heads, 1, length), f32)),
    ]
    in_specs = [
        deep(KEY, VALUE), deep(states, KEY + VALUE), deep(length, VALUE), deep(length, VALUE),
        deep(states, VALUE), deep(length, VALUE), deep(length, CHUNK), deep(length, CHUNK),
        deep(length, VALUE), deep(length, KEY),
        narrow, narrow, wide,
        tall(length + EDGE, KEY), tall(length + EDGE, KEY), tall(length + EDGE, VALUE),
        tall(taps, KEY), tall(taps, KEY), tall(taps, VALUE),
        deep(1, length), deep(1, length),
    ]
    scratch = [
        pltpu.VMEM((length, KEY), f32), pltpu.VMEM((length, KEY), f32), pltpu.VMEM((length, VALUE), f32),
        pltpu.VMEM((length + 2 * EDGE, KEY), f32), pltpu.VMEM((length + EDGE, KEY), f32),
        pltpu.VMEM((length + 2 * EDGE, VALUE), f32), pltpu.VMEM((length + EDGE, VALUE), f32),
    ]
    args = (
        gstate, after, dmixed, dcorr, begin, corr, inverse, att, u, w, qn, kn, vn,
        query_ext, key_ext, value_ext, conv_query, conv_key, conv_value, ld, beta,
    )
    return call_heads(backward_kernel, heads, in_specs, outputs, scratch, args)


def weight_kernel(count, first, *refs):
    lefts, rights, out_ref = refs[:count], refs[count : 2 * count], refs[-1]
    at = first
    for left, right in zip(lefts, rights):
        width = right.shape[1]
        out_ref[:, at : at + width] = dot(left[...], right[...], 0, 0).astype(bf16)
        at += width


def weight_gradients(pairs, room=0, into=None):
    lefts = [left for left, right in pairs]
    rights = [right for left, right in pairs]
    length, width = lefts[0].shape
    block = 256
    total = sum(r.shape[1] for r in rights)
    args = lefts + rights
    out = shape_of((width, room + total), bf16) if into is None else shape_of(into.shape, bf16)
    in_specs = [pl.BlockSpec((length, block), lambda i: (0, i)) for left in lefts]
    in_specs += [pl.BlockSpec(r.shape, lambda i: (0, 0)) for r in rights]
    aliases = {}
    if into is not None:
        aliases = {len(args): 0}
        args = args + [into]
        in_specs.append(pl.BlockSpec(memory_space=pl.ANY))
    return pl.pallas_call(
        functools.partial(weight_kernel, len(pairs), room),
        grid=(width // block,),
        in_specs=in_specs,
        out_specs=pl.BlockSpec((block, room + total), lambda i: (i, 0)),
        out_shape=out,
        input_output_aliases=aliases,
        compiler_params=pltpu.CompilerParams(vmem_limit_bytes=VMEM_BYTES),
        cost_estimate=COST,
    )(*args)


def ffn_kernel(
    x_ref, branch_ref, gain_ref, wg_ref, wu_ref, wd_ref, cot_ref,
    normed_ref, hidden_ref, dgate_ref, dup_ref, part_ref,
):
    middle = x_ref[...].astype(f32) + branch_ref[...].astype(f32)
    normed = row_norm(middle, gain_ref[...]).astype(bf16)
    normed_ref[...] = normed
    gate = dot(normed, wg_ref[...])
    up = dot(normed, wu_ref[...])
    sig = jax.nn.sigmoid(gate)
    act = gate * sig
    hidden_ref[...] = (act * up).astype(bf16)
    dhidden = dot(cot_ref[...], wd_ref[...], 1, 1)
    dgate = (dhidden * up * (sig * (1.0 + gate * (1.0 - sig)))).astype(bf16)
    dup = (dhidden * act).astype(bf16)
    dgate_ref[...] = dgate
    dup_ref[...] = dup
    part_ref[...] = (dot(dgate, wg_ref[...], 1, 1) + dot(dup, wu_ref[...], 1, 1)).astype(bf16)


def run_ffn(x, branch, gain, w_ffn_gate, w_ffn_up, w_ffn_down, cotangent):
    length, width = x.shape
    hidden = w_ffn_gate.shape[1]
    block = length // 2

    def rows(cols):
        return pl.BlockSpec((block, cols), lambda i: (i, 0))

    return pl.pallas_call(
        ffn_kernel,
        grid=(length // block,),
        in_specs=[
            rows(width), rows(width), shared(1, width), shared(width, hidden), shared(width, hidden),
            shared(hidden, width), rows(width),
        ],
        out_specs=[rows(width), rows(hidden), rows(hidden), rows(hidden), rows(width)],
        out_shape=[
            shape_of((length, width), bf16),
            shape_of((length, hidden), bf16),
            shape_of((length, hidden), bf16),
            shape_of((length, hidden), bf16),
            shape_of((length, width), bf16),
        ],
        compiler_params=pltpu.CompilerParams(vmem_limit_bytes=VMEM_BYTES),
        cost_estimate=COST,
    )(x, branch, gain, w_ffn_gate, w_ffn_up, w_ffn_down, cotangent)


def shard_kernel(places_ref, left_ref, right_ref, out_ref):
    out_ref[...] = dot(left_ref[...], right_ref[...], 0, 0).astype(out_ref.dtype)


def shard_products(left, right, places, count, size, dtype):
    length, width = left.shape
    piece = width // size
    if piece % 128:
        view = left.reshape(length, size, piece)
        chosen = jnp.take(view, places, axis=1).reshape(length, count * piece)
        return lax.dot_general(
            chosen, right, (((0,), (0,)), ((), ())), preferred_element_type=f32
        ).astype(dtype)
    return pl.pallas_call(
        shard_kernel,
        grid_spec=pltpu.PrefetchScalarGridSpec(
            num_scalar_prefetch=1,
            grid=(count,),
            in_specs=[
                pl.BlockSpec((length, piece), lambda g, places: (0, places[g])),
                pl.BlockSpec(right.shape, lambda g, places: (0, 0)),
            ],
            out_specs=pl.BlockSpec((piece, right.shape[1]), lambda g, places: (g, 0)),
        ),
        out_shape=shape_of((count * piece, right.shape[1]), dtype),
        compiler_params=pltpu.CompilerParams(vmem_limit_bytes=VMEM_BYTES),
        cost_estimate=COST,
    )(places, left, right)


def from_behind(block, axis, distance):
    devices = range(lax.axis_size(axis))
    route = [(i - distance, i) for i in devices if i - distance in devices]
    return lax.ppermute(block, axis, route)


def swap_with(block, axis, distance):
    route = [(i, i ^ distance) for i in range(lax.axis_size(axis))]
    return lax.ppermute(block, axis, route)


def exchange_rounds(tasks, beside=None):
    results, asked = [None] * len(tasks), {}

    def advance(which, got):
        try:
            asked[which] = tasks[which].send(got)
        except StopIteration as end:
            results[which] = end.value
            asked.pop(which, None)

    for which in range(len(tasks)):
        advance(which, None)
    number = 0
    while asked:
        number += 1
        got = {which: tuple(swap_with(*one) for one in wanted) for which, wanted in asked.items()}
        if number == 2 and beside is not None:
            got, beside = lax.optimization_barrier((got, beside))
        else:
            got = lax.optimization_barrier(got)
        for which in list(asked):
            advance(which, got[which])
    return results if beside is None else (results, beside)


def continue_with(task, got):
    try:
        wanted = task.send(got)
        while True:
            wanted = task.send((yield wanted))
    except StopIteration as end:
        return end.value


def group_sum(block, axis):
    size = lax.axis_size(axis)
    distance = 1
    while distance < size:
        reach = min(4, size // distance)
        arrived = yield [(block, axis, distance * step) for step in range(1, reach)]
        if reach == 4:
            block = (block + arrived[0]) + (arrived[1] + arrived[2])
        else:
            block = block + arrived[0]
        distance *= reach
    return block


def small_sums(block, shared):
    shared = yield from group_sum(shared, "head")
    rows = -(-shared.shape[0] // block.shape[1])
    padded = jnp.pad(shared, (0, rows * block.shape[1] - shared.shape[0])).reshape(rows, -1)
    total = yield from group_sum(jnp.concatenate([block, padded], axis=0), "seq")
    return total[: block.shape[0]], total[block.shape[0] :].reshape(-1)[: shared.shape[0]]


def sum_over_heads(partial):
    rows = partial.shape[0] // 2
    odd = lax.axis_index("head") % 2 == 1
    low, high = partial[:rows], partial[rows:]
    own = jnp.where(odd, high, low).astype(f32)
    (got,) = yield [(jnp.where(odd, low, high), "head", 1)]
    own = own + got.astype(f32)
    distance = 2
    while distance < lax.axis_size("head"):
        sent = own.astype(bf16)
        (got,) = yield [(sent, "head", distance)]
        own = sent.astype(f32) + got.astype(f32)
        distance *= 2
    kept = own.astype(bf16)
    (other,) = yield [(kept, "head", 1)]
    return jnp.concatenate([jnp.where(odd, other, kept), jnp.where(odd, kept, other)], axis=0)


def exclusive_scan(joined, sign, beside):
    own_t, own_b = joined[..., :KEY], joined[..., KEY:]
    send = joined
    before_t = before_b = None
    distance = 1
    size = lax.axis_size("seq")

    def product(a, b):
        return jnp.einsum("hij,hjk->hik", a, b, precision=lax.Precision.HIGH)

    while distance < size:
        last = distance * 2 >= size
        got = from_behind(
            (send[..., KEY:] if last else send).astype(bf16), "seq", sign * distance
        )
        if before_t is None:
            got, beside = lax.optimization_barrier((got, beside))
        got = got.astype(f32)
        if before_t is None:
            before_t, before_b = got[..., :KEY], got[..., KEY:]
        else:
            moved = product(before_t, got)
            if last:
                before_b = before_b + moved
            else:
                before_t, before_b = moved[..., :KEY], before_b + moved[..., KEY:]
        if not last:
            send = product(own_t, jnp.concatenate([before_t, before_b], axis=-1))
            send = jnp.concatenate([send[..., :KEY], send[..., KEY:] + own_b], axis=-1)
        distance *= 2
    return before_b, beside


def halving_scatter(left, right, order):
    size = lax.axis_size("seq")
    bits = size.bit_length() - 1
    here = lax.axis_index("seq")
    order = [bit for bit in order if bit < bits] + list(range(len(order), bits))
    first = order[0]
    count = size // 2
    slots = jnp.arange(count, dtype=jnp.int32)
    shards = (slots // 2**first) * 2 ** (first + 1) + slots % 2**first
    mine = (here // 2**first) % 2
    sent = shard_products(left, right, shards + (1 - mine) * 2**first, count, size, bf16)
    (got,) = yield [(sent, "seq", 2**first)]
    held = shard_products(left, right, shards + mine * 2**first, count, size, f32)
    held = held + got.astype(f32)
    axes = [bit for bit in range(bits)[::-1] if bit != first]
    held = held.reshape((2,) * (bits - 1) + (held.shape[0] // count, right.shape[1]))
    for bit in order[1:]:
        axis = axes.index(bit)
        axes.remove(bit)
        mine = (here // 2**bit) % 2
        sent = lax.dynamic_index_in_dim(held, 1 - mine, axis, keepdims=False).astype(bf16)
        (got,) = yield [(sent, "seq", 2**bit)]
        held = lax.dynamic_index_in_dim(held, mine, axis, keepdims=False) + got.astype(f32)
    return held


def inner_rows(first_operand, second_operand):
    return lax.dot_general(
        first_operand, second_operand, (((0,), (0,)), ((), ())), preferred_element_type=f32
    )


def matmul_bf(first_operand, second_operand):
    return jnp.dot(first_operand, second_operand, preferred_element_type=f32)


def against_rows(first_operand, second_operand):
    return lax.dot_general(
        first_operand, second_operand, (((1,), (1,)), ((), ())), preferred_element_type=f32
    )


def per_device(
    block_input,
    norm1_gain,
    w_query,
    w_key,
    w_value,
    w_gate,
    w_decay,
    w_beta,
    conv_query,
    conv_key,
    conv_value,
    decay_rate,
    out_gain,
    w_out,
    norm2_gain,
    w_ffn_gate,
    w_ffn_up,
    w_ffn_down,
    cotangent,
):
    length = block_input.shape[0]
    head_count = w_decay.shape[1]
    key_cols = w_query.shape[1]
    value_cols = w_value.shape[1]
    ff_cols = w_ffn_gate.shape[1]
    edge_input = from_behind(block_input[length - EDGE :], "seq", 1)
    gain1 = norm1_gain.astype(f32)
    (
        normed, decay_cols, query_ext, key_ext, value_ext, log_decay, beta3,
        qn, kn, vn, inverse, att, u, w, starts, composite,
    ) = prepare(
        block_input, edge_input, gain1[None], w_query, w_key, w_value, w_decay.T, w_beta.T,
        decay_rate[None], conv_query, conv_key, conv_value,
    )
    inputs32 = block_input.astype(f32)
    gate_pre = matmul_bf(normed, w_gate)
    state_in, gate_pre = exclusive_scan(composite, 1, gate_pre)
    gain_row = out_gain.astype(f32)[None]
    gated, mixed, corr, begin, branch_part = run_forward(
        qn, log_decay, att, u, w, starts, state_in, gate_pre, gain_row, w_out
    )
    (branch,) = exchange_rounds([sum_over_heads(branch_part)])
    gain2 = norm2_gain.astype(f32)
    normed2, hidden, grad_fgate, grad_fup, grad_part = run_ffn(
        block_input, branch, gain2[None], w_ffn_gate, w_ffn_up, w_ffn_down, cotangent
    )
    early = weight_gradients([(normed2, grad_fgate), (normed2, grad_fup), (cotangent, hidden)])
    (grad_normed2,), early = exchange_rounds([sum_over_heads(grad_part)], early)
    grad_normed2 = grad_normed2.astype(f32)
    early = lax.psum_scatter(early, "seq", scatter_dimension=0, tiled=True).astype(f32)
    middle = inputs32 + branch.astype(f32)
    norm2_back = jax.vjp(row_norm, middle, gain2)[1]
    ffn_part = matmul_bf(hidden, w_ffn_down).astype(bf16)
    grad_middle_n, grad_gain2 = norm2_back(grad_normed2)
    grad_middle = cotangent.astype(f32) + grad_middle_n
    grad_branch = grad_middle.astype(bf16)
    grad_gated = against_rows(grad_branch, w_out)
    grad_gp, grad_mixed, grad_corr, grad_outgain, after, composite_back = gate_back(
        grad_gated, mixed, gate_pre, gain_row, qn, kn, log_decay, att, w
    )
    composite_back, ffn_part = lax.optimization_barrier((composite_back, ffn_part))
    (ffn_out,) = exchange_rounds([sum_over_heads(ffn_part)])
    layer_out = (middle + ffn_out.astype(f32)).astype(bf16)
    grad_state, (grad_branch, gated, grad_gp) = exclusive_scan(
        composite_back, -1, (grad_branch, gated, grad_gp)
    )
    task_wg = halving_scatter(normed, grad_gp, [1, 0])
    task_wout = halving_scatter(grad_branch, gated, [0, 1])
    grad_state, wanted = lax.optimization_barrier(
        (grad_state, [next(task)[0][0] for task in (task_wg, task_wout)])
    )
    got_wg = swap_with(wanted[0], "seq", min(2, lax.axis_size("seq") // 2))
    got_wout = swap_with(wanted[1], "seq", 1)
    (
        grad_qp, grad_kp, grad_vp, tail_q, tail_k, tail_v, edge_q, edge_k, edge_v,
        taps_q, taps_k, taps_v, grad_log, grad_beta,
    ) = run_backward(
        grad_state, after, grad_mixed, grad_corr, begin, corr, inverse, att, u, w,
        qn, kn, vn, query_ext, key_ext, value_ext,
        conv_query, conv_key, conv_value, log_decay, beta3,
    )
    edge_q, got_wg, got_wout = lax.optimization_barrier((edge_q, got_wg, got_wout))
    edges = from_behind(jnp.concatenate([edge_q, edge_k, edge_v], axis=1), "seq", -1)
    tails = (jnp.concatenate([tail_q, tail_k, tail_v], axis=1) + edges).astype(bf16)

    grad_qp = jnp.concatenate([grad_qp[: length - 8], tails[:, :key_cols]], axis=0)
    grad_kp = jnp.concatenate([grad_kp[: length - 8], tails[:, key_cols : 2 * key_cols]], axis=0)
    grad_vp = jnp.concatenate([grad_vp[: length - 8], tails[:, 2 * key_cols :]], axis=0)
    decay_pre = decay_cols.T
    soft = jax.nn.softplus(decay_pre)
    rate = decay_rate[:, None]
    beta_gate = beta3.reshape(head_count, length)
    w_scalars = jnp.concatenate([w_decay, w_beta], axis=1)
    normal1 = row_norm(inputs32, 1.0)
    grad_log = grad_log.reshape(head_count, length)
    grad_beta = grad_beta.reshape(head_count, length)
    grad_dp = (-rate * jax.nn.sigmoid(decay_pre) * grad_log).astype(bf16)
    grad_bp = (beta_gate * (1.0 - beta_gate) * grad_beta).astype(bf16)
    grad_rate = -jnp.sum(grad_log * soft, axis=1)
    grad_scalars = jnp.concatenate([grad_dp, grad_bp], axis=0)
    grad_normed_part = (
        against_rows(grad_qp, w_query)
        + against_rows(grad_kp, w_key)
        + against_rows(grad_vp, w_value)
        + against_rows(grad_gp, w_gate)
        + lax.dot_general(
            grad_scalars, w_scalars, (((0,), (1,)), ((), ())), preferred_element_type=f32
        )
    )
    grad_gain1 = jnp.sum(grad_normed_part * normal1, axis=0)
    width = grad_gain1.shape[0]
    taps_count = conv_query.shape[0]
    grad_outgain = jnp.sum(grad_outgain, axis=(0, 1))
    small = jnp.concatenate(
        [
            jnp.concatenate([taps_q, taps_k, taps_v], axis=1),
            grad_gain2[None],
            jnp.pad(grad_rate, (0, width - head_count))[None],
            matmul_bf(grad_scalars, normed),
        ],
        axis=0,
    )
    late_qk, late_v, grad_normed, small_pair, grad_wg, grad_wout = exchange_rounds(
        [
            halving_scatter(normed, jnp.concatenate([grad_qp, grad_kp], axis=1), [0, 1]),
            halving_scatter(normed, grad_vp, [1, 0]),
            sum_over_heads(grad_normed_part.astype(bf16)),
            small_sums(small, jnp.concatenate([grad_gain1, grad_outgain])),
            continue_with(task_wg, (got_wg,)),
            continue_with(task_wout, (got_wout,)),
        ]
    )
    small, shared_sum = small_pair
    norm1_back = jax.vjp(row_norm, inputs32, gain1)[1]
    grad_input = grad_middle + norm1_back(grad_normed.astype(f32))[0]
    taps_sum = small[:taps_count]
    gain2_sum = small[taps_count]
    rate_sum = small[taps_count + 1, :head_count]
    scalars_sum = small[taps_count + 2 : taps_count + 2 + 2 * head_count]
    gain1_sum, outgain_sum = shared_sum[:width], shared_sum[width:]

    def own_part(vec):
        piece = vec.shape[-1] // lax.axis_size("seq")
        return lax.dynamic_slice_in_dim(vec, lax.axis_index("seq") * piece, piece, axis=-1)

    scalars_sum = own_part(scalars_sum).T
    return (
        layer_out,
        grad_input,
        own_part(gain1_sum),
        late_qk[:, :key_cols],
        late_qk[:, key_cols:],
        late_v,
        grad_wg,
        scalars_sum[:, :head_count],
        scalars_sum[:, head_count:],
        taps_sum[:, :key_cols],
        taps_sum[:, key_cols : 2 * key_cols],
        taps_sum[:, 2 * key_cols :],
        rate_sum,
        own_part(outgain_sum),
        grad_wout.T,
        own_part(gain2_sum),
        early[:, :ff_cols],
        early[:, ff_cols : 2 * ff_cols],
        early[:, 2 * ff_cols :].T,
    )


def solution(mesh):
    return jax.shard_map(
        per_device,
        mesh=mesh,
        in_specs=(
            P("seq", None),
            P(),
            P(None, "head"),
            P(None, "head"),
            P(None, "head"),
            P(None, "head"),
            P(None, "head"),
            P(None, "head"),
            P(None, "head"),
            P(None, "head"),
            P(None, "head"),
            P("head"),
            P(),
            P("head", None),
            P(),
            P(None, "head"),
            P(None, "head"),
            P("head", None),
            P("seq", None),
        ),
        out_specs=(
            P("seq", None),
            P("seq", None),
            P("seq"),
            P("seq", "head"),
            P("seq", "head"),
            P("seq", "head"),
            P("seq", "head"),
            P("seq", "head"),
            P("seq", "head"),
            P(None, "head"),
            P(None, "head"),
            P(None, "head"),
            P("head"),
            P("seq"),
            P("head", "seq"),
            P("seq"),
            P("seq", "head"),
            P("seq", "head"),
            P("head", "seq"),
        ),
        check_vma=False,
    )
```

```python
import functools

import jax
import jax.numpy as jnp
from jax import lax
from jax.experimental import pallas as pl
from jax.experimental.pallas import tpu as pltpu
from jax.sharding import PartitionSpec as P

KEY = 128
VALUE = 256
CHUNK = 128
EDGE = 16
SUB = 16
VMEM_BYTES = 60 * 1024 * 1024
COST = pl.CostEstimate(flops=0, bytes_accessed=0, transcendentals=0)

epsilon = 1e-06
f32 = jnp.float32
bf16 = jnp.bfloat16
highest_precision = lax.Precision.HIGHEST


def dot(first, second, over_first=1, over_second=0):
    return lax.dot_general(
        first.astype(bf16),
        second.astype(bf16),
        (((over_first,), (over_second,)), ((), ())),
        preferred_element_type=f32,
    )


def halves(values):
    high = values.astype(bf16)
    return high, (values - high.astype(f32)).astype(bf16)


def dot_fine(first, second):
    first_high, first_low = halves(first)
    second_high, second_low = halves(second)
    width = second.shape[1]
    wide = dot(first_high, jnp.concatenate([second_high, second_low], axis=1))
    return wide[:, :width] + wide[:, width:] + dot(first_low, second_high)


def grid_places(extent):
    rows = lax.broadcasted_iota(jnp.int32, (extent, extent), 0)
    cols = lax.broadcasted_iota(jnp.int32, (extent, extent), 1)
    return rows, cols


def as_row(column, diagonal):
    return jnp.sum(jnp.where(diagonal, column, 0.0), axis=0, keepdims=True)


def as_column(row, diagonal):
    return jnp.sum(jnp.where(diagonal, row, 0.0), axis=1, keepdims=True)


def unit_lower_inverses(systems, rows, cols):
    extent = systems[0].shape[0]
    count = extent // SUB
    units = len(systems)
    same = rows // SUB == cols // SUB
    packed = jnp.concatenate(
        [jnp.sum(jnp.where(same, s, 0.0).reshape(count, SUB, extent), axis=0) for s in systems], axis=0
    )
    stacked = jnp.concatenate(halves(packed), axis=0)
    shape = (units, SUB, extent)
    places = lax.broadcasted_iota(jnp.int32, shape, 1)
    solved = (places == lax.broadcasted_iota(jnp.int32, shape, 2) % SUB).astype(f32)
    for j in range(SUB - 1):
        spread = dot(stacked, (same & (rows % SUB == j)).astype(f32))
        column = spread[: units * SUB] + spread[units * SUB :]
        solved = solved - column.reshape(shape) * solved[:, j : j + 1, :]
    inverses = [
        jnp.where(same, jnp.concatenate([solved[n]] * count, axis=0), 0.0) for n in range(units)
    ]
    size = SUB
    while size < extent:
        below = (rows // (2 * size) == cols // (2 * size)) & (rows // size > cols // size)
        joined = [
            dot_fine(inverse, jnp.where(below, s, 0.0)) for inverse, s in zip(inverses, systems)
        ]
        joined = [dot_fine(product, inverse) for product, inverse in zip(joined, inverses)]
        inverses = [inverse - product for inverse, product in zip(inverses, joined)]
        size *= 2
    return inverses


def decay_terms(ld_row, rows, cols):
    cum_col = jnp.sum(jnp.where(rows >= cols, ld_row, 0.0), axis=1, keepdims=True)
    cum_row = as_row(cum_col, rows == cols)
    last = cum_col[CHUNK - 1 :, :]
    between = jnp.where(rows >= cols, jnp.exp(jnp.where(rows >= cols, cum_col - cum_row, 0.0)), 0.0)
    return between, jnp.exp(cum_col), jnp.exp(last - cum_col), jnp.exp(last)


def conv_sum(padded_ref, taps_ref, length):
    taps = taps_ref[...].astype(f32)
    summed = taps[0:1] * padded_ref[EDGE : EDGE + length, :]
    for offset in range(1, taps_ref.shape[0]):
        summed = summed + taps[offset : offset + 1] * padded_ref[EDGE - offset : EDGE - offset + length, :]
    return summed


def unit_rows(values, scale, heads):
    parts = []
    for h in range(heads):
        part = values[:, h * KEY : (h + 1) * KEY]
        parts.append(
            part * (lax.rsqrt(jnp.sum(part * part, axis=-1, keepdims=True) + epsilon) * scale)
        )
    return jnp.concatenate(parts, axis=1)


def row_norm(values, gain_vec):
    return (
        values * lax.rsqrt(jnp.mean(values * values, axis=-1, keepdims=True) + epsilon) * gain_vec
    )


def prep_kernel(
    x_ref, edge_ref, gain_ref, wq_ref, wk_ref, wv_ref, wd_ref, wb_ref, rate_ref, tq_ref, tk_ref, tv_ref,
    normed_ref, normed_ext_ref, decay_ref, q_ref, k_ref, v_ref, ld_ref, beta_ref,
    qn_ref, kn_ref, vn_ref, inv_ref, att_ref, u_ref, w_ref, start_ref, final_ref,
    wide_scr, narrow_scr,
):
    length = qn_ref.shape[0]
    heads = ld_ref.shape[0]
    chunks = length // CHUNK
    gain = gain_ref[...]
    normed_ext_ref[:EDGE, :] = row_norm(edge_ref[...].astype(f32), gain).astype(bf16)
    normed = row_norm(x_ref[...].astype(f32), gain).astype(bf16)
    normed_ext_ref[EDGE:, :] = normed
    normed_ref[...] = normed
    decay_pre = dot(normed, wd_ref[...], 1, 1)
    decay_ref[...] = decay_pre
    softplus = jnp.maximum(decay_pre, 0.0) + jnp.log1p(jnp.exp(-jnp.abs(decay_pre)))
    log_decay = -rate_ref[...] * softplus
    beta_gate = jax.nn.sigmoid(dot(normed, wb_ref[...], 1, 1))
    pre = dot(normed_ext_ref[...], wk_ref[...]).astype(bf16)
    k_ref[...] = pre
    narrow_scr[...] = pre.astype(f32)
    z = conv_sum(narrow_scr, tk_ref, length)
    kn_ref[...] = unit_rows(z * jax.nn.sigmoid(z), 1.0, heads).astype(bf16)
    pre = dot(normed_ext_ref[...], wq_ref[...]).astype(bf16)
    q_ref[...] = pre
    narrow_scr[...] = pre.astype(f32)
    z = conv_sum(narrow_scr, tq_ref, length)
    qn_ref[...] = unit_rows(z * jax.nn.sigmoid(z), KEY ** (-0.5), heads).astype(bf16)
    pre = dot(normed_ext_ref[...], wv_ref[...]).astype(bf16)
    v_ref[...] = pre
    wide_scr[...] = pre.astype(f32)
    z = conv_sum(wide_scr, tv_ref, length)
    vn_ref[...] = (z * jax.nn.sigmoid(z)).astype(bf16)

    rows, cols = grid_places(CHUNK)
    diagonal = rows == cols
    units = [(h, c) for c in range(chunks) for h in range(heads)]
    systems, vectors = [], []
    for h, c in units:
        at = slice(c * CHUNK, (c + 1) * CHUNK)
        keyed = slice(h * KEY, (h + 1) * KEY)
        ld_row = as_row(log_decay[at, h : h + 1], diagonal)
        ld_ref[h, :, at] = ld_row
        between, grow, tail, whole = decay_terms(ld_row, rows, cols)
        beta = beta_gate[at, h : h + 1]
        beta_ref[h, :, at] = as_row(beta, diagonal)
        keys = kn_ref[at, keyed]
        products = dot(jnp.concatenate([keys, qn_ref[at, keyed]], axis=0), keys, 1, 1)
        systems.append(jnp.where(rows > cols, beta * between * products[:CHUNK], 0.0))
        att_ref[h, at, :] = (products[CHUNK:] * between).astype(bf16)
        vectors.append((beta, grow, tail, whole))
    inverses = unit_lower_inverses(systems, rows, cols)
    kept = []
    for (h, c), inverse, (beta, grow, tail, whole) in zip(units, inverses, vectors):
        at = slice(c * CHUNK, (c + 1) * CHUNK)
        keys32 = kn_ref[at, h * KEY : (h + 1) * KEY].astype(f32)
        values32 = vn_ref[at, h * VALUE : (h + 1) * VALUE].astype(f32)
        inv_ref[h, at, :] = inverse.astype(bf16)
        solved = dot(inverse, jnp.concatenate([(beta * grow) * keys32, beta * values32], axis=1))
        w_ref[h, at, :] = solved[:, :KEY].astype(bf16)
        u_ref[h, at, :] = solved[:, KEY:].astype(bf16)
        kept.append((tail * keys32).astype(bf16))
    begin = jnp.concatenate([diagonal.astype(f32), jnp.zeros((KEY, VALUE), f32)], axis=1)
    states = [begin] * heads
    for (h, c), tail_keys, (beta, grow, tail, whole) in zip(units, kept, vectors):
        at = slice(c * CHUNK, (c + 1) * CHUNK)
        state = states[h]
        start_ref[h, c * KEY : (c + 1) * KEY, :] = state.astype(bf16)
        source = jnp.concatenate([jnp.zeros((CHUNK, KEY), f32), u_ref[h, at, :].astype(f32)], axis=1)
        corrected = source - dot(w_ref[h, at, :], state)
        states[h] = whole * state + dot(tail_keys, corrected, 0, 0)
    for h in range(heads):
        final_ref[h, :, :] = states[h]


def forward_kernel(
    qn_ref, ld_ref, att_ref, u_ref, w_ref, start_ref, state_ref, gate_ref, gain_ref, wout_ref,
    gated_ref, mixed_ref, corr_ref, begin_ref, branch_ref, sum_scr,
):
    length = qn_ref.shape[0]
    rows, cols = grid_places(CHUNK)
    entering = state_ref[0]
    gain = gain_ref[...]
    for c in range(length // CHUNK):
        at = slice(c * CHUNK, (c + 1) * CHUNK)
        places = slice(c * KEY, (c + 1) * KEY)
        between, grow, tail, whole = decay_terms(ld_ref[0, :, at], rows, cols)
        begin = start_ref[0, places, KEY:].astype(f32) + dot(start_ref[0, places, :KEY], entering)
        begin_ref[0, places, :] = begin.astype(bf16)
        corrected = u_ref[0, at, :].astype(f32) - dot(w_ref[0, at, :], begin)
        corr_ref[0, at, :] = corrected.astype(bf16)
        mixed = dot(grow * qn_ref[at, :].astype(f32), begin) + dot(att_ref[0, at, :], corrected)
        mixed_ref[at, :] = mixed
        root = lax.rsqrt(jnp.mean(mixed * mixed, axis=-1, keepdims=True) + epsilon)
        gate = gate_ref[at, :]
        gated_ref[at, :] = (mixed * root * gain * (gate * jax.nn.sigmoid(gate))).astype(bf16)
    part = dot(gated_ref[...], wout_ref[...])

    @pl.when(pl.program_id(0) == 0)
    def start_sum():
        sum_scr[...] = part

    @pl.when(pl.program_id(0) > 0)
    def add_sum():
        sum_scr[...] += part

    @pl.when(pl.program_id(0) == pl.num_programs(0) - 1)
    def give_sum():
        branch_ref[...] = sum_scr[...].astype(bf16)


def gate_back_kernel(
    dgated_ref, mixed_ref, gate_ref, gain_ref, qn_ref, kn_ref, ld_ref, att_ref, w_ref,
    dgate_ref, dmixed_ref, dcorr_ref, dgain_ref, after_ref, final_ref,
):
    length = qn_ref.shape[0]
    rows, cols = grid_places(CHUNK)
    gain = gain_ref[...]
    kept = []
    dgain = jnp.zeros((1, VALUE), f32)
    for c in range(length // CHUNK):
        at = slice(c * CHUNK, (c + 1) * CHUNK)
        mixed, gate, dgated = mixed_ref[at, :], gate_ref[at, :], dgated_ref[at, :]
        root = lax.rsqrt(jnp.mean(mixed * mixed, axis=-1, keepdims=True) + epsilon)
        normal = mixed * root
        sig = jax.nn.sigmoid(gate)
        act = gate * sig
        dgain = dgain + jnp.sum(dgated * normal * act, axis=0, keepdims=True)
        dgate_ref[at, :] = (dgated * normal * gain * (sig * (1.0 + gate * (1.0 - sig)))).astype(bf16)
        dnormal = dgated * act * gain
        dmixed = root * (dnormal - normal * jnp.mean(dnormal * normal, axis=-1, keepdims=True))
        dmixed_ref[0, at, :] = dmixed.astype(bf16)
        between, grow, tail, whole = decay_terms(ld_ref[0, :, at], rows, cols)
        dcorr = dot(att_ref[0, at, :], dmixed, 0, 0)
        dcorr_ref[0, at, :] = dcorr.astype(bf16)
        gradient = dot(grow * qn_ref[at, :].astype(f32), dmixed, 0, 0) - dot(w_ref[0, at, :], dcorr, 0, 0)
        kept.append((gradient, (tail * kn_ref[at, :].astype(f32)).astype(bf16), whole))
    dgain_ref[0, :, :] = dgain
    pending = jnp.concatenate([(rows == cols).astype(f32), jnp.zeros((KEY, VALUE), f32)], axis=1)
    for c in reversed(range(length // CHUNK)):
        gradient, tail_keys, whole = kept[c]
        at = slice(c * CHUNK, (c + 1) * CHUNK)
        after_ref[0, c * KEY : (c + 1) * KEY, :] = pending.astype(bf16)
        source = jnp.concatenate([jnp.zeros((KEY, KEY), f32), gradient], axis=1)
        pending = whole * pending + source - dot(w_ref[0, at, :], dot(tail_keys, pending), 0, 0)
    final_ref[0, :, :] = pending


def silu_slope(z):
    sig = jax.nn.sigmoid(z)
    return z * sig, sig * (1.0 + z * (1.0 - sig))


def conv_back(dz, taps_ref, dz_scr, pre_scr, dpre_ref, dtaps_ref):
    length = dz.shape[0]
    reach = taps_ref.shape[0] - 1
    taps = taps_ref[...].astype(f32)
    dz_scr[EDGE : EDGE + length, :] = dz
    total = taps[0:1] * dz
    sums = [jnp.sum(dz * pre_scr[EDGE : EDGE + length, :], axis=0, keepdims=True)]
    for offset in range(1, reach + 1):
        total = total + taps[offset : offset + 1] * dz_scr[EDGE + offset : EDGE + offset + length, :]
        sums.append(
            jnp.sum(dz * pre_scr[EDGE - offset : EDGE - offset + length, :], axis=0, keepdims=True)
        )
    dpre_ref[EDGE:, :] = total.astype(bf16)
    edge = taps[1:2] * dz_scr[EDGE - 7 : EDGE + 1, :]
    for offset in range(2, reach + 1):
        edge = edge + taps[offset : offset + 1] * dz_scr[EDGE - 8 + offset : EDGE + offset, :]
    dpre_ref[:EDGE, :] = jnp.concatenate([jnp.zeros_like(edge), edge], axis=0).astype(bf16)
    dtaps_ref[...] = jnp.concatenate(sums, axis=0)


def backward_kernel(
    gstate_ref, after_ref, dmixed_ref, dcorr_ref, begin_ref, corr_ref, inv_ref, att_ref, u_ref, w_ref,
    qn_ref, kn_ref, vn_ref, q_ref, k_ref, v_ref, tq_ref, tk_ref, tv_ref,
    ld_ref, beta_ref,
    dq_ref, dk_ref, dv_ref, dtq_ref, dtk_ref, dtv_ref, dld_ref, dbeta_ref,
    dqn_scr, dkn_scr, dvn_scr, dn_scr, pn_scr, dw_scr, pw_scr,
):
    length = qn_ref.shape[0]
    rows, cols = grid_places(CHUNK)
    diagonal = rows == cols
    leaving = gstate_ref[0]
    for c in range(length // CHUNK):
        at = slice(c * CHUNK, (c + 1) * CHUNK)
        places = slice(c * KEY, (c + 1) * KEY)
        between, grow, tail, whole = decay_terms(ld_ref[0, :, at], rows, cols)
        beta = as_column(beta_ref[0, :, at], diagonal)
        keys, queries = kn_ref[at, :], qn_ref[at, :]
        keys32, queries32, values32 = keys.astype(f32), queries.astype(f32), vn_ref[at, :].astype(f32)
        dstate = after_ref[0, places, KEY:].astype(f32) + dot(after_ref[0, places, :KEY], leaving)
        dmixed, corrected, begin = dmixed_ref[0, at, :], corr_ref[0, at, :], begin_ref[0, places, :]
        dcorr = dcorr_ref[0, at, :].astype(f32) + dot(tail * keys32, dstate)
        datt = dot(dmixed, corrected, 1, 1)
        from_begin = dot(jnp.concatenate([dmixed, dcorr.astype(bf16)], axis=0), begin, 1, 1)
        dgrown, dw = from_begin[:CHUNK], -from_begin[CHUNK:]
        dtail_keys = dot(corrected, dstate, 1, 1)
        dwhole = jnp.sum(dstate * begin.astype(f32))
        back = dot(inv_ref[0, at, :], jnp.concatenate([dw, dcorr], axis=1), 0, 0)
        dright_keys, dright_values = back[:, :KEY], back[:, KEY:]
        dsystem = -dot(
            back, jnp.concatenate([w_ref[0, at, :], u_ref[0, at, :]], axis=1), 1, 1
        )
        products = dot(jnp.concatenate([keys, queries], axis=0), keys, 1, 1)
        decayed = jnp.where(rows > cols, between * products[:CHUNK], 0.0)
        dsys_decayed = dsystem * decayed
        dbeta = jnp.sum(dsys_decayed, axis=1, keepdims=True)
        pairs = beta * dsys_decayed + datt * (between * products[CHUNK:])
        dkk = jnp.where(rows > cols, dsystem * (beta * between), 0.0)
        dqk = datt * between
        dqk16, dkk16 = dqk.astype(bf16), dkk.astype(bf16)
        dqn_scr[at, :] = dot(dqk16, keys) + grow * dgrown
        dkn_scr[at, :] = (
            dot(jnp.concatenate([dqk16, dkk16], axis=0), jnp.concatenate([queries, keys], axis=0), 0, 0)
            + dot(dkk16, keys)
            + tail * dtail_keys
            + (beta * grow) * dright_keys
        )
        dvn_scr[at, :] = beta * dright_values
        keys_part = grow * jnp.sum(dright_keys * keys32, axis=1, keepdims=True)
        dbeta = dbeta + jnp.sum(dright_values * values32, axis=1, keepdims=True) + keys_part
        from_tail = tail * jnp.sum(dtail_keys * keys32, axis=1, keepdims=True)
        dcum = (
            jnp.sum(pairs, axis=1, keepdims=True)
            - as_column(jnp.sum(pairs, axis=0, keepdims=True), diagonal)
            + grow * jnp.sum(dgrown * queries32, axis=1, keepdims=True)
            + beta * keys_part
            - from_tail
        )
        dlast = whole * dwhole + jnp.sum(from_tail, axis=0, keepdims=True)
        dld_ref[0, :, at] = jnp.sum(jnp.where(rows >= cols, dcum, 0.0), axis=0, keepdims=True) + dlast
        dbeta_ref[0, :, at] = as_row(dbeta, diagonal)

    for scr in (dn_scr, dw_scr):
        scr[0:EDGE, :] = jnp.zeros((EDGE, scr.shape[1]), f32)
        scr[EDGE + length :, :] = jnp.zeros((EDGE, scr.shape[1]), f32)
    pn_scr[...] = q_ref[...].astype(f32)
    act, slope = silu_slope(conv_sum(pn_scr, tq_ref, length))
    root = lax.rsqrt(jnp.sum(act * act, axis=-1, keepdims=True) + epsilon)
    normal = act * root
    dy = dqn_scr[...] * KEY ** (-0.5)
    dz = root * (dy - normal * jnp.sum(normal * dy, axis=-1, keepdims=True)) * slope
    conv_back(dz, tq_ref, dn_scr, pn_scr, dq_ref, dtq_ref)
    pn_scr[...] = k_ref[...].astype(f32)
    act, slope = silu_slope(conv_sum(pn_scr, tk_ref, length))
    root = lax.rsqrt(jnp.sum(act * act, axis=-1, keepdims=True) + epsilon)
    normal = act * root
    dy = dkn_scr[...]
    dz = root * (dy - normal * jnp.sum(normal * dy, axis=-1, keepdims=True)) * slope
    conv_back(dz, tk_ref, dn_scr, pn_scr, dk_ref, dtk_ref)
    pw_scr[...] = v_ref[...].astype(f32)
    act, slope = silu_slope(conv_sum(pw_scr, tv_ref, length))
    conv_back(dvn_scr[...] * slope, tv_ref, dw_scr, pw_scr, dv_ref, dtv_ref)


def tall(rows, cols):
    return pl.BlockSpec((rows, cols), lambda h: (0, h))


def deep(rows, cols):
    return pl.BlockSpec((1, rows, cols), lambda h: (h, 0, 0))


def shared(rows, cols):
    return pl.BlockSpec((rows, cols), lambda h: (0, 0))


def shape_of(dims, dtype):
    return jax.ShapeDtypeStruct(dims, dtype)


def call_heads(kernel, head_count, in_specs, outputs, scratch, args):
    out_specs = [spec for spec, shape in outputs]
    out_shape = [shape for spec, shape in outputs]
    return pl.pallas_call(
        kernel,
        grid=(head_count,),
        in_specs=in_specs,
        out_specs=out_specs,
        out_shape=out_shape,
        scratch_shapes=scratch,
        compiler_params=pltpu.CompilerParams(vmem_limit_bytes=VMEM_BYTES),
        cost_estimate=COST,
    )(*args)


def prepare(x, edge, gain, w_query, w_key, w_value, w_decay, w_beta, rate, conv_query, conv_key, conv_value):
    length, width = x.shape
    heads = w_decay.shape[0]
    states = (length // CHUNK) * KEY
    ncols, wcols = heads * KEY, heads * VALUE
    out_shape = [
        shape_of((length, width), bf16),
        shape_of((length + EDGE, width), bf16),
        shape_of((length, heads), f32),
        shape_of((length + EDGE, ncols), bf16),
        shape_of((length + EDGE, ncols), bf16),
        shape_of((length + EDGE, wcols), bf16),
        shape_of((heads, 1, length), f32),
        shape_of((heads, 1, length), f32),
        shape_of((length, ncols), bf16),
        shape_of((length, ncols), bf16),
        shape_of((length, wcols), bf16),
        shape_of((heads, length, CHUNK), bf16),
        shape_of((heads, length, CHUNK), bf16),
        shape_of((heads, length, VALUE), bf16),
        shape_of((heads, length, KEY), bf16),
        shape_of((heads, states, KEY + VALUE), bf16),
        shape_of((heads, KEY, KEY + VALUE), f32),
    ]
    args = (
        x, edge, gain, w_query, w_key, w_value, w_decay, w_beta, rate, conv_query, conv_key, conv_value
    )
    return pl.pallas_call(
        prep_kernel,
        out_shape=out_shape,
        in_specs=[pl.BlockSpec(memory_space=pltpu.VMEM)] * len(args),
        out_specs=[pl.BlockSpec(memory_space=pltpu.VMEM)] * len(out_shape),
        scratch_shapes=[
            pltpu.VMEM((length + EDGE, wcols), f32),
            pltpu.VMEM((length + EDGE, ncols), f32),
        ],
        compiler_params=pltpu.CompilerParams(vmem_limit_bytes=VMEM_BYTES),
        cost_estimate=COST,
    )(*args)


def run_forward(qn, ld, att, u, w, starts, state_in, gate_pre, gain, w_out):
    length = qn.shape[0]
    heads = ld.shape[0]
    states = starts.shape[1]
    wide = tall(length, VALUE)
    wshape = (length, heads * VALUE)
    outputs = [
        (wide, shape_of(wshape, bf16)),
        (wide, shape_of(wshape, f32)),
        (deep(length, VALUE), shape_of((heads, length, VALUE), bf16)),
        (deep(states, VALUE), shape_of((heads, states, VALUE), bf16)),
        (shared(length, w_out.shape[1]), shape_of((length, w_out.shape[1]), bf16)),
    ]
    in_specs = [
        tall(length, KEY), deep(1, length), deep(length, CHUNK), deep(length, VALUE), deep(length, KEY),
        deep(states, KEY + VALUE), deep(KEY, VALUE), wide, shared(1, VALUE),
        pl.BlockSpec((VALUE, w_out.shape[1]), lambda h: (h, 0)),
    ]
    args = (qn, ld, att, u, w, starts, state_in, gate_pre, gain, w_out)
    scratch = [pltpu.VMEM((length, w_out.shape[1]), f32)]
    return call_heads(forward_kernel, heads, in_specs, outputs, scratch, args)


def gate_back(dgated, mixed, gate_pre, gain, qn, kn, ld, att, w):
    length = qn.shape[0]
    heads = ld.shape[0]
    states = (length // CHUNK) * KEY
    wide = tall(length, VALUE)
    outputs = [
        (wide, shape_of((length, heads * VALUE), bf16)),
        (deep(length, VALUE), shape_of((heads, length, VALUE), bf16)),
        (deep(length, VALUE), shape_of((heads, length, VALUE), bf16)),
        (deep(1, VALUE), shape_of((heads, 1, VALUE), f32)),
        (deep(states, KEY + VALUE), shape_of((heads, states, KEY + VALUE), bf16)),
        (deep(KEY, KEY + VALUE), shape_of((heads, KEY, KEY + VALUE), f32)),
    ]
    in_specs = [
        wide, wide, wide, shared(1, VALUE), tall(length, KEY), tall(length, KEY), deep(1, length),
        deep(length, CHUNK), deep(length, KEY),
    ]
    args = (dgated, mixed, gate_pre, gain, qn, kn, ld, att, w)
    return call_heads(gate_back_kernel, heads, in_specs, outputs, [], args)


def run_backward(
    gstate, after, dmixed, dcorr, begin, corr, inverse, att, u, w, qn, kn, vn,
    query_ext, key_ext, value_ext, conv_query, conv_key, conv_value, ld, beta,
):
    length = qn.shape[0]
    heads = ld.shape[0]
    states = after.shape[1]
    taps = conv_query.shape[0]
    narrow, wide = tall(length, KEY), tall(length, VALUE)
    ncols, wcols = heads * KEY, heads * VALUE
    outputs = [
        (tall(length + EDGE, KEY), shape_of((length + EDGE, ncols), bf16)),
        (tall(length + EDGE, KEY), shape_of((length + EDGE, ncols), bf16)),
        (tall(length + EDGE, VALUE), shape_of((length + EDGE, wcols), bf16)),
        (tall(taps, KEY), shape_of((taps, ncols), f32)),
        (tall(taps, KEY), shape_of((taps, ncols), f32)),
        (tall(taps, VALUE), shape_of((taps, wcols), f32)),
        (deep(1, length), shape_of((heads, 1, length), f32)),
        (deep(1, length), shape_of((heads, 1, length), f32)),
    ]
    in_specs = [
        deep(KEY, VALUE), deep(states, KEY + VALUE), deep(length, VALUE), deep(length, VALUE),
        deep(states, VALUE), deep(length, VALUE), deep(length, CHUNK), deep(length, CHUNK),
        deep(length, VALUE), deep(length, KEY),
        narrow, narrow, wide,
        tall(length + EDGE, KEY), tall(length + EDGE, KEY), tall(length + EDGE, VALUE),
        tall(taps, KEY), tall(taps, KEY), tall(taps, VALUE),
        deep(1, length), deep(1, length),
    ]
    scratch = [
        pltpu.VMEM((length, KEY), f32), pltpu.VMEM((length, KEY), f32), pltpu.VMEM((length, VALUE), f32),
        pltpu.VMEM((length + 2 * EDGE, KEY), f32), pltpu.VMEM((length + EDGE, KEY), f32),
        pltpu.VMEM((length + 2 * EDGE, VALUE), f32), pltpu.VMEM((length + EDGE, VALUE), f32),
    ]
    args = (
        gstate, after, dmixed, dcorr, begin, corr, inverse, att, u, w, qn, kn, vn,
        query_ext, key_ext, value_ext, conv_query, conv_key, conv_value, ld, beta,
    )
    return call_heads(backward_kernel, heads, in_specs, outputs, scratch, args)


def ffn_kernel(
    x_ref, branch_ref, gain_ref, wg_ref, wu_ref, wd_ref, cot_ref,
    normed_ref, hidden_ref, dgate_ref, dup_ref, part_ref,
):
    middle = x_ref[...].astype(f32) + branch_ref[...].astype(f32)
    normed = row_norm(middle, gain_ref[...]).astype(bf16)
    normed_ref[...] = normed
    gate = dot(normed, wg_ref[...], 1, 1)
    up = dot(normed, wu_ref[...], 1, 1)
    sig = jax.nn.sigmoid(gate)
    act = gate * sig
    hidden_ref[...] = (act * up).astype(bf16)
    dhidden = dot(cot_ref[...], wd_ref[...], 1, 1)
    dgate = (dhidden * up * (sig * (1.0 + gate * (1.0 - sig)))).astype(bf16)
    dup = (dhidden * act).astype(bf16)
    dgate_ref[...] = dgate
    dup_ref[...] = dup
    part_ref[...] = (dot(dgate, wg_ref[...]) + dot(dup, wu_ref[...])).astype(bf16)


def run_ffn(x, branch, gain, w_ffn_gate, w_ffn_up, w_ffn_down, cotangent):
    length, width = x.shape
    hidden = w_ffn_gate.shape[0]
    block = length // 2

    def rows(cols):
        return pl.BlockSpec((block, cols), lambda i: (i, 0))

    return pl.pallas_call(
        ffn_kernel,
        grid=(length // block,),
        in_specs=[
            rows(width), rows(width), shared(1, width), shared(hidden, width), shared(hidden, width),
            shared(hidden, width), rows(width),
        ],
        out_specs=[rows(width), rows(hidden), rows(hidden), rows(hidden), rows(width)],
        out_shape=[
            shape_of((length, width), bf16),
            shape_of((length, hidden), bf16),
            shape_of((length, hidden), bf16),
            shape_of((length, hidden), bf16),
            shape_of((length, width), bf16),
        ],
        compiler_params=pltpu.CompilerParams(vmem_limit_bytes=VMEM_BYTES),
        cost_estimate=COST,
    )(x, branch, gain, w_ffn_gate, w_ffn_up, w_ffn_down, cotangent)


def shard_kernel(plan, count, piece, places_ref, *refs):
    outs = refs[-2 * len(plan) :]
    for number, pairs in enumerate(plan):
        for which in range(2):
            out_ref = outs[2 * number + which]
            chosen = {}
            at = 0
            for left, right in pairs:
                if left not in chosen:
                    chosen[left] = jnp.concatenate(
                        [
                            refs[left][:, pl.ds(pl.multiple_of(places_ref[number, which, g] * piece, 128), piece)]
                            for g in range(count)
                        ],
                        axis=1,
                    )
                width = refs[right].shape[1]
                out_ref[:, at : at + width] = dot(chosen[left], refs[right][...], 0, 0).astype(out_ref.dtype)
                at += width


def shard_products(chains, home_type):
    size = lax.axis_size("seq")
    here = lax.axis_index("seq")
    count = size // 2
    slots = jnp.arange(count, dtype=jnp.int32)
    places = []
    for bit, pairs in chains:
        shards = (slots // 2**bit) * 2 ** (bit + 1) + slots % 2**bit
        mine = (here // 2**bit) % 2
        places.append(jnp.stack([shards + (1 - mine) * 2**bit, shards + mine * 2**bit]))
    width = chains[0][1][0][0].shape[1]
    piece = width // size
    if piece % 128:
        results = []
        for (bit, pairs), chosen in zip(chains, places):
            parts = []
            for which, kind in ((0, bf16), (1, home_type)):
                columns = [
                    lax.dot_general(
                        jnp.take(left.reshape(-1, size, piece), chosen[which], axis=1).reshape(
                            left.shape[0], -1
                        ),
                        right,
                        (((0,), (0,)), ((), ())),
                        preferred_element_type=f32,
                    )
                    for left, right in pairs
                ]
                parts.append(jnp.concatenate(columns, axis=1).astype(kind))
            results.append(tuple(parts))
        return results
    args, plan, out_shape = [], [], []

    def slot_of(array):
        for number, known in enumerate(args):
            if known is array:
                return number
        args.append(array)
        return len(args) - 1

    for bit, pairs in chains:
        plan.append([(slot_of(left), slot_of(right)) for left, right in pairs])
        total = sum(right.shape[1] for left, right in pairs)
        out_shape += [shape_of((count * piece, total), bf16), shape_of((count * piece, total), home_type)]
    whole = pl.BlockSpec(memory_space=pltpu.VMEM)
    flat = pl.pallas_call(
        functools.partial(shard_kernel, plan, count, piece),
        in_specs=[pl.BlockSpec(memory_space=pltpu.SMEM)] + [whole] * len(args),
        out_specs=[whole] * len(out_shape),
        out_shape=out_shape,
        compiler_params=pltpu.CompilerParams(vmem_limit_bytes=VMEM_BYTES),
        cost_estimate=COST,
    )(jnp.stack(places), *args)
    return [(flat[2 * number], flat[2 * number + 1]) for number in range(len(chains))]


def turn_kernel(cuts, *refs):
    ins, outs = refs[: len(cuts)], refs[len(cuts) :]
    for (low, high), in_ref, out_ref in zip(cuts, ins, outs):
        out_ref[...] = in_ref[:, low:high].T


def turned(pieces):
    if pieces[0][0].shape[0] % 128:
        return [array[:, low:high].T for array, low, high in pieces]
    whole = pl.BlockSpec(memory_space=pltpu.VMEM)
    return pl.pallas_call(
        functools.partial(turn_kernel, [(low, high) for array, low, high in pieces]),
        in_specs=[whole] * len(pieces),
        out_specs=[whole] * len(pieces),
        out_shape=[shape_of((high - low, array.shape[0]), f32) for array, low, high in pieces],
        compiler_params=pltpu.CompilerParams(vmem_limit_bytes=VMEM_BYTES),
        cost_estimate=COST,
    )(*[array for array, low, high in pieces])


def from_behind(block, axis, distance):
    devices = range(lax.axis_size(axis))
    route = [(i - distance, i) for i in devices if i - distance in devices]
    return lax.ppermute(block, axis, route)


def swap_with(block, axis, distance):
    route = [(i, i ^ distance) for i in range(lax.axis_size(axis))]
    return lax.ppermute(block, axis, route)


def exchange_rounds(tasks, box=None, beside=None):
    results, asked = [None] * len(tasks), {}

    def advance(which, got):
        try:
            asked[which] = tasks[which].send(got)
        except StopIteration as end:
            results[which] = end.value
            asked.pop(which, None)

    for which in range(len(tasks)):
        advance(which, None)
    number = 0
    while asked:
        number += 1
        got = {which: tuple(exchange() for exchange in wanted) for which, wanted in asked.items()}
        names = [name for name in (beside or {}).get(number, ()) if name in box]
        got, values = lax.optimization_barrier((got, [box[name] for name in names]))
        for name, value in zip(names, values):
            box[name] = value
        for which in list(asked):
            advance(which, got[which])
    return results


def swap(block, axis, distance):
    return lambda: swap_with(block, axis, distance)


def together(first, second):
    wanted = [next(first), next(second)]
    while True:
        got = yield wanted[0] + wanted[1]
        cut = len(wanted[0])
        results = []
        for which, (task, part) in enumerate(((first, got[:cut]), (second, got[cut:]))):
            try:
                wanted[which] = task.send(part)
            except StopIteration as end:
                results.append(end.value)
        if results:
            return results


def pause(rounds):
    for _ in range(rounds):
        yield []


def group_sum(block, axis):
    size = lax.axis_size(axis)
    distance = 1
    while distance < size:
        reach = min(4, size // distance)
        arrived = yield [swap(block, axis, distance * step) for step in range(1, reach)]
        if reach == 4:
            block = (block + arrived[0]) + (arrived[1] + arrived[2])
        else:
            block = block + arrived[0]
        distance *= reach
    return block


def small_sums(block, shared):
    shared = yield from group_sum(shared, "head")
    rows = -(-shared.shape[0] // block.shape[1])
    padded = jnp.pad(shared, (0, rows * block.shape[1] - shared.shape[0])).reshape(rows, -1)
    total = yield from group_sum(jnp.concatenate([block, padded], axis=0), "seq")
    return total[: block.shape[0]], total[block.shape[0] :].reshape(-1)[: shared.shape[0]]


def sum_over_heads(partial):
    rows = partial.shape[0] // 2
    odd = lax.axis_index("head") % 2 == 1
    low, high = partial[:rows], partial[rows:]
    own = jnp.where(odd, high, low).astype(f32)
    (got,) = yield [swap(jnp.where(odd, low, high), "head", 1)]
    own = own + got.astype(f32)
    distance = 2
    while distance < lax.axis_size("head"):
        sent = own.astype(bf16)
        (got,) = yield [swap(sent, "head", distance)]
        own = sent.astype(f32) + got.astype(f32)
        distance *= 2
    kept = own.astype(bf16)
    (other,) = yield [swap(kept, "head", 1)]
    return jnp.concatenate([jnp.where(odd, other, kept), jnp.where(odd, kept, other)], axis=0)


def exclusive_scan(joined, sign):
    own_t, own_b = joined[..., :KEY], joined[..., KEY:]
    send = joined
    before_t = before_b = None
    distance = 1
    size = lax.axis_size("seq")

    def product(a, b):
        return jnp.einsum("hij,hjk->hik", a, b, precision=lax.Precision.HIGH)

    while distance < size:
        last = distance * 2 >= size
        sent = (send[..., KEY:] if last else send).astype(bf16)
        (got,) = yield [functools.partial(from_behind, sent, "seq", sign * distance)]
        got = got.astype(f32)
        if before_t is None:
            before_t, before_b = got[..., :KEY], got[..., KEY:]
        else:
            moved = product(before_t, got)
            if last:
                before_b = before_b + moved
            else:
                before_t, before_b = moved[..., :KEY], before_b + moved[..., KEY:]
        if not last:
            send = product(own_t, jnp.concatenate([before_t, before_b], axis=-1))
            send = jnp.concatenate([send[..., :KEY], send[..., KEY:] + own_b], axis=-1)
        distance *= 2
    return before_b


def halving_scatter(products, order, pauses=(), hold=None):
    size = lax.axis_size("seq")
    bits = size.bit_length() - 1
    here = lax.axis_index("seq")
    order = [bit for bit in order if bit < bits] + list(range(len(order), bits))
    pauses = list(pauses) + [0] * bits
    away, home = products
    (got,) = yield [swap(away, "seq", 2 ** order[0])]
    held = home.astype(f32) + got.astype(f32)
    axes = [bit for bit in range(bits)[::-1] if bit != order[0]]
    held = held.reshape((2,) * (bits - 1) + (held.shape[0] // 2 ** (bits - 1), held.shape[1]))
    for number, bit in enumerate(order[1:]):
        axis = axes.index(bit)
        axes.remove(bit)
        mine = (here // 2**bit) % 2
        sent = lax.dynamic_index_in_dim(held, 1 - mine, axis, keepdims=False).astype(bf16)
        if pauses[number]:
            yield from pause(pauses[number])
            sent = hold(sent)
        (got,) = yield [swap(sent, "seq", 2**bit)]
        held = lax.dynamic_index_in_dim(held, mine, axis, keepdims=False) + got.astype(f32)
    return held


def inner_rows(first_operand, second_operand):
    return lax.dot_general(
        first_operand, second_operand, (((0,), (0,)), ((), ())), preferred_element_type=f32
    )


def matmul_bf(first_operand, second_operand):
    return jnp.dot(first_operand, second_operand, preferred_element_type=f32)


def against_rows(first_operand, second_operand):
    return lax.dot_general(
        first_operand, second_operand, (((1,), (1,)), ((), ())), preferred_element_type=f32
    )


def per_device(
    block_input,
    norm1_gain,
    w_query,
    w_key,
    w_value,
    w_gate,
    w_decay,
    w_beta,
    conv_query,
    conv_key,
    conv_value,
    decay_rate,
    out_gain,
    w_out,
    norm2_gain,
    w_ffn_gate,
    w_ffn_up,
    w_ffn_down,
    cotangent,
):
    length = block_input.shape[0]
    head_count = w_decay.shape[1]
    key_cols = w_query.shape[1]
    value_cols = w_value.shape[1]
    ff_cols = w_ffn_gate.shape[1]
    edge_input = from_behind(block_input[length - EDGE :], "seq", 1)
    gain1 = norm1_gain.astype(f32)
    (
        normed, normed_ext, decay_cols, query_ext, key_ext, value_ext, log_decay, beta3,
        qn, kn, vn, inverse, att, u, w, starts, composite,
    ) = prepare(
        block_input, edge_input, gain1[None], w_query, w_key, w_value, w_decay.T, w_beta.T,
        decay_rate[None], conv_query, conv_key, conv_value,
    )
    inputs32 = block_input.astype(f32)
    gate_pre = matmul_bf(normed, w_gate)
    box = {"gate": gate_pre}
    (state_in,) = exchange_rounds([exclusive_scan(composite, 1)], box, {1: ["gate"]})
    gate_pre = box["gate"]
    gain_row = out_gain.astype(f32)[None]
    gated, mixed, corr, begin, branch_part = run_forward(
        qn, log_decay, att, u, w, starts, state_in, gate_pre, gain_row, w_out
    )
    (branch,) = exchange_rounds([sum_over_heads(branch_part)])
    gain2 = norm2_gain.astype(f32)
    normed2, hidden, grad_fgate, grad_fup, grad_part = run_ffn(
        block_input, branch, gain2[None], w_ffn_gate.T, w_ffn_up.T, w_ffn_down, cotangent
    )
    bits = lax.axis_size("seq").bit_length() - 1
    near, far = 0, min(1, bits - 1)
    half = ff_cols // 2 // 128 * 128
    ffn_near, ffn_far = shard_products(
        [
            (near, [(normed2, grad_fgate), (cotangent, hidden[:, :half])]),
            (far, [(normed2, grad_fup), (cotangent, hidden[:, half:])]),
        ],
        bf16,
    )
    box = {}

    def after_scan(sent):
        return lax.optimization_barrier((sent, box["state"]))[0]

    ffn_tasks = [
        halving_scatter(ffn_near, [0, 1], [0, bits - 2], after_scan),
        halving_scatter(ffn_far, [1, 0], [0, bits - 2], after_scan),
    ]
    ffn_got = [tuple(exchange() for exchange in next(task)) for task in ffn_tasks]
    box["away"] = (ffn_near[0], ffn_far[0])
    (grad_normed2,) = exchange_rounds([sum_over_heads(grad_part)], box, {2: ["away"]})
    grad_normed2 = grad_normed2.astype(f32)
    middle = inputs32 + branch.astype(f32)
    norm2_back = jax.vjp(row_norm, middle, gain2)[1]
    ffn_part = matmul_bf(hidden, w_ffn_down).astype(bf16)
    grad_middle_n, grad_gain2 = norm2_back(grad_normed2)
    grad_middle = cotangent.astype(f32) + grad_middle_n
    grad_branch = grad_middle.astype(bf16)
    grad_gated = against_rows(grad_branch, w_out)
    grad_gp, grad_mixed, grad_corr, grad_outgain, after, composite_back = gate_back(
        grad_gated, mixed, gate_pre, gain_row, qn, kn, log_decay, att, w
    )
    composite_back, ffn_part = lax.optimization_barrier((composite_back, ffn_part))
    pad_rows = ((length - 8, 0), (0, 0))
    taps_count = conv_query.shape[0]
    width = w_query.shape[0]

    def main_task():
        grad_state = yield from exclusive_scan(composite_back, -1)
        box["state"] = grad_state
        dq, dk, dv, taps_q, taps_k, taps_v, grad_log, grad_beta = run_backward(
            grad_state, after, grad_mixed, grad_corr, begin, corr, inverse, att, u, w,
            qn, kn, vn, query_ext, key_ext, value_ext,
            conv_query, conv_key, conv_value, log_decay, beta3,
        )
        box["late"] = shard_products(
            [(near, [(normed_ext, dq), (normed_ext, dk)]), (far, [(normed_ext, dv)])], f32
        )
        part_ext = against_rows(dq, w_query) + against_rows(dk, w_key) + against_rows(dv, w_value)
        decay_pre = decay_cols.T
        soft = jax.nn.softplus(decay_pre)
        rate = decay_rate[:, None]
        beta_gate = beta3.reshape(head_count, length)
        grad_log = grad_log.reshape(head_count, length)
        grad_beta = grad_beta.reshape(head_count, length)
        grad_dp = (-rate * jax.nn.sigmoid(decay_pre) * grad_log).astype(bf16)
        grad_bp = (beta_gate * (1.0 - beta_gate) * grad_beta).astype(bf16)
        grad_rate = -jnp.sum(grad_log * soft, axis=1)
        grad_scalars = jnp.concatenate([grad_dp, grad_bp], axis=0)
        w_scalars = jnp.concatenate([w_decay, w_beta], axis=1)
        edges = part_ext[EDGE - 8 : EDGE]
        (edges,) = yield [functools.partial(from_behind, edges, "seq", -1)]
        part = (
            part_ext[EDGE:]
            + against_rows(grad_gp, w_gate)
            + lax.dot_general(
                grad_scalars, w_scalars, (((0,), (1,)), ((), ())), preferred_element_type=f32
            )
            + jnp.pad(edges, pad_rows)
        )
        box["shared"] = jnp.concatenate(
            [jnp.sum(part * row_norm(inputs32, 1.0), axis=0), jnp.sum(grad_outgain, axis=(0, 1))]
        )
        box["small"] = jnp.concatenate(
            [
                jnp.concatenate([taps_q, taps_k, taps_v], axis=1),
                grad_gain2[None],
                jnp.pad(grad_rate, (0, width - head_count))[None],
                matmul_bf(grad_scalars, normed),
            ],
            axis=0,
        )
        return (yield from sum_over_heads(part.astype(bf16)))

    def ffn_rest(task, got, name):
        wanted = [lambda block=block: block for block in got]
        try:
            while True:
                wanted = task.send((yield wanted))
        except StopIteration as end:
            held = end.value
        box[name] = turned([(held, 0, ff_cols), (held, ff_cols, held.shape[1])])

    def ffn_sum_task():
        steps = sum_over_heads(ffn_part)
        got = yield next(steps)
        wanted = steps.send(got)
        yield from pause(bits - 1)
        try:
            while True:
                wanted = steps.send((yield wanted))
        except StopIteration as end:
            box["out"] = (middle + end.value.astype(f32)).astype(bf16)

    def mid_task():
        yield from pause(bits)
        products = shard_products([(near, [(grad_branch, gated)]), (far, [(normed, grad_gp)])], f32)
        products = after_scan(products)
        first, second = halving_scatter(products[0], [0, 1]), halving_scatter(products[1], [1, 0])
        grad_wout, grad_wg = yield from together(first, second)
        box["mid"] = (*turned([(grad_wout, 0, grad_wout.shape[1])]), grad_wg)

    def late_task():
        yield from pause(bits + 1)
        first, second = box["late"]
        return (yield from together(halving_scatter(first, [0, 1]), halving_scatter(second, [1, 0])))

    def small_task():
        yield from pause(bits + 1)
        return (yield from small_sums(box["small"], box["shared"]))

    grad_normed, late, small_pair = exchange_rounds(
        [main_task(), late_task(), small_task(), mid_task(), ffn_sum_task()]
        + [ffn_rest(task, got, name) for task, got, name in zip(ffn_tasks, ffn_got, ("near", "far"))],
        box,
        {bits + 3: ["near", "far"], bits + 4: ["out", "mid"]},
    )[:3]
    late_qk, late_v = late
    small, shared_sum = small_pair
    grad_wout, grad_wg = box["mid"]
    grad_wfg, down_near = box["near"]
    grad_wfu, down_far = box["far"]
    layer_out = box["out"]
    norm1_back = jax.vjp(row_norm, inputs32, gain1)[1]
    grad_input = grad_middle + norm1_back(grad_normed.astype(f32))[0]
    taps_sum = small[:taps_count]
    gain2_sum = small[taps_count]
    rate_sum = small[taps_count + 1, :head_count]
    scalars_sum = small[taps_count + 2 : taps_count + 2 + 2 * head_count]
    gain1_sum, outgain_sum = shared_sum[:width], shared_sum[width:]

    def own_part(vec):
        piece = vec.shape[-1] // lax.axis_size("seq")
        return lax.dynamic_slice_in_dim(vec, lax.axis_index("seq") * piece, piece, axis=-1)

    scalars_sum = own_part(scalars_sum).T
    return (
        layer_out,
        grad_input,
        own_part(gain1_sum),
        late_qk[:, :key_cols],
        late_qk[:, key_cols:],
        late_v,
        grad_wg,
        scalars_sum[:, :head_count],
        scalars_sum[:, head_count:],
        taps_sum[:, :key_cols],
        taps_sum[:, key_cols : 2 * key_cols],
        taps_sum[:, 2 * key_cols :],
        rate_sum,
        own_part(outgain_sum),
        grad_wout,
        own_part(gain2_sum),
        grad_wfg.T,
        grad_wfu.T,
        jnp.concatenate([down_near, down_far], axis=0),
    )


def solution(mesh):
    return jax.shard_map(
        per_device,
        mesh=mesh,
        in_specs=(
            P("seq", None),
            P(),
            P(None, "head"),
            P(None, "head"),
            P(None, "head"),
            P(None, "head"),
            P(None, "head"),
            P(None, "head"),
            P(None, "head"),
            P(None, "head"),
            P(None, "head"),
            P("head"),
            P(),
            P("head", None),
            P(),
            P(None, "head"),
            P(None, "head"),
            P("head", None),
            P("seq", None),
        ),
        out_specs=(
            P("seq", None),
            P("seq", None),
            P("seq"),
            P("seq", "head"),
            P("seq", "head"),
            P("seq", "head"),
            P("seq", "head"),
            P("seq", "head"),
            P("seq", "head"),
            P(None, "head"),
            P(None, "head"),
            P(None, "head"),
            P("head"),
            P("seq"),
            P("head", "seq"),
            P("seq"),
            P("seq", "head"),
            P("seq", "head"),
            P("head", "seq"),
        ),
        check_vma=False,
    )
```

```python
import functools

import jax
import jax.numpy as jnp
from jax import lax
from jax.experimental import pallas as pl
from jax.experimental.pallas import tpu as pltpu
from jax.sharding import PartitionSpec as P

KEY = 128
VALUE = 256
CHUNK = 128
EDGE = 16
SUB = 16
VMEM_BYTES = 32 * 1024 * 1024
COST = pl.CostEstimate(flops=0, bytes_accessed=0, transcendentals=0)

epsilon = 1e-06
f32 = jnp.float32
bf16 = jnp.bfloat16
highest_precision = lax.Precision.HIGHEST


def dot(first, second, over_first=1, over_second=0):
    return lax.dot_general(
        first.astype(bf16),
        second.astype(bf16),
        (((over_first,), (over_second,)), ((), ())),
        preferred_element_type=f32,
    )


def halves(values):
    high = values.astype(bf16)
    return high, (values - high.astype(f32)).astype(bf16)


def dot_fine(first, second):
    first_high, first_low = halves(first)
    second_high, second_low = halves(second)
    width = second.shape[1]
    wide = dot(first_high, jnp.concatenate([second_high, second_low], axis=1))
    return wide[:, :width] + wide[:, width:] + dot(first_low, second_high)


def grid_places(extent):
    rows = lax.broadcasted_iota(jnp.int32, (extent, extent), 0)
    cols = lax.broadcasted_iota(jnp.int32, (extent, extent), 1)
    return rows, cols


def as_row(column, diagonal):
    return jnp.sum(jnp.where(diagonal, column, 0.0), axis=0, keepdims=True)


def as_column(row, diagonal):
    return jnp.sum(jnp.where(diagonal, row, 0.0), axis=1, keepdims=True)


def unit_lower_inverses(systems, rows, cols):
    extent = systems[0].shape[0]
    count = extent // SUB
    units = len(systems)
    same = rows // SUB == cols // SUB
    packed = jnp.concatenate(
        [jnp.sum(jnp.where(same, s, 0.0).reshape(count, SUB, extent), axis=0) for s in systems], axis=0
    )
    stacked = jnp.concatenate(halves(packed), axis=0)
    shape = (units, SUB, extent)
    places = lax.broadcasted_iota(jnp.int32, shape, 1)
    solved = (places == lax.broadcasted_iota(jnp.int32, shape, 2) % SUB).astype(f32)
    for j in range(SUB - 1):
        spread = dot(stacked, (same & (rows % SUB == j)).astype(f32))
        column = spread[: units * SUB] + spread[units * SUB :]
        solved = solved - column.reshape(shape) * solved[:, j : j + 1, :]
    inverses = [
        jnp.where(same, jnp.concatenate([solved[n]] * count, axis=0), 0.0) for n in range(units)
    ]
    size = SUB
    while size < extent:
        below = (rows // (2 * size) == cols // (2 * size)) & (rows // size > cols // size)
        joined = [
            dot_fine(inverse, jnp.where(below, s, 0.0)) for inverse, s in zip(inverses, systems)
        ]
        joined = [dot_fine(product, inverse) for product, inverse in zip(joined, inverses)]
        inverses = [inverse - product for inverse, product in zip(inverses, joined)]
        size *= 2
    return inverses


def decay_terms(ld_row, rows, cols):
    cum_col = jnp.sum(jnp.where(rows >= cols, ld_row, 0.0), axis=1, keepdims=True)
    cum_row = as_row(cum_col, rows == cols)
    last = cum_col[CHUNK - 1 :, :]
    between = jnp.where(rows >= cols, jnp.exp(jnp.where(rows >= cols, cum_col - cum_row, 0.0)), 0.0)
    return between, jnp.exp(cum_col), jnp.exp(last - cum_col), jnp.exp(last)


def conv_sum(padded_ref, taps_ref, length):
    taps = taps_ref[...].astype(f32)
    summed = taps[0:1] * padded_ref[EDGE : EDGE + length, :]
    for offset in range(1, taps_ref.shape[0]):
        summed = summed + taps[offset : offset + 1] * padded_ref[EDGE - offset : EDGE - offset + length, :]
    return summed


def unit_rows(values, scale, heads):
    parts = []
    for h in range(heads):
        part = values[:, h * KEY : (h + 1) * KEY]
        parts.append(
            part * (lax.rsqrt(jnp.sum(part * part, axis=-1, keepdims=True) + epsilon) * scale)
        )
    return jnp.concatenate(parts, axis=1)


def row_norm(values, gain_vec):
    return (
        values * lax.rsqrt(jnp.mean(values * values, axis=-1, keepdims=True) + epsilon) * gain_vec
    )


def prep_kernel(
    x_ref, edge_ref, gain_ref, wq_ref, wk_ref, wv_ref, wd_ref, wb_ref, rate_ref, tq_ref, tk_ref, tv_ref,
    normed_ref, normed_ext_ref, decay_ref, q_ref, k_ref, v_ref, ld_ref, beta_ref,
    qn_ref, kn_ref, vn_ref, inv_ref, att_ref, u_ref, w_ref, start_ref, final_ref,
    wide_scr, narrow_scr,
):
    length = qn_ref.shape[0]
    heads = ld_ref.shape[0]
    chunks = length // CHUNK
    gain = gain_ref[...]
    normed_ext_ref[:EDGE, :] = row_norm(edge_ref[...].astype(f32), gain).astype(bf16)
    normed = row_norm(x_ref[...].astype(f32), gain).astype(bf16)
    normed_ext_ref[EDGE:, :] = normed
    normed_ref[...] = normed
    decay_pre = dot(normed, wd_ref[...], 1, 1)
    decay_ref[...] = decay_pre
    softplus = jnp.maximum(decay_pre, 0.0) + jnp.log1p(jnp.exp(-jnp.abs(decay_pre)))
    log_decay = -rate_ref[...] * softplus
    beta_gate = jax.nn.sigmoid(dot(normed, wb_ref[...], 1, 1))
    pre = dot(normed_ext_ref[...], wk_ref[...]).astype(bf16)
    k_ref[...] = pre
    narrow_scr[...] = pre.astype(f32)
    z = conv_sum(narrow_scr, tk_ref, length)
    kn_ref[...] = unit_rows(z * jax.nn.sigmoid(z), 1.0, heads).astype(bf16)
    pre = dot(normed_ext_ref[...], wq_ref[...]).astype(bf16)
    q_ref[...] = pre
    narrow_scr[...] = pre.astype(f32)
    z = conv_sum(narrow_scr, tq_ref, length)
    qn_ref[...] = unit_rows(z * jax.nn.sigmoid(z), KEY ** (-0.5), heads).astype(bf16)
    pre = dot(normed_ext_ref[...], wv_ref[...]).astype(bf16)
    v_ref[...] = pre
    wide_scr[...] = pre.astype(f32)
    z = conv_sum(wide_scr, tv_ref, length)
    vn_ref[...] = (z * jax.nn.sigmoid(z)).astype(bf16)

    rows, cols = grid_places(CHUNK)
    diagonal = rows == cols
    units = [(h, c) for c in range(chunks) for h in range(heads)]
    systems, vectors = [], []
    for h, c in units:
        at = slice(c * CHUNK, (c + 1) * CHUNK)
        keyed = slice(h * KEY, (h + 1) * KEY)
        ld_row = as_row(log_decay[at, h : h + 1], diagonal)
        ld_ref[h, :, at] = ld_row
        between, grow, tail, whole = decay_terms(ld_row, rows, cols)
        beta = beta_gate[at, h : h + 1]
        beta_ref[h, :, at] = as_row(beta, diagonal)
        keys = kn_ref[at, keyed]
        products = dot(jnp.concatenate([keys, qn_ref[at, keyed]], axis=0), keys, 1, 1)
        systems.append(jnp.where(rows > cols, beta * between * products[:CHUNK], 0.0))
        att_ref[h, at, :] = (products[CHUNK:] * between).astype(bf16)
        vectors.append((beta, grow, tail, whole))
    inverses = unit_lower_inverses(systems, rows, cols)
    kept = []
    for (h, c), inverse, (beta, grow, tail, whole) in zip(units, inverses, vectors):
        at = slice(c * CHUNK, (c + 1) * CHUNK)
        keys32 = kn_ref[at, h * KEY : (h + 1) * KEY].astype(f32)
        values32 = vn_ref[at, h * VALUE : (h + 1) * VALUE].astype(f32)
        inv_ref[h, at, :] = inverse.astype(bf16)
        solved = dot(inverse, jnp.concatenate([(beta * grow) * keys32, beta * values32], axis=1))
        w_ref[h, at, :] = solved[:, :KEY].astype(bf16)
        u_ref[h, at, :] = solved[:, KEY:].astype(bf16)
        kept.append((tail * keys32).astype(bf16))
    begin = jnp.concatenate([diagonal.astype(f32), jnp.zeros((KEY, VALUE), f32)], axis=1)
    states = [begin] * heads
    for (h, c), tail_keys, (beta, grow, tail, whole) in zip(units, kept, vectors):
        at = slice(c * CHUNK, (c + 1) * CHUNK)
        state = states[h]
        start_ref[h, c * KEY : (c + 1) * KEY, :] = state.astype(bf16)
        source = jnp.concatenate([jnp.zeros((CHUNK, KEY), f32), u_ref[h, at, :].astype(f32)], axis=1)
        corrected = source - dot(w_ref[h, at, :], state)
        states[h] = whole * state + dot(tail_keys, corrected, 0, 0)
    for h in range(heads):
        final_ref[h, :, :] = states[h]


def forward_kernel(
    qn_ref, ld_ref, att_ref, u_ref, w_ref, start_ref, state_ref, gate_ref, gain_ref, wout_ref,
    gated_ref, mixed_ref, corr_ref, begin_ref, branch_ref, sum_scr,
):
    length = qn_ref.shape[0]
    rows, cols = grid_places(CHUNK)
    entering = state_ref[0]
    gain = gain_ref[...]
    for c in range(length // CHUNK):
        at = slice(c * CHUNK, (c + 1) * CHUNK)
        places = slice(c * KEY, (c + 1) * KEY)
        between, grow, tail, whole = decay_terms(ld_ref[0, :, at], rows, cols)
        begin = start_ref[0, places, KEY:].astype(f32) + dot(start_ref[0, places, :KEY], entering)
        begin_ref[0, places, :] = begin.astype(bf16)
        corrected = u_ref[0, at, :].astype(f32) - dot(w_ref[0, at, :], begin)
        corr_ref[0, at, :] = corrected.astype(bf16)
        mixed = dot(grow * qn_ref[at, :].astype(f32), begin) + dot(att_ref[0, at, :], corrected)
        mixed_ref[at, :] = mixed
        root = lax.rsqrt(jnp.mean(mixed * mixed, axis=-1, keepdims=True) + epsilon)
        gate = gate_ref[at, :]
        gated_ref[at, :] = (mixed * root * gain * (gate * jax.nn.sigmoid(gate))).astype(bf16)
    part = dot(gated_ref[...], wout_ref[...])

    @pl.when(pl.program_id(0) == 0)
    def start_sum():
        sum_scr[...] = part

    @pl.when(pl.program_id(0) > 0)
    def add_sum():
        sum_scr[...] += part

    @pl.when(pl.program_id(0) == pl.num_programs(0) - 1)
    def give_sum():
        branch_ref[...] = sum_scr[...].astype(bf16)


def gate_back_kernel(
    dgated_ref, mixed_ref, gate_ref, gain_ref, qn_ref, kn_ref, ld_ref, att_ref, w_ref,
    dgate_ref, dmixed_ref, dcorr_ref, dgain_ref, after_ref, final_ref,
):
    length = qn_ref.shape[0]
    rows, cols = grid_places(CHUNK)
    gain = gain_ref[...]
    kept = []
    dgain = jnp.zeros((1, VALUE), f32)
    for c in range(length // CHUNK):
        at = slice(c * CHUNK, (c + 1) * CHUNK)
        mixed, gate, dgated = mixed_ref[at, :], gate_ref[at, :], dgated_ref[at, :]
        root = lax.rsqrt(jnp.mean(mixed * mixed, axis=-1, keepdims=True) + epsilon)
        normal = mixed * root
        sig = jax.nn.sigmoid(gate)
        act = gate * sig
        dgain = dgain + jnp.sum(dgated * normal * act, axis=0, keepdims=True)
        dgate_ref[at, :] = (dgated * normal * gain * (sig * (1.0 + gate * (1.0 - sig)))).astype(bf16)
        dnormal = dgated * act * gain
        dmixed = root * (dnormal - normal * jnp.mean(dnormal * normal, axis=-1, keepdims=True))
        dmixed_ref[0, at, :] = dmixed.astype(bf16)
        between, grow, tail, whole = decay_terms(ld_ref[0, :, at], rows, cols)
        dcorr = dot(att_ref[0, at, :], dmixed, 0, 0)
        dcorr_ref[0, at, :] = dcorr.astype(bf16)
        gradient = dot(grow * qn_ref[at, :].astype(f32), dmixed, 0, 0) - dot(w_ref[0, at, :], dcorr, 0, 0)
        kept.append((gradient, (tail * kn_ref[at, :].astype(f32)).astype(bf16), whole))
    dgain_ref[0, :, :] = dgain
    pending = jnp.concatenate([(rows == cols).astype(f32), jnp.zeros((KEY, VALUE), f32)], axis=1)
    for c in reversed(range(length // CHUNK)):
        gradient, tail_keys, whole = kept[c]
        at = slice(c * CHUNK, (c + 1) * CHUNK)
        after_ref[0, c * KEY : (c + 1) * KEY, :] = pending.astype(bf16)
        source = jnp.concatenate([jnp.zeros((KEY, KEY), f32), gradient], axis=1)
        pending = whole * pending + source - dot(w_ref[0, at, :], dot(tail_keys, pending), 0, 0)
    final_ref[0, :, :] = pending


def silu_slope(z):
    sig = jax.nn.sigmoid(z)
    return z * sig, sig * (1.0 + z * (1.0 - sig))


def conv_back(dz, taps_ref, dz_scr, pre_scr, dpre_ref, dtaps_ref):
    length = dz.shape[0]
    reach = taps_ref.shape[0] - 1
    taps = taps_ref[...].astype(f32)
    dz_scr[EDGE : EDGE + length, :] = dz
    total = taps[0:1] * dz
    sums = [jnp.sum(dz * pre_scr[EDGE : EDGE + length, :], axis=0, keepdims=True)]
    for offset in range(1, reach + 1):
        total = total + taps[offset : offset + 1] * dz_scr[EDGE + offset : EDGE + offset + length, :]
        sums.append(
            jnp.sum(dz * pre_scr[EDGE - offset : EDGE - offset + length, :], axis=0, keepdims=True)
        )
    dpre_ref[EDGE:, :] = total.astype(bf16)
    edge = taps[1:2] * dz_scr[EDGE - 7 : EDGE + 1, :]
    for offset in range(2, reach + 1):
        edge = edge + taps[offset : offset + 1] * dz_scr[EDGE - 8 + offset : EDGE + offset, :]
    dpre_ref[:EDGE, :] = jnp.concatenate([jnp.zeros_like(edge), edge], axis=0).astype(bf16)
    dtaps_ref[...] = jnp.concatenate(sums, axis=0)


def backward_kernel(
    gstate_ref, after_ref, dmixed_ref, dcorr_ref, begin_ref, corr_ref, inv_ref, att_ref, u_ref, w_ref,
    qn_ref, kn_ref, vn_ref, q_ref, k_ref, v_ref, tq_ref, tk_ref, tv_ref,
    ld_ref, beta_ref,
    dq_ref, dk_ref, dv_ref, dtq_ref, dtk_ref, dtv_ref, dld_ref, dbeta_ref,
    dqn_scr, dkn_scr, dvn_scr, dn_scr, pn_scr, dw_scr, pw_scr,
):
    length = qn_ref.shape[0]
    rows, cols = grid_places(CHUNK)
    diagonal = rows == cols
    leaving = gstate_ref[0]
    for c in range(length // CHUNK):
        at = slice(c * CHUNK, (c + 1) * CHUNK)
        places = slice(c * KEY, (c + 1) * KEY)
        between, grow, tail, whole = decay_terms(ld_ref[0, :, at], rows, cols)
        beta = as_column(beta_ref[0, :, at], diagonal)
        keys, queries = kn_ref[at, :], qn_ref[at, :]
        keys32, queries32, values32 = keys.astype(f32), queries.astype(f32), vn_ref[at, :].astype(f32)
        dstate = after_ref[0, places, KEY:].astype(f32) + dot(after_ref[0, places, :KEY], leaving)
        dmixed, corrected, begin = dmixed_ref[0, at, :], corr_ref[0, at, :], begin_ref[0, places, :]
        dcorr = dcorr_ref[0, at, :].astype(f32) + dot(tail * keys32, dstate)
        datt = dot(dmixed, corrected, 1, 1)
        from_begin = dot(jnp.concatenate([dmixed, dcorr.astype(bf16)], axis=0), begin, 1, 1)
        dgrown, dw = from_begin[:CHUNK], -from_begin[CHUNK:]
        dtail_keys = dot(corrected, dstate, 1, 1)
        dwhole = jnp.sum(dstate * begin.astype(f32))
        back = dot(inv_ref[0, at, :], jnp.concatenate([dw, dcorr], axis=1), 0, 0)
        dright_keys, dright_values = back[:, :KEY], back[:, KEY:]
        dsystem = -dot(
            back, jnp.concatenate([w_ref[0, at, :], u_ref[0, at, :]], axis=1), 1, 1
        )
        products = dot(jnp.concatenate([keys, queries], axis=0), keys, 1, 1)
        decayed = jnp.where(rows > cols, between * products[:CHUNK], 0.0)
        dsys_decayed = dsystem * decayed
        dbeta = jnp.sum(dsys_decayed, axis=1, keepdims=True)
        pairs = beta * dsys_decayed + datt * (between * products[CHUNK:])
        dkk = jnp.where(rows > cols, dsystem * (beta * between), 0.0)
        dqk = datt * between
        dqk16, dkk16 = dqk.astype(bf16), dkk.astype(bf16)
        dqn_scr[at, :] = dot(dqk16, keys) + grow * dgrown
        dkn_scr[at, :] = (
            dot(jnp.concatenate([dqk16, dkk16], axis=0), jnp.concatenate([queries, keys], axis=0), 0, 0)
            + dot(dkk16, keys)
            + tail * dtail_keys
            + (beta * grow) * dright_keys
        )
        dvn_scr[at, :] = beta * dright_values
        keys_part = grow * jnp.sum(dright_keys * keys32, axis=1, keepdims=True)
        dbeta = dbeta + jnp.sum(dright_values * values32, axis=1, keepdims=True) + keys_part
        from_tail = tail * jnp.sum(dtail_keys * keys32, axis=1, keepdims=True)
        dcum = (
            jnp.sum(pairs, axis=1, keepdims=True)
            - as_column(jnp.sum(pairs, axis=0, keepdims=True), diagonal)
            + grow * jnp.sum(dgrown * queries32, axis=1, keepdims=True)
            + beta * keys_part
            - from_tail
        )
        dlast = whole * dwhole + jnp.sum(from_tail, axis=0, keepdims=True)
        dld_ref[0, :, at] = jnp.sum(jnp.where(rows >= cols, dcum, 0.0), axis=0, keepdims=True) + dlast
        dbeta_ref[0, :, at] = as_row(dbeta, diagonal)

    for scr in (dn_scr, dw_scr):
        scr[0:EDGE, :] = jnp.zeros((EDGE, scr.shape[1]), f32)
        scr[EDGE + length :, :] = jnp.zeros((EDGE, scr.shape[1]), f32)
    pn_scr[...] = q_ref[...].astype(f32)
    act, slope = silu_slope(conv_sum(pn_scr, tq_ref, length))
    root = lax.rsqrt(jnp.sum(act * act, axis=-1, keepdims=True) + epsilon)
    normal = act * root
    dy = dqn_scr[...] * KEY ** (-0.5)
    dz = root * (dy - normal * jnp.sum(normal * dy, axis=-1, keepdims=True)) * slope
    conv_back(dz, tq_ref, dn_scr, pn_scr, dq_ref, dtq_ref)
    pn_scr[...] = k_ref[...].astype(f32)
    act, slope = silu_slope(conv_sum(pn_scr, tk_ref, length))
    root = lax.rsqrt(jnp.sum(act * act, axis=-1, keepdims=True) + epsilon)
    normal = act * root
    dy = dkn_scr[...]
    dz = root * (dy - normal * jnp.sum(normal * dy, axis=-1, keepdims=True)) * slope
    conv_back(dz, tk_ref, dn_scr, pn_scr, dk_ref, dtk_ref)
    pw_scr[...] = v_ref[...].astype(f32)
    act, slope = silu_slope(conv_sum(pw_scr, tv_ref, length))
    conv_back(dvn_scr[...] * slope, tv_ref, dw_scr, pw_scr, dv_ref, dtv_ref)


def tall(rows, cols):
    return pl.BlockSpec((rows, cols), lambda h: (0, h))


def deep(rows, cols):
    return pl.BlockSpec((1, rows, cols), lambda h: (h, 0, 0))


def shared(rows, cols):
    return pl.BlockSpec((rows, cols), lambda h: (0, 0))


def shape_of(dims, dtype):
    return jax.ShapeDtypeStruct(dims, dtype)


def call_heads(kernel, head_count, in_specs, outputs, scratch, args, cost=COST):
    out_specs = [spec for spec, shape in outputs]
    out_shape = [shape for spec, shape in outputs]
    return pl.pallas_call(
        kernel,
        grid=(head_count,),
        in_specs=in_specs,
        out_specs=out_specs,
        out_shape=out_shape,
        scratch_shapes=scratch,
        compiler_params=pltpu.CompilerParams(vmem_limit_bytes=VMEM_BYTES),
        cost_estimate=cost,
    )(*args)


def prepare(x, edge, gain, w_query, w_key, w_value, w_decay, w_beta, rate, conv_query, conv_key, conv_value):
    length, width = x.shape
    heads = w_decay.shape[0]
    states = (length // CHUNK) * KEY
    ncols, wcols = heads * KEY, heads * VALUE
    out_shape = [
        shape_of((length, width), bf16),
        shape_of((length + EDGE, width), bf16),
        shape_of((length, heads), f32),
        shape_of((length + EDGE, ncols), bf16),
        shape_of((length + EDGE, ncols), bf16),
        shape_of((length + EDGE, wcols), bf16),
        shape_of((heads, 1, length), f32),
        shape_of((heads, 1, length), f32),
        shape_of((length, ncols), bf16),
        shape_of((length, ncols), bf16),
        shape_of((length, wcols), bf16),
        shape_of((heads, length, CHUNK), bf16),
        shape_of((heads, length, CHUNK), bf16),
        shape_of((heads, length, VALUE), bf16),
        shape_of((heads, length, KEY), bf16),
        shape_of((heads, states, KEY + VALUE), bf16),
        shape_of((heads, KEY, KEY + VALUE), f32),
    ]
    args = (
        x, edge, gain, w_query, w_key, w_value, w_decay, w_beta, rate, conv_query, conv_key, conv_value
    )
    return pl.pallas_call(
        prep_kernel,
        out_shape=out_shape,
        in_specs=[pl.BlockSpec(memory_space=pltpu.VMEM)] * len(args),
        out_specs=[pl.BlockSpec(memory_space=pltpu.VMEM)] * len(out_shape),
        scratch_shapes=[
            pltpu.VMEM((length + EDGE, wcols), f32),
            pltpu.VMEM((length + EDGE, ncols), f32),
        ],
        compiler_params=pltpu.CompilerParams(vmem_limit_bytes=VMEM_BYTES),
        cost_estimate=COST,
    )(*args)


def run_forward(qn, ld, att, u, w, starts, state_in, gate_pre, gain, w_out):
    length = qn.shape[0]
    heads = ld.shape[0]
    states = starts.shape[1]
    wide = tall(length, VALUE)
    wshape = (length, heads * VALUE)
    outputs = [
        (wide, shape_of(wshape, bf16)),
        (wide, shape_of(wshape, f32)),
        (deep(length, VALUE), shape_of((heads, length, VALUE), bf16)),
        (deep(states, VALUE), shape_of((heads, states, VALUE), bf16)),
        (shared(length, w_out.shape[1]), shape_of((length, w_out.shape[1]), bf16)),
    ]
    in_specs = [
        tall(length, KEY), deep(1, length), deep(length, CHUNK), deep(length, VALUE), deep(length, KEY),
        deep(states, KEY + VALUE), deep(KEY, VALUE), wide, shared(1, VALUE),
        pl.BlockSpec((VALUE, w_out.shape[1]), lambda h: (h, 0)),
    ]
    args = (qn, ld, att, u, w, starts, state_in, gate_pre, gain, w_out)
    scratch = [pltpu.VMEM((length, w_out.shape[1]), f32)]
    return call_heads(forward_kernel, heads, in_specs, outputs, scratch, args)


def gate_back(dgated, mixed, gate_pre, gain, qn, kn, ld, att, w):
    length = qn.shape[0]
    heads = ld.shape[0]
    states = (length // CHUNK) * KEY
    wide = tall(length, VALUE)
    outputs = [
        (wide, shape_of((length, heads * VALUE), bf16)),
        (deep(length, VALUE), shape_of((heads, length, VALUE), bf16)),
        (deep(length, VALUE), shape_of((heads, length, VALUE), bf16)),
        (deep(1, VALUE), shape_of((heads, 1, VALUE), f32)),
        (deep(states, KEY + VALUE), shape_of((heads, states, KEY + VALUE), bf16)),
        (deep(KEY, KEY + VALUE), shape_of((heads, KEY, KEY + VALUE), f32)),
    ]
    in_specs = [
        wide, wide, wide, shared(1, VALUE), tall(length, KEY), tall(length, KEY), deep(1, length),
        deep(length, CHUNK), deep(length, KEY),
    ]
    args = (dgated, mixed, gate_pre, gain, qn, kn, ld, att, w)
    return call_heads(gate_back_kernel, heads, in_specs, outputs, [], args)


def run_backward(
    gstate, after, dmixed, dcorr, begin, corr, inverse, att, u, w, qn, kn, vn,
    query_ext, key_ext, value_ext, conv_query, conv_key, conv_value, ld, beta,
):
    length = qn.shape[0]
    heads = ld.shape[0]
    states = after.shape[1]
    taps = conv_query.shape[0]
    narrow, wide = tall(length, KEY), tall(length, VALUE)
    ncols, wcols = heads * KEY, heads * VALUE
    outputs = [
        (tall(length + EDGE, KEY), shape_of((length + EDGE, ncols), bf16)),
        (tall(length + EDGE, KEY), shape_of((length + EDGE, ncols), bf16)),
        (tall(length + EDGE, VALUE), shape_of((length + EDGE, wcols), bf16)),
        (tall(taps, KEY), shape_of((taps, ncols), f32)),
        (tall(taps, KEY), shape_of((taps, ncols), f32)),
        (tall(taps, VALUE), shape_of((taps, wcols), f32)),
        (deep(1, length), shape_of((heads, 1, length), f32)),
        (deep(1, length), shape_of((heads, 1, length), f32)),
    ]
    in_specs = [
        deep(KEY, VALUE), deep(states, KEY + VALUE), deep(length, VALUE), deep(length, VALUE),
        deep(states, VALUE), deep(length, VALUE), deep(length, CHUNK), deep(length, CHUNK),
        deep(length, VALUE), deep(length, KEY),
        narrow, narrow, wide,
        tall(length + EDGE, KEY), tall(length + EDGE, KEY), tall(length + EDGE, VALUE),
        tall(taps, KEY), tall(taps, KEY), tall(taps, VALUE),
        deep(1, length), deep(1, length),
    ]
    scratch = [
        pltpu.VMEM((length, KEY), f32), pltpu.VMEM((length, KEY), f32), pltpu.VMEM((length, VALUE), f32),
        pltpu.VMEM((length + 2 * EDGE, KEY), f32), pltpu.VMEM((length + EDGE, KEY), f32),
        pltpu.VMEM((length + 2 * EDGE, VALUE), f32), pltpu.VMEM((length + EDGE, VALUE), f32),
    ]
    args = (
        gstate, after, dmixed, dcorr, begin, corr, inverse, att, u, w, qn, kn, vn,
        query_ext, key_ext, value_ext, conv_query, conv_key, conv_value, ld, beta,
    )
    return call_heads(backward_kernel, heads, in_specs, outputs, scratch, args, pl.CostEstimate(flops=0, bytes_accessed=40000000, transcendentals=0))


def ffn_kernel(
    x_ref, branch_ref, gain_ref, wg_ref, wu_ref, wd_ref, cot_ref,
    normed_ref, hidden_ref, dgate_ref, dup_ref, part_ref,
):
    middle = x_ref[...].astype(f32) + branch_ref[...].astype(f32)
    normed = row_norm(middle, gain_ref[...]).astype(bf16)
    normed_ref[...] = normed
    gate = dot(normed, wg_ref[...], 1, 1)
    up = dot(normed, wu_ref[...], 1, 1)
    sig = jax.nn.sigmoid(gate)
    act = gate * sig
    hidden_ref[...] = (act * up).astype(bf16)
    dhidden = dot(cot_ref[...], wd_ref[...], 1, 1)
    dgate = (dhidden * up * (sig * (1.0 + gate * (1.0 - sig)))).astype(bf16)
    dup = (dhidden * act).astype(bf16)
    dgate_ref[...] = dgate
    dup_ref[...] = dup
    part_ref[...] = (dot(dgate, wg_ref[...]) + dot(dup, wu_ref[...])).astype(bf16)


def run_ffn(x, branch, gain, w_ffn_gate, w_ffn_up, w_ffn_down, cotangent):
    length, width = x.shape
    hidden = w_ffn_gate.shape[0]
    block = length // 2

    def rows(cols):
        return pl.BlockSpec((block, cols), lambda i: (i, 0))

    return pl.pallas_call(
        ffn_kernel,
        grid=(length // block,),
        in_specs=[
            rows(width), rows(width), shared(1, width), shared(hidden, width), shared(hidden, width),
            shared(hidden, width), rows(width),
        ],
        out_specs=[rows(width), rows(hidden), rows(hidden), rows(hidden), rows(width)],
        out_shape=[
            shape_of((length, width), bf16),
            shape_of((length, hidden), bf16),
            shape_of((length, hidden), bf16),
            shape_of((length, hidden), bf16),
            shape_of((length, width), bf16),
        ],
        compiler_params=pltpu.CompilerParams(vmem_limit_bytes=VMEM_BYTES),
        cost_estimate=COST,
    )(x, branch, gain, w_ffn_gate, w_ffn_up, w_ffn_down, cotangent)


def shard_kernel(plan, count, piece, places_ref, *refs):
    outs = refs[-2 * len(plan) :]
    for number, pairs in enumerate(plan):
        for which in range(2):
            out_ref = outs[2 * number + which]
            chosen = {}
            at = 0
            for left, right in pairs:
                if left not in chosen:
                    chosen[left] = jnp.concatenate(
                        [
                            refs[left][:, pl.ds(pl.multiple_of(places_ref[number, which, g] * piece, 128), piece)]
                            for g in range(count)
                        ],
                        axis=1,
                    )
                width = refs[right].shape[1]
                out_ref[:, at : at + width] = dot(chosen[left], refs[right][...], 0, 0).astype(out_ref.dtype)
                at += width


def shard_products(chains, home_type):
    size = lax.axis_size("seq")
    here = lax.axis_index("seq")
    count = size // 2
    slots = jnp.arange(count, dtype=jnp.int32)
    places = []
    for bit, pairs in chains:
        shards = (slots // 2**bit) * 2 ** (bit + 1) + slots % 2**bit
        mine = (here // 2**bit) % 2
        places.append(jnp.stack([shards + (1 - mine) * 2**bit, shards + mine * 2**bit]))
    width = chains[0][1][0][0].shape[1]
    piece = width // size
    if piece % 128:
        results = []
        for (bit, pairs), chosen in zip(chains, places):
            parts = []
            for which, kind in ((0, bf16), (1, home_type)):
                columns = [
                    lax.dot_general(
                        jnp.take(left.reshape(-1, size, piece), chosen[which], axis=1).reshape(
                            left.shape[0], -1
                        ),
                        right,
                        (((0,), (0,)), ((), ())),
                        preferred_element_type=f32,
                    )
                    for left, right in pairs
                ]
                parts.append(jnp.concatenate(columns, axis=1).astype(kind))
            results.append(tuple(parts))
        return results
    args, plan, out_shape = [], [], []

    def slot_of(array):
        for number, known in enumerate(args):
            if known is array:
                return number
        args.append(array)
        return len(args) - 1

    for bit, pairs in chains:
        plan.append([(slot_of(left), slot_of(right)) for left, right in pairs])
        total = sum(right.shape[1] for left, right in pairs)
        out_shape += [shape_of((count * piece, total), bf16), shape_of((count * piece, total), home_type)]
    whole = pl.BlockSpec(memory_space=pltpu.VMEM)
    flat = pl.pallas_call(
        functools.partial(shard_kernel, plan, count, piece),
        in_specs=[pl.BlockSpec(memory_space=pltpu.SMEM)] + [whole] * len(args),
        out_specs=[whole] * len(out_shape),
        out_shape=out_shape,
        compiler_params=pltpu.CompilerParams(vmem_limit_bytes=VMEM_BYTES),
        cost_estimate=COST,
    )(jnp.stack(places), *args)
    return [(flat[2 * number], flat[2 * number + 1]) for number in range(len(chains))]


def turn_kernel(cuts, *refs):
    ins, outs = refs[: len(cuts)], refs[len(cuts) :]
    for (low, high), in_ref, out_ref in zip(cuts, ins, outs):
        out_ref[...] = in_ref[:, low:high].T


def turned(pieces):
    if pieces[0][0].shape[0] % 128:
        return [array[:, low:high].T for array, low, high in pieces]
    whole = pl.BlockSpec(memory_space=pltpu.VMEM)
    return pl.pallas_call(
        functools.partial(turn_kernel, [(low, high) for array, low, high in pieces]),
        in_specs=[whole] * len(pieces),
        out_specs=[whole] * len(pieces),
        out_shape=[shape_of((high - low, array.shape[0]), f32) for array, low, high in pieces],
        compiler_params=pltpu.CompilerParams(vmem_limit_bytes=VMEM_BYTES),
        cost_estimate=COST,
    )(*[array for array, low, high in pieces])


def from_behind(block, axis, distance):
    devices = range(lax.axis_size(axis))
    route = [(i - distance, i) for i in devices if i - distance in devices]
    return lax.ppermute(block, axis, route)


def swap_with(block, axis, distance):
    route = [(i, i ^ distance) for i in range(lax.axis_size(axis))]
    return lax.ppermute(block, axis, route)


def exchange_rounds(tasks, box=None, beside=None):
    results, asked = [None] * len(tasks), {}

    def advance(which, got):
        try:
            asked[which] = tasks[which].send(got)
        except StopIteration as end:
            results[which] = end.value
            asked.pop(which, None)

    for which in range(len(tasks)):
        advance(which, None)
    number = 0
    while asked:
        number += 1
        got = {which: tuple(exchange() for exchange in wanted) for which, wanted in asked.items()}
        names = [name for name in (beside or {}).get(number, ()) if name in box]
        got, values = lax.optimization_barrier((got, [box[name] for name in names]))
        for name, value in zip(names, values):
            box[name] = value
        for which in list(asked):
            advance(which, got[which])
    return results


def swap(block, axis, distance):
    return functools.partial(swap_with, block, axis, distance)


def together(first, second):
    wanted = [next(first), next(second)]
    while True:
        blocks = [part[0].args[0] for part in wanted if part]
        cut = len(wanted[0])
        if len(blocks) == 3 and wanted[0][0].args[1:] == wanted[1][0].args[1:]:
            width = blocks[0].shape[-1]
            (both,) = yield [swap(jnp.concatenate(blocks, axis=-1), *wanted[0][0].args[1:])]
            got = (both[..., :width], both[..., width:])
        else:
            got = yield wanted[0] + wanted[1]
        results = []
        for which, (task, part) in enumerate(((first, got[:cut]), (second, got[cut:]))):
            try:
                wanted[which] = task.send(part)
            except StopIteration as end:
                results.append(end.value)
        if results:
            return results


def pause(rounds):
    for _ in range(rounds):
        yield []


def group_sum(block, axis):
    size = lax.axis_size(axis)
    distance = 1
    while distance < size:
        reach = min(4, size // distance)
        arrived = yield [swap(block, axis, distance * step) for step in range(1, reach)]
        if reach == 4:
            block = (block + arrived[0]) + (arrived[1] + arrived[2])
        else:
            block = block + arrived[0]
        distance *= reach
    return block


def sum_over_heads(partial):
    rows = partial.shape[0] // 2
    odd = lax.axis_index("head") % 2 == 1
    low, high = partial[:rows], partial[rows:]
    own = jnp.where(odd, high, low).astype(f32)
    (got,) = yield [swap(jnp.where(odd, low, high), "head", 1)]
    own = own + got.astype(f32)
    distance = 2
    while distance < lax.axis_size("head"):
        sent = own.astype(bf16)
        (got,) = yield [swap(sent, "head", distance)]
        own = sent.astype(f32) + got.astype(f32)
        distance *= 2
    kept = own.astype(bf16)
    (other,) = yield [swap(kept, "head", 1)]
    return jnp.concatenate([jnp.where(odd, other, kept), jnp.where(odd, kept, other)], axis=0)


def exclusive_scan(joined, sign):
    own_t, own_b = joined[..., :KEY], joined[..., KEY:]
    send = joined
    before_t = before_b = None
    distance = 1
    size = lax.axis_size("seq")

    def product(a, b):
        return jnp.einsum("hij,hjk->hik", a, b, precision=lax.Precision.HIGH)

    while distance < size:
        last = distance * 2 >= size
        sent = (send[..., KEY:] if last else send).astype(bf16)
        (got,) = yield [functools.partial(from_behind, sent, "seq", sign * distance)]
        got = got.astype(f32)
        if before_t is None:
            before_t, before_b = got[..., :KEY], got[..., KEY:]
        else:
            moved = product(before_t, got)
            if last:
                before_b = before_b + moved
            else:
                before_t, before_b = moved[..., :KEY], before_b + moved[..., KEY:]
        if not last:
            send = product(own_t, jnp.concatenate([before_t, before_b], axis=-1))
            send = jnp.concatenate([send[..., :KEY], send[..., KEY:] + own_b], axis=-1)
        distance *= 2
    return before_b


def halving_scatter(products, order, pauses=(), box=None, name=None, hold=None):
    size = lax.axis_size("seq")
    bits = size.bit_length() - 1
    here = lax.axis_index("seq")
    order = [bit for bit in order if bit < bits] + list(range(len(order), bits))
    pauses = list(pauses) + [0] * bits
    away, home = products
    (got,) = yield [swap(away, "seq", 2 ** order[0])]
    held = home.astype(f32) + got.astype(f32)
    axes = [bit for bit in range(bits)[::-1] if bit != order[0]]
    held = held.reshape((2,) * (bits - 1) + (held.shape[0] // 2 ** (bits - 1), held.shape[1]))
    for number, bit in enumerate(order[1:]):
        axis = axes.index(bit)
        axes.remove(bit)
        mine = (here // 2**bit) % 2
        sent = lax.dynamic_index_in_dim(held, 1 - mine, axis, keepdims=False).astype(bf16)
        if pauses[number]:
            box[name] = sent
            yield from pause(pauses[number])
            sent = box[name]
        elif hold is not None:
            sent = hold(sent)
        elif hold is not None:
            sent = hold(sent)
        (got,) = yield [swap(sent, "seq", 2**bit)]
        held = lax.dynamic_index_in_dim(held, mine, axis, keepdims=False) + got.astype(f32)
    return held


def inner_rows(first_operand, second_operand):
    return lax.dot_general(
        first_operand, second_operand, (((0,), (0,)), ((), ())), preferred_element_type=f32
    )


def matmul_bf(first_operand, second_operand):
    return jnp.dot(first_operand, second_operand, preferred_element_type=f32)


def against_rows(first_operand, second_operand):
    return lax.dot_general(
        first_operand, second_operand, (((1,), (1,)), ((), ())), preferred_element_type=f32
    )


def per_device(
    block_input,
    norm1_gain,
    w_query,
    w_key,
    w_value,
    w_gate,
    w_decay,
    w_beta,
    conv_query,
    conv_key,
    conv_value,
    decay_rate,
    out_gain,
    w_out,
    norm2_gain,
    w_ffn_gate,
    w_ffn_up,
    w_ffn_down,
    cotangent,
):
    length = block_input.shape[0]
    head_count = w_decay.shape[1]
    key_cols = w_query.shape[1]
    value_cols = w_value.shape[1]
    ff_cols = w_ffn_gate.shape[1]
    edge_input = from_behind(block_input[length - EDGE :], "seq", 1)
    gain1 = norm1_gain.astype(f32)
    (
        normed, normed_ext, decay_cols, query_ext, key_ext, value_ext, log_decay, beta3,
        qn, kn, vn, inverse, att, u, w, starts, composite,
    ) = prepare(
        block_input, edge_input, gain1[None], w_query, w_key, w_value, w_decay.T, w_beta.T,
        decay_rate[None], conv_query, conv_key, conv_value,
    )
    inputs32 = block_input.astype(f32)
    gate_pre = matmul_bf(normed, w_gate)
    box = {"gate": gate_pre}
    (state_in,) = exchange_rounds([exclusive_scan(composite, 1)], box, {1: ["gate"]})
    gate_pre = box["gate"]
    gain_row = out_gain.astype(f32)[None]
    gated, mixed, corr, begin, branch_part = run_forward(
        qn, log_decay, att, u, w, starts, state_in, gate_pre, gain_row, w_out
    )
    (branch,) = exchange_rounds([sum_over_heads(branch_part)])
    gain2 = norm2_gain.astype(f32)
    normed2, hidden, grad_fgate, grad_fup, grad_part = run_ffn(
        block_input, branch, gain2[None], w_ffn_gate.T, w_ffn_up.T, w_ffn_down, cotangent
    )
    bits = lax.axis_size("seq").bit_length() - 1
    near, far = 0, min(1, bits - 1)
    half = ff_cols // 2 // 128 * 128
    ffn_near, ffn_far = shard_products(
        [
            (near, [(normed2, grad_fgate), (cotangent, hidden[:, :half])]),
            (far, [(normed2, grad_fup), (cotangent, hidden[:, half:])]),
        ],
        bf16,
    )
    box = {}

    def after_scan(sent):
        return lax.optimization_barrier((sent, box["state"]))[0]

    ffn_tasks = [
        halving_scatter(ffn_near, [0, 1], [bits - 2, 0], box, "sent near", after_scan),
        halving_scatter(ffn_far, [1, 0], [bits - 2, 0], box, "sent far", after_scan),
    ]
    ffn_pair = together(*ffn_tasks)
    ffn_got = tuple(exchange() for exchange in next(ffn_pair))
    box["away"] = (ffn_near[0], ffn_far[0])
    (grad_normed2,) = exchange_rounds([sum_over_heads(grad_part)], box, {2: ["away"]})
    grad_normed2 = grad_normed2.astype(f32)
    middle = inputs32 + branch.astype(f32)
    norm2_back = jax.vjp(row_norm, middle, gain2)[1]
    ffn_part = matmul_bf(hidden, w_ffn_down).astype(bf16)
    grad_middle_n, grad_gain2 = norm2_back(grad_normed2)
    grad_middle = cotangent.astype(f32) + grad_middle_n
    grad_branch = grad_middle.astype(bf16)
    grad_gated = against_rows(grad_branch, w_out)
    grad_gp, grad_mixed, grad_corr, grad_outgain, after, composite_back = gate_back(
        grad_gated, mixed, gate_pre, gain_row, qn, kn, log_decay, att, w
    )
    box["ffn part"] = ffn_part
    pad_rows = ((length - 8, 0), (0, 0))
    taps_count = conv_query.shape[0]
    width = w_query.shape[0]

    def given(blocks):
        return [lambda block=block: block for block in blocks]

    def main_task():
        grad_state = yield from exclusive_scan(composite_back, -1)
        box["state"] = grad_state
        dq, dk, dv, taps_q, taps_k, taps_v, grad_log, grad_beta = run_backward(
            grad_state, after, grad_mixed, grad_corr, begin, corr, inverse, att, u, w,
            qn, kn, vn, query_ext, key_ext, value_ext,
            conv_query, conv_key, conv_value, log_decay, beta3,
        )
        box["late"] = shard_products(
            [(near, [(normed_ext, dq), (normed_ext, dk)]), (far, [(normed_ext, dv)])], f32
        )
        part_ext = against_rows(dq, w_query) + against_rows(dk, w_key) + against_rows(dv, w_value)
        decay_pre = decay_cols.T
        soft = jax.nn.softplus(decay_pre)
        rate = decay_rate[:, None]
        beta_gate = beta3.reshape(head_count, length)
        grad_log = grad_log.reshape(head_count, length)
        grad_beta = grad_beta.reshape(head_count, length)
        grad_dp = (-rate * jax.nn.sigmoid(decay_pre) * grad_log).astype(bf16)
        grad_bp = (beta_gate * (1.0 - beta_gate) * grad_beta).astype(bf16)
        grad_rate = -jnp.sum(grad_log * soft, axis=1)
        grad_scalars = jnp.concatenate([grad_dp, grad_bp], axis=0)
        w_scalars = jnp.concatenate([w_decay, w_beta], axis=1)
        box["small"] = jnp.concatenate(
            [
                jnp.concatenate([taps_q, taps_k, taps_v], axis=1),
                grad_gain2[None],
                jnp.pad(grad_rate, (0, width - head_count))[None],
                matmul_bf(grad_scalars, normed),
            ],
            axis=0,
        )
        edges = part_ext[EDGE - 8 : EDGE]
        (edges,) = yield [functools.partial(from_behind, edges, "seq", -1)]
        part = (
            part_ext[EDGE:]
            + against_rows(grad_gp, w_gate)
            + lax.dot_general(
                grad_scalars, w_scalars, (((0,), (1,)), ((), ())), preferred_element_type=f32
            )
            + jnp.pad(edges, pad_rows)
        )
        box["shared"] = jnp.concatenate(
            [jnp.sum(part * row_norm(inputs32, 1.0), axis=0), jnp.sum(grad_outgain, axis=(0, 1))]
        )
        return (yield from sum_over_heads(part.astype(bf16)))

    def ffn_rest(task, got):
        wanted = given(got)
        try:
            while True:
                wanted = task.send((yield wanted))
        except StopIteration as end:
            held = end.value
        for name, part in zip(("near", "far"), held):
            box[name] = turned([(part, 0, ff_cols), (part, ff_cols, part.shape[1])])

    def ffn_sum_task():
        yield from pause(1)
        steps = sum_over_heads(box["ffn part"])
        got = yield next(steps)
        wanted = steps.send(got)
        yield from pause(bits - 2)
        try:
            while True:
                wanted = steps.send((yield wanted))
        except StopIteration as end:
            box["out"] = (middle + end.value.astype(f32)).astype(bf16)

    def mid_task():
        yield from pause(bits)
        products = shard_products([(near, [(grad_branch, gated)]), (far, [(normed, grad_gp)])], f32)
        products = after_scan(products)
        first, second = halving_scatter(products[0], [0, 1]), halving_scatter(products[1], [1, 0])
        mid = together(first, second)
        wanted = next(mid)
        try:
            wanted = mid.send((yield wanted))
            wanted = mid.send((yield wanted))
            yield from pause(1)
            while True:
                wanted = mid.send((yield wanted))
        except StopIteration as end:
            grad_wout, grad_wg = end.value
        box["mid"] = (*turned([(grad_wout, 0, grad_wout.shape[1])]), grad_wg)

    def late_task():
        yield from pause(bits)
        first, second = box["late"]
        return (yield from together(halving_scatter(first, [0, 1]), halving_scatter(second, [1, 0])))

    def small_task():
        yield from pause(bits + 1)
        box["small"] = yield from group_sum(box["small"], "seq")

    def shared_task():
        yield from pause(bits + 1)
        shared = yield from group_sum(box["shared"], "head")
        return (yield from group_sum(shared.reshape(-1, 128), "seq")).reshape(-1)

    grad_normed, late, shared_sum = exchange_rounds(
        [main_task(), late_task(), shared_task(), small_task(), mid_task(), ffn_sum_task()]
        + [ffn_rest(ffn_pair, ffn_got)],
        box,
        {1: ["ffn part"], 2: ["sent near", "sent far"], bits + 2: ["near", "far"], bits + 3: ["out"]},
    )[:3]
    late_qk, late_v = late
    small = box["small"]
    grad_wout, grad_wg = box["mid"]
    grad_wfg, down_near = box["near"]
    grad_wfu, down_far = box["far"]
    layer_out = box["out"]
    norm1_back = jax.vjp(row_norm, inputs32, gain1)[1]
    grad_input = grad_middle + norm1_back(grad_normed.astype(f32))[0]
    taps_sum = small[:taps_count]
    gain2_sum = small[taps_count]
    rate_sum = small[taps_count + 1, :head_count]
    scalars_sum = small[taps_count + 2 : taps_count + 2 + 2 * head_count]
    gain1_sum, outgain_sum = shared_sum[:width], shared_sum[width:]

    def own_part(vec):
        piece = vec.shape[-1] // lax.axis_size("seq")
        return lax.dynamic_slice_in_dim(vec, lax.axis_index("seq") * piece, piece, axis=-1)

    scalars_sum = own_part(scalars_sum).T
    return (
        layer_out,
        grad_input,
        own_part(gain1_sum),
        late_qk[:, :key_cols],
        late_qk[:, key_cols:],
        late_v,
        grad_wg,
        scalars_sum[:, :head_count],
        scalars_sum[:, head_count:],
        taps_sum[:, :key_cols],
        taps_sum[:, key_cols : 2 * key_cols],
        taps_sum[:, 2 * key_cols :],
        rate_sum,
        own_part(outgain_sum),
        grad_wout,
        own_part(gain2_sum),
        grad_wfg.T,
        grad_wfu.T,
        jnp.concatenate([down_near, down_far], axis=0),
    )


def solution(mesh):
    return jax.shard_map(
        per_device,
        mesh=mesh,
        in_specs=(
            P("seq", None),
            P(),
            P(None, "head"),
            P(None, "head"),
            P(None, "head"),
            P(None, "head"),
            P(None, "head"),
            P(None, "head"),
            P(None, "head"),
            P(None, "head"),
            P(None, "head"),
            P("head"),
            P(),
            P("head", None),
            P(),
            P(None, "head"),
            P(None, "head"),
            P("head", None),
            P("seq", None),
        ),
        out_specs=(
            P("seq", None),
            P("seq", None),
            P("seq"),
            P("seq", "head"),
            P("seq", "head"),
            P("seq", "head"),
            P("seq", "head"),
            P("seq", "head"),
            P("seq", "head"),
            P(None, "head"),
            P(None, "head"),
            P(None, "head"),
            P("head"),
            P("seq"),
            P("head", "seq"),
            P("seq"),
            P("seq", "head"),
            P("seq", "head"),
            P("head", "seq"),
        ),
        check_vma=False,
    )
```

```python
import functools

import jax
import jax.numpy as jnp
from jax import lax
from jax.experimental import pallas as pl
from jax.experimental.pallas import tpu as pltpu
from jax.sharding import PartitionSpec as P

KEY = 128
VALUE = 256
CHUNK = 128
EDGE = 16
SUB = 16
VMEM_BYTES = 32 * 1024 * 1024
VMEM_LARGE = 60 * 1024 * 1024
COST = pl.CostEstimate(flops=0, bytes_accessed=0, transcendentals=0)

epsilon = 1e-06
f32 = jnp.float32
bf16 = jnp.bfloat16
highest_precision = lax.Precision.HIGHEST


def dot(first, second, over_first=1, over_second=0):
    return lax.dot_general(
        first.astype(bf16),
        second.astype(bf16),
        (((over_first,), (over_second,)), ((), ())),
        preferred_element_type=f32,
    )


def halves(values):
    high = values.astype(bf16)
    return high, (values - high.astype(f32)).astype(bf16)


def dot_fine(first, second):
    first_high, first_low = halves(first)
    second_high, second_low = halves(second)
    width = second.shape[1]
    wide = dot(first_high, jnp.concatenate([second_high, second_low], axis=1))
    return wide[:, :width] + wide[:, width:] + dot(first_low, second_high)


def grid_places(extent):
    rows = lax.broadcasted_iota(jnp.int32, (extent, extent), 0)
    cols = lax.broadcasted_iota(jnp.int32, (extent, extent), 1)
    return rows, cols


def as_row(column, diagonal):
    return jnp.sum(jnp.where(diagonal, column, 0.0), axis=0, keepdims=True)


def as_column(row, diagonal):
    return jnp.sum(jnp.where(diagonal, row, 0.0), axis=1, keepdims=True)


def unit_lower_inverses(systems, rows, cols):
    extent = systems[0].shape[0]
    count = extent // SUB
    units = len(systems)
    same = rows // SUB == cols // SUB
    packed = jnp.concatenate(
        [jnp.sum(jnp.where(same, s, 0.0).reshape(count, SUB, extent), axis=0) for s in systems], axis=0
    )
    stacked = jnp.concatenate(halves(packed), axis=0)
    shape = (units, SUB, extent)
    places = lax.broadcasted_iota(jnp.int32, shape, 1)
    solved = (places == lax.broadcasted_iota(jnp.int32, shape, 2) % SUB).astype(f32)
    for j in range(SUB - 1):
        spread = dot(stacked, (same & (rows % SUB == j)).astype(f32))
        column = spread[: units * SUB] + spread[units * SUB :]
        solved = solved - column.reshape(shape) * solved[:, j : j + 1, :]
    inverses = [
        jnp.where(same, jnp.concatenate([solved[n]] * count, axis=0), 0.0) for n in range(units)
    ]
    size = SUB
    while size < extent:
        below = (rows // (2 * size) == cols // (2 * size)) & (rows // size > cols // size)
        joined = [
            dot_fine(inverse, jnp.where(below, s, 0.0)) for inverse, s in zip(inverses, systems)
        ]
        joined = [dot_fine(product, inverse) for product, inverse in zip(joined, inverses)]
        inverses = [inverse - product for inverse, product in zip(inverses, joined)]
        size *= 2
    return inverses


def decay_terms(ld_row, rows, cols):
    cum_col = jnp.sum(jnp.where(rows >= cols, ld_row, 0.0), axis=1, keepdims=True)
    cum_row = as_row(cum_col, rows == cols)
    last = cum_col[CHUNK - 1 :, :]
    between = jnp.where(rows >= cols, jnp.exp(jnp.where(rows >= cols, cum_col - cum_row, 0.0)), 0.0)
    return between, jnp.exp(cum_col), jnp.exp(last - cum_col), jnp.exp(last)


def conv_sum(padded_ref, taps_ref, length):
    taps = taps_ref[...].astype(f32)
    summed = taps[0:1] * padded_ref[EDGE : EDGE + length, :]
    for offset in range(1, taps_ref.shape[0]):
        summed = summed + taps[offset : offset + 1] * padded_ref[EDGE - offset : EDGE - offset + length, :]
    return summed


def unit_rows(values, scale, heads):
    parts = []
    for h in range(heads):
        part = values[:, h * KEY : (h + 1) * KEY]
        parts.append(
            part * (lax.rsqrt(jnp.sum(part * part, axis=-1, keepdims=True) + epsilon) * scale)
        )
    return jnp.concatenate(parts, axis=1)


def row_norm(values, gain_vec):
    return (
        values * lax.rsqrt(jnp.mean(values * values, axis=-1, keepdims=True) + epsilon) * gain_vec
    )


def prep_kernel(
    x_ref, edge_ref, gain_ref, wq_ref, wk_ref, wv_ref, wd_ref, wb_ref, rate_ref, tq_ref, tk_ref, tv_ref,
    normed_ref, normed_ext_ref, decay_ref, q_ref, k_ref, v_ref, ld_ref, beta_ref,
    qn_ref, kn_ref, vn_ref, inv_ref, att_ref, u_ref, w_ref, start_ref, final_ref,
    wide_scr, narrow_scr,
):
    length = qn_ref.shape[0]
    heads = ld_ref.shape[0]
    chunks = length // CHUNK
    gain = gain_ref[...]
    normed_ext_ref[:EDGE, :] = row_norm(edge_ref[...].astype(f32), gain).astype(bf16)
    normed = row_norm(x_ref[...].astype(f32), gain).astype(bf16)
    normed_ext_ref[EDGE:, :] = normed
    normed_ref[...] = normed
    decay_pre = dot(normed, wd_ref[...], 1, 1)
    decay_ref[...] = decay_pre
    softplus = jnp.maximum(decay_pre, 0.0) + jnp.log1p(jnp.exp(-jnp.abs(decay_pre)))
    log_decay = -rate_ref[...] * softplus
    beta_gate = jax.nn.sigmoid(dot(normed, wb_ref[...], 1, 1))
    pre = dot(normed_ext_ref[...], wk_ref[...]).astype(bf16)
    k_ref[...] = pre
    narrow_scr[...] = pre.astype(f32)
    z = conv_sum(narrow_scr, tk_ref, length)
    kn_ref[...] = unit_rows(z * jax.nn.sigmoid(z), 1.0, heads).astype(bf16)
    pre = dot(normed_ext_ref[...], wq_ref[...]).astype(bf16)
    q_ref[...] = pre
    narrow_scr[...] = pre.astype(f32)
    z = conv_sum(narrow_scr, tq_ref, length)
    qn_ref[...] = unit_rows(z * jax.nn.sigmoid(z), KEY ** (-0.5), heads).astype(bf16)
    pre = dot(normed_ext_ref[...], wv_ref[...]).astype(bf16)
    v_ref[...] = pre
    wide_scr[...] = pre.astype(f32)
    z = conv_sum(wide_scr, tv_ref, length)
    vn_ref[...] = (z * jax.nn.sigmoid(z)).astype(bf16)

    rows, cols = grid_places(CHUNK)
    diagonal = rows == cols
    units = [(h, c) for c in range(chunks) for h in range(heads)]
    systems, vectors = [], []
    for h, c in units:
        at = slice(c * CHUNK, (c + 1) * CHUNK)
        keyed = slice(h * KEY, (h + 1) * KEY)
        ld_row = as_row(log_decay[at, h : h + 1], diagonal)
        ld_ref[h, :, at] = ld_row
        between, grow, tail, whole = decay_terms(ld_row, rows, cols)
        beta = beta_gate[at, h : h + 1]
        beta_ref[h, :, at] = as_row(beta, diagonal)
        keys = kn_ref[at, keyed]
        products = dot(jnp.concatenate([keys, qn_ref[at, keyed]], axis=0), keys, 1, 1)
        systems.append(jnp.where(rows > cols, beta * between * products[:CHUNK], 0.0))
        att_ref[h, at, :] = (products[CHUNK:] * between).astype(bf16)
        vectors.append((beta, grow, tail, whole))
    inverses = unit_lower_inverses(systems, rows, cols)
    kept = []
    for (h, c), inverse, (beta, grow, tail, whole) in zip(units, inverses, vectors):
        at = slice(c * CHUNK, (c + 1) * CHUNK)
        keys32 = kn_ref[at, h * KEY : (h + 1) * KEY].astype(f32)
        values32 = vn_ref[at, h * VALUE : (h + 1) * VALUE].astype(f32)
        inv_ref[h, at, :] = inverse.astype(bf16)
        solved = dot(inverse, jnp.concatenate([(beta * grow) * keys32, beta * values32], axis=1))
        w_ref[h, at, :] = solved[:, :KEY].astype(bf16)
        u_ref[h, at, :] = solved[:, KEY:].astype(bf16)
        kept.append((tail * keys32).astype(bf16))
    begin = jnp.concatenate([diagonal.astype(f32), jnp.zeros((KEY, VALUE), f32)], axis=1)
    states = [begin] * heads
    for (h, c), tail_keys, (beta, grow, tail, whole) in zip(units, kept, vectors):
        at = slice(c * CHUNK, (c + 1) * CHUNK)
        state = states[h]
        start_ref[h, c * KEY : (c + 1) * KEY, :] = state.astype(bf16)
        source = jnp.concatenate([jnp.zeros((CHUNK, KEY), f32), u_ref[h, at, :].astype(f32)], axis=1)
        corrected = source - dot(w_ref[h, at, :], state)
        states[h] = whole * state + dot(tail_keys, corrected, 0, 0)
    for h in range(heads):
        final_ref[h, :, :] = states[h]


def forward_kernel(
    qn_ref, ld_ref, att_ref, u_ref, w_ref, start_ref, state_ref, gate_ref, gain_ref, wout_ref,
    gated_ref, mixed_ref, corr_ref, begin_ref, branch_ref, sum_scr,
):
    length = qn_ref.shape[0]
    rows, cols = grid_places(CHUNK)
    entering = state_ref[0]
    gain = gain_ref[...]
    for c in range(length // CHUNK):
        at = slice(c * CHUNK, (c + 1) * CHUNK)
        places = slice(c * KEY, (c + 1) * KEY)
        between, grow, tail, whole = decay_terms(ld_ref[0, :, at], rows, cols)
        begin = start_ref[0, places, KEY:].astype(f32) + dot(start_ref[0, places, :KEY], entering)
        begin_ref[0, places, :] = begin.astype(bf16)
        corrected = u_ref[0, at, :].astype(f32) - dot(w_ref[0, at, :], begin)
        corr_ref[0, at, :] = corrected.astype(bf16)
        mixed = dot(grow * qn_ref[at, :].astype(f32), begin) + dot(att_ref[0, at, :], corrected)
        mixed_ref[at, :] = mixed
        root = lax.rsqrt(jnp.mean(mixed * mixed, axis=-1, keepdims=True) + epsilon)
        gate = gate_ref[at, :]
        gated_ref[at, :] = (mixed * root * gain * (gate * jax.nn.sigmoid(gate))).astype(bf16)
    part = dot(gated_ref[...], wout_ref[...])

    @pl.when(pl.program_id(0) == 0)
    def start_sum():
        sum_scr[...] = part

    @pl.when(pl.program_id(0) > 0)
    def add_sum():
        sum_scr[...] += part

    @pl.when(pl.program_id(0) == pl.num_programs(0) - 1)
    def give_sum():
        branch_ref[...] = sum_scr[...].astype(bf16)


def gate_back_kernel(
    dgated_ref, mixed_ref, gate_ref, gain_ref, qn_ref, kn_ref, ld_ref, att_ref, w_ref,
    dgate_ref, dmixed_ref, dcorr_ref, dgain_ref, after_ref, final_ref,
):
    length = qn_ref.shape[0]
    rows, cols = grid_places(CHUNK)
    gain = gain_ref[...]
    kept = []
    dgain = jnp.zeros((1, VALUE), f32)
    for c in range(length // CHUNK):
        at = slice(c * CHUNK, (c + 1) * CHUNK)
        mixed, gate, dgated = mixed_ref[at, :], gate_ref[at, :], dgated_ref[at, :]
        root = lax.rsqrt(jnp.mean(mixed * mixed, axis=-1, keepdims=True) + epsilon)
        normal = mixed * root
        sig = jax.nn.sigmoid(gate)
        act = gate * sig
        dgain = dgain + jnp.sum(dgated * normal * act, axis=0, keepdims=True)
        dgate_ref[at, :] = (dgated * normal * gain * (sig * (1.0 + gate * (1.0 - sig)))).astype(bf16)
        dnormal = dgated * act * gain
        dmixed = root * (dnormal - normal * jnp.mean(dnormal * normal, axis=-1, keepdims=True))
        dmixed_ref[0, at, :] = dmixed.astype(bf16)
        between, grow, tail, whole = decay_terms(ld_ref[0, :, at], rows, cols)
        dcorr = dot(att_ref[0, at, :], dmixed, 0, 0)
        dcorr_ref[0, at, :] = dcorr.astype(bf16)
        gradient = dot(grow * qn_ref[at, :].astype(f32), dmixed, 0, 0) - dot(w_ref[0, at, :], dcorr, 0, 0)
        kept.append((gradient, (tail * kn_ref[at, :].astype(f32)).astype(bf16), whole))
    dgain_ref[0, :, :] = dgain
    pending = jnp.concatenate([(rows == cols).astype(f32), jnp.zeros((KEY, VALUE), f32)], axis=1)
    for c in reversed(range(length // CHUNK)):
        gradient, tail_keys, whole = kept[c]
        at = slice(c * CHUNK, (c + 1) * CHUNK)
        after_ref[0, c * KEY : (c + 1) * KEY, :] = pending.astype(bf16)
        source = jnp.concatenate([jnp.zeros((KEY, KEY), f32), gradient], axis=1)
        pending = whole * pending + source - dot(w_ref[0, at, :], dot(tail_keys, pending), 0, 0)
    final_ref[0, :, :] = pending


def silu_slope(z):
    sig = jax.nn.sigmoid(z)
    return z * sig, sig * (1.0 + z * (1.0 - sig))


def conv_back(dz, taps_ref, dz_scr, pre_scr, dpre_ref, dtaps_ref):
    length = dz.shape[0]
    reach = taps_ref.shape[0] - 1
    taps = taps_ref[...].astype(f32)
    dz_scr[EDGE : EDGE + length, :] = dz
    total = taps[0:1] * dz
    sums = [jnp.sum(dz * pre_scr[EDGE : EDGE + length, :], axis=0, keepdims=True)]
    for offset in range(1, reach + 1):
        total = total + taps[offset : offset + 1] * dz_scr[EDGE + offset : EDGE + offset + length, :]
        sums.append(
            jnp.sum(dz * pre_scr[EDGE - offset : EDGE - offset + length, :], axis=0, keepdims=True)
        )
    dpre_ref[EDGE:, :] = total.astype(bf16)
    edge = taps[1:2] * dz_scr[EDGE - 7 : EDGE + 1, :]
    for offset in range(2, reach + 1):
        edge = edge + taps[offset : offset + 1] * dz_scr[EDGE - 8 + offset : EDGE + offset, :]
    dpre_ref[:EDGE, :] = jnp.concatenate([jnp.zeros_like(edge), edge], axis=0).astype(bf16)
    dtaps_ref[...] = jnp.concatenate(sums, axis=0)


def backward_kernel(
    gstate_ref, after_ref, dmixed_ref, dcorr_ref, begin_ref, corr_ref, inv_ref, att_ref, u_ref, w_ref,
    qn_ref, kn_ref, vn_ref, q_ref, k_ref, v_ref, tq_ref, tk_ref, tv_ref,
    ld_ref, beta_ref,
    dq_ref, dk_ref, dv_ref, dtq_ref, dtk_ref, dtv_ref, dld_ref, dbeta_ref,
    dqn_scr, dkn_scr, dvn_scr, dn_scr, pn_scr, dw_scr, pw_scr,
):
    length = qn_ref.shape[0]
    rows, cols = grid_places(CHUNK)
    diagonal = rows == cols
    leaving = gstate_ref[0]
    for c in range(length // CHUNK):
        at = slice(c * CHUNK, (c + 1) * CHUNK)
        places = slice(c * KEY, (c + 1) * KEY)
        between, grow, tail, whole = decay_terms(ld_ref[0, :, at], rows, cols)
        beta = as_column(beta_ref[0, :, at], diagonal)
        keys, queries = kn_ref[at, :], qn_ref[at, :]
        keys32, queries32, values32 = keys.astype(f32), queries.astype(f32), vn_ref[at, :].astype(f32)
        dstate = after_ref[0, places, KEY:].astype(f32) + dot(after_ref[0, places, :KEY], leaving)
        dmixed, corrected, begin = dmixed_ref[0, at, :], corr_ref[0, at, :], begin_ref[0, places, :]
        dcorr = dcorr_ref[0, at, :].astype(f32) + dot(tail * keys32, dstate)
        datt = dot(dmixed, corrected, 1, 1)
        from_begin = dot(jnp.concatenate([dmixed, dcorr.astype(bf16)], axis=0), begin, 1, 1)
        dgrown, dw = from_begin[:CHUNK], -from_begin[CHUNK:]
        dtail_keys = dot(corrected, dstate, 1, 1)
        dwhole = jnp.sum(dstate * begin.astype(f32))
        back = dot(inv_ref[0, at, :], jnp.concatenate([dw, dcorr], axis=1), 0, 0)
        dright_keys, dright_values = back[:, :KEY], back[:, KEY:]
        dsystem = -dot(
            back, jnp.concatenate([w_ref[0, at, :], u_ref[0, at, :]], axis=1), 1, 1
        )
        products = dot(jnp.concatenate([keys, queries], axis=0), keys, 1, 1)
        decayed = jnp.where(rows > cols, between * products[:CHUNK], 0.0)
        dsys_decayed = dsystem * decayed
        dbeta = jnp.sum(dsys_decayed, axis=1, keepdims=True)
        pairs = beta * dsys_decayed + datt * (between * products[CHUNK:])
        dkk = jnp.where(rows > cols, dsystem * (beta * between), 0.0)
        dqk = datt * between
        dqk16, dkk16 = dqk.astype(bf16), dkk.astype(bf16)
        dqn_scr[at, :] = dot(dqk16, keys) + grow * dgrown
        dkn_scr[at, :] = (
            dot(jnp.concatenate([dqk16, dkk16], axis=0), jnp.concatenate([queries, keys], axis=0), 0, 0)
            + dot(dkk16, keys)
            + tail * dtail_keys
            + (beta * grow) * dright_keys
        )
        dvn_scr[at, :] = beta * dright_values
        keys_part = grow * jnp.sum(dright_keys * keys32, axis=1, keepdims=True)
        dbeta = dbeta + jnp.sum(dright_values * values32, axis=1, keepdims=True) + keys_part
        from_tail = tail * jnp.sum(dtail_keys * keys32, axis=1, keepdims=True)
        dcum = (
            jnp.sum(pairs, axis=1, keepdims=True)
            - as_column(jnp.sum(pairs, axis=0, keepdims=True), diagonal)
            + grow * jnp.sum(dgrown * queries32, axis=1, keepdims=True)
            + beta * keys_part
            - from_tail
        )
        dlast = whole * dwhole + jnp.sum(from_tail, axis=0, keepdims=True)
        dld_ref[0, :, at] = jnp.sum(jnp.where(rows >= cols, dcum, 0.0), axis=0, keepdims=True) + dlast
        dbeta_ref[0, :, at] = as_row(dbeta, diagonal)

    for scr in (dn_scr, dw_scr):
        scr[0:EDGE, :] = jnp.zeros((EDGE, scr.shape[1]), f32)
        scr[EDGE + length :, :] = jnp.zeros((EDGE, scr.shape[1]), f32)
    pn_scr[...] = q_ref[...].astype(f32)
    act, slope = silu_slope(conv_sum(pn_scr, tq_ref, length))
    root = lax.rsqrt(jnp.sum(act * act, axis=-1, keepdims=True) + epsilon)
    normal = act * root
    dy = dqn_scr[...] * KEY ** (-0.5)
    dz = root * (dy - normal * jnp.sum(normal * dy, axis=-1, keepdims=True)) * slope
    conv_back(dz, tq_ref, dn_scr, pn_scr, dq_ref, dtq_ref)
    pn_scr[...] = k_ref[...].astype(f32)
    act, slope = silu_slope(conv_sum(pn_scr, tk_ref, length))
    root = lax.rsqrt(jnp.sum(act * act, axis=-1, keepdims=True) + epsilon)
    normal = act * root
    dy = dkn_scr[...]
    dz = root * (dy - normal * jnp.sum(normal * dy, axis=-1, keepdims=True)) * slope
    conv_back(dz, tk_ref, dn_scr, pn_scr, dk_ref, dtk_ref)
    pw_scr[...] = v_ref[...].astype(f32)
    act, slope = silu_slope(conv_sum(pw_scr, tv_ref, length))
    conv_back(dvn_scr[...] * slope, tv_ref, dw_scr, pw_scr, dv_ref, dtv_ref)


def tall(rows, cols):
    return pl.BlockSpec((rows, cols), lambda h: (0, h))


def deep(rows, cols):
    return pl.BlockSpec((1, rows, cols), lambda h: (h, 0, 0))


def shared(rows, cols):
    return pl.BlockSpec((rows, cols), lambda h: (0, 0))


def shape_of(dims, dtype):
    return jax.ShapeDtypeStruct(dims, dtype)


def call_heads(kernel, head_count, in_specs, outputs, scratch, args, vmem=VMEM_BYTES):
    out_specs = [spec for spec, shape in outputs]
    out_shape = [shape for spec, shape in outputs]
    return pl.pallas_call(
        kernel,
        grid=(head_count,),
        in_specs=in_specs,
        out_specs=out_specs,
        out_shape=out_shape,
        scratch_shapes=scratch,
        compiler_params=pltpu.CompilerParams(vmem_limit_bytes=vmem),
        cost_estimate=COST,
    )(*args)


def prepare(x, edge, gain, w_query, w_key, w_value, w_decay, w_beta, rate, conv_query, conv_key, conv_value):
    length, width = x.shape
    heads = w_decay.shape[0]
    states = (length // CHUNK) * KEY
    ncols, wcols = heads * KEY, heads * VALUE
    out_shape = [
        shape_of((length, width), bf16),
        shape_of((length + EDGE, width), bf16),
        shape_of((length, heads), f32),
        shape_of((length + EDGE, ncols), bf16),
        shape_of((length + EDGE, ncols), bf16),
        shape_of((length + EDGE, wcols), bf16),
        shape_of((heads, 1, length), f32),
        shape_of((heads, 1, length), f32),
        shape_of((length, ncols), bf16),
        shape_of((length, ncols), bf16),
        shape_of((length, wcols), bf16),
        shape_of((heads, length, CHUNK), bf16),
        shape_of((heads, length, CHUNK), bf16),
        shape_of((heads, length, VALUE), bf16),
        shape_of((heads, length, KEY), bf16),
        shape_of((heads, states, KEY + VALUE), bf16),
        shape_of((heads, KEY, KEY + VALUE), f32),
    ]
    args = (
        x, edge, gain, w_query, w_key, w_value, w_decay, w_beta, rate, conv_query, conv_key, conv_value
    )
    return pl.pallas_call(
        prep_kernel,
        out_shape=out_shape,
        in_specs=[pl.BlockSpec(memory_space=pltpu.VMEM)] * len(args),
        out_specs=[pl.BlockSpec(memory_space=pltpu.VMEM)] * len(out_shape),
        scratch_shapes=[
            pltpu.VMEM((length + EDGE, wcols), f32),
            pltpu.VMEM((length + EDGE, ncols), f32),
        ],
        compiler_params=pltpu.CompilerParams(vmem_limit_bytes=VMEM_LARGE),
        cost_estimate=COST,
    )(*args)


def run_forward(qn, ld, att, u, w, starts, state_in, gate_pre, gain, w_out):
    length = qn.shape[0]
    heads = ld.shape[0]
    states = starts.shape[1]
    wide = tall(length, VALUE)
    wshape = (length, heads * VALUE)
    outputs = [
        (wide, shape_of(wshape, bf16)),
        (wide, shape_of(wshape, f32)),
        (deep(length, VALUE), shape_of((heads, length, VALUE), bf16)),
        (deep(states, VALUE), shape_of((heads, states, VALUE), bf16)),
        (shared(length, w_out.shape[1]), shape_of((length, w_out.shape[1]), bf16)),
    ]
    in_specs = [
        tall(length, KEY), deep(1, length), deep(length, CHUNK), deep(length, VALUE), deep(length, KEY),
        deep(states, KEY + VALUE), deep(KEY, VALUE), wide, shared(1, VALUE),
        pl.BlockSpec((VALUE, w_out.shape[1]), lambda h: (h, 0)),
    ]
    args = (qn, ld, att, u, w, starts, state_in, gate_pre, gain, w_out)
    scratch = [pltpu.VMEM((length, w_out.shape[1]), f32)]
    return call_heads(forward_kernel, heads, in_specs, outputs, scratch, args, VMEM_LARGE)


def gate_back(dgated, mixed, gate_pre, gain, qn, kn, ld, att, w):
    length = qn.shape[0]
    heads = ld.shape[0]
    states = (length // CHUNK) * KEY
    wide = tall(length, VALUE)
    outputs = [
        (wide, shape_of((length, heads * VALUE), bf16)),
        (deep(length, VALUE), shape_of((heads, length, VALUE), bf16)),
        (deep(length, VALUE), shape_of((heads, length, VALUE), bf16)),
        (deep(1, VALUE), shape_of((heads, 1, VALUE), f32)),
        (deep(states, KEY + VALUE), shape_of((heads, states, KEY + VALUE), bf16)),
        (deep(KEY, KEY + VALUE), shape_of((heads, KEY, KEY + VALUE), f32)),
    ]
    in_specs = [
        wide, wide, wide, shared(1, VALUE), tall(length, KEY), tall(length, KEY), deep(1, length),
        deep(length, CHUNK), deep(length, KEY),
    ]
    args = (dgated, mixed, gate_pre, gain, qn, kn, ld, att, w)
    return call_heads(gate_back_kernel, heads, in_specs, outputs, [], args)


def run_backward(
    gstate, after, dmixed, dcorr, begin, corr, inverse, att, u, w, qn, kn, vn,
    query_ext, key_ext, value_ext, conv_query, conv_key, conv_value, ld, beta,
):
    length = qn.shape[0]
    heads = ld.shape[0]
    states = after.shape[1]
    taps = conv_query.shape[0]
    narrow, wide = tall(length, KEY), tall(length, VALUE)
    ncols, wcols = heads * KEY, heads * VALUE
    outputs = [
        (tall(length + EDGE, KEY), shape_of((length + EDGE, ncols), bf16)),
        (tall(length + EDGE, KEY), shape_of((length + EDGE, ncols), bf16)),
        (tall(length + EDGE, VALUE), shape_of((length + EDGE, wcols), bf16)),
        (tall(taps, KEY), shape_of((taps, ncols), f32)),
        (tall(taps, KEY), shape_of((taps, ncols), f32)),
        (tall(taps, VALUE), shape_of((taps, wcols), f32)),
        (deep(1, length), shape_of((heads, 1, length), f32)),
        (deep(1, length), shape_of((heads, 1, length), f32)),
    ]
    in_specs = [
        deep(KEY, VALUE), deep(states, KEY + VALUE), deep(length, VALUE), deep(length, VALUE),
        deep(states, VALUE), deep(length, VALUE), deep(length, CHUNK), deep(length, CHUNK),
        deep(length, VALUE), deep(length, KEY),
        narrow, narrow, wide,
        tall(length + EDGE, KEY), tall(length + EDGE, KEY), tall(length + EDGE, VALUE),
        tall(taps, KEY), tall(taps, KEY), tall(taps, VALUE),
        deep(1, length), deep(1, length),
    ]
    scratch = [
        pltpu.VMEM((length, KEY), f32), pltpu.VMEM((length, KEY), f32), pltpu.VMEM((length, VALUE), f32),
        pltpu.VMEM((length + 2 * EDGE, KEY), f32), pltpu.VMEM((length + EDGE, KEY), f32),
        pltpu.VMEM((length + 2 * EDGE, VALUE), f32), pltpu.VMEM((length + EDGE, VALUE), f32),
    ]
    args = (
        gstate, after, dmixed, dcorr, begin, corr, inverse, att, u, w, qn, kn, vn,
        query_ext, key_ext, value_ext, conv_query, conv_key, conv_value, ld, beta,
    )
    return call_heads(backward_kernel, heads, in_specs, outputs, scratch, args)


def ffn_kernel(
    x_ref, branch_ref, gain_ref, wg_ref, wu_ref, wd_ref, cot_ref,
    normed_ref, hidden_ref, dgate_ref, dup_ref, part_ref,
):
    middle = x_ref[...].astype(f32) + branch_ref[...].astype(f32)
    normed = row_norm(middle, gain_ref[...]).astype(bf16)
    normed_ref[...] = normed
    gate = dot(normed, wg_ref[...], 1, 1)
    up = dot(normed, wu_ref[...], 1, 1)
    sig = jax.nn.sigmoid(gate)
    act = gate * sig
    hidden_ref[...] = (act * up).astype(bf16)
    dhidden = dot(cot_ref[...], wd_ref[...], 1, 1)
    dgate = (dhidden * up * (sig * (1.0 + gate * (1.0 - sig)))).astype(bf16)
    dup = (dhidden * act).astype(bf16)
    dgate_ref[...] = dgate
    dup_ref[...] = dup
    part_ref[...] = (dot(dgate, wg_ref[...]) + dot(dup, wu_ref[...])).astype(bf16)


def run_ffn(x, branch, gain, w_ffn_gate, w_ffn_up, w_ffn_down, cotangent):
    length, width = x.shape
    hidden = w_ffn_gate.shape[0]
    block = length // 2

    def rows(cols):
        return pl.BlockSpec((block, cols), lambda i: (i, 0))

    return pl.pallas_call(
        ffn_kernel,
        grid=(length // block,),
        in_specs=[
            rows(width), rows(width), shared(1, width), shared(hidden, width), shared(hidden, width),
            shared(hidden, width), rows(width),
        ],
        out_specs=[rows(width), rows(hidden), rows(hidden), rows(hidden), rows(width)],
        out_shape=[
            shape_of((length, width), bf16),
            shape_of((length, hidden), bf16),
            shape_of((length, hidden), bf16),
            shape_of((length, hidden), bf16),
            shape_of((length, width), bf16),
        ],
        compiler_params=pltpu.CompilerParams(vmem_limit_bytes=VMEM_BYTES),
        cost_estimate=COST,
    )(x, branch, gain, w_ffn_gate, w_ffn_up, w_ffn_down, cotangent)


def shard_kernel(plan, count, piece, places_ref, *refs):
    outs = refs[-2 * len(plan) :]
    for number, pairs in enumerate(plan):
        for which in range(2):
            out_ref = outs[2 * number + which]
            chosen = {}
            at = 0
            for left, right in pairs:
                if left not in chosen:
                    chosen[left] = jnp.concatenate(
                        [
                            refs[left][:, pl.ds(pl.multiple_of(places_ref[number, which, g] * piece, 128), piece)]
                            for g in range(count)
                        ],
                        axis=1,
                    )
                width = refs[right].shape[1]
                out_ref[:, at : at + width] = dot(chosen[left], refs[right][...], 0, 0).astype(out_ref.dtype)
                at += width


def shard_products(chains, home_type):
    size = lax.axis_size("seq")
    here = lax.axis_index("seq")
    count = size // 2
    slots = jnp.arange(count, dtype=jnp.int32)
    places = []
    for bit, pairs in chains:
        shards = (slots // 2**bit) * 2 ** (bit + 1) + slots % 2**bit
        mine = (here // 2**bit) % 2
        places.append(jnp.stack([shards + (1 - mine) * 2**bit, shards + mine * 2**bit]))
    width = chains[0][1][0][0].shape[1]
    piece = width // size
    if piece % 128:
        results = []
        for (bit, pairs), chosen in zip(chains, places):
            parts = []
            for which, kind in ((0, bf16), (1, home_type)):
                columns = [
                    lax.dot_general(
                        jnp.take(left.reshape(-1, size, piece), chosen[which], axis=1).reshape(
                            left.shape[0], -1
                        ),
                        right,
                        (((0,), (0,)), ((), ())),
                        preferred_element_type=f32,
                    )
                    for left, right in pairs
                ]
                parts.append(jnp.concatenate(columns, axis=1).astype(kind))
            results.append(tuple(parts))
        return results
    args, plan, out_shape = [], [], []

    def slot_of(array):
        for number, known in enumerate(args):
            if known is array:
                return number
        args.append(array)
        return len(args) - 1

    for bit, pairs in chains:
        plan.append([(slot_of(left), slot_of(right)) for left, right in pairs])
        total = sum(right.shape[1] for left, right in pairs)
        out_shape += [shape_of((count * piece, total), bf16), shape_of((count * piece, total), home_type)]
    whole = pl.BlockSpec(memory_space=pltpu.VMEM)
    flat = pl.pallas_call(
        functools.partial(shard_kernel, plan, count, piece),
        in_specs=[pl.BlockSpec(memory_space=pltpu.SMEM)] + [whole] * len(args),
        out_specs=[whole] * len(out_shape),
        out_shape=out_shape,
        compiler_params=pltpu.CompilerParams(vmem_limit_bytes=VMEM_BYTES),
        cost_estimate=COST,
    )(jnp.stack(places), *args)
    return [(flat[2 * number], flat[2 * number + 1]) for number in range(len(chains))]


def turn_kernel(cuts, *refs):
    ins, outs = refs[: len(cuts)], refs[len(cuts) :]
    for (low, high), in_ref, out_ref in zip(cuts, ins, outs):
        out_ref[...] = in_ref[:, low:high].T


def turned(pieces):
    if pieces[0][0].shape[0] % 128:
        return [array[:, low:high].T for array, low, high in pieces]
    whole = pl.BlockSpec(memory_space=pltpu.VMEM)
    return pl.pallas_call(
        functools.partial(turn_kernel, [(low, high) for array, low, high in pieces]),
        in_specs=[whole] * len(pieces),
        out_specs=[whole] * len(pieces),
        out_shape=[shape_of((high - low, array.shape[0]), f32) for array, low, high in pieces],
        compiler_params=pltpu.CompilerParams(vmem_limit_bytes=VMEM_BYTES),
        cost_estimate=COST,
    )(*[array for array, low, high in pieces])


def from_behind(block, axis, distance):
    devices = range(lax.axis_size(axis))
    route = [(i - distance, i) for i in devices if i - distance in devices]
    return lax.ppermute(block, axis, route)


def swap_with(block, axis, distance):
    route = [(i, i ^ distance) for i in range(lax.axis_size(axis))]
    return lax.ppermute(block, axis, route)


def exchange_rounds(tasks, box=None, beside=None):
    results, asked = [None] * len(tasks), {}

    def advance(which, got):
        try:
            asked[which] = tasks[which].send(got)
        except StopIteration as end:
            results[which] = end.value
            asked.pop(which, None)

    for which in range(len(tasks)):
        advance(which, None)
    number = 0
    while asked:
        number += 1
        got = {which: tuple(exchange() for exchange in wanted) for which, wanted in asked.items()}
        names = [name for name in (beside or {}).get(number, ()) if name in box]
        got, values = lax.optimization_barrier((got, [box[name] for name in names]))
        for name, value in zip(names, values):
            box[name] = value
        for which in list(asked):
            advance(which, got[which])
    return results


def swap(block, axis, distance):
    return functools.partial(swap_with, block, axis, distance)


def together(tasks):
    wanted = [next(task)[0] for task in tasks]
    arrived = yield wanted
    while True:
        wanted, results = [], []
        for task, got in zip(tasks, arrived):
            try:
                wanted.append(task.send((got,))[0])
            except StopIteration as end:
                results.append(end.value)
        if results:
            return results
        groups = {}
        for which, exchange in enumerate(wanted):
            groups.setdefault(exchange.args[1:], []).append(which)
        joined = [
            swap(jnp.concatenate([wanted[which].args[0] for which in members], axis=-1), *route)
            for route, members in groups.items()
        ]
        got = yield joined
        arrived = [None] * len(tasks)
        for block, members in zip(got, groups.values()):
            at = 0
            for which in members:
                width = wanted[which].args[0].shape[-1]
                arrived[which] = block[..., at : at + width]
                at += width


def pause(rounds):
    for _ in range(rounds):
        yield []


def group_sum(block, axis):
    size = lax.axis_size(axis)
    distance = 1
    while distance < size:
        reach = min(4, size // distance)
        arrived = yield [swap(block, axis, distance * step) for step in range(1, reach)]
        if reach == 4:
            block = (block + arrived[0]) + (arrived[1] + arrived[2])
        else:
            block = block + arrived[0]
        distance *= reach
    return block


def sum_over_heads(partial):
    rows = partial.shape[0] // 2
    odd = lax.axis_index("head") % 2 == 1
    low, high = partial[:rows], partial[rows:]
    own = jnp.where(odd, high, low).astype(f32)
    (got,) = yield [swap(jnp.where(odd, low, high), "head", 1)]
    own = own + got.astype(f32)
    distance = 2
    while distance < lax.axis_size("head"):
        sent = own.astype(bf16)
        (got,) = yield [swap(sent, "head", distance)]
        own = sent.astype(f32) + got.astype(f32)
        distance *= 2
    kept = own.astype(bf16)
    (other,) = yield [swap(kept, "head", 1)]
    return jnp.concatenate([jnp.where(odd, other, kept), jnp.where(odd, kept, other)], axis=0)


def exclusive_scan(joined, sign):
    own_t, own_b = joined[..., :KEY], joined[..., KEY:]
    send = joined
    before_t = before_b = None
    distance = 1
    size = lax.axis_size("seq")

    def product(a, b):
        return jnp.einsum("hij,hjk->hik", a, b, precision=lax.Precision.HIGH)

    while distance < size:
        last = distance * 2 >= size
        sent = (send[..., KEY:] if last else send).astype(bf16)
        (got,) = yield [functools.partial(from_behind, sent, "seq", sign * distance)]
        got = got.astype(f32)
        if before_t is None:
            before_t, before_b = got[..., :KEY], got[..., KEY:]
        else:
            moved = product(before_t, got)
            if last:
                before_b = before_b + moved
            else:
                before_t, before_b = moved[..., :KEY], before_b + moved[..., KEY:]
        if not last:
            send = product(own_t, jnp.concatenate([before_t, before_b], axis=-1))
            send = jnp.concatenate([send[..., :KEY], send[..., KEY:] + own_b], axis=-1)
        distance *= 2
    return before_b


def halving_scatter(products, order, pauses=(), box=None, name=None, hold=None):
    size = lax.axis_size("seq")
    bits = size.bit_length() - 1
    here = lax.axis_index("seq")
    order = [bit for bit in order if bit < bits] + list(range(len(order), bits))
    pauses = list(pauses) + [0] * bits
    away, home = products
    (got,) = yield [swap(away, "seq", 2 ** order[0])]
    held = home.astype(f32) + got.astype(f32)
    axes = [bit for bit in range(bits)[::-1] if bit != order[0]]
    held = held.reshape((2,) * (bits - 1) + (held.shape[0] // 2 ** (bits - 1), held.shape[1]))
    for number, bit in enumerate(order[1:]):
        axis = axes.index(bit)
        axes.remove(bit)
        mine = (here // 2**bit) % 2
        sent = lax.dynamic_index_in_dim(held, 1 - mine, axis, keepdims=False).astype(bf16)
        if pauses[number]:
            box[name] = sent
            yield from pause(pauses[number])
            sent = box[name]
        elif hold is not None:
            sent = hold(sent)
        elif hold is not None:
            sent = hold(sent)
        (got,) = yield [swap(sent, "seq", 2**bit)]
        held = lax.dynamic_index_in_dim(held, mine, axis, keepdims=False) + got.astype(f32)
    return held


def inner_rows(first_operand, second_operand):
    return lax.dot_general(
        first_operand, second_operand, (((0,), (0,)), ((), ())), preferred_element_type=f32
    )


def matmul_bf(first_operand, second_operand):
    return jnp.dot(first_operand, second_operand, preferred_element_type=f32)


def against_rows(first_operand, second_operand):
    return lax.dot_general(
        first_operand, second_operand, (((1,), (1,)), ((), ())), preferred_element_type=f32
    )


def per_device(
    block_input,
    norm1_gain,
    w_query,
    w_key,
    w_value,
    w_gate,
    w_decay,
    w_beta,
    conv_query,
    conv_key,
    conv_value,
    decay_rate,
    out_gain,
    w_out,
    norm2_gain,
    w_ffn_gate,
    w_ffn_up,
    w_ffn_down,
    cotangent,
):
    length = block_input.shape[0]
    head_count = w_decay.shape[1]
    key_cols = w_query.shape[1]
    value_cols = w_value.shape[1]
    ff_cols = w_ffn_gate.shape[1]
    edge_input = from_behind(block_input[length - EDGE :], "seq", 1)
    gain1 = norm1_gain.astype(f32)
    (
        normed, normed_ext, decay_cols, query_ext, key_ext, value_ext, log_decay, beta3,
        qn, kn, vn, inverse, att, u, w, starts, composite,
    ) = prepare(
        block_input, edge_input, gain1[None], w_query, w_key, w_value, w_decay.T, w_beta.T,
        decay_rate[None], conv_query, conv_key, conv_value,
    )
    inputs32 = block_input.astype(f32)
    gate_pre = matmul_bf(normed, w_gate)
    box = {"gate": gate_pre}
    (state_in,) = exchange_rounds([exclusive_scan(composite, 1)], box, {1: ["gate"]})
    gate_pre = box["gate"]
    gain_row = out_gain.astype(f32)[None]
    gated, mixed, corr, begin, branch_part = run_forward(
        qn, log_decay, att, u, w, starts, state_in, gate_pre, gain_row, w_out
    )
    (branch,) = exchange_rounds([sum_over_heads(branch_part)])
    gain2 = norm2_gain.astype(f32)
    normed2, hidden, grad_fgate, grad_fup, grad_part = run_ffn(
        block_input, branch, gain2[None], w_ffn_gate.T, w_ffn_up.T, w_ffn_down, cotangent
    )
    bits = lax.axis_size("seq").bit_length() - 1
    near, far = 0, min(1, bits - 1)
    half = ff_cols // 2 // 128 * 128
    ffn_near, ffn_far = shard_products(
        [
            (near, [(normed2, grad_fgate), (cotangent, hidden[:, :half])]),
            (far, [(normed2, grad_fup), (cotangent, hidden[:, half:])]),
        ],
        bf16,
    )
    box = {}

    def after_scan(sent):
        return lax.optimization_barrier((sent, box["state"]))[0]

    ffn_tasks = [
        halving_scatter(ffn_near, [0, 1], [bits - 2, 0], box, "sent near", after_scan),
        halving_scatter(ffn_far, [1, 0], [bits - 2, 0], box, "sent far", after_scan),
    ]
    ffn_got = [tuple(exchange() for exchange in next(task)) for task in ffn_tasks]
    box["away"] = (ffn_near[0], ffn_far[0])
    (grad_normed2,) = exchange_rounds([sum_over_heads(grad_part)], box, {2: ["away"]})
    grad_normed2 = grad_normed2.astype(f32)
    middle = inputs32 + branch.astype(f32)
    norm2_back = jax.vjp(row_norm, middle, gain2)[1]
    ffn_part = matmul_bf(hidden, w_ffn_down).astype(bf16)
    grad_middle_n, grad_gain2 = norm2_back(grad_normed2)
    grad_middle = cotangent.astype(f32) + grad_middle_n
    grad_branch = grad_middle.astype(bf16)
    grad_gated = against_rows(grad_branch, w_out)
    grad_gp, grad_mixed, grad_corr, grad_outgain, after, composite_back = gate_back(
        grad_gated, mixed, gate_pre, gain_row, qn, kn, log_decay, att, w
    )
    box["ffn part"] = ffn_part
    pad_rows = ((length - 8, 0), (0, 0))
    taps_count = conv_query.shape[0]
    width = w_query.shape[0]

    def given(blocks):
        return [lambda block=block: block for block in blocks]

    def main_task():
        grad_state = yield from exclusive_scan(composite_back, -1)
        box["state"] = grad_state
        dq, dk, dv, taps_q, taps_k, taps_v, grad_log, grad_beta = run_backward(
            grad_state, after, grad_mixed, grad_corr, begin, corr, inverse, att, u, w,
            qn, kn, vn, query_ext, key_ext, value_ext,
            conv_query, conv_key, conv_value, log_decay, beta3,
        )
        box["late"] = shard_products(
            [(near, [(normed_ext, dq), (normed_ext, dk)]), (far, [(normed_ext, dv)])], f32
        )
        part_ext = against_rows(dq, w_query) + against_rows(dk, w_key) + against_rows(dv, w_value)
        decay_pre = decay_cols.T
        soft = jax.nn.softplus(decay_pre)
        rate = decay_rate[:, None]
        beta_gate = beta3.reshape(head_count, length)
        grad_log = grad_log.reshape(head_count, length)
        grad_beta = grad_beta.reshape(head_count, length)
        grad_dp = (-rate * jax.nn.sigmoid(decay_pre) * grad_log).astype(bf16)
        grad_bp = (beta_gate * (1.0 - beta_gate) * grad_beta).astype(bf16)
        grad_rate = -jnp.sum(grad_log * soft, axis=1)
        grad_scalars = jnp.concatenate([grad_dp, grad_bp], axis=0)
        w_scalars = jnp.concatenate([w_decay, w_beta], axis=1)
        box["small"] = jnp.concatenate(
            [
                jnp.concatenate([taps_q, taps_k, taps_v], axis=1),
                grad_gain2[None],
                jnp.pad(grad_rate, (0, width - head_count))[None],
                matmul_bf(grad_scalars, normed),
            ],
            axis=0,
        )
        edges = part_ext[EDGE - 8 : EDGE]
        part = (
            part_ext[EDGE:]
            + against_rows(grad_gp, w_gate)
            + lax.dot_general(
                grad_scalars, w_scalars, (((0,), (1,)), ((), ())), preferred_element_type=f32
            )
        )
        edge_normal = row_norm(edge_input[EDGE - 8 :].astype(f32), 1.0)
        gain_part = jnp.sum(part * row_norm(inputs32, 1.0), axis=0) + jnp.sum(edges * edge_normal, axis=0)
        gains = jnp.concatenate([gain_part, jnp.sum(grad_outgain, axis=(0, 1))])
        box["shared"] = jnp.pad(gains, (0, 2 * width - gains.shape[0])).reshape(-1, 128)
        (edges,) = yield [functools.partial(from_behind, edges, "seq", -1)]
        part = part + jnp.pad(edges, pad_rows)
        return (yield from sum_over_heads(part.astype(bf16)))

    def ffn_rest(task, got, name):
        wanted = given(got)
        try:
            while True:
                wanted = task.send((yield wanted))
        except StopIteration as end:
            held = end.value
        box[name] = turned([(held, 0, ff_cols), (held, ff_cols, held.shape[1])])

    def ffn_sum_task():
        yield from pause(1)
        steps = sum_over_heads(box["ffn part"])
        got = yield next(steps)
        wanted = steps.send(got)
        yield from pause(bits - 2)
        try:
            while True:
                wanted = steps.send((yield wanted))
        except StopIteration as end:
            box["out"] = (middle + end.value.astype(f32)).astype(bf16)

    mid_products = shard_products([(near, [(grad_branch, gated), (normed, grad_gp)])], f32)[0]
    box["mid away"] = mid_products[0]

    def mid_task():
        yield from pause(1)
        steps = halving_scatter(mid_products, [0, 1])
        got = [exchange() for exchange in next(steps)]
        yield from pause(1)
        wanted = given(got)
        try:
            while True:
                wanted = steps.send((yield wanted))
        except StopIteration as end:
            held = end.value
        return turned([(held, 0, gated.shape[1])])[0], held[:, gated.shape[1] :]

    def late_task():
        yield from pause(bits)
        first, second = box["late"]
        return (yield from together([halving_scatter(first, [0, 1]), halving_scatter(second, [1, 0])]))

    def small_task():
        yield from pause(bits)
        shared = yield from group_sum(box["shared"], "head")
        rows = jnp.concatenate([box["small"], shared.reshape(-1, width)], axis=0)
        distance = 1
        while distance < 2**bits:
            (got,) = yield [swap(rows, "seq", distance)]
            rows = rows + got
            distance *= 2
        return rows

    grad_normed, late, mid, small = exchange_rounds(
        [main_task(), late_task(), mid_task(), small_task(), ffn_sum_task()]
        + [ffn_rest(task, got, name) for task, got, name in zip(ffn_tasks, ffn_got, ("near", "far"))],
        box,
        {1: ["ffn part", "mid away"], 2: ["sent near", "sent far"], bits + 2: ["near", "far"], bits + 3: ["out"]},
    )[:4]
    late_qk, late_v = late
    grad_wout, grad_wg = mid
    grad_wfg, down_near = box["near"]
    grad_wfu, down_far = box["far"]
    layer_out = box["out"]
    shared_sum = small[-2:].reshape(-1)
    norm1_back = jax.vjp(row_norm, inputs32, gain1)[1]
    grad_input = grad_middle + norm1_back(grad_normed.astype(f32))[0]
    taps_sum = small[:taps_count]
    gain2_sum = small[taps_count]
    rate_sum = small[taps_count + 1, :head_count]
    scalars_sum = small[taps_count + 2 : taps_count + 2 + 2 * head_count]
    gain1_sum, outgain_sum = shared_sum[:width], shared_sum[width : width + VALUE]

    def own_part(vec):
        piece = vec.shape[-1] // lax.axis_size("seq")
        return lax.dynamic_slice_in_dim(vec, lax.axis_index("seq") * piece, piece, axis=-1)

    scalars_sum = own_part(scalars_sum).T
    return (
        layer_out,
        grad_input,
        own_part(gain1_sum),
        late_qk[:, :key_cols],
        late_qk[:, key_cols:],
        late_v,
        grad_wg,
        scalars_sum[:, :head_count],
        scalars_sum[:, head_count:],
        taps_sum[:, :key_cols],
        taps_sum[:, key_cols : 2 * key_cols],
        taps_sum[:, 2 * key_cols :],
        rate_sum,
        own_part(outgain_sum),
        grad_wout,
        own_part(gain2_sum),
        grad_wfg.T,
        grad_wfu.T,
        jnp.concatenate([down_near, down_far], axis=0),
    )


def solution(mesh):
    return jax.shard_map(
        per_device,
        mesh=mesh,
        in_specs=(
            P("seq", None),
            P(),
            P(None, "head"),
            P(None, "head"),
            P(None, "head"),
            P(None, "head"),
            P(None, "head"),
            P(None, "head"),
            P(None, "head"),
            P(None, "head"),
            P(None, "head"),
            P("head"),
            P(),
            P("head", None),
            P(),
            P(None, "head"),
            P(None, "head"),
            P("head", None),
            P("seq", None),
        ),
        out_specs=(
            P("seq", None),
            P("seq", None),
            P("seq"),
            P("seq", "head"),
            P("seq", "head"),
            P("seq", "head"),
            P("seq", "head"),
            P("seq", "head"),
            P("seq", "head"),
            P(None, "head"),
            P(None, "head"),
            P(None, "head"),
            P("head"),
            P("seq"),
            P("head", "seq"),
            P("seq"),
            P("seq", "head"),
            P("seq", "head"),
            P("head", "seq"),
        ),
        check_vma=False,
    )
```

```python
import functools

import jax
import jax.numpy as jnp
from jax import lax
from jax.experimental import pallas as pl
from jax.experimental.pallas import tpu as pltpu
from jax.sharding import PartitionSpec as P

KEY = 128
VALUE = 256
CHUNK = 128
EDGE = 16
SUB = 16
VMEM_BYTES = 60 * 1024 * 1024
COST = pl.CostEstimate(flops=0, bytes_accessed=0, transcendentals=0)

epsilon = 1e-06
f32 = jnp.float32
bf16 = jnp.bfloat16
highest_precision = lax.Precision.HIGHEST


def dot(first, second, over_first=1, over_second=0):
    return lax.dot_general(
        first.astype(bf16),
        second.astype(bf16),
        (((over_first,), (over_second,)), ((), ())),
        preferred_element_type=f32,
    )


def halves(values):
    high = values.astype(bf16)
    return high, (values - high.astype(f32)).astype(bf16)


def dot_fine(first, second):
    first_high, first_low = halves(first)
    second_high, second_low = halves(second)
    width = second.shape[1]
    wide = dot(first_high, jnp.concatenate([second_high, second_low], axis=1))
    return wide[:, :width] + wide[:, width:] + dot(first_low, second_high)


def grid_places(extent):
    rows = lax.broadcasted_iota(jnp.int32, (extent, extent), 0)
    cols = lax.broadcasted_iota(jnp.int32, (extent, extent), 1)
    return rows, cols


def as_row(column, diagonal):
    return jnp.sum(jnp.where(diagonal, column, 0.0), axis=0, keepdims=True)


def as_column(row, diagonal):
    return jnp.sum(jnp.where(diagonal, row, 0.0), axis=1, keepdims=True)


def unit_lower_inverses(systems, rows, cols):
    extent = systems[0].shape[0]
    count = extent // SUB
    units = len(systems)
    same = rows // SUB == cols // SUB
    packed = jnp.concatenate(
        [jnp.sum(jnp.where(same, s, 0.0).reshape(count, SUB, extent), axis=0) for s in systems], axis=0
    )
    stacked = jnp.concatenate(halves(packed), axis=0)
    shape = (units, SUB, extent)
    places = lax.broadcasted_iota(jnp.int32, shape, 1)
    solved = (places == lax.broadcasted_iota(jnp.int32, shape, 2) % SUB).astype(f32)
    for j in range(SUB - 1):
        spread = dot(stacked, (same & (rows % SUB == j)).astype(f32))
        column = spread[: units * SUB] + spread[units * SUB :]
        solved = solved - column.reshape(shape) * solved[:, j : j + 1, :]
    inverses = [
        jnp.where(same, jnp.concatenate([solved[n]] * count, axis=0), 0.0) for n in range(units)
    ]
    size = SUB
    while size < extent:
        below = (rows // (2 * size) == cols // (2 * size)) & (rows // size > cols // size)
        joined = [
            dot_fine(inverse, jnp.where(below, s, 0.0)) for inverse, s in zip(inverses, systems)
        ]
        joined = [dot_fine(product, inverse) for product, inverse in zip(joined, inverses)]
        inverses = [inverse - product for inverse, product in zip(inverses, joined)]
        size *= 2
    return inverses


def decay_terms(ld_row, rows, cols):
    cum_col = jnp.sum(jnp.where(rows >= cols, ld_row, 0.0), axis=1, keepdims=True)
    cum_row = as_row(cum_col, rows == cols)
    last = cum_col[CHUNK - 1 :, :]
    between = jnp.where(rows >= cols, jnp.exp(jnp.where(rows >= cols, cum_col - cum_row, 0.0)), 0.0)
    return between, jnp.exp(cum_col), jnp.exp(last - cum_col), jnp.exp(last)


def conv_sum(padded_ref, taps_ref, length):
    taps = taps_ref[...].astype(f32)
    summed = taps[0:1] * padded_ref[EDGE : EDGE + length, :]
    for offset in range(1, taps_ref.shape[0]):
        summed = summed + taps[offset : offset + 1] * padded_ref[EDGE - offset : EDGE - offset + length, :]
    return summed


def unit_rows(values, scale, heads):
    parts = []
    for h in range(heads):
        part = values[:, h * KEY : (h + 1) * KEY]
        parts.append(
            part * (lax.rsqrt(jnp.sum(part * part, axis=-1, keepdims=True) + epsilon) * scale)
        )
    return jnp.concatenate(parts, axis=1)


def row_norm(values, gain_vec):
    return (
        values * lax.rsqrt(jnp.mean(values * values, axis=-1, keepdims=True) + epsilon) * gain_vec
    )


def prep_kernel(
    x_ref, edge_ref, gain_ref, wq_ref, wk_ref, wv_ref, wd_ref, wb_ref, rate_ref, tq_ref, tk_ref, tv_ref,
    normed_ref, normed_ext_ref, decay_ref, q_ref, k_ref, v_ref, ld_ref, beta_ref,
    qn_ref, kn_ref, vn_ref, inv_ref, att_ref, u_ref, w_ref, start_ref, final_ref,
    wide_scr, narrow_scr,
):
    length = qn_ref.shape[0]
    heads = ld_ref.shape[0]
    chunks = length // CHUNK
    gain = gain_ref[...]
    normed_ext_ref[:EDGE, :] = row_norm(edge_ref[...].astype(f32), gain).astype(bf16)
    normed = row_norm(x_ref[...].astype(f32), gain).astype(bf16)
    normed_ext_ref[EDGE:, :] = normed
    normed_ref[...] = normed
    decay_pre = dot(normed, wd_ref[...], 1, 1)
    decay_ref[...] = decay_pre
    softplus = jnp.maximum(decay_pre, 0.0) + jnp.log1p(jnp.exp(-jnp.abs(decay_pre)))
    log_decay = -rate_ref[...] * softplus
    beta_gate = jax.nn.sigmoid(dot(normed, wb_ref[...], 1, 1))
    pre = dot(normed_ext_ref[...], wk_ref[...]).astype(bf16)
    k_ref[...] = pre
    narrow_scr[...] = pre.astype(f32)
    z = conv_sum(narrow_scr, tk_ref, length)
    kn_ref[...] = unit_rows(z * jax.nn.sigmoid(z), 1.0, heads).astype(bf16)
    pre = dot(normed_ext_ref[...], wq_ref[...]).astype(bf16)
    q_ref[...] = pre
    narrow_scr[...] = pre.astype(f32)
    z = conv_sum(narrow_scr, tq_ref, length)
    qn_ref[...] = unit_rows(z * jax.nn.sigmoid(z), KEY ** (-0.5), heads).astype(bf16)
    pre = dot(normed_ext_ref[...], wv_ref[...]).astype(bf16)
    v_ref[...] = pre
    wide_scr[...] = pre.astype(f32)
    z = conv_sum(wide_scr, tv_ref, length)
    vn_ref[...] = (z * jax.nn.sigmoid(z)).astype(bf16)

    rows, cols = grid_places(CHUNK)
    diagonal = rows == cols
    units = [(h, c) for c in range(chunks) for h in range(heads)]
    systems, vectors = [], []
    for h, c in units:
        at = slice(c * CHUNK, (c + 1) * CHUNK)
        keyed = slice(h * KEY, (h + 1) * KEY)
        ld_row = as_row(log_decay[at, h : h + 1], diagonal)
        ld_ref[h, :, at] = ld_row
        between, grow, tail, whole = decay_terms(ld_row, rows, cols)
        beta = beta_gate[at, h : h + 1]
        beta_ref[h, :, at] = as_row(beta, diagonal)
        keys = kn_ref[at, keyed]
        products = dot(jnp.concatenate([keys, qn_ref[at, keyed]], axis=0), keys, 1, 1)
        systems.append(jnp.where(rows > cols, beta * between * products[:CHUNK], 0.0))
        att_ref[h, at, :] = (products[CHUNK:] * between).astype(bf16)
        vectors.append((beta, grow, tail, whole))
    inverses = unit_lower_inverses(systems, rows, cols)
    kept = []
    for (h, c), inverse, (beta, grow, tail, whole) in zip(units, inverses, vectors):
        at = slice(c * CHUNK, (c + 1) * CHUNK)
        keys32 = kn_ref[at, h * KEY : (h + 1) * KEY].astype(f32)
        values32 = vn_ref[at, h * VALUE : (h + 1) * VALUE].astype(f32)
        inv_ref[h, at, :] = inverse.astype(bf16)
        solved = dot(inverse, jnp.concatenate([(beta * grow) * keys32, beta * values32], axis=1))
        w_ref[h, at, :] = solved[:, :KEY].astype(bf16)
        u_ref[h, at, :] = solved[:, KEY:].astype(bf16)
        kept.append((tail * keys32).astype(bf16))
    begin = jnp.concatenate([diagonal.astype(f32), jnp.zeros((KEY, VALUE), f32)], axis=1)
    states = [begin] * heads
    for (h, c), tail_keys, (beta, grow, tail, whole) in zip(units, kept, vectors):
        at = slice(c * CHUNK, (c + 1) * CHUNK)
        state = states[h]
        start_ref[h, c * KEY : (c + 1) * KEY, :] = state.astype(bf16)
        source = jnp.concatenate([jnp.zeros((CHUNK, KEY), f32), u_ref[h, at, :].astype(f32)], axis=1)
        corrected = source - dot(w_ref[h, at, :], state)
        states[h] = whole * state + dot(tail_keys, corrected, 0, 0)
    for h in range(heads):
        final_ref[h, :, :] = states[h]


def forward_kernel(
    odd_ref, qn_ref, ld_ref, att_ref, u_ref, w_ref, start_ref, state_ref, gate_ref, gain_ref, wout_ref,
    gated_ref, mixed_ref, corr_ref, begin_ref, own_ref, sent_ref, sum_scr,
):
    length = qn_ref.shape[0]
    rows, cols = grid_places(CHUNK)
    entering = state_ref[0]
    gain = gain_ref[...]
    for c in range(length // CHUNK):
        at = slice(c * CHUNK, (c + 1) * CHUNK)
        places = slice(c * KEY, (c + 1) * KEY)
        between, grow, tail, whole = decay_terms(ld_ref[0, :, at], rows, cols)
        begin = start_ref[0, places, KEY:].astype(f32) + dot(start_ref[0, places, :KEY], entering)
        begin_ref[0, places, :] = begin.astype(bf16)
        corrected = u_ref[0, at, :].astype(f32) - dot(w_ref[0, at, :], begin)
        corr_ref[0, at, :] = corrected.astype(bf16)
        mixed = dot(grow * qn_ref[at, :].astype(f32), begin) + dot(att_ref[0, at, :], corrected)
        mixed_ref[at, :] = mixed
        root = lax.rsqrt(jnp.mean(mixed * mixed, axis=-1, keepdims=True) + epsilon)
        gate = gate_ref[at, :]
        gated_ref[at, :] = (mixed * root * gain * (gate * jax.nn.sigmoid(gate))).astype(bf16)
    part = dot(gated_ref[...], wout_ref[...])

    @pl.when(pl.program_id(0) == 0)
    def start_sum():
        sum_scr[...] = part

    @pl.when(pl.program_id(0) > 0)
    def add_sum():
        sum_scr[...] += part

    @pl.when(pl.program_id(0) == pl.num_programs(0) - 1)
    def give_sum():
        half = length // 2
        at = pl.multiple_of(odd_ref[0] * half, half)
        own_ref[...] = sum_scr[pl.ds(at, half), :].astype(bf16)
        sent_ref[...] = sum_scr[pl.ds(pl.multiple_of(half - at, half), half), :].astype(bf16)


def gate_back_kernel(
    dgated_ref, mixed_ref, gate_ref, gain_ref, qn_ref, kn_ref, ld_ref, att_ref, w_ref,
    dgate_ref, dmixed_ref, dcorr_ref, dgain_ref, after_ref, final_ref,
):
    length = qn_ref.shape[0]
    rows, cols = grid_places(CHUNK)
    gain = gain_ref[...]
    kept = []
    dgain = jnp.zeros((1, VALUE), f32)
    for c in range(length // CHUNK):
        at = slice(c * CHUNK, (c + 1) * CHUNK)
        mixed, gate, dgated = mixed_ref[at, :], gate_ref[at, :], dgated_ref[at, :]
        root = lax.rsqrt(jnp.mean(mixed * mixed, axis=-1, keepdims=True) + epsilon)
        normal = mixed * root
        sig = jax.nn.sigmoid(gate)
        act = gate * sig
        dgain = dgain + jnp.sum(dgated * normal * act, axis=0, keepdims=True)
        dgate_ref[at, :] = (dgated * normal * gain * (sig * (1.0 + gate * (1.0 - sig)))).astype(bf16)
        dnormal = dgated * act * gain
        dmixed = root * (dnormal - normal * jnp.mean(dnormal * normal, axis=-1, keepdims=True))
        dmixed_ref[0, at, :] = dmixed.astype(bf16)
        between, grow, tail, whole = decay_terms(ld_ref[0, :, at], rows, cols)
        dcorr = dot(att_ref[0, at, :], dmixed, 0, 0)
        dcorr_ref[0, at, :] = dcorr.astype(bf16)
        gradient = dot(grow * qn_ref[at, :].astype(f32), dmixed, 0, 0) - dot(w_ref[0, at, :], dcorr, 0, 0)
        kept.append((gradient, (tail * kn_ref[at, :].astype(f32)).astype(bf16), whole))
    dgain_ref[0, :, :] = dgain
    pending = jnp.concatenate([(rows == cols).astype(f32), jnp.zeros((KEY, VALUE), f32)], axis=1)
    for c in reversed(range(length // CHUNK)):
        gradient, tail_keys, whole = kept[c]
        at = slice(c * CHUNK, (c + 1) * CHUNK)
        after_ref[0, c * KEY : (c + 1) * KEY, :] = pending.astype(bf16)
        source = jnp.concatenate([jnp.zeros((KEY, KEY), f32), gradient], axis=1)
        pending = whole * pending + source - dot(w_ref[0, at, :], dot(tail_keys, pending), 0, 0)
    final_ref[0, :, :] = pending


def silu_slope(z):
    sig = jax.nn.sigmoid(z)
    return z * sig, sig * (1.0 + z * (1.0 - sig))


def conv_back(dz, taps_ref, dz_scr, pre_scr, dpre_ref, dtaps_ref):
    length = dz.shape[0]
    reach = taps_ref.shape[0] - 1
    taps = taps_ref[...].astype(f32)
    dz_scr[EDGE : EDGE + length, :] = dz
    total = taps[0:1] * dz
    sums = [jnp.sum(dz * pre_scr[EDGE : EDGE + length, :], axis=0, keepdims=True)]
    for offset in range(1, reach + 1):
        total = total + taps[offset : offset + 1] * dz_scr[EDGE + offset : EDGE + offset + length, :]
        sums.append(
            jnp.sum(dz * pre_scr[EDGE - offset : EDGE - offset + length, :], axis=0, keepdims=True)
        )
    dpre_ref[EDGE:, :] = total.astype(bf16)
    edge = taps[1:2] * dz_scr[EDGE - 7 : EDGE + 1, :]
    for offset in range(2, reach + 1):
        edge = edge + taps[offset : offset + 1] * dz_scr[EDGE - 8 + offset : EDGE + offset, :]
    dpre_ref[:EDGE, :] = jnp.concatenate([jnp.zeros_like(edge), edge], axis=0).astype(bf16)
    dtaps_ref[...] = jnp.concatenate(sums, axis=0)


def backward_kernel(
    gstate_ref, after_ref, dmixed_ref, dcorr_ref, begin_ref, corr_ref, inv_ref, att_ref, u_ref, w_ref,
    qn_ref, kn_ref, vn_ref, q_ref, k_ref, v_ref, tq_ref, tk_ref, tv_ref,
    ld_ref, beta_ref,
    dq_ref, dk_ref, dv_ref, dtq_ref, dtk_ref, dtv_ref, dld_ref, dbeta_ref,
    dqn_scr, dkn_scr, dvn_scr, dn_scr, pn_scr, dw_scr, pw_scr,
):
    length = qn_ref.shape[0]
    rows, cols = grid_places(CHUNK)
    diagonal = rows == cols
    leaving = gstate_ref[0]
    for c in range(length // CHUNK):
        at = slice(c * CHUNK, (c + 1) * CHUNK)
        places = slice(c * KEY, (c + 1) * KEY)
        between, grow, tail, whole = decay_terms(ld_ref[0, :, at], rows, cols)
        beta = as_column(beta_ref[0, :, at], diagonal)
        keys, queries = kn_ref[at, :], qn_ref[at, :]
        keys32, queries32, values32 = keys.astype(f32), queries.astype(f32), vn_ref[at, :].astype(f32)
        dstate = after_ref[0, places, KEY:].astype(f32) + dot(after_ref[0, places, :KEY], leaving)
        dmixed, corrected, begin = dmixed_ref[0, at, :], corr_ref[0, at, :], begin_ref[0, places, :]
        dcorr = dcorr_ref[0, at, :].astype(f32) + dot(tail * keys32, dstate)
        datt = dot(dmixed, corrected, 1, 1)
        from_begin = dot(jnp.concatenate([dmixed, dcorr.astype(bf16)], axis=0), begin, 1, 1)
        dgrown, dw = from_begin[:CHUNK], -from_begin[CHUNK:]
        dtail_keys = dot(corrected, dstate, 1, 1)
        dwhole = jnp.sum(dstate * begin.astype(f32))
        back = dot(inv_ref[0, at, :], jnp.concatenate([dw, dcorr], axis=1), 0, 0)
        dright_keys, dright_values = back[:, :KEY], back[:, KEY:]
        dsystem = -dot(
            back, jnp.concatenate([w_ref[0, at, :], u_ref[0, at, :]], axis=1), 1, 1
        )
        products = dot(jnp.concatenate([keys, queries], axis=0), keys, 1, 1)
        decayed = jnp.where(rows > cols, between * products[:CHUNK], 0.0)
        dsys_decayed = dsystem * decayed
        dbeta = jnp.sum(dsys_decayed, axis=1, keepdims=True)
        pairs = beta * dsys_decayed + datt * (between * products[CHUNK:])
        dkk = jnp.where(rows > cols, dsystem * (beta * between), 0.0)
        dqk = datt * between
        dqk16, dkk16 = dqk.astype(bf16), dkk.astype(bf16)
        dqn_scr[at, :] = dot(dqk16, keys) + grow * dgrown
        dkn_scr[at, :] = (
            dot(jnp.concatenate([dqk16, dkk16], axis=0), jnp.concatenate([queries, keys], axis=0), 0, 0)
            + dot(dkk16, keys)
            + tail * dtail_keys
            + (beta * grow) * dright_keys
        )
        dvn_scr[at, :] = beta * dright_values
        keys_part = grow * jnp.sum(dright_keys * keys32, axis=1, keepdims=True)
        dbeta = dbeta + jnp.sum(dright_values * values32, axis=1, keepdims=True) + keys_part
        from_tail = tail * jnp.sum(dtail_keys * keys32, axis=1, keepdims=True)
        dcum = (
            jnp.sum(pairs, axis=1, keepdims=True)
            - as_column(jnp.sum(pairs, axis=0, keepdims=True), diagonal)
            + grow * jnp.sum(dgrown * queries32, axis=1, keepdims=True)
            + beta * keys_part
            - from_tail
        )
        dlast = whole * dwhole + jnp.sum(from_tail, axis=0, keepdims=True)
        dld_ref[0, :, at] = jnp.sum(jnp.where(rows >= cols, dcum, 0.0), axis=0, keepdims=True) + dlast
        dbeta_ref[0, :, at] = as_row(dbeta, diagonal)

    for scr in (dn_scr, dw_scr):
        scr[0:EDGE, :] = jnp.zeros((EDGE, scr.shape[1]), f32)
        scr[EDGE + length :, :] = jnp.zeros((EDGE, scr.shape[1]), f32)
    pn_scr[...] = q_ref[...].astype(f32)
    act, slope = silu_slope(conv_sum(pn_scr, tq_ref, length))
    root = lax.rsqrt(jnp.sum(act * act, axis=-1, keepdims=True) + epsilon)
    normal = act * root
    dy = dqn_scr[...] * KEY ** (-0.5)
    dz = root * (dy - normal * jnp.sum(normal * dy, axis=-1, keepdims=True)) * slope
    conv_back(dz, tq_ref, dn_scr, pn_scr, dq_ref, dtq_ref)
    pn_scr[...] = k_ref[...].astype(f32)
    act, slope = silu_slope(conv_sum(pn_scr, tk_ref, length))
    root = lax.rsqrt(jnp.sum(act * act, axis=-1, keepdims=True) + epsilon)
    normal = act * root
    dy = dkn_scr[...]
    dz = root * (dy - normal * jnp.sum(normal * dy, axis=-1, keepdims=True)) * slope
    conv_back(dz, tk_ref, dn_scr, pn_scr, dk_ref, dtk_ref)
    pw_scr[...] = v_ref[...].astype(f32)
    act, slope = silu_slope(conv_sum(pw_scr, tv_ref, length))
    conv_back(dvn_scr[...] * slope, tv_ref, dw_scr, pw_scr, dv_ref, dtv_ref)


def tall(rows, cols):
    return pl.BlockSpec((rows, cols), lambda h: (0, h))


def deep(rows, cols):
    return pl.BlockSpec((1, rows, cols), lambda h: (h, 0, 0))


def shared(rows, cols):
    return pl.BlockSpec((rows, cols), lambda h: (0, 0))


def shape_of(dims, dtype):
    return jax.ShapeDtypeStruct(dims, dtype)


def call_heads(kernel, head_count, in_specs, outputs, scratch, args):
    out_specs = [spec for spec, shape in outputs]
    out_shape = [shape for spec, shape in outputs]
    return pl.pallas_call(
        kernel,
        grid=(head_count,),
        in_specs=in_specs,
        out_specs=out_specs,
        out_shape=out_shape,
        scratch_shapes=scratch,
        compiler_params=pltpu.CompilerParams(vmem_limit_bytes=VMEM_BYTES),
        cost_estimate=COST,
    )(*args)


def prepare(x, edge, gain, w_query, w_key, w_value, w_decay, w_beta, rate, conv_query, conv_key, conv_value):
    length, width = x.shape
    heads = w_decay.shape[0]
    states = (length // CHUNK) * KEY
    ncols, wcols = heads * KEY, heads * VALUE
    out_shape = [
        shape_of((length, width), bf16),
        shape_of((length + EDGE, width), bf16),
        shape_of((length, heads), f32),
        shape_of((length + EDGE, ncols), bf16),
        shape_of((length + EDGE, ncols), bf16),
        shape_of((length + EDGE, wcols), bf16),
        shape_of((heads, 1, length), f32),
        shape_of((heads, 1, length), f32),
        shape_of((length, ncols), bf16),
        shape_of((length, ncols), bf16),
        shape_of((length, wcols), bf16),
        shape_of((heads, length, CHUNK), bf16),
        shape_of((heads, length, CHUNK), bf16),
        shape_of((heads, length, VALUE), bf16),
        shape_of((heads, length, KEY), bf16),
        shape_of((heads, states, KEY + VALUE), bf16),
        shape_of((heads, KEY, KEY + VALUE), f32),
    ]
    args = (
        x, edge, gain, w_query, w_key, w_value, w_decay, w_beta, rate, conv_query, conv_key, conv_value
    )
    return pl.pallas_call(
        prep_kernel,
        out_shape=out_shape,
        in_specs=[pl.BlockSpec(memory_space=pltpu.VMEM)] * len(args),
        out_specs=[pl.BlockSpec(memory_space=pltpu.VMEM)] * len(out_shape),
        scratch_shapes=[
            pltpu.VMEM((length + EDGE, wcols), f32),
            pltpu.VMEM((length + EDGE, ncols), f32),
        ],
        compiler_params=pltpu.CompilerParams(vmem_limit_bytes=VMEM_BYTES),
        cost_estimate=COST,
    )(*args)


def run_forward(odd, qn, ld, att, u, w, starts, state_in, gate_pre, gain, w_out):
    length = qn.shape[0]
    heads = ld.shape[0]
    states = starts.shape[1]
    wide = tall(length, VALUE)
    wshape = (length, heads * VALUE)
    outputs = [
        (wide, shape_of(wshape, bf16)),
        (wide, shape_of(wshape, f32)),
        (deep(length, VALUE), shape_of((heads, length, VALUE), bf16)),
        (deep(states, VALUE), shape_of((heads, states, VALUE), bf16)),
        (shared(length // 2, w_out.shape[1]), shape_of((length // 2, w_out.shape[1]), bf16)),
        (shared(length // 2, w_out.shape[1]), shape_of((length // 2, w_out.shape[1]), bf16)),
    ]
    in_specs = [
        pl.BlockSpec(memory_space=pltpu.SMEM),
        tall(length, KEY), deep(1, length), deep(length, CHUNK), deep(length, VALUE), deep(length, KEY),
        deep(states, KEY + VALUE), deep(KEY, VALUE), wide, shared(1, VALUE),
        pl.BlockSpec((VALUE, w_out.shape[1]), lambda h: (h, 0)),
    ]
    args = (odd, qn, ld, att, u, w, starts, state_in, gate_pre, gain, w_out)
    scratch = [pltpu.VMEM((length, w_out.shape[1]), f32)]
    return call_heads(forward_kernel, heads, in_specs, outputs, scratch, args)


def gate_back(dgated, mixed, gate_pre, gain, qn, kn, ld, att, w):
    length = qn.shape[0]
    heads = ld.shape[0]
    states = (length // CHUNK) * KEY
    wide = tall(length, VALUE)
    outputs = [
        (wide, shape_of((length, heads * VALUE), bf16)),
        (deep(length, VALUE), shape_of((heads, length, VALUE), bf16)),
        (deep(length, VALUE), shape_of((heads, length, VALUE), bf16)),
        (deep(1, VALUE), shape_of((heads, 1, VALUE), f32)),
        (deep(states, KEY + VALUE), shape_of((heads, states, KEY + VALUE), bf16)),
        (deep(KEY, KEY + VALUE), shape_of((heads, KEY, KEY + VALUE), f32)),
    ]
    in_specs = [
        wide, wide, wide, shared(1, VALUE), tall(length, KEY), tall(length, KEY), deep(1, length),
        deep(length, CHUNK), deep(length, KEY),
    ]
    args = (dgated, mixed, gate_pre, gain, qn, kn, ld, att, w)
    return call_heads(gate_back_kernel, heads, in_specs, outputs, [], args)


def run_backward(
    gstate, after, dmixed, dcorr, begin, corr, inverse, att, u, w, qn, kn, vn,
    query_ext, key_ext, value_ext, conv_query, conv_key, conv_value, ld, beta,
):
    length = qn.shape[0]
    heads = ld.shape[0]
    states = after.shape[1]
    taps = conv_query.shape[0]
    narrow, wide = tall(length, KEY), tall(length, VALUE)
    ncols, wcols = heads * KEY, heads * VALUE
    outputs = [
        (tall(length + EDGE, KEY), shape_of((length + EDGE, ncols), bf16)),
        (tall(length + EDGE, KEY), shape_of((length + EDGE, ncols), bf16)),
        (tall(length + EDGE, VALUE), shape_of((length + EDGE, wcols), bf16)),
        (tall(taps, KEY), shape_of((taps, ncols), f32)),
        (tall(taps, KEY), shape_of((taps, ncols), f32)),
        (tall(taps, VALUE), shape_of((taps, wcols), f32)),
        (deep(1, length), shape_of((heads, 1, length), f32)),
        (deep(1, length), shape_of((heads, 1, length), f32)),
    ]
    in_specs = [
        deep(KEY, VALUE), deep(states, KEY + VALUE), deep(length, VALUE), deep(length, VALUE),
        deep(states, VALUE), deep(length, VALUE), deep(length, CHUNK), deep(length, CHUNK),
        deep(length, VALUE), deep(length, KEY),
        narrow, narrow, wide,
        tall(length + EDGE, KEY), tall(length + EDGE, KEY), tall(length + EDGE, VALUE),
        tall(taps, KEY), tall(taps, KEY), tall(taps, VALUE),
        deep(1, length), deep(1, length),
    ]
    scratch = [
        pltpu.VMEM((length, KEY), f32), pltpu.VMEM((length, KEY), f32), pltpu.VMEM((length, VALUE), f32),
        pltpu.VMEM((length + 2 * EDGE, KEY), f32), pltpu.VMEM((length + EDGE, KEY), f32),
        pltpu.VMEM((length + 2 * EDGE, VALUE), f32), pltpu.VMEM((length + EDGE, VALUE), f32),
    ]
    args = (
        gstate, after, dmixed, dcorr, begin, corr, inverse, att, u, w, qn, kn, vn,
        query_ext, key_ext, value_ext, conv_query, conv_key, conv_value, ld, beta,
    )
    return call_heads(backward_kernel, heads, in_specs, outputs, scratch, args)


def ffn_kernel(
    odd_ref, x_ref, kept_ref, other_ref, gain_ref, wg_ref, wu_ref, wd_ref, cot_ref,
    normed_ref, hidden_ref, dgate_ref, dup_ref, own_ref, sent_ref,
):
    mine = pl.program_id(0) == odd_ref[0]
    branch = jnp.where(mine, kept_ref[...].astype(f32), other_ref[...].astype(f32))
    middle = x_ref[...].astype(f32) + branch
    normed = row_norm(middle, gain_ref[...]).astype(bf16)
    normed_ref[...] = normed
    gate = dot(normed, wg_ref[...], 1, 1)
    up = dot(normed, wu_ref[...], 1, 1)
    sig = jax.nn.sigmoid(gate)
    act = gate * sig
    hidden_ref[...] = (act * up).astype(bf16)
    dhidden = dot(cot_ref[...], wd_ref[...], 1, 1)
    dgate = (dhidden * up * (sig * (1.0 + gate * (1.0 - sig)))).astype(bf16)
    dup = (dhidden * act).astype(bf16)
    dgate_ref[...] = dgate
    dup_ref[...] = dup
    part = (dot(dgate, wg_ref[...]) + dot(dup, wu_ref[...])).astype(bf16)

    @pl.when(mine)
    def give_own():
        own_ref[...] = part

    @pl.when(jnp.logical_not(mine))
    def give_sent():
        sent_ref[...] = part


def run_ffn(odd, x, kept, other, gain, w_ffn_gate, w_ffn_up, w_ffn_down, cotangent):
    length, width = x.shape
    hidden = w_ffn_gate.shape[0]
    block = length // 2

    def rows(cols):
        return pl.BlockSpec((block, cols), lambda i: (i, 0))

    return pl.pallas_call(
        ffn_kernel,
        grid=(length // block,),
        in_specs=[
            pl.BlockSpec(memory_space=pltpu.SMEM),
            rows(width), shared(block, width), shared(block, width), shared(1, width), shared(hidden, width), shared(hidden, width),
            shared(hidden, width), rows(width),
        ],
        out_specs=[rows(width), rows(hidden), rows(hidden), rows(hidden), shared(block, width), shared(block, width)],
        out_shape=[
            shape_of((length, width), bf16),
            shape_of((length, hidden), bf16),
            shape_of((length, hidden), bf16),
            shape_of((length, hidden), bf16),
            shape_of((block, width), bf16),
            shape_of((block, width), bf16),
        ],
        compiler_params=pltpu.CompilerParams(vmem_limit_bytes=VMEM_BYTES),
        cost_estimate=COST,
    )(odd, x, kept, other, gain, w_ffn_gate, w_ffn_up, w_ffn_down, cotangent)


def shard_kernel(plan, count, piece, places_ref, *refs):
    outs = refs[-2 * len(plan) :]
    for number, pairs in enumerate(plan):
        for which in range(2):
            out_ref = outs[2 * number + which]
            chosen = {}
            at = 0
            for left, right in pairs:
                if left not in chosen:
                    chosen[left] = jnp.concatenate(
                        [
                            refs[left][:, pl.ds(pl.multiple_of(places_ref[number, which, g] * piece, 128), piece)]
                            for g in range(count)
                        ],
                        axis=1,
                    )
                width = refs[right].shape[1]
                out_ref[:, at : at + width] = dot(chosen[left], refs[right][...], 0, 0).astype(out_ref.dtype)
                at += width
            if at < out_ref.shape[1]:
                out_ref[:, at:] = jnp.zeros((out_ref.shape[0], out_ref.shape[1] - at), out_ref.dtype)


def shard_products(chains, home_type):
    size = lax.axis_size("seq")
    here = lax.axis_index("seq")
    count = size // 2
    slots = jnp.arange(count, dtype=jnp.int32)
    places = []
    for bit, pairs in chains:
        shards = (slots // 2**bit) * 2 ** (bit + 1) + slots % 2**bit
        mine = (here // 2**bit) % 2
        places.append(jnp.stack([shards + (1 - mine) * 2**bit, shards + mine * 2**bit]))
    width = chains[0][1][0][0].shape[1]
    piece = width // size
    if piece % 128:
        results = []
        for (bit, pairs), chosen in zip(chains, places):
            parts = []
            for which, kind in ((0, bf16), (1, home_type)):
                columns = [
                    lax.dot_general(
                        jnp.take(left.reshape(-1, size, piece), chosen[which], axis=1).reshape(
                            left.shape[0], -1
                        ),
                        right,
                        (((0,), (0,)), ((), ())),
                        preferred_element_type=f32,
                    )
                    for left, right in pairs
                ]
                parts.append(jnp.concatenate(columns, axis=1).astype(kind))
            results.append(tuple(parts))
        return results
    args, plan, out_shape = [], [], []

    def slot_of(array):
        for number, known in enumerate(args):
            if known is array:
                return number
        args.append(array)
        return len(args) - 1

    for bit, pairs in chains:
        plan.append([(slot_of(left), slot_of(right)) for left, right in pairs])
        total = -(-sum(right.shape[1] for left, right in pairs) // 128) * 128
        out_shape += [shape_of((count * piece, total), bf16), shape_of((count * piece, total), home_type)]
    whole = pl.BlockSpec(memory_space=pltpu.VMEM)
    flat = pl.pallas_call(
        functools.partial(shard_kernel, plan, count, piece),
        in_specs=[pl.BlockSpec(memory_space=pltpu.SMEM)] + [whole] * len(args),
        out_specs=[whole] * len(out_shape),
        out_shape=out_shape,
        compiler_params=pltpu.CompilerParams(vmem_limit_bytes=VMEM_BYTES),
        cost_estimate=COST,
    )(jnp.stack(places), *args)
    return [(flat[2 * number], flat[2 * number + 1]) for number in range(len(chains))]


def turn_kernel(cuts, *refs):
    ins, outs = refs[: len(cuts)], refs[len(cuts) :]
    for (low, high), in_ref, out_ref in zip(cuts, ins, outs):
        out_ref[...] = in_ref[:, low:high].T


def turned(pieces):
    if pieces[0][0].shape[0] % 128:
        return [array[:, low:high].T for array, low, high in pieces]
    whole = pl.BlockSpec(memory_space=pltpu.VMEM)
    return pl.pallas_call(
        functools.partial(turn_kernel, [(low, high) for array, low, high in pieces]),
        in_specs=[whole] * len(pieces),
        out_specs=[whole] * len(pieces),
        out_shape=[shape_of((high - low, array.shape[0]), f32) for array, low, high in pieces],
        compiler_params=pltpu.CompilerParams(vmem_limit_bytes=VMEM_BYTES),
        cost_estimate=COST,
    )(*[array for array, low, high in pieces])


def from_behind(block, axis, distance):
    devices = range(lax.axis_size(axis))
    route = [(i - distance, i) for i in devices if i - distance in devices]
    return lax.ppermute(block, axis, route)


def swap_with(block, axis, distance):
    route = [(i, i ^ distance) for i in range(lax.axis_size(axis))]
    return lax.ppermute(block, axis, route)


def exchange_rounds(tasks, box=None, beside=None):
    results, asked = [None] * len(tasks), {}

    def advance(which, got):
        try:
            asked[which] = tasks[which].send(got)
        except StopIteration as end:
            results[which] = end.value
            asked.pop(which, None)

    for which in range(len(tasks)):
        advance(which, None)
    number = 0
    while asked:
        number += 1
        got = {which: tuple(exchange() for exchange in wanted) for which, wanted in asked.items()}
        names = [name for name in (beside or {}).get(number, ()) if name in box]
        got, values = lax.optimization_barrier((got, [box[name] for name in names]))
        for name, value in zip(names, values):
            box[name] = value
        for which in list(asked):
            advance(which, got[which])
    return results


def swap(block, axis, distance):
    return functools.partial(swap_with, block, axis, distance)


def together(first, second):
    wanted = [next(first)[0], next(second)[0]]
    while True:
        blocks = [exchange.args[0] for exchange in wanted]
        if wanted[0].args[1:] == wanted[1].args[1:]:
            width = blocks[0].shape[-1]
            (both,) = yield [swap(jnp.concatenate(blocks, axis=-1), *wanted[0].args[1:])]
            got = (both[..., :width], both[..., width:])
        else:
            got = yield wanted
        results = []
        for which, task in enumerate((first, second)):
            try:
                wanted[which] = task.send((got[which],))[0]
            except StopIteration as end:
                results.append(end.value)
        if results:
            return results


def pause(rounds):
    for _ in range(rounds):
        yield []


def group_sum(block, axis):
    size = lax.axis_size(axis)
    distance = 1
    while distance < size:
        reach = min(4, size // distance)
        arrived = yield [swap(block, axis, distance * step) for step in range(1, reach)]
        if reach == 4:
            block = (block + arrived[0]) + (arrived[1] + arrived[2])
        else:
            block = block + arrived[0]
        distance *= reach
    return block


def head_is_odd():
    return lax.axis_index("head") % 2


def halves_of(block):
    rows = block.shape[0] // 2
    odd = head_is_odd() == 1
    low, high = block[:rows], block[rows:]
    return jnp.where(odd, high, low), jnp.where(odd, low, high)


def whole_of(halves):
    kept, other = halves
    odd = head_is_odd() == 1
    return jnp.concatenate([jnp.where(odd, other, kept), jnp.where(odd, kept, other)], axis=0)


def sum_over_heads(halves):
    own, sent = halves
    (got,) = yield [swap(sent, "head", 1)]
    own = own.astype(f32) + got.astype(f32)
    distance = 2
    while distance < lax.axis_size("head"):
        sent = own.astype(bf16)
        (got,) = yield [swap(sent, "head", distance)]
        own = sent.astype(f32) + got.astype(f32)
        distance *= 2
    kept = own.astype(bf16)
    (other,) = yield [swap(kept, "head", 1)]
    return kept, other


def exclusive_scan(joined, sign):
    own_t, own_b = joined[..., :KEY], joined[..., KEY:]
    send = joined
    before_t = before_b = None
    distance = 1
    size = lax.axis_size("seq")

    def product(a, b):
        return jnp.einsum("hij,hjk->hik", a, b, precision=lax.Precision.HIGH)

    while distance < size:
        last = distance * 2 >= size
        sent = (send[..., KEY:] if last else send).astype(bf16)
        (got,) = yield [functools.partial(from_behind, sent, "seq", sign * distance)]
        got = got.astype(f32)
        if before_t is None:
            before_t, before_b = got[..., :KEY], got[..., KEY:]
        else:
            moved = product(before_t, got)
            if last:
                before_b = before_b + moved
            else:
                before_t, before_b = moved[..., :KEY], before_b + moved[..., KEY:]
        if not last:
            send = product(own_t, jnp.concatenate([before_t, before_b], axis=-1))
            send = jnp.concatenate([send[..., :KEY], send[..., KEY:] + own_b], axis=-1)
        distance *= 2
    return before_b


def halving_scatter(products, order, pauses=(), box=None, name=None, hold=None):
    size = lax.axis_size("seq")
    bits = size.bit_length() - 1
    here = lax.axis_index("seq")
    order = [bit for bit in order if bit < bits] + list(range(len(order), bits))
    pauses = list(pauses) + [0] * bits
    away, home = products
    (got,) = yield [swap(away, "seq", 2 ** order[0])]
    held = home.astype(f32) + got.astype(f32)
    axes = [bit for bit in range(bits)[::-1] if bit != order[0]]
    held = held.reshape((2,) * (bits - 1) + (held.shape[0] // 2 ** (bits - 1), held.shape[1]))
    for number, bit in enumerate(order[1:]):
        axis = axes.index(bit)
        axes.remove(bit)
        mine = (here // 2**bit) % 2
        sent = lax.dynamic_index_in_dim(held, 1 - mine, axis, keepdims=False).astype(bf16)
        if pauses[number]:
            box[name] = sent
            yield from pause(pauses[number])
            sent = box[name]
        elif hold is not None:
            sent = hold(sent)
        (got,) = yield [swap(sent, "seq", 2**bit)]
        held = lax.dynamic_index_in_dim(held, mine, axis, keepdims=False) + got.astype(f32)
    return held


def inner_rows(first_operand, second_operand):
    return lax.dot_general(
        first_operand, second_operand, (((0,), (0,)), ((), ())), preferred_element_type=f32
    )


def matmul_bf(first_operand, second_operand):
    return jnp.dot(first_operand, second_operand, preferred_element_type=f32)


def against_rows(first_operand, second_operand):
    return lax.dot_general(
        first_operand, second_operand, (((1,), (1,)), ((), ())), preferred_element_type=f32
    )


def per_device(
    block_input,
    norm1_gain,
    w_query,
    w_key,
    w_value,
    w_gate,
    w_decay,
    w_beta,
    conv_query,
    conv_key,
    conv_value,
    decay_rate,
    out_gain,
    w_out,
    norm2_gain,
    w_ffn_gate,
    w_ffn_up,
    w_ffn_down,
    cotangent,
):
    length = block_input.shape[0]
    head_count = w_decay.shape[1]
    key_cols = w_query.shape[1]
    value_cols = w_value.shape[1]
    ff_cols = w_ffn_gate.shape[1]
    edge_input = from_behind(block_input[length - EDGE :], "seq", 1)
    gain1 = norm1_gain.astype(f32)
    (
        normed, normed_ext, decay_cols, query_ext, key_ext, value_ext, log_decay, beta3,
        qn, kn, vn, inverse, att, u, w, starts, composite,
    ) = prepare(
        block_input, edge_input, gain1[None], w_query, w_key, w_value, w_decay.T, w_beta.T,
        decay_rate[None], conv_query, conv_key, conv_value,
    )
    inputs32 = block_input.astype(f32)
    gate_pre = matmul_bf(normed, w_gate)
    box = {"gate": gate_pre}
    (state_in,) = exchange_rounds([exclusive_scan(composite, 1)], box, {1: ["gate"]})
    gate_pre = box["gate"]
    gain_row = out_gain.astype(f32)[None]
    odd = head_is_odd().astype(jnp.int32).reshape(1)
    gated, mixed, corr, begin, branch_own, branch_sent = run_forward(
        odd,
        qn, log_decay, att, u, w, starts, state_in, gate_pre, gain_row, w_out
    )
    (branch_halves,) = exchange_rounds([sum_over_heads((branch_own, branch_sent))])
    branch = whole_of(branch_halves)
    gain2 = norm2_gain.astype(f32)
    normed2, hidden, grad_fgate, grad_fup, part_own, part_sent = run_ffn(
        odd, block_input, *branch_halves, gain2[None], w_ffn_gate.T, w_ffn_up.T, w_ffn_down, cotangent
    )
    bits = lax.axis_size("seq").bit_length() - 1
    near, far = 0, min(1, bits - 1)
    half = ff_cols // 2 // 128 * 128
    ffn_near, ffn_far = shard_products(
        [
            (near, [(normed2, grad_fgate), (cotangent, hidden[:, :half])]),
            (far, [(normed2, grad_fup), (cotangent, hidden[:, half:])]),
        ],
        bf16,
    )
    box = {}

    def after_scan(sent):
        return lax.optimization_barrier((sent, box["state"]))[0]

    ffn_tasks = [
        halving_scatter(ffn_near, [0, 1], [bits - 2, 0], box, "sent near", after_scan),
        halving_scatter(ffn_far, [1, 0], [bits - 2, 0], box, "sent far", after_scan),
    ]
    ffn_got = [tuple(exchange() for exchange in next(task)) for task in ffn_tasks]
    box["away"] = (ffn_near[0], ffn_far[0])
    (back_halves,) = exchange_rounds([sum_over_heads((part_own, part_sent))], box, {2: ["away"]})
    grad_normed2 = whole_of(back_halves).astype(f32)
    middle = inputs32 + branch.astype(f32)
    norm2_back = jax.vjp(row_norm, middle, gain2)[1]
    ffn_part = matmul_bf(hidden, w_ffn_down).astype(bf16)
    grad_middle_n, grad_gain2 = norm2_back(grad_normed2)
    grad_middle = cotangent.astype(f32) + grad_middle_n
    grad_branch = grad_middle.astype(bf16)
    grad_gated = against_rows(grad_branch, w_out)
    grad_gp, grad_mixed, grad_corr, grad_outgain, after, composite_back = gate_back(
        grad_gated, mixed, gate_pre, gain_row, qn, kn, log_decay, att, w
    )
    box["ffn part"] = ffn_part
    box["scalars"] = (decay_cols, decay_rate)
    pad_rows = ((length - 8, 0), (0, 0))
    taps_count = conv_query.shape[0]
    width = w_query.shape[0]

    def main_task():
        grad_state = yield from exclusive_scan(composite_back, -1)
        box["state"] = grad_state
        dq, dk, dv, taps_q, taps_k, taps_v, grad_log, grad_beta = run_backward(
            grad_state, after, grad_mixed, grad_corr, begin, corr, inverse, att, u, w,
            qn, kn, vn, query_ext, key_ext, value_ext,
            conv_query, conv_key, conv_value, log_decay, beta3,
        )
        box["late"] = shard_products(
            [(near, [(normed_ext, dq), (normed_ext, dk)]), (far, [(normed_ext, dv)])], f32
        )
        part_ext = against_rows(dq, w_query) + against_rows(dk, w_key) + against_rows(dv, w_value)
        decay_now, rate_now = box["scalars"]
        decay_pre = decay_now.T
        soft = jax.nn.softplus(decay_pre)
        rate = rate_now[:, None]
        beta_gate = beta3.reshape(head_count, length)
        grad_log = grad_log.reshape(head_count, length)
        grad_beta = grad_beta.reshape(head_count, length)
        grad_dp = (-rate * jax.nn.sigmoid(decay_pre) * grad_log).astype(bf16)
        grad_bp = (beta_gate * (1.0 - beta_gate) * grad_beta).astype(bf16)
        grad_rate = -jnp.sum(grad_log * soft, axis=1)
        grad_scalars = jnp.concatenate([grad_dp, grad_bp], axis=0)
        w_scalars = jnp.concatenate([w_decay, w_beta], axis=1)
        edges = part_ext[EDGE - 8 : EDGE]
        part = (
            part_ext[EDGE:]
            + against_rows(grad_gp, w_gate)
            + lax.dot_general(
                grad_scalars, w_scalars, (((0,), (1,)), ((), ())), preferred_element_type=f32
            )
        )
        edge_normal = row_norm(edge_input[EDGE - 8 :].astype(f32), 1.0)
        gain_part = jnp.sum(part * row_norm(inputs32, 1.0), axis=0) + jnp.sum(edges * edge_normal, axis=0)
        gains = jnp.concatenate([gain_part, jnp.sum(grad_outgain, axis=(0, 1))])
        box["shared"] = jnp.pad(gains, (0, 2 * width - gains.shape[0])).reshape(-1, 128)
        box["small"] = jnp.concatenate(
            [
                jnp.concatenate([taps_q, taps_k, taps_v], axis=1),
                grad_gain2[None],
                jnp.pad(grad_rate, (0, width - head_count))[None],
                matmul_bf(grad_scalars, normed),
            ],
            axis=0,
        )
        (edges,) = yield [functools.partial(from_behind, edges, "seq", -1)]
        part = part + jnp.pad(edges, pad_rows)
        kept, other = yield from sum_over_heads(halves_of(part.astype(bf16)))
        return whole_of((kept, other))

    def ffn_rest(task, got, name):
        wanted = [lambda block=block: block for block in got]
        try:
            while True:
                wanted = task.send((yield wanted))
        except StopIteration as end:
            held = end.value
        box[name] = turned([(held, 0, ff_cols), (held, ff_cols, ff_cols + (half if name == "near" else ff_cols - half))])

    def ffn_sum_task():
        yield from pause(1)
        steps = sum_over_heads(halves_of(box["ffn part"]))
        got = yield next(steps)
        wanted = steps.send(got)
        yield from pause(bits - 2)
        try:
            while True:
                wanted = steps.send((yield wanted))
        except StopIteration as end:
            box["out"] = (middle + whole_of(end.value).astype(f32)).astype(bf16)

    def mid_task():
        yield from pause(bits)
        products = shard_products([(near, [(grad_branch, gated)]), (far, [(normed, grad_gp)])], f32)
        products = after_scan(products)
        first, second = halving_scatter(products[0], [0, 1]), halving_scatter(products[1], [1, 0])
        grad_wout, grad_wg = yield from together(first, second)
        box["mid"] = (*turned([(grad_wout, 0, grad_wout.shape[1])]), grad_wg)

    def late_task():
        yield from pause(bits + 1)
        first, second = box["late"]
        return (yield from together(halving_scatter(first, [0, 1]), halving_scatter(second, [1, 0])))

    def small_task():
        yield from pause(bits + 1)
        shared = yield from group_sum(box["shared"], "head")
        rows = jnp.concatenate([box["small"], shared.reshape(-1, width)], axis=0)
        return (yield from group_sum(rows, "seq"))

    grad_normed, late, small = exchange_rounds(
        [main_task(), late_task(), small_task(), mid_task(), ffn_sum_task()]
        + [ffn_rest(task, got, name) for task, got, name in zip(ffn_tasks, ffn_got, ("near", "far"))],
        box,
        {1: ["ffn part", "scalars"], 2: ["sent near", "sent far"], bits + 2: ["near", "far"], bits + 3: ["out"]},
    )[:3]
    late_qk, late_v = late
    grad_wout, grad_wg = box["mid"]
    grad_wfg, down_near = box["near"]
    grad_wfu, down_far = box["far"]
    layer_out = box["out"]
    shared_sum = small[-2:].reshape(-1)
    norm1_back = jax.vjp(row_norm, inputs32, gain1)[1]
    grad_input = grad_middle + norm1_back(grad_normed.astype(f32))[0]
    taps_sum = small[:taps_count]
    gain2_sum = small[taps_count]
    rate_sum = small[taps_count + 1, :head_count]
    scalars_sum = small[taps_count + 2 : taps_count + 2 + 2 * head_count]
    gain1_sum, outgain_sum = shared_sum[:width], shared_sum[width : width + VALUE]

    def own_part(vec):
        piece = vec.shape[-1] // lax.axis_size("seq")
        return lax.dynamic_slice_in_dim(vec, lax.axis_index("seq") * piece, piece, axis=-1)

    scalars_sum = own_part(scalars_sum).T
    return (
        layer_out,
        grad_input,
        own_part(gain1_sum),
        late_qk[:, :key_cols],
        late_qk[:, key_cols:],
        late_v,
        grad_wg,
        scalars_sum[:, :head_count],
        scalars_sum[:, head_count:],
        taps_sum[:, :key_cols],
        taps_sum[:, key_cols : 2 * key_cols],
        taps_sum[:, 2 * key_cols :],
        rate_sum,
        own_part(outgain_sum),
        grad_wout,
        own_part(gain2_sum),
        grad_wfg.T,
        grad_wfu.T,
        jnp.concatenate([down_near, down_far], axis=0),
    )


def solution(mesh):
    return jax.shard_map(
        per_device,
        mesh=mesh,
        in_specs=(
            P("seq", None),
            P(),
            P(None, "head"),
            P(None, "head"),
            P(None, "head"),
            P(None, "head"),
            P(None, "head"),
            P(None, "head"),
            P(None, "head"),
            P(None, "head"),
            P(None, "head"),
            P("head"),
            P(),
            P("head", None),
            P(),
            P(None, "head"),
            P(None, "head"),
            P("head", None),
            P("seq", None),
        ),
        out_specs=(
            P("seq", None),
            P("seq", None),
            P("seq"),
            P("seq", "head"),
            P("seq", "head"),
            P("seq", "head"),
            P("seq", "head"),
            P("seq", "head"),
            P("seq", "head"),
            P(None, "head"),
            P(None, "head"),
            P(None, "head"),
            P("head"),
            P("seq"),
            P("head", "seq"),
            P("seq"),
            P("seq", "head"),
            P("seq", "head"),
            P("head", "seq"),
        ),
        check_vma=False,
    )
```

```python
import functools

import jax
import jax.numpy as jnp
from jax import lax
from jax.experimental import pallas as pl
from jax.experimental.pallas import tpu as pltpu
from jax.sharding import PartitionSpec as P

KEY = 128
VALUE = 256
CHUNK = 128
EDGE = 16
SUB = 16
VMEM_BYTES = 60 * 1024 * 1024
COST = pl.CostEstimate(flops=0, bytes_accessed=0, transcendentals=0)

epsilon = 1e-06
f32 = jnp.float32
bf16 = jnp.bfloat16
highest_precision = lax.Precision.HIGHEST


def dot(first, second, over_first=1, over_second=0):
    return lax.dot_general(
        first.astype(bf16),
        second.astype(bf16),
        (((over_first,), (over_second,)), ((), ())),
        preferred_element_type=f32,
    )


def halves(values):
    high = values.astype(bf16)
    return high, (values - high.astype(f32)).astype(bf16)


def dot_fine(first, second):
    first_high, first_low = halves(first)
    second_high, second_low = halves(second)
    width = second.shape[1]
    wide = dot(first_high, jnp.concatenate([second_high, second_low], axis=1))
    return wide[:, :width] + wide[:, width:] + dot(first_low, second_high)


def grid_places(extent):
    rows = lax.broadcasted_iota(jnp.int32, (extent, extent), 0)
    cols = lax.broadcasted_iota(jnp.int32, (extent, extent), 1)
    return rows, cols


def as_row(column, diagonal):
    return jnp.sum(jnp.where(diagonal, column, 0.0), axis=0, keepdims=True)


def as_column(row, diagonal):
    return jnp.sum(jnp.where(diagonal, row, 0.0), axis=1, keepdims=True)


def unit_lower_inverses(systems, rows, cols):
    extent = systems[0].shape[0]
    count = extent // SUB
    units = len(systems)
    same = rows // SUB == cols // SUB
    packed = jnp.concatenate(
        [jnp.sum(jnp.where(same, s, 0.0).reshape(count, SUB, extent), axis=0) for s in systems], axis=0
    )
    stacked = jnp.concatenate(halves(packed), axis=0)
    shape = (units, SUB, extent)
    places = lax.broadcasted_iota(jnp.int32, shape, 1)
    solved = (places == lax.broadcasted_iota(jnp.int32, shape, 2) % SUB).astype(f32)
    for j in range(SUB - 1):
        spread = dot(stacked, (same & (rows % SUB == j)).astype(f32))
        column = spread[: units * SUB] + spread[units * SUB :]
        solved = solved - column.reshape(shape) * solved[:, j : j + 1, :]
    inverses = [
        jnp.where(same, jnp.concatenate([solved[n]] * count, axis=0), 0.0) for n in range(units)
    ]
    size = SUB
    while size < extent:
        below = (rows // (2 * size) == cols // (2 * size)) & (rows // size > cols // size)
        joined = [
            dot_fine(inverse, jnp.where(below, s, 0.0)) for inverse, s in zip(inverses, systems)
        ]
        joined = [dot_fine(product, inverse) for product, inverse in zip(joined, inverses)]
        inverses = [inverse - product for inverse, product in zip(inverses, joined)]
        size *= 2
    return inverses


def decay_terms(ld_row, rows, cols):
    cum_col = jnp.sum(jnp.where(rows >= cols, ld_row, 0.0), axis=1, keepdims=True)
    cum_row = as_row(cum_col, rows == cols)
    last = cum_col[CHUNK - 1 :, :]
    between = jnp.where(rows >= cols, jnp.exp(jnp.where(rows >= cols, cum_col - cum_row, 0.0)), 0.0)
    return between, jnp.exp(cum_col), jnp.exp(last - cum_col), jnp.exp(last)


def conv_sum(padded_ref, taps_ref, length):
    taps = taps_ref[...].astype(f32)
    summed = taps[0:1] * padded_ref[EDGE : EDGE + length, :]
    for offset in range(1, taps_ref.shape[0]):
        summed = summed + taps[offset : offset + 1] * padded_ref[EDGE - offset : EDGE - offset + length, :]
    return summed


def unit_rows(values, scale, heads):
    parts = []
    for h in range(heads):
        part = values[:, h * KEY : (h + 1) * KEY]
        parts.append(
            part * (lax.rsqrt(jnp.sum(part * part, axis=-1, keepdims=True) + epsilon) * scale)
        )
    return jnp.concatenate(parts, axis=1)


def row_norm(values, gain_vec):
    return (
        values * lax.rsqrt(jnp.mean(values * values, axis=-1, keepdims=True) + epsilon) * gain_vec
    )


def prep_kernel(
    x_ref, edge_ref, gain_ref, wq_ref, wk_ref, wv_ref, wd_ref, wb_ref, rate_ref, tq_ref, tk_ref, tv_ref,
    normed_ref, normed_ext_ref, decay_ref, q_ref, k_ref, v_ref, ld_ref, beta_ref,
    qn_ref, kn_ref, vn_ref, inv_ref, att_ref, u_ref, w_ref, start_ref, final_ref,
    wide_scr, narrow_scr,
):
    length = qn_ref.shape[0]
    heads = ld_ref.shape[0]
    chunks = length // CHUNK
    gain = gain_ref[...]
    normed_ext_ref[:EDGE, :] = row_norm(edge_ref[...].astype(f32), gain).astype(bf16)
    normed = row_norm(x_ref[...].astype(f32), gain).astype(bf16)
    normed_ext_ref[EDGE:, :] = normed
    normed_ref[...] = normed
    decay_pre = dot(normed, wd_ref[...], 1, 1)
    decay_ref[...] = decay_pre
    softplus = jnp.maximum(decay_pre, 0.0) + jnp.log1p(jnp.exp(-jnp.abs(decay_pre)))
    log_decay = -rate_ref[...] * softplus
    beta_gate = jax.nn.sigmoid(dot(normed, wb_ref[...], 1, 1))
    pre = dot(normed_ext_ref[...], wk_ref[...]).astype(bf16)
    k_ref[...] = pre
    narrow_scr[...] = pre.astype(f32)
    z = conv_sum(narrow_scr, tk_ref, length)
    kn_ref[...] = unit_rows(z * jax.nn.sigmoid(z), 1.0, heads).astype(bf16)
    pre = dot(normed_ext_ref[...], wq_ref[...]).astype(bf16)
    q_ref[...] = pre
    narrow_scr[...] = pre.astype(f32)
    z = conv_sum(narrow_scr, tq_ref, length)
    qn_ref[...] = unit_rows(z * jax.nn.sigmoid(z), KEY ** (-0.5), heads).astype(bf16)
    pre = dot(normed_ext_ref[...], wv_ref[...]).astype(bf16)
    v_ref[...] = pre
    wide_scr[...] = pre.astype(f32)
    z = conv_sum(wide_scr, tv_ref, length)
    vn_ref[...] = (z * jax.nn.sigmoid(z)).astype(bf16)

    rows, cols = grid_places(CHUNK)
    diagonal = rows == cols
    units = [(h, c) for c in range(chunks) for h in range(heads)]
    systems, vectors = [], []
    for h, c in units:
        at = slice(c * CHUNK, (c + 1) * CHUNK)
        keyed = slice(h * KEY, (h + 1) * KEY)
        ld_row = as_row(log_decay[at, h : h + 1], diagonal)
        ld_ref[h, :, at] = ld_row
        between, grow, tail, whole = decay_terms(ld_row, rows, cols)
        beta = beta_gate[at, h : h + 1]
        beta_ref[h, :, at] = as_row(beta, diagonal)
        keys = kn_ref[at, keyed]
        products = dot(jnp.concatenate([keys, qn_ref[at, keyed]], axis=0), keys, 1, 1)
        systems.append(jnp.where(rows > cols, beta * between * products[:CHUNK], 0.0))
        att_ref[h, at, :] = (products[CHUNK:] * between).astype(bf16)
        vectors.append((beta, grow, tail, whole))
    inverses = unit_lower_inverses(systems, rows, cols)
    kept = []
    for (h, c), inverse, (beta, grow, tail, whole) in zip(units, inverses, vectors):
        at = slice(c * CHUNK, (c + 1) * CHUNK)
        keys32 = kn_ref[at, h * KEY : (h + 1) * KEY].astype(f32)
        values32 = vn_ref[at, h * VALUE : (h + 1) * VALUE].astype(f32)
        inv_ref[h, at, :] = inverse.astype(bf16)
        solved = dot(inverse, jnp.concatenate([(beta * grow) * keys32, beta * values32], axis=1))
        w_ref[h, at, :] = solved[:, :KEY].astype(bf16)
        u_ref[h, at, :] = solved[:, KEY:].astype(bf16)
        kept.append((tail * keys32).astype(bf16))
    begin = jnp.concatenate([diagonal.astype(f32), jnp.zeros((KEY, VALUE), f32)], axis=1)
    states = [begin] * heads
    for (h, c), tail_keys, (beta, grow, tail, whole) in zip(units, kept, vectors):
        at = slice(c * CHUNK, (c + 1) * CHUNK)
        state = states[h]
        start_ref[h, c * KEY : (c + 1) * KEY, :] = state.astype(bf16)
        source = jnp.concatenate([jnp.zeros((CHUNK, KEY), f32), u_ref[h, at, :].astype(f32)], axis=1)
        corrected = source - dot(w_ref[h, at, :], state)
        states[h] = whole * state + dot(tail_keys, corrected, 0, 0)
    for h in range(heads):
        final_ref[h, :, :] = states[h]


def forward_kernel(
    odd_ref, qn_ref, ld_ref, att_ref, u_ref, w_ref, start_ref, state_ref, gate_ref, gain_ref, wout_ref,
    gated_ref, mixed_ref, corr_ref, begin_ref, own_ref, sent_ref, sum_scr,
):
    length = qn_ref.shape[0]
    rows, cols = grid_places(CHUNK)
    entering = state_ref[0]
    gain = gain_ref[...]
    for c in range(length // CHUNK):
        at = slice(c * CHUNK, (c + 1) * CHUNK)
        places = slice(c * KEY, (c + 1) * KEY)
        between, grow, tail, whole = decay_terms(ld_ref[0, :, at], rows, cols)
        begin = start_ref[0, places, KEY:].astype(f32) + dot(start_ref[0, places, :KEY], entering)
        begin_ref[0, places, :] = begin.astype(bf16)
        corrected = u_ref[0, at, :].astype(f32) - dot(w_ref[0, at, :], begin)
        corr_ref[0, at, :] = corrected.astype(bf16)
        mixed = dot(grow * qn_ref[at, :].astype(f32), begin) + dot(att_ref[0, at, :], corrected)
        mixed_ref[at, :] = mixed
        root = lax.rsqrt(jnp.mean(mixed * mixed, axis=-1, keepdims=True) + epsilon)
        gate = gate_ref[at, :]
        gated_ref[at, :] = (mixed * root * gain * (gate * jax.nn.sigmoid(gate))).astype(bf16)
    part = dot(gated_ref[...], wout_ref[...])

    @pl.when(pl.program_id(0) == 0)
    def start_sum():
        sum_scr[...] = part

    @pl.when(pl.program_id(0) > 0)
    def add_sum():
        sum_scr[...] += part

    @pl.when(pl.program_id(0) == pl.num_programs(0) - 1)
    def give_sum():
        half = length // 2
        at = pl.multiple_of(odd_ref[0] * half, half)
        own_ref[...] = sum_scr[pl.ds(at, half), :].astype(bf16)
        sent_ref[...] = sum_scr[pl.ds(pl.multiple_of(half - at, half), half), :].astype(bf16)


def gate_back_kernel(
    dgated_ref, mixed_ref, gate_ref, gain_ref, qn_ref, kn_ref, ld_ref, att_ref, w_ref,
    dgate_ref, dmixed_ref, dcorr_ref, dgain_ref, after_ref, final_ref,
):
    length = qn_ref.shape[0]
    rows, cols = grid_places(CHUNK)
    gain = gain_ref[...]
    kept = []
    dgain = jnp.zeros((1, VALUE), f32)
    for c in range(length // CHUNK):
        at = slice(c * CHUNK, (c + 1) * CHUNK)
        mixed, gate, dgated = mixed_ref[at, :], gate_ref[at, :], dgated_ref[at, :]
        root = lax.rsqrt(jnp.mean(mixed * mixed, axis=-1, keepdims=True) + epsilon)
        normal = mixed * root
        sig = jax.nn.sigmoid(gate)
        act = gate * sig
        dgain = dgain + jnp.sum(dgated * normal * act, axis=0, keepdims=True)
        dgate_ref[at, :] = (dgated * normal * gain * (sig * (1.0 + gate * (1.0 - sig)))).astype(bf16)
        dnormal = dgated * act * gain
        dmixed = root * (dnormal - normal * jnp.mean(dnormal * normal, axis=-1, keepdims=True))
        dmixed_ref[0, at, :] = dmixed.astype(bf16)
        between, grow, tail, whole = decay_terms(ld_ref[0, :, at], rows, cols)
        dcorr = dot(att_ref[0, at, :], dmixed, 0, 0)
        dcorr_ref[0, at, :] = dcorr.astype(bf16)
        gradient = dot(grow * qn_ref[at, :].astype(f32), dmixed, 0, 0) - dot(w_ref[0, at, :], dcorr, 0, 0)
        kept.append((gradient, (tail * kn_ref[at, :].astype(f32)).astype(bf16), whole))
    dgain_ref[0, :, :] = dgain
    pending = jnp.concatenate([(rows == cols).astype(f32), jnp.zeros((KEY, VALUE), f32)], axis=1)
    for c in reversed(range(length // CHUNK)):
        gradient, tail_keys, whole = kept[c]
        at = slice(c * CHUNK, (c + 1) * CHUNK)
        after_ref[0, c * KEY : (c + 1) * KEY, :] = pending.astype(bf16)
        source = jnp.concatenate([jnp.zeros((KEY, KEY), f32), gradient], axis=1)
        pending = whole * pending + source - dot(w_ref[0, at, :], dot(tail_keys, pending), 0, 0)
    final_ref[0, :, :] = pending


def silu_slope(z):
    sig = jax.nn.sigmoid(z)
    return z * sig, sig * (1.0 + z * (1.0 - sig))


def conv_back(dz, taps_ref, dz_scr, pre_scr, dpre_ref, dtaps_ref):
    length = dz.shape[0]
    reach = taps_ref.shape[0] - 1
    taps = taps_ref[...].astype(f32)
    dz_scr[EDGE : EDGE + length, :] = dz
    total = taps[0:1] * dz
    sums = [jnp.sum(dz * pre_scr[EDGE : EDGE + length, :], axis=0, keepdims=True)]
    for offset in range(1, reach + 1):
        total = total + taps[offset : offset + 1] * dz_scr[EDGE + offset : EDGE + offset + length, :]
        sums.append(
            jnp.sum(dz * pre_scr[EDGE - offset : EDGE - offset + length, :], axis=0, keepdims=True)
        )
    dpre_ref[EDGE:, :] = total.astype(bf16)
    edge = taps[1:2] * dz_scr[EDGE - 7 : EDGE + 1, :]
    for offset in range(2, reach + 1):
        edge = edge + taps[offset : offset + 1] * dz_scr[EDGE - 8 + offset : EDGE + offset, :]
    dpre_ref[:EDGE, :] = jnp.concatenate([jnp.zeros_like(edge), edge], axis=0).astype(bf16)
    dtaps_ref[...] = jnp.concatenate(sums, axis=0)


def backward_kernel(
    gstate_ref, after_ref, dmixed_ref, dcorr_ref, begin_ref, corr_ref, inv_ref, att_ref, u_ref, w_ref,
    qn_ref, kn_ref, vn_ref, q_ref, k_ref, v_ref, tq_ref, tk_ref, tv_ref,
    ld_ref, beta_ref,
    dq_ref, dk_ref, dv_ref, dtq_ref, dtk_ref, dtv_ref, dld_ref, dbeta_ref,
    dqn_scr, dkn_scr, dvn_scr, dn_scr, pn_scr, dw_scr, pw_scr,
):
    length = qn_ref.shape[0]
    rows, cols = grid_places(CHUNK)
    diagonal = rows == cols
    leaving = gstate_ref[0]
    for c in range(length // CHUNK):
        at = slice(c * CHUNK, (c + 1) * CHUNK)
        places = slice(c * KEY, (c + 1) * KEY)
        between, grow, tail, whole = decay_terms(ld_ref[0, :, at], rows, cols)
        beta = as_column(beta_ref[0, :, at], diagonal)
        keys, queries = kn_ref[at, :], qn_ref[at, :]
        keys32, queries32, values32 = keys.astype(f32), queries.astype(f32), vn_ref[at, :].astype(f32)
        dstate = after_ref[0, places, KEY:].astype(f32) + dot(after_ref[0, places, :KEY], leaving)
        dmixed, corrected, begin = dmixed_ref[0, at, :], corr_ref[0, at, :], begin_ref[0, places, :]
        dcorr = dcorr_ref[0, at, :].astype(f32) + dot(tail * keys32, dstate)
        datt = dot(dmixed, corrected, 1, 1)
        from_begin = dot(jnp.concatenate([dmixed, dcorr.astype(bf16)], axis=0), begin, 1, 1)
        dgrown, dw = from_begin[:CHUNK], -from_begin[CHUNK:]
        dtail_keys = dot(corrected, dstate, 1, 1)
        dwhole = jnp.sum(dstate * begin.astype(f32))
        back = dot(inv_ref[0, at, :], jnp.concatenate([dw, dcorr], axis=1), 0, 0)
        dright_keys, dright_values = back[:, :KEY], back[:, KEY:]
        dsystem = -dot(
            back, jnp.concatenate([w_ref[0, at, :], u_ref[0, at, :]], axis=1), 1, 1
        )
        products = dot(jnp.concatenate([keys, queries], axis=0), keys, 1, 1)
        decayed = jnp.where(rows > cols, between * products[:CHUNK], 0.0)
        dsys_decayed = dsystem * decayed
        dbeta = jnp.sum(dsys_decayed, axis=1, keepdims=True)
        pairs = beta * dsys_decayed + datt * (between * products[CHUNK:])
        dkk = jnp.where(rows > cols, dsystem * (beta * between), 0.0)
        dqk = datt * between
        dqk16, dkk16 = dqk.astype(bf16), dkk.astype(bf16)
        dqn_scr[at, :] = dot(dqk16, keys) + grow * dgrown
        dkn_scr[at, :] = (
            dot(jnp.concatenate([dqk16, dkk16], axis=0), jnp.concatenate([queries, keys], axis=0), 0, 0)
            + dot(dkk16, keys)
            + tail * dtail_keys
            + (beta * grow) * dright_keys
        )
        dvn_scr[at, :] = beta * dright_values
        keys_part = grow * jnp.sum(dright_keys * keys32, axis=1, keepdims=True)
        dbeta = dbeta + jnp.sum(dright_values * values32, axis=1, keepdims=True) + keys_part
        from_tail = tail * jnp.sum(dtail_keys * keys32, axis=1, keepdims=True)
        dcum = (
            jnp.sum(pairs, axis=1, keepdims=True)
            - as_column(jnp.sum(pairs, axis=0, keepdims=True), diagonal)
            + grow * jnp.sum(dgrown * queries32, axis=1, keepdims=True)
            + beta * keys_part
            - from_tail
        )
        dlast = whole * dwhole + jnp.sum(from_tail, axis=0, keepdims=True)
        dld_ref[0, :, at] = jnp.sum(jnp.where(rows >= cols, dcum, 0.0), axis=0, keepdims=True) + dlast
        dbeta_ref[0, :, at] = as_row(dbeta, diagonal)

    for scr in (dn_scr, dw_scr):
        scr[0:EDGE, :] = jnp.zeros((EDGE, scr.shape[1]), f32)
        scr[EDGE + length :, :] = jnp.zeros((EDGE, scr.shape[1]), f32)
    pn_scr[...] = q_ref[...].astype(f32)
    act, slope = silu_slope(conv_sum(pn_scr, tq_ref, length))
    root = lax.rsqrt(jnp.sum(act * act, axis=-1, keepdims=True) + epsilon)
    normal = act * root
    dy = dqn_scr[...] * KEY ** (-0.5)
    dz = root * (dy - normal * jnp.sum(normal * dy, axis=-1, keepdims=True)) * slope
    conv_back(dz, tq_ref, dn_scr, pn_scr, dq_ref, dtq_ref)
    pn_scr[...] = k_ref[...].astype(f32)
    act, slope = silu_slope(conv_sum(pn_scr, tk_ref, length))
    root = lax.rsqrt(jnp.sum(act * act, axis=-1, keepdims=True) + epsilon)
    normal = act * root
    dy = dkn_scr[...]
    dz = root * (dy - normal * jnp.sum(normal * dy, axis=-1, keepdims=True)) * slope
    conv_back(dz, tk_ref, dn_scr, pn_scr, dk_ref, dtk_ref)
    pw_scr[...] = v_ref[...].astype(f32)
    act, slope = silu_slope(conv_sum(pw_scr, tv_ref, length))
    conv_back(dvn_scr[...] * slope, tv_ref, dw_scr, pw_scr, dv_ref, dtv_ref)


def tall(rows, cols):
    return pl.BlockSpec((rows, cols), lambda h: (0, h))


def deep(rows, cols):
    return pl.BlockSpec((1, rows, cols), lambda h: (h, 0, 0))


def shared(rows, cols):
    return pl.BlockSpec((rows, cols), lambda h: (0, 0))


def shape_of(dims, dtype):
    return jax.ShapeDtypeStruct(dims, dtype)


def call_heads(kernel, head_count, in_specs, outputs, scratch, args):
    out_specs = [spec for spec, shape in outputs]
    out_shape = [shape for spec, shape in outputs]
    return pl.pallas_call(
        kernel,
        grid=(head_count,),
        in_specs=in_specs,
        out_specs=out_specs,
        out_shape=out_shape,
        scratch_shapes=scratch,
        compiler_params=pltpu.CompilerParams(vmem_limit_bytes=VMEM_BYTES),
        cost_estimate=COST,
    )(*args)


def prepare(x, edge, gain, w_query, w_key, w_value, w_decay, w_beta, rate, conv_query, conv_key, conv_value):
    length, width = x.shape
    heads = w_decay.shape[0]
    states = (length // CHUNK) * KEY
    ncols, wcols = heads * KEY, heads * VALUE
    out_shape = [
        shape_of((length, width), bf16),
        shape_of((length + EDGE, width), bf16),
        shape_of((length, heads), f32),
        shape_of((length + EDGE, ncols), bf16),
        shape_of((length + EDGE, ncols), bf16),
        shape_of((length + EDGE, wcols), bf16),
        shape_of((heads, 1, length), f32),
        shape_of((heads, 1, length), f32),
        shape_of((length, ncols), bf16),
        shape_of((length, ncols), bf16),
        shape_of((length, wcols), bf16),
        shape_of((heads, length, CHUNK), bf16),
        shape_of((heads, length, CHUNK), bf16),
        shape_of((heads, length, VALUE), bf16),
        shape_of((heads, length, KEY), bf16),
        shape_of((heads, states, KEY + VALUE), bf16),
        shape_of((heads, KEY, KEY + VALUE), f32),
    ]
    args = (
        x, edge, gain, w_query, w_key, w_value, w_decay, w_beta, rate, conv_query, conv_key, conv_value
    )
    return pl.pallas_call(
        prep_kernel,
        out_shape=out_shape,
        in_specs=[pl.BlockSpec(memory_space=pltpu.VMEM)] * len(args),
        out_specs=[pl.BlockSpec(memory_space=pltpu.VMEM)] * len(out_shape),
        scratch_shapes=[
            pltpu.VMEM((length + EDGE, wcols), f32),
            pltpu.VMEM((length + EDGE, ncols), f32),
        ],
        compiler_params=pltpu.CompilerParams(vmem_limit_bytes=VMEM_BYTES),
        cost_estimate=COST,
    )(*args)


def run_forward(odd, qn, ld, att, u, w, starts, state_in, gate_pre, gain, w_out):
    length = qn.shape[0]
    heads = ld.shape[0]
    states = starts.shape[1]
    wide = tall(length, VALUE)
    wshape = (length, heads * VALUE)
    outputs = [
        (wide, shape_of(wshape, bf16)),
        (wide, shape_of(wshape, f32)),
        (deep(length, VALUE), shape_of((heads, length, VALUE), bf16)),
        (deep(states, VALUE), shape_of((heads, states, VALUE), bf16)),
        (shared(length // 2, w_out.shape[1]), shape_of((length // 2, w_out.shape[1]), bf16)),
        (shared(length // 2, w_out.shape[1]), shape_of((length // 2, w_out.shape[1]), bf16)),
    ]
    in_specs = [
        pl.BlockSpec(memory_space=pltpu.SMEM),
        tall(length, KEY), deep(1, length), deep(length, CHUNK), deep(length, VALUE), deep(length, KEY),
        deep(states, KEY + VALUE), deep(KEY, VALUE), wide, shared(1, VALUE),
        pl.BlockSpec((VALUE, w_out.shape[1]), lambda h: (h, 0)),
    ]
    args = (odd, qn, ld, att, u, w, starts, state_in, gate_pre, gain, w_out)
    scratch = [pltpu.VMEM((length, w_out.shape[1]), f32)]
    return call_heads(forward_kernel, heads, in_specs, outputs, scratch, args)


def gate_back(dgated, mixed, gate_pre, gain, qn, kn, ld, att, w):
    length = qn.shape[0]
    heads = ld.shape[0]
    states = (length // CHUNK) * KEY
    wide = tall(length, VALUE)
    outputs = [
        (wide, shape_of((length, heads * VALUE), bf16)),
        (deep(length, VALUE), shape_of((heads, length, VALUE), bf16)),
        (deep(length, VALUE), shape_of((heads, length, VALUE), bf16)),
        (deep(1, VALUE), shape_of((heads, 1, VALUE), f32)),
        (deep(states, KEY + VALUE), shape_of((heads, states, KEY + VALUE), bf16)),
        (deep(KEY, KEY + VALUE), shape_of((heads, KEY, KEY + VALUE), f32)),
    ]
    in_specs = [
        wide, wide, wide, shared(1, VALUE), tall(length, KEY), tall(length, KEY), deep(1, length),
        deep(length, CHUNK), deep(length, KEY),
    ]
    args = (dgated, mixed, gate_pre, gain, qn, kn, ld, att, w)
    return call_heads(gate_back_kernel, heads, in_specs, outputs, [], args)


def run_backward(
    gstate, after, dmixed, dcorr, begin, corr, inverse, att, u, w, qn, kn, vn,
    query_ext, key_ext, value_ext, conv_query, conv_key, conv_value, ld, beta,
):
    length = qn.shape[0]
    heads = ld.shape[0]
    states = after.shape[1]
    taps = conv_query.shape[0]
    narrow, wide = tall(length, KEY), tall(length, VALUE)
    ncols, wcols = heads * KEY, heads * VALUE
    outputs = [
        (tall(length + EDGE, KEY), shape_of((length + EDGE, ncols), bf16)),
        (tall(length + EDGE, KEY), shape_of((length + EDGE, ncols), bf16)),
        (tall(length + EDGE, VALUE), shape_of((length + EDGE, wcols), bf16)),
        (tall(taps, KEY), shape_of((taps, ncols), f32)),
        (tall(taps, KEY), shape_of((taps, ncols), f32)),
        (tall(taps, VALUE), shape_of((taps, wcols), f32)),
        (deep(1, length), shape_of((heads, 1, length), f32)),
        (deep(1, length), shape_of((heads, 1, length), f32)),
    ]
    in_specs = [
        deep(KEY, VALUE), deep(states, KEY + VALUE), deep(length, VALUE), deep(length, VALUE),
        deep(states, VALUE), deep(length, VALUE), deep(length, CHUNK), deep(length, CHUNK),
        deep(length, VALUE), deep(length, KEY),
        narrow, narrow, wide,
        tall(length + EDGE, KEY), tall(length + EDGE, KEY), tall(length + EDGE, VALUE),
        tall(taps, KEY), tall(taps, KEY), tall(taps, VALUE),
        deep(1, length), deep(1, length),
    ]
    scratch = [
        pltpu.VMEM((length, KEY), f32), pltpu.VMEM((length, KEY), f32), pltpu.VMEM((length, VALUE), f32),
        pltpu.VMEM((length + 2 * EDGE, KEY), f32), pltpu.VMEM((length + EDGE, KEY), f32),
        pltpu.VMEM((length + 2 * EDGE, VALUE), f32), pltpu.VMEM((length + EDGE, VALUE), f32),
    ]
    args = (
        gstate, after, dmixed, dcorr, begin, corr, inverse, att, u, w, qn, kn, vn,
        query_ext, key_ext, value_ext, conv_query, conv_key, conv_value, ld, beta,
    )
    return call_heads(backward_kernel, heads, in_specs, outputs, scratch, args)


def ffn_kernel(
    odd_ref, x_ref, kept_ref, other_ref, gain_ref, wg_ref, wu_ref, wd_ref, cot_ref,
    normed_ref, hidden_ref, dgate_ref, dup_ref, own_ref, sent_ref,
):
    mine = pl.program_id(0) == odd_ref[0]
    branch = jnp.where(mine, kept_ref[...].astype(f32), other_ref[...].astype(f32))
    middle = x_ref[...].astype(f32) + branch
    normed = row_norm(middle, gain_ref[...]).astype(bf16)
    normed_ref[...] = normed
    gate = dot(normed, wg_ref[...], 1, 1)
    up = dot(normed, wu_ref[...], 1, 1)
    sig = jax.nn.sigmoid(gate)
    act = gate * sig
    hidden_ref[...] = (act * up).astype(bf16)
    dhidden = dot(cot_ref[...], wd_ref[...], 1, 1)
    dgate = (dhidden * up * (sig * (1.0 + gate * (1.0 - sig)))).astype(bf16)
    dup = (dhidden * act).astype(bf16)
    dgate_ref[...] = dgate
    dup_ref[...] = dup
    part = (dot(dgate, wg_ref[...]) + dot(dup, wu_ref[...])).astype(bf16)

    @pl.when(mine)
    def give_own():
        own_ref[...] = part

    @pl.when(jnp.logical_not(mine))
    def give_sent():
        sent_ref[...] = part


def run_ffn(odd, x, kept, other, gain, w_ffn_gate, w_ffn_up, w_ffn_down, cotangent):
    length, width = x.shape
    hidden = w_ffn_gate.shape[0]
    block = length // 2

    def rows(cols):
        return pl.BlockSpec((block, cols), lambda i: (i, 0))

    return pl.pallas_call(
        ffn_kernel,
        grid=(length // block,),
        in_specs=[
            pl.BlockSpec(memory_space=pltpu.SMEM),
            rows(width), shared(block, width), shared(block, width), shared(1, width), shared(hidden, width), shared(hidden, width),
            shared(hidden, width), rows(width),
        ],
        out_specs=[rows(width), rows(hidden), rows(hidden), rows(hidden), shared(block, width), shared(block, width)],
        out_shape=[
            shape_of((length, width), bf16),
            shape_of((length, hidden), bf16),
            shape_of((length, hidden), bf16),
            shape_of((length, hidden), bf16),
            shape_of((block, width), bf16),
            shape_of((block, width), bf16),
        ],
        compiler_params=pltpu.CompilerParams(vmem_limit_bytes=VMEM_BYTES),
        cost_estimate=COST,
    )(odd, x, kept, other, gain, w_ffn_gate, w_ffn_up, w_ffn_down, cotangent)


def shard_kernel(plan, count, piece, places_ref, *refs):
    outs = refs[-2 * len(plan) :]
    for number, pairs in enumerate(plan):
        for which in range(2):
            out_ref = outs[2 * number + which]
            chosen = {}
            at = 0
            for left, right in pairs:
                if left not in chosen:
                    chosen[left] = jnp.concatenate(
                        [
                            refs[left][:, pl.ds(pl.multiple_of(places_ref[number, which, g] * piece, 128), piece)]
                            for g in range(count)
                        ],
                        axis=1,
                    )
                width = refs[right].shape[1]
                out_ref[:, at : at + width] = dot(chosen[left], refs[right][...], 0, 0).astype(out_ref.dtype)
                at += width
            if at < out_ref.shape[1]:
                out_ref[:, at:] = jnp.zeros((out_ref.shape[0], out_ref.shape[1] - at), out_ref.dtype)


def shard_products(chains, home_type):
    size = lax.axis_size("seq")
    here = lax.axis_index("seq")
    count = size // 2
    slots = jnp.arange(count, dtype=jnp.int32)
    places = []
    for bit, pairs in chains:
        shards = (slots // 2**bit) * 2 ** (bit + 1) + slots % 2**bit
        mine = (here // 2**bit) % 2
        places.append(jnp.stack([shards + (1 - mine) * 2**bit, shards + mine * 2**bit]))
    width = chains[0][1][0][0].shape[1]
    piece = width // size
    if piece % 128:
        results = []
        for (bit, pairs), chosen in zip(chains, places):
            parts = []
            for which, kind in ((0, bf16), (1, home_type)):
                columns = [
                    lax.dot_general(
                        jnp.take(left.reshape(-1, size, piece), chosen[which], axis=1).reshape(
                            left.shape[0], -1
                        ),
                        right,
                        (((0,), (0,)), ((), ())),
                        preferred_element_type=f32,
                    )
                    for left, right in pairs
                ]
                parts.append(jnp.concatenate(columns, axis=1).astype(kind))
            results.append(tuple(parts))
        return results
    args, plan, out_shape = [], [], []

    def slot_of(array):
        for number, known in enumerate(args):
            if known is array:
                return number
        args.append(array)
        return len(args) - 1

    for bit, pairs in chains:
        plan.append([(slot_of(left), slot_of(right)) for left, right in pairs])
        total = -(-sum(right.shape[1] for left, right in pairs) // 128) * 128
        out_shape += [shape_of((count * piece, total), bf16), shape_of((count * piece, total), home_type)]
    whole = pl.BlockSpec(memory_space=pltpu.VMEM)
    flat = pl.pallas_call(
        functools.partial(shard_kernel, plan, count, piece),
        in_specs=[pl.BlockSpec(memory_space=pltpu.SMEM)] + [whole] * len(args),
        out_specs=[whole] * len(out_shape),
        out_shape=out_shape,
        compiler_params=pltpu.CompilerParams(vmem_limit_bytes=VMEM_BYTES),
        cost_estimate=COST,
    )(jnp.stack(places), *args)
    return [(flat[2 * number], flat[2 * number + 1]) for number in range(len(chains))]


def turn_kernel(cuts, *refs):
    ins, outs = refs[: len(cuts)], refs[len(cuts) :]
    for (low, high), in_ref, out_ref in zip(cuts, ins, outs):
        out_ref[...] = in_ref[:, low:high].T


def turned(pieces):
    if pieces[0][0].shape[0] % 128:
        return [array[:, low:high].T for array, low, high in pieces]
    whole = pl.BlockSpec(memory_space=pltpu.VMEM)
    return pl.pallas_call(
        functools.partial(turn_kernel, [(low, high) for array, low, high in pieces]),
        in_specs=[whole] * len(pieces),
        out_specs=[whole] * len(pieces),
        out_shape=[shape_of((high - low, array.shape[0]), f32) for array, low, high in pieces],
        compiler_params=pltpu.CompilerParams(vmem_limit_bytes=VMEM_BYTES),
        cost_estimate=COST,
    )(*[array for array, low, high in pieces])


def from_behind(block, axis, distance):
    devices = range(lax.axis_size(axis))
    route = [(i - distance, i) for i in devices if i - distance in devices]
    return lax.ppermute(block, axis, route)


def swap_with(block, axis, distance):
    route = [(i, i ^ distance) for i in range(lax.axis_size(axis))]
    return lax.ppermute(block, axis, route)


def exchange_rounds(tasks, box=None, beside=None):
    results, asked = [None] * len(tasks), {}

    def advance(which, got):
        try:
            asked[which] = tasks[which].send(got)
        except StopIteration as end:
            results[which] = end.value
            asked.pop(which, None)

    for which in range(len(tasks)):
        advance(which, None)
    number = 0
    while asked:
        number += 1
        got = {which: tuple(exchange() for exchange in wanted) for which, wanted in asked.items()}
        names = [name for name in (beside or {}).get(number, ()) if name in box]
        got, values = lax.optimization_barrier((got, [box[name] for name in names]))
        for name, value in zip(names, values):
            box[name] = value
        if box is not None:
            box["arrived"] = got
        for which in list(asked):
            advance(which, got[which])
    return results


def swap(block, axis, distance):
    return functools.partial(swap_with, block, axis, distance)


def together(first, second):
    wanted = [next(first)[0], next(second)[0]]
    while True:
        blocks = [exchange.args[0] for exchange in wanted]
        if wanted[0].args[1:] == wanted[1].args[1:]:
            width = blocks[0].shape[-1]
            (both,) = yield [swap(jnp.concatenate(blocks, axis=-1), *wanted[0].args[1:])]
            got = (both[..., :width], both[..., width:])
        else:
            got = yield wanted
        results = []
        for which, task in enumerate((first, second)):
            try:
                wanted[which] = task.send((got[which],))[0]
            except StopIteration as end:
                results.append(end.value)
        if results:
            return results


def pause(rounds):
    for _ in range(rounds):
        yield []


def group_sum(block, axis):
    size = lax.axis_size(axis)
    distance = 1
    while distance < size:
        reach = min(4, size // distance)
        arrived = yield [swap(block, axis, distance * step) for step in range(1, reach)]
        if reach == 4:
            block = (block + arrived[0]) + (arrived[1] + arrived[2])
        else:
            block = block + arrived[0]
        distance *= reach
    return block


def head_is_odd():
    return lax.axis_index("head") % 2


def halves_of(block):
    rows = block.shape[0] // 2
    odd = head_is_odd() == 1
    low, high = block[:rows], block[rows:]
    return jnp.where(odd, high, low), jnp.where(odd, low, high)


def whole_of(halves):
    kept, other = halves
    odd = head_is_odd() == 1
    return jnp.concatenate([jnp.where(odd, other, kept), jnp.where(odd, kept, other)], axis=0)


def sum_over_heads(halves):
    own, sent = halves
    (got,) = yield [swap(sent, "head", 1)]
    own = own.astype(f32) + got.astype(f32)
    distance = 2
    while distance < lax.axis_size("head"):
        sent = own.astype(bf16)
        (got,) = yield [swap(sent, "head", distance)]
        own = sent.astype(f32) + got.astype(f32)
        distance *= 2
    kept = own.astype(bf16)
    (other,) = yield [swap(kept, "head", 1)]
    return kept, other


def exclusive_scan(joined, sign):
    own_t, own_b = joined[..., :KEY], joined[..., KEY:]
    send = joined
    before_t = before_b = None
    distance = 1
    size = lax.axis_size("seq")

    def product(a, b):
        return jnp.einsum("hij,hjk->hik", a, b, precision=lax.Precision.HIGH)

    while distance < size:
        last = distance * 2 >= size
        sent = (send[..., KEY:] if last else send).astype(bf16)
        (got,) = yield [functools.partial(from_behind, sent, "seq", sign * distance)]
        got = got.astype(f32)
        if before_t is None:
            before_t, before_b = got[..., :KEY], got[..., KEY:]
        else:
            moved = product(before_t, got)
            if last:
                before_b = before_b + moved
            else:
                before_t, before_b = moved[..., :KEY], before_b + moved[..., KEY:]
        if not last:
            send = product(own_t, jnp.concatenate([before_t, before_b], axis=-1))
            send = jnp.concatenate([send[..., :KEY], send[..., KEY:] + own_b], axis=-1)
        distance *= 2
    return before_b


def halving_scatter(products, order, pauses=(), box=None, name=None, hold=None):
    size = lax.axis_size("seq")
    bits = size.bit_length() - 1
    here = lax.axis_index("seq")
    order = [bit for bit in order if bit < bits] + list(range(len(order), bits))
    pauses = list(pauses) + [0] * bits
    away, home = products
    (got,) = yield [swap(away, "seq", 2 ** order[0])]
    held = home.astype(f32) + got.astype(f32)
    axes = [bit for bit in range(bits)[::-1] if bit != order[0]]
    held = held.reshape((2,) * (bits - 1) + (held.shape[0] // 2 ** (bits - 1), held.shape[1]))
    for number, bit in enumerate(order[1:]):
        axis = axes.index(bit)
        axes.remove(bit)
        mine = (here // 2**bit) % 2
        sent = lax.dynamic_index_in_dim(held, 1 - mine, axis, keepdims=False).astype(bf16)
        if pauses[number]:
            box[name] = sent
            yield from pause(pauses[number])
            sent = box[name]
        elif hold is not None:
            sent = hold(sent)
        (got,) = yield [swap(sent, "seq", 2**bit)]
        held = lax.dynamic_index_in_dim(held, mine, axis, keepdims=False) + got.astype(f32)
    return held


def inner_rows(first_operand, second_operand):
    return lax.dot_general(
        first_operand, second_operand, (((0,), (0,)), ((), ())), preferred_element_type=f32
    )


def matmul_bf(first_operand, second_operand):
    return jnp.dot(first_operand, second_operand, preferred_element_type=f32)


def against_rows(first_operand, second_operand):
    return lax.dot_general(
        first_operand, second_operand, (((1,), (1,)), ((), ())), preferred_element_type=f32
    )


def per_device(
    block_input,
    norm1_gain,
    w_query,
    w_key,
    w_value,
    w_gate,
    w_decay,
    w_beta,
    conv_query,
    conv_key,
    conv_value,
    decay_rate,
    out_gain,
    w_out,
    norm2_gain,
    w_ffn_gate,
    w_ffn_up,
    w_ffn_down,
    cotangent,
):
    length = block_input.shape[0]
    head_count = w_decay.shape[1]
    key_cols = w_query.shape[1]
    value_cols = w_value.shape[1]
    ff_cols = w_ffn_gate.shape[1]
    edge_input = from_behind(block_input[length - EDGE :], "seq", 1)
    gain1 = norm1_gain.astype(f32)
    (
        normed, normed_ext, decay_cols, query_ext, key_ext, value_ext, log_decay, beta3,
        qn, kn, vn, inverse, att, u, w, starts, composite,
    ) = prepare(
        block_input, edge_input, gain1[None], w_query, w_key, w_value, w_decay.T, w_beta.T,
        decay_rate[None], conv_query, conv_key, conv_value,
    )
    inputs32 = block_input.astype(f32)
    gate_pre = matmul_bf(normed, w_gate)
    box = {"gate": gate_pre}
    (state_in,) = exchange_rounds([exclusive_scan(composite, 1)], box, {1: ["gate"]})
    gate_pre = box["gate"]
    gain_row = out_gain.astype(f32)[None]
    odd = head_is_odd().astype(jnp.int32).reshape(1)
    gated, mixed, corr, begin, branch_own, branch_sent = run_forward(
        odd,
        qn, log_decay, att, u, w, starts, state_in, gate_pre, gain_row, w_out
    )
    (branch_halves,) = exchange_rounds([sum_over_heads((branch_own, branch_sent))])
    branch = whole_of(branch_halves)
    gain2 = norm2_gain.astype(f32)
    normed2, hidden, grad_fgate, grad_fup, part_own, part_sent = run_ffn(
        odd, block_input, *branch_halves, gain2[None], w_ffn_gate.T, w_ffn_up.T, w_ffn_down, cotangent
    )
    bits = lax.axis_size("seq").bit_length() - 1
    near, far = 0, min(1, bits - 1)
    half = ff_cols // 2 // 128 * 128
    ffn_near, ffn_far = shard_products(
        [
            (near, [(normed2, grad_fgate), (cotangent, hidden[:, :half])]),
            (far, [(normed2, grad_fup), (cotangent, hidden[:, half:])]),
        ],
        bf16,
    )
    box = {}

    def after_scan(sent):
        return lax.optimization_barrier((sent, box["state"]))[0]

    ffn_tasks = [
        halving_scatter(ffn_near, [0, 1], [bits - 2, 0], box, "sent near", after_scan),
        halving_scatter(ffn_far, [1, 0], [bits - 2, 0], box, "sent far", after_scan),
    ]
    ffn_got = [tuple(exchange() for exchange in next(task)) for task in ffn_tasks]
    box["away"] = (ffn_near[0], ffn_far[0])
    (back_halves,) = exchange_rounds([sum_over_heads((part_own, part_sent))], box, {2: ["away"]})
    grad_normed2 = whole_of(back_halves).astype(f32)
    middle = inputs32 + branch.astype(f32)
    norm2_back = jax.vjp(row_norm, middle, gain2)[1]
    ffn_part = matmul_bf(hidden, w_ffn_down).astype(bf16)
    grad_middle_n, grad_gain2 = norm2_back(grad_normed2)
    grad_middle = cotangent.astype(f32) + grad_middle_n
    grad_branch = grad_middle.astype(bf16)
    grad_gated = against_rows(grad_branch, w_out)
    grad_gp, grad_mixed, grad_corr, grad_outgain, after, composite_back = gate_back(
        grad_gated, mixed, gate_pre, gain_row, qn, kn, log_decay, att, w
    )
    box["ffn part"] = ffn_part
    box["scalars"] = (decay_cols, decay_rate)
    pad_rows = ((length - 8, 0), (0, 0))
    taps_count = conv_query.shape[0]
    width = w_query.shape[0]

    def main_task():
        grad_state = yield from exclusive_scan(composite_back, -1)
        box["state"] = grad_state
        dq, dk, dv, taps_q, taps_k, taps_v, grad_log, grad_beta = run_backward(
            grad_state, after, grad_mixed, grad_corr, begin, corr, inverse, att, u, w,
            qn, kn, vn, query_ext, key_ext, value_ext,
            conv_query, conv_key, conv_value, log_decay, beta3,
        )
        box["late"] = shard_products(
            [(near, [(normed_ext, dq), (normed_ext, dk)]), (far, [(normed_ext, dv)])], f32
        )
        part_ext = against_rows(dq, w_query) + against_rows(dk, w_key) + against_rows(dv, w_value)
        decay_now, rate_now = box["scalars"]
        decay_pre = decay_now.T
        soft = jax.nn.softplus(decay_pre)
        rate = rate_now[:, None]
        beta_gate = beta3.reshape(head_count, length)
        grad_log = grad_log.reshape(head_count, length)
        grad_beta = grad_beta.reshape(head_count, length)
        grad_dp = (-rate * jax.nn.sigmoid(decay_pre) * grad_log).astype(bf16)
        grad_bp = (beta_gate * (1.0 - beta_gate) * grad_beta).astype(bf16)
        grad_rate = -jnp.sum(grad_log * soft, axis=1)
        grad_scalars = jnp.concatenate([grad_dp, grad_bp], axis=0)
        w_scalars = jnp.concatenate([w_decay, w_beta], axis=1)
        edges = part_ext[EDGE - 8 : EDGE]
        part = (
            part_ext[EDGE:]
            + against_rows(grad_gp, w_gate)
            + lax.dot_general(
                grad_scalars, w_scalars, (((0,), (1,)), ((), ())), preferred_element_type=f32
            )
        )
        edge_normal = row_norm(edge_input[EDGE - 8 :].astype(f32), 1.0)
        gain_part = jnp.sum(part * row_norm(inputs32, 1.0), axis=0) + jnp.sum(edges * edge_normal, axis=0)
        gains = jnp.concatenate([gain_part, jnp.sum(grad_outgain, axis=(0, 1))])
        box["shared"] = jnp.pad(gains, (0, 2 * width - gains.shape[0])).reshape(-1, 128)
        box["small"] = jnp.concatenate(
            [
                jnp.concatenate([taps_q, taps_k, taps_v], axis=1),
                grad_gain2[None],
                jnp.pad(grad_rate, (0, width - head_count))[None],
                matmul_bf(grad_scalars, normed),
            ],
            axis=0,
        )
        (edges,) = yield [functools.partial(from_behind, edges, "seq", -1)]
        part = part + jnp.pad(edges, pad_rows)
        kept, other = yield from sum_over_heads(halves_of(part.astype(bf16)))
        return whole_of((kept, other))

    def ffn_rest(task, got, name):
        wanted = [lambda block=block: block for block in got]
        try:
            while True:
                wanted = task.send((yield wanted))
        except StopIteration as end:
            held = end.value
        yield from pause(1)
        held = lax.optimization_barrier((held, box["arrived"]))[0]
        box[name] = turned([(held, 0, ff_cols), (held, ff_cols, ff_cols + (half if name == "near" else ff_cols - half))])

    def ffn_sum_task():
        yield from pause(1)
        steps = sum_over_heads(halves_of(box["ffn part"]))
        got = yield next(steps)
        wanted = steps.send(got)
        yield from pause(bits - 2)
        try:
            while True:
                wanted = steps.send((yield wanted))
        except StopIteration as end:
            box["out"] = (middle + whole_of(end.value).astype(f32)).astype(bf16)

    def mid_task():
        yield from pause(bits)
        products = shard_products([(near, [(grad_branch, gated)]), (far, [(normed, grad_gp)])], f32)
        products = after_scan(products)
        first, second = halving_scatter(products[0], [0, 1]), halving_scatter(products[1], [1, 0])
        grad_wout, grad_wg = yield from together(first, second)
        box["mid"] = (*turned([(grad_wout, 0, grad_wout.shape[1])]), grad_wg)

    def late_task():
        yield from pause(bits + 1)
        first, second = box["late"]
        return (yield from together(halving_scatter(first, [0, 1]), halving_scatter(second, [1, 0])))

    def small_task():
        yield from pause(bits + 1)
        shared = yield from group_sum(box["shared"], "head")
        rows = jnp.concatenate([box["small"], shared.reshape(-1, width)], axis=0)
        return (yield from group_sum(rows, "seq"))

    grad_normed, late, small = exchange_rounds(
        [main_task(), late_task(), small_task(), mid_task(), ffn_sum_task()]
        + [ffn_rest(task, got, name) for task, got, name in zip(ffn_tasks, ffn_got, ("near", "far"))],
        box,
        {1: ["ffn part", "scalars"], 2: ["sent near", "sent far"], bits + 4: ["near", "far", "out"]},
    )[:3]
    late_qk, late_v = late
    grad_wout, grad_wg = box["mid"]
    grad_wfg, down_near = box["near"]
    grad_wfu, down_far = box["far"]
    layer_out = box["out"]
    shared_sum = small[-2:].reshape(-1)
    norm1_back = jax.vjp(row_norm, inputs32, gain1)[1]
    grad_input = grad_middle + norm1_back(grad_normed.astype(f32))[0]
    taps_sum = small[:taps_count]
    gain2_sum = small[taps_count]
    rate_sum = small[taps_count + 1, :head_count]
    scalars_sum = small[taps_count + 2 : taps_count + 2 + 2 * head_count]
    gain1_sum, outgain_sum = shared_sum[:width], shared_sum[width : width + VALUE]

    def own_part(vec):
        piece = vec.shape[-1] // lax.axis_size("seq")
        return lax.dynamic_slice_in_dim(vec, lax.axis_index("seq") * piece, piece, axis=-1)

    scalars_sum = own_part(scalars_sum).T
    return (
        layer_out,
        grad_input,
        own_part(gain1_sum),
        late_qk[:, :key_cols],
        late_qk[:, key_cols:],
        late_v,
        grad_wg,
        scalars_sum[:, :head_count],
        scalars_sum[:, head_count:],
        taps_sum[:, :key_cols],
        taps_sum[:, key_cols : 2 * key_cols],
        taps_sum[:, 2 * key_cols :],
        rate_sum,
        own_part(outgain_sum),
        grad_wout,
        own_part(gain2_sum),
        grad_wfg.T,
        grad_wfu.T,
        jnp.concatenate([down_near, down_far], axis=0),
    )


def solution(mesh):
    return jax.shard_map(
        per_device,
        mesh=mesh,
        in_specs=(
            P("seq", None),
            P(),
            P(None, "head"),
            P(None, "head"),
            P(None, "head"),
            P(None, "head"),
            P(None, "head"),
            P(None, "head"),
            P(None, "head"),
            P(None, "head"),
            P(None, "head"),
            P("head"),
            P(),
            P("head", None),
            P(),
            P(None, "head"),
            P(None, "head"),
            P("head", None),
            P("seq", None),
        ),
        out_specs=(
            P("seq", None),
            P("seq", None),
            P("seq"),
            P("seq", "head"),
            P("seq", "head"),
            P("seq", "head"),
            P("seq", "head"),
            P("seq", "head"),
            P("seq", "head"),
            P(None, "head"),
            P(None, "head"),
            P(None, "head"),
            P("head"),
            P("seq"),
            P("head", "seq"),
            P("seq"),
            P("seq", "head"),
            P("seq", "head"),
            P("head", "seq"),
        ),
        check_vma=False,
    )
```
